32 devices in a mesh: groups: 2 (over x), blk: 16 (over z, y, core).
Axes of the slice: x: 2, y: 2, z: 4, core: 2. Of those that a mesh axis runs over, the one named last changes fastest.
Arguments:
- rhs: bfloat16 [512, 64, 128], P(('groups', 'blk')), parts along dimension 0, may hold values from -6 to 6
- near_blocks: bfloat16 [4096, 128, 128], P(('groups', 'blk')), parts along dimension 0, may hold values from -0.1875 to 0.1875
- near_owner: int32 [4096, 1], P(('groups', 'blk')), parts along dimension 0, may hold values from 0 to 15; in each aligned block of 128 rows (0 to 127, 128 to 255, ...) at most 16 rows name the same one
- near_slot: int32 [4096], P(('groups', 'blk')), parts along dimension 0, may hold values from 0 to 15
- near_offset: int32 [4096], P(('groups', 'blk')), parts along dimension 0, may hold values from -16 to 16
- far_coupling: bfloat16 [8192, 16, 16], P(('groups', 'blk')), parts along dimension 0, may hold values from -1.5 to 1.5
- far_slot: int32 [8192], P(('groups', 'blk')), parts along dimension 0, may hold values from 0 to 15
- far_dev: int32 [8192, 1], P(('groups', 'blk')), parts along dimension 0, may hold values from 0 to 15; in each aligned block of 256 rows (0 to 255, 256 to 511, ...) at most 32 rows name the same one
- far_cslot: int32 [8192], P(('groups', 'blk')), parts along dimension 0, may hold values from 0 to 15
- basis_out: bfloat16 [512, 16, 128], P(('groups', 'blk')), parts along dimension 0, may hold values from -0.375 to 0.375
- basis_in: bfloat16 [512, 16, 128], P(('groups', 'blk')), parts along dimension 0, may hold values from -0.5 to 0.5
Outputs:
- field: bfloat16 [512, 64, 128], P(('groups', 'blk')), parts along dimension 0
The draws below stay inside these ranges and needn't reach their ends.
There are 2 independent parts, one for each index of `groups`. The reference program is written for one: setup_inputs(seed, part) draws one part's arguments, and reference() takes and returns one part's arrays. A program takes and returns all parts, laid end to end along the dimension named above; each array names one. Nothing has to cross between parts.
Inputs may be any that keep to these rules, and one draw needn't show every extreme that they name: `near_owner`: among the rows of one device, at most 16 have the same owner, and some owner has exactly 16 of them in every draw. `far_dev`: among the rows of one device, at most 32 name the same device, and some device is named exactly 32 times in every draw.
All inputs are finite; a program needn't handle non-finite values.
Results may differ from the reference program's by a relative error of at most 0.0051.
Values may be sent and summed in bfloat16 or wider, within the bound.
No kernel may reach another device: no remote copies, remote signals or barrier semaphores. Data moves between devices by JAX's collectives and lax.ppermute only.
A program may use at most 128 MiB of HBM per device.

```python
import math
import jax
import jax.numpy as jnp
import numpy as np
from jax import lax

B = 128
R = 64
K = 16
FAR_PER = 16
C_DEV = 16
NC = 256
NB_DEV = 128
FAR_DEV = 256
CAP = 16
FCAP = 32
NBLOCKS = 2048
FARS = 4096
N_BLK = 16


def with_ends(drawn, key, smallest, largest):
    extent = drawn.shape
    index_at = [jax.random.randint(jax.random.fold_in(key, axis), (), 0, extent[axis]) for axis in range(len(extent))]
    drawn = drawn.at[tuple(index_at)].set(smallest)
    longest = extent.index(max(extent))
    index_at[longest] = (index_at[longest] + 1) % extent[longest]
    return drawn.at[tuple(index_at)].set(largest)


def steps_of(own_key, extent, split, low, high):
    gain = 1.0
    for axis_at, parts in split:
        heights = jax.random.uniform(jax.random.fold_in(jax.random.fold_in(own_key, 6), axis_at), (parts,), jnp.float32, low / len(split), high / len(split))
        gain = gain * jnp.repeat(jnp.exp(heights), extent[axis_at] // parts).reshape((-1,) + (1,) * (len(extent) - 1 - axis_at))
    return gain


def deal_out(stream_key, own, number, rows, number_of, top, bound, skew):
    sequence = jax.random.permutation(stream_key, number_of)
    packed, ordinary = load_shares(number_of, rows * top, bound, skew, True), load_shares(number_of, rows * top, bound, skew, False)
    places = jnp.arange(number_of)

    def named(lengths, turn):
        used = int((lengths > 0).sum())
        fixed = max(1, used // 4)
        moved = fixed + (places - fixed + turn * (used - fixed)) % max(1, number_of - fixed)
        return jnp.zeros((number_of,), jnp.int32).at[sequence[jnp.where(places < fixed, places, moved)]].set(jnp.asarray(lengths, jnp.int32))

    lengths = jnp.where(number % 4 == 0, named(packed, number // 4), named(ordinary, number - number // 4 - 1))
    mixed = jax.random.permutation(jax.random.fold_in(own, 3), number_of)
    giver, receiver = mixed[0:number_of // 2 * 2:2], mixed[1:number_of // 2 * 2:2]
    margin = jnp.minimum(lengths[giver] - 1, bound - lengths[receiver]) // 2
    margin = jnp.where((giver == sequence[0]) | (receiver == sequence[0]) | (lengths[receiver] == 0), 0, jnp.maximum(margin, 0))
    moved = jax.random.randint(jax.random.fold_in(own, 4), (number_of // 2,), 0, 1 << 20) % (margin + 1)
    lengths = lengths.at[giver].add(-moved).at[receiver].add(moved)
    labels = jnp.searchsorted(jnp.cumsum(lengths), jnp.arange(rows * top), side="right").astype(jnp.int32)
    table = labels.reshape(top, rows).T
    table = table[jax.random.permutation(jax.random.fold_in(own, 1), rows)]
    turn = jax.random.randint(jax.random.fold_in(own, 2), (rows, 1), 0, top)
    return jnp.take_along_axis(table, (jnp.arange(top)[None, :] + turn) % top, axis=1)


def load_shares(amount, total, most, skew, full):
    weights = [(1 << 20) // math.isqrt(rank ** skew) + 1 for rank in range(1, amount + 1)]
    largest = most if full else min(most, max(-(-total // amount), total * weights[0] // sum(weights)))
    least = 1 if total - largest >= amount - 1 else 0
    counts, surplus = [largest] + [least] * (amount - 1), total - largest - least * (amount - 1)
    while surplus > 0:
        candidates = [i for i in range(1, amount) if counts[i] < largest] or [i for i in range(1, amount) if counts[i] < most]
        whole, remaining = sum([weights[i] for i in candidates]), surplus
        for i in candidates:
            extra = min(most - counts[i], max(1, remaining * weights[i] // whole), surplus)
            counts[i] = counts[i] + extra
            surplus = surplus - extra
    return np.array(counts)


def normal_values(key, dims, scale, most, cuts=(), kind=jnp.bfloat16):
    result = jax.random.normal(key, dims, jnp.float32) * scale
    if len(cuts) > 0:
        result = steps_of(key, dims, cuts, -0.22, 0.18) * result
    return jnp.clip(result, min=-most, max=most).astype(kind)


def setup_inputs(seed: int = 0, part: int = 0) -> dict:
    arg_keys = jax.random.split(jax.random.key(seed), 12)
    own_keys = jax.random.split(jax.random.fold_in(arg_keys[11], part), 12)
    rhs = normal_values(own_keys[0], (NC, R, B), 1.0, 6.0, ((0, 16),))
    near_blocks = normal_values(own_keys[1], (NBLOCKS, B, B), (8 * B) ** -0.5, 0.1875, ((0, 16),))
    near_owner_keys = jax.random.split(jax.random.fold_in(own_keys[2], 1), NBLOCKS // NB_DEV)
    near_owner_turns = jax.random.permutation(jax.random.fold_in(own_keys[2], 3), NBLOCKS // NB_DEV)
    near_owner = jax.vmap(lambda own, number: deal_out(jax.random.fold_in(own_keys[2], 2), own, number, NB_DEV, N_BLK, 1, CAP, 2))(near_owner_keys, near_owner_turns).reshape((NBLOCKS, 1))
    near_slot = with_ends(jax.random.randint(own_keys[3], (NBLOCKS,), 0, C_DEV), jax.random.fold_in(own_keys[3], 1), 0, C_DEV - 1).astype(jnp.int32)
    near_offset = with_ends(jax.random.randint(own_keys[4], (NBLOCKS,), 0 - C_DEV, C_DEV + 1), jax.random.fold_in(own_keys[4], 1), 0 - C_DEV, C_DEV).astype(jnp.int32)
    far_coupling = normal_values(own_keys[5], (FARS, K, K), K ** -0.5, 1.5, ((0, 16),))
    far_slot = with_ends(jax.random.randint(own_keys[6], (FARS,), 0, C_DEV), jax.random.fold_in(own_keys[6], 1), 0, C_DEV - 1).astype(jnp.int32)
    far_dev_keys = jax.random.split(jax.random.fold_in(own_keys[7], 1), FARS // FAR_DEV)
    far_dev_turns = jax.random.permutation(jax.random.fold_in(own_keys[7], 3), FARS // FAR_DEV)
    far_dev = jax.vmap(lambda own, number: deal_out(jax.random.fold_in(own_keys[7], 2), own, number, FAR_DEV, N_BLK, 1, FCAP, 1))(far_dev_keys, far_dev_turns).reshape((FARS, 1))
    far_cslot = with_ends(jax.random.randint(own_keys[8], (FARS,), 0, C_DEV), jax.random.fold_in(own_keys[8], 1), 0, C_DEV - 1).astype(jnp.int32)
    basis_out = normal_values(own_keys[9], (NC, K, B), (FAR_PER * K) ** -0.5, 0.375, ((0, 16),))
    basis_in = normal_values(own_keys[10], (NC, K, B), B ** -0.5, 0.5, ((0, 16),))
    return dict(rhs=rhs, near_blocks=near_blocks, near_owner=near_owner, near_slot=near_slot, near_offset=near_offset, far_coupling=far_coupling, far_slot=far_slot, far_dev=far_dev, far_cslot=far_cslot, basis_out=basis_out, basis_in=basis_in)


def reference(rhs, near_blocks, near_owner, near_slot, near_offset, far_coupling, far_slot, far_dev, far_cslot, basis_out, basis_in):
    row_ids = near_owner[:, 0] * C_DEV + near_slot
    col_ids = jnp.mod(row_ids + near_offset, NC).astype(jnp.int32)
    block_sets = near_blocks.reshape(N_BLK, NB_DEV, B, B)
    row_sets = row_ids.reshape(N_BLK, NB_DEV)
    col_sets = col_ids.reshape(N_BLK, NB_DEV)

    def near_step(total, span):
        blocks, rows, cols = span
        columns = jnp.take(rhs, cols, axis=0).astype(jnp.float32)
        products = jnp.einsum("srj,sij->sri", columns, blocks.astype(jnp.float32))
        return total.at[rows].add(products), None

    near, _ = lax.scan(near_step, jnp.zeros((NC, R, B), jnp.float32), (block_sets, row_sets, col_sets))
    coef = jnp.einsum("ckj,crj->crk", basis_in.astype(jnp.float32), rhs.astype(jnp.float32)).astype(jnp.bfloat16)
    owner_dev = jnp.arange(FARS, dtype=jnp.int32) // FAR_DEV
    far_rows = owner_dev * C_DEV + far_slot
    far_cols = far_dev[:, 0] * C_DEV + far_cslot
    picked = jnp.take(coef, far_cols, axis=0).astype(jnp.float32)
    coupled = jnp.einsum("pkq,prq->prk", far_coupling.astype(jnp.float32), picked)
    gathered = jnp.zeros((NC, R, K), jnp.float32).at[far_rows].add(coupled).astype(jnp.bfloat16)
    far = jnp.einsum("crk,ckb->crb", gathered.astype(jnp.float32), basis_out.astype(jnp.float32))
    return (near + far).astype(jnp.bfloat16)
```

```python
import functools

import jax
import jax.numpy as jnp
from jax import lax
from jax.experimental import pallas as pl
from jax.experimental.pallas import tpu as pltpu
from jax.sharding import PartitionSpec as P

CHUNKS = 2
DENSE_BYTES = 16 << 20
VMEM_BYTES = 48 << 20


def with_halo(cells, sides, width):
    for axis, dim in sides:
        count = lax.axis_size(axis)
        head = lax.slice_in_dim(cells, 0, width, axis=dim)
        tail = lax.slice_in_dim(cells, cells.shape[dim] - width, cells.shape[dim], axis=dim)
        cells = jnp.concatenate(
            [
                lax.ppermute(tail, axis, [(i, (i + 1) % count) for i in range(count)]),
                cells,
                lax.ppermute(head, axis, [((i + 1) % count, i) for i in range(count)]),
            ],
            axis=dim,
        )
    return cells


def place_ranks(targets, count):
    onehot = (targets[:, None] == jnp.arange(count, dtype=jnp.int32)[None, :]).astype(jnp.int32)
    before = jnp.cumsum(onehot, axis=0) - onehot
    return jnp.sum(before * onehot, axis=1)


def routed(
    rhs,
    near_blocks,
    near_owner,
    near_slot,
    near_offset,
    far_coupling,
    far_slot,
    far_dev,
    far_cslot,
    basis_out,
    basis_in,
):
    clusters = rhs.shape[0]
    directions = rhs.shape[1]
    unknowns = rhs.shape[2]
    cycle_size = lax.axis_size("blk")
    stored = near_blocks.shape[0]
    capacity = max(2, 2 * stored // cycle_size)
    owners = near_owner[:, 0]
    target = owners * capacity + place_ranks(owners, cycle_size)
    outbox = (
        jnp.zeros((cycle_size * capacity, unknowns, unknowns), near_blocks.dtype)
        .at[target]
        .set(near_blocks)
    )
    labels = (
        jnp.zeros((cycle_size * capacity, 2), jnp.int32)
        .at[target]
        .set(jnp.stack([near_slot, near_offset], axis=1))
    )
    window = with_halo(rhs, (("blk", 0),), clusters)
    inbox, in_labels = (
        lax.all_to_all(outbox, "blk", split_axis=0, concat_axis=0, tiled=True),
        lax.all_to_all(labels, "blk", split_axis=0, concat_axis=0, tiled=True),
    )
    position = clusters + in_labels[:, 0] + in_labels[:, 1]
    columns = jnp.take(window, position, axis=0)
    products = jnp.einsum("srj,sij->sri", columns, inbox, preferred_element_type=jnp.float32)
    selector = (in_labels[:, 0][None, :] == jnp.arange(clusters, dtype=jnp.int32)[:, None]).astype(
        jnp.float32
    )
    near_sum = jnp.dot(
        selector,
        products.reshape(products.shape[0], -1),
        precision=lax.Precision.HIGHEST,
        preferred_element_type=jnp.float32,
    ).reshape(clusters, directions, unknowns)
    coef_local = jnp.einsum(
        "ckj,crj->crk", basis_in, rhs, preferred_element_type=jnp.float32
    ).astype(jnp.bfloat16)
    rank_k = basis_in.shape[1]
    coef_local = coef_local.reshape(clusters, directions * rank_k)
    pairs = far_slot.shape[0]
    wanted = far_dev[:, 0] * clusters + far_cslot
    piece = lax.all_gather(coef_local, "blk", axis=0, tiled=True)
    chosen = jnp.take(piece, wanted, axis=0)
    coupled = jnp.einsum(
        "pkq,prq->prk",
        far_coupling,
        chosen.reshape(pairs, directions, rank_k),
        preferred_element_type=jnp.float32,
    )
    row_pick = (far_slot[None, :] == jnp.arange(clusters, dtype=jnp.int32)[:, None]).astype(
        jnp.float32
    )
    gathered = jnp.dot(
        row_pick,
        coupled.reshape(pairs, -1),
        precision=lax.Precision.HIGHEST,
        preferred_element_type=jnp.float32,
    )
    gathered = gathered.astype(jnp.bfloat16).reshape(clusters, directions, rank_k)
    far_sum = jnp.einsum("crk,ckb->crb", gathered, basis_out, preferred_element_type=jnp.float32)
    return (near_sum + far_sum).astype(jnp.bfloat16)


def vmem(*shape_dtype):
    return pl.BlockSpec(memory_space=pltpu.VMEM)


def payload_kernel(rhs_ref, basis_ref, out_ref):
    clusters, directions, unknowns = rhs_ref.shape
    rank_k = basis_ref.shape[1]
    half = clusters // 2
    base = clusters * directions
    out_ref[0:base, :] = rhs_ref[...].reshape(base, unknowns)
    for c in range(half):
        parts = [
            lax.dot_general(
                basis_ref[e],
                rhs_ref[e],
                (((1,), (1,)), ((), ())),
                preferred_element_type=jnp.float32,
            )
            for e in (c, c + half)
        ]
        out_ref[base + c * rank_k : base + (c + 1) * rank_k, :] = jnp.concatenate(
            parts, axis=1
        ).astype(out_ref.dtype)


def near_kernel(batch, chunks, pos_ref, row_ref, all_ref, blocks_ref, *rest):
    sends, keeps, acc = rest[:chunks], rest[chunks : 2 * chunks], rest[2 * chunks]
    directions, unknowns = acc.shape[1:]
    acc[...] = jnp.zeros_like(acc)

    def body(step, carry):
        first = step * batch
        products = []
        for k in range(batch):
            start = pl.multiple_of(row_ref[first + k], directions)
            products.append(
                lax.dot_general(
                    all_ref[pl.ds(start, directions), :],
                    blocks_ref[first + k],
                    (((1,), (1,)), ((), ())),
                    preferred_element_type=jnp.float32,
                )
            )
        for k in range(batch):
            at = pos_ref[first + k]
            acc[at] = acc[at] + products[k]
        return carry

    lax.fori_loop(0, blocks_ref.shape[0] // batch, body, 0)
    size = sends[0].shape[0]
    for j in range(chunks):
        keeps[j][...] = acc[2 * j * size : (2 * j + 1) * size]
        sends[j][...] = acc[(2 * j + 1) * size : (2 * j + 2) * size].astype(sends[j].dtype)


def far_kernel(
    step_pairs, row_ref, all_ref, couple_ref, low_ref, high_ref, basis_ref, out_ref, picked, weight
):
    clusters, rank_k, unknowns = basis_ref.shape
    pairs = couple_ref.shape[1] // rank_k
    directions = out_ref.shape[0] // clusters
    span = step_pairs * rank_k

    def pick(p, carry):
        start = pl.multiple_of(row_ref[p], rank_k)
        picked[pl.ds(pl.multiple_of(p * rank_k, rank_k), rank_k), :] = all_ref[
            pl.ds(start, rank_k), :
        ]
        return carry

    lax.fori_loop(0, pairs, pick, 0, unroll=8)
    sums = []
    for hot_ref in (low_ref, high_ref):
        total = jnp.zeros((clusters * rank_k, unknowns), jnp.float32)
        for j in range(pairs // step_pairs):
            lanes = slice(j * span, (j + 1) * span)
            couple = couple_ref[:, lanes]
            for s in range(clusters):
                weight[s * rank_k : (s + 1) * rank_k, :] = couple * hot_ref[s : s + 1, lanes]
            total = total + jnp.dot(
                weight[...], picked[lanes, :], preferred_element_type=jnp.float32
            )
        sums.append(total)
    total = sums[0] + pltpu.roll(sums[1], unknowns // 2, axis=1)
    gathered = jnp.transpose(total)[0:directions, :].astype(jnp.bfloat16)
    lane = lax.broadcasted_iota(jnp.int32, gathered.shape, 1) // rank_k
    basis = basis_ref[...].reshape(clusters * rank_k, unknowns)
    for s in range(clusters):
        own = jnp.where(lane == s, gathered.astype(jnp.float32), 0.0).astype(jnp.bfloat16)
        out_ref[s * directions : (s + 1) * directions, :] = jnp.dot(
            own, basis, preferred_element_type=jnp.float32
        )


def stationary(
    rhs,
    near_blocks,
    near_owner,
    near_slot,
    near_offset,
    far_coupling,
    far_slot,
    far_dev,
    far_cslot,
    basis_out,
    basis_in,
):
    clusters, directions, unknowns = rhs.shape
    rank_k = basis_in.shape[1]
    count = lax.axis_size("blk")
    depth = count // 4
    me = lax.axis_index("blk")
    stored = near_blocks.shape[0]
    pairs = far_slot.shape[0]
    params = pltpu.CompilerParams(vmem_limit_bytes=VMEM_BYTES)

    rows = clusters * directions + clusters // 2 * rank_k
    payload = pl.pallas_call(
        payload_kernel,
        out_shape=jax.ShapeDtypeStruct((rows, unknowns), jnp.bfloat16),
        in_specs=[vmem(), vmem()],
        out_specs=vmem(),
        compiler_params=params,
        name="payload",
    )(rhs, basis_in)
    everyone = lax.all_gather(payload, "blk", axis=0, tiled=True)

    owner = near_owner[:, 0]
    per = clusters // CHUNKS
    relative = (
        ((owner ^ me) & 1) * (2 * depth)
        + (((owner ^ me) >> 1) & 1) * depth
        + ((owner >> 2) - (me >> 2) + depth) % depth
    )
    chunk = near_slot // per
    halves = 2 * depth * per
    position = (
        chunk * (2 * halves) + relative * per + near_slot % per
    )
    column = (owner * clusters + near_slot + near_offset) % (count * clusters)
    column_row = (column // clusters) * rows + (column % clusters) * directions

    send_shape = jax.ShapeDtypeStruct((halves, directions, unknowns), jnp.bfloat16)
    keep_shape = jax.ShapeDtypeStruct((halves, directions, unknowns), jnp.float32)
    partial_sums = pl.pallas_call(
        functools.partial(near_kernel, 4, CHUNKS),
        out_shape=[send_shape] * CHUNKS + [keep_shape] * CHUNKS,
        grid_spec=pltpu.PrefetchScalarGridSpec(
            num_scalar_prefetch=2,
            grid=(1,),
            in_specs=[vmem(), vmem()],
            out_specs=[vmem()] * (2 * CHUNKS),
            scratch_shapes=[
                pltpu.VMEM((count * clusters, directions, unknowns), jnp.float32)
            ],
        ),
        compiler_params=params,
        name="near",
    )(position, column_row, everyone, near_blocks)

    picked_row = (
        far_dev[:, 0] * rows + clusters * directions + (far_cslot % (clusters // 2)) * rank_k
    )
    couple = jnp.transpose(far_coupling, (1, 0, 2)).reshape(rank_k, pairs * rank_k)
    slots = jnp.arange(clusters, dtype=jnp.int32)[:, None]
    high = far_cslot >= clusters // 2

    def hot(mask):
        picks = ((far_slot[None, :] == slots) & mask[None, :]).astype(jnp.bfloat16)
        return jnp.repeat(picks, rank_k, axis=1)

    step_pairs = 32
    far = pl.pallas_call(
        functools.partial(far_kernel, step_pairs),
        out_shape=jax.ShapeDtypeStruct((clusters * directions, unknowns), jnp.float32),
        grid_spec=pltpu.PrefetchScalarGridSpec(
            num_scalar_prefetch=1,
            grid=(1,),
            in_specs=[vmem()] * 5,
            out_specs=vmem(),
            scratch_shapes=[
                pltpu.VMEM((pairs * rank_k, unknowns), jnp.bfloat16),
                pltpu.VMEM((clusters * rank_k, step_pairs * rank_k), jnp.bfloat16),
            ],
        ),
        compiler_params=params,
        cost_estimate=pl.CostEstimate(
            flops=4 * clusters * rank_k * pairs * rank_k * unknowns,
            bytes_accessed=16 << 20,
            transcendentals=0,
        ),
        name="far",
    )(picked_row, everyone, couple, hot(~high), hot(high), basis_out)
    far = far.reshape(clusters, directions, unknowns)

    core = [(i, i ^ 1) for i in range(count)]
    side = [(i, i ^ 2) for i in range(count)]
    fields = []
    for j in range(CHUNKS):
        send, keep = partial_sums[j], partial_sums[CHUNKS + j]
        got = lax.ppermute(send, "blk", core).astype(jnp.float32)
        half = depth * per
        got = lax.ppermute((keep + got)[half:].astype(jnp.bfloat16), "blk", side).astype(
            jnp.float32
        ) + (keep + got)[:half]
        total = got[:per] + far[j * per : (j + 1) * per]
        for k in range(1, depth):
            total = total + lax.ppermute(
                got[k * per : (k + 1) * per].astype(jnp.bfloat16),
                "blk",
                [(i, (i + 4 * k) % count) for i in range(count)],
            ).astype(jnp.float32)
        fields.append(total.astype(jnp.bfloat16))
    return jnp.concatenate(fields, axis=0)


def on_device(*args):
    rhs = args[0]
    count = lax.axis_size("blk")
    if count % 4 == 0 and count * rhs.size * 4 <= DENSE_BYTES:
        return stationary(*args)
    return routed(*args)


def solution(mesh):
    placed = (
        P(("groups", "blk"), None, None),
        P(("groups", "blk"), None, None),
        P(("groups", "blk"), None),
        P(("groups", "blk")),
        P(("groups", "blk")),
        P(("groups", "blk"), None, None),
        P(("groups", "blk")),
        P(("groups", "blk"), None),
        P(("groups", "blk")),
        P(("groups", "blk"), None, None),
        P(("groups", "blk"), None, None),
    )
    return jax.shard_map(
        on_device,
        mesh=mesh,
        in_specs=placed,
        out_specs=P(("groups", "blk"), None, None),
        check_vma=False,
    )
```

```python
import functools

import jax
import jax.numpy as jnp
from jax import lax
from jax.experimental import pallas as pl
from jax.experimental.pallas import tpu as pltpu
from jax.sharding import PartitionSpec as P

NEAR = 2
SUBS = 1
DENSE_BYTES = 16 << 20
NEAR_VMEM = 24 << 20
FAR_VMEM = 16 << 20


def with_halo(cells, sides, width):
    for axis, dim in sides:
        count = lax.axis_size(axis)
        head = lax.slice_in_dim(cells, 0, width, axis=dim)
        tail = lax.slice_in_dim(cells, cells.shape[dim] - width, cells.shape[dim], axis=dim)
        cells = jnp.concatenate(
            [
                lax.ppermute(tail, axis, [(i, (i + 1) % count) for i in range(count)]),
                cells,
                lax.ppermute(head, axis, [((i + 1) % count, i) for i in range(count)]),
            ],
            axis=dim,
        )
    return cells


def place_ranks(targets, count):
    onehot = (targets[:, None] == jnp.arange(count, dtype=jnp.int32)[None, :]).astype(jnp.int32)
    before = jnp.cumsum(onehot, axis=0) - onehot
    return jnp.sum(before * onehot, axis=1)


def routed(
    rhs,
    near_blocks,
    near_owner,
    near_slot,
    near_offset,
    far_coupling,
    far_slot,
    far_dev,
    far_cslot,
    basis_out,
    basis_in,
):
    clusters = rhs.shape[0]
    directions = rhs.shape[1]
    unknowns = rhs.shape[2]
    cycle_size = lax.axis_size("blk")
    stored = near_blocks.shape[0]
    capacity = max(2, 2 * stored // cycle_size)
    owners = near_owner[:, 0]
    target = owners * capacity + place_ranks(owners, cycle_size)
    outbox = (
        jnp.zeros((cycle_size * capacity, unknowns, unknowns), near_blocks.dtype)
        .at[target]
        .set(near_blocks)
    )
    labels = (
        jnp.zeros((cycle_size * capacity, 2), jnp.int32)
        .at[target]
        .set(jnp.stack([near_slot, near_offset], axis=1))
    )
    window = with_halo(rhs, (("blk", 0),), clusters)
    inbox, in_labels = (
        lax.all_to_all(outbox, "blk", split_axis=0, concat_axis=0, tiled=True),
        lax.all_to_all(labels, "blk", split_axis=0, concat_axis=0, tiled=True),
    )
    position = clusters + in_labels[:, 0] + in_labels[:, 1]
    columns = jnp.take(window, position, axis=0)
    products = jnp.einsum("srj,sij->sri", columns, inbox, preferred_element_type=jnp.float32)
    selector = (in_labels[:, 0][None, :] == jnp.arange(clusters, dtype=jnp.int32)[:, None]).astype(
        jnp.float32
    )
    near_sum = jnp.dot(
        selector,
        products.reshape(products.shape[0], -1),
        precision=lax.Precision.HIGHEST,
        preferred_element_type=jnp.float32,
    ).reshape(clusters, directions, unknowns)
    coef_local = jnp.einsum(
        "ckj,crj->crk", basis_in, rhs, preferred_element_type=jnp.float32
    ).astype(jnp.bfloat16)
    rank_k = basis_in.shape[1]
    coef_local = coef_local.reshape(clusters, directions * rank_k)
    pairs = far_slot.shape[0]
    wanted = far_dev[:, 0] * clusters + far_cslot
    piece = lax.all_gather(coef_local, "blk", axis=0, tiled=True)
    chosen = jnp.take(piece, wanted, axis=0)
    coupled = jnp.einsum(
        "pkq,prq->prk",
        far_coupling,
        chosen.reshape(pairs, directions, rank_k),
        preferred_element_type=jnp.float32,
    )
    row_pick = (far_slot[None, :] == jnp.arange(clusters, dtype=jnp.int32)[:, None]).astype(
        jnp.float32
    )
    gathered = jnp.dot(
        row_pick,
        coupled.reshape(pairs, -1),
        precision=lax.Precision.HIGHEST,
        preferred_element_type=jnp.float32,
    )
    gathered = gathered.astype(jnp.bfloat16).reshape(clusters, directions, rank_k)
    far_sum = jnp.einsum("crk,ckb->crb", gathered, basis_out, preferred_element_type=jnp.float32)
    return (near_sum + far_sum).astype(jnp.bfloat16)


def whole(space=pltpu.VMEM):
    return pl.BlockSpec(memory_space=space)


def coef_kernel(rhs_ref, basis_ref, out_ref):
    clusters = rhs_ref.shape[0]
    rank_k = basis_ref.shape[1]
    half = clusters // 2
    rows = []
    for c in range(half):
        parts = [
            lax.dot_general(
                basis_ref[e],
                rhs_ref[e],
                (((1,), (1,)), ((), ())),
                preferred_element_type=jnp.float32,
            )
            for e in (c, c + half)
        ]
        rows.append(jnp.concatenate(parts, axis=1))
    for q in range(rank_k):
        out_ref[q * half : (q + 1) * half, :] = jnp.concatenate(
            [row[q : q + 1] for row in rows], axis=0
        )


def near_kernel(part, batch, starts_ref, block_ref, pos_ref, row_ref, *rest):
    shards, rest = rest[: part["shards"]], rest[part["shards"] :]
    blocks_hbm, rest = rest[0], rest[1:]
    subs = part["subs"]
    sends, keeps = rest[:subs], rest[subs : 2 * subs]
    columns, blocks, acc, sems = rest[2 * subs :]
    directions, unknowns = acc.shape[1:]
    load = pltpu.make_async_copy(blocks_hbm, blocks, sems.at[len(shards)])
    load.start()
    copies = [
        pltpu.make_async_copy(shard, columns.at[k], sems.at[k]) for k, shard in enumerate(shards)
    ]
    for copy in copies:
        copy.start()
    acc[...] = jnp.zeros_like(acc)
    for copy in copies:
        copy.wait()
    load.wait()
    begin, end = starts_ref[part["at"]], starts_ref[part["at"] + 1]
    last = blocks.shape[0] - 1
    dummy = acc.shape[0] - 1

    def body(step, carry):
        first = begin + step * batch
        products = []
        for k in range(batch):
            at = jnp.minimum(first + k, last)
            row = row_ref[at]
            products.append(
                lax.dot_general(
                    columns[row // columns.shape[1], row % columns.shape[1]],
                    blocks[block_ref[at]],
                    (((1,), (1,)), ((), ())),
                    preferred_element_type=jnp.float32,
                )
            )
        for k in range(batch):
            at = jnp.where(first + k < end, pos_ref[jnp.minimum(first + k, last)], dummy)
            acc[at] = acc[at] + products[k]
        return carry

    lax.fori_loop(0, (end - begin + batch - 1) // batch, body, 0)
    size = sends[0].shape[0]
    for j in range(subs):
        keeps[j][...] = acc[2 * j * size : (2 * j + 1) * size]
        sends[j][...] = acc[(2 * j + 1) * size : (2 * j + 2) * size].astype(sends[j].dtype)


def far_kernel(coef_ref, couple_ref, slot_ref, pick_ref, half_ref, basis_ref, out_ref):
    clusters, rank_k, unknowns = basis_ref.shape
    pairs = couple_ref.shape[2]
    directions = out_ref.shape[1]
    half = clusters // 2
    count = coef_ref.shape[0] // (rank_k * half)
    coef = coef_ref[...].astype(jnp.float32).reshape(count, rank_k, half, unknowns)
    hot = (
        lax.broadcasted_iota(jnp.int32, (clusters, pairs), 0)
        == jnp.broadcast_to(slot_ref[...], (clusters, pairs))
    ).astype(jnp.float32).astype(jnp.bfloat16)
    pick = pick_ref[...]
    keep = half_ref[...]
    total = jnp.zeros((clusters * rank_k, unknowns), jnp.float32)
    for q in range(rank_k):
        table = coef[:, q].reshape(count * half, unknowns).astype(jnp.bfloat16)
        chosen = jnp.dot(pick, table, preferred_element_type=jnp.float32).astype(jnp.bfloat16)
        chosen = chosen * keep
        couple = couple_ref[q]
        weight = jnp.concatenate([couple * hot[s : s + 1] for s in range(clusters)], axis=0)
        total = total + jnp.dot(weight, chosen, preferred_element_type=jnp.float32)
    total = total + pltpu.roll(total, unknowns // 2, axis=1)
    gathered = jnp.transpose(total)[0:directions, :].astype(jnp.bfloat16).astype(jnp.float32)
    lane = lax.broadcasted_iota(jnp.int32, gathered.shape, 1) // rank_k
    basis = basis_ref[...].reshape(clusters * rank_k, unknowns)
    for s in range(clusters):
        own = jnp.where(lane == s, gathered, 0.0).astype(jnp.bfloat16)
        out_ref[s] = jnp.dot(own, basis, preferred_element_type=jnp.float32)


def ring_gather(shard, count):
    chips = count // 2
    depth = chips // 2

    def device(place, core):
        place = place % chips
        z, y = (place, 0) if place < depth else (chips - 1 - place, 1)
        return (z * 2 + y) * 2 + core

    ring = [(device(p, c), device(p + 1 - 2 * c, c)) for p in range(chips) for c in range(2)]
    mate = [(i, i ^ 1) for i in range(count)]
    slots = {0: shard, 1: lax.ppermute(shard, "blk", mate)}
    flow = [slots[0], slots[1]]
    for t in range(1, depth + 1):
        for x in range(2 if t < depth else 1):
            flow[x] = lax.ppermute(flow[x], "blk", ring)
            slots[2 * t + x] = flow[x]
            slots[2 * (chips - t) + 1 - x] = lax.ppermute(flow[x], "blk", mate)
    return [slots[k] for k in range(count)]


def ring_slot(device, me, count):
    chips = count // 2
    depth = chips // 2

    def place(d):
        z, y = d >> 2, (d >> 1) & 1
        return jnp.where(y == 0, z, chips - 1 - z)

    sign = 1 - 2 * (me & 1)
    back = (sign * (place(me) - place(device)) + chips) % chips
    return 2 * back + ((device ^ me) & 1)


def stationary(
    rhs,
    near_blocks,
    near_owner,
    near_slot,
    near_offset,
    far_coupling,
    far_slot,
    far_dev,
    far_cslot,
    basis_out,
    basis_in,
):
    clusters, directions, unknowns = rhs.shape
    rank_k = basis_in.shape[1]
    count = lax.axis_size("blk")
    depth = count // 4
    me = lax.axis_index("blk")
    stored = near_blocks.shape[0]
    pairs = far_slot.shape[0]
    half = clusters // 2

    shards = ring_gather(rhs, count)

    coef = pl.pallas_call(
        coef_kernel,
        out_shape=jax.ShapeDtypeStruct((half * rank_k, unknowns), jnp.float32),
        in_specs=[whole(), whole()],
        out_specs=whole(),
        name="coef",
    )(rhs, basis_in).astype(jnp.bfloat16)

    owner = near_owner[:, 0]
    chunks = NEAR * SUBS
    per = clusters // chunks
    relative = (
        ((owner ^ me) & 1) * (2 * depth)
        + (((owner ^ me) >> 1) & 1) * depth
        + ((owner >> 2) - (me >> 2) + depth) % depth
    )
    size = 2 * depth * per
    position = (near_slot // per) % SUBS * (2 * size) + relative * per + near_slot % per
    column = (owner * clusters + near_slot + near_offset) % (count * clusters)
    column_row = ring_slot(column // clusters, me, count) * clusters + column % clusters
    key = near_slot // (per * SUBS)
    index = jnp.arange(stored, dtype=jnp.int32)
    ahead = (key[None, :] < key[:, None]) | (
        (key[None, :] == key[:, None]) & (index[None, :] < index[:, None])
    )
    rank = jnp.sum(ahead.astype(jnp.int32), axis=1)
    here = rank[None, :] == index[:, None]
    block_at, position, column_row = [
        jnp.sum(jnp.where(here, values[None, :], 0), axis=1)
        for values in (index, position, column_row)
    ]
    starts = jnp.sum(
        (key[None, :] < jnp.arange(NEAR + 1, dtype=jnp.int32)[:, None]).astype(jnp.int32), axis=1
    )

    low = far_cslot % half
    pick = (
        (far_dev[:, 0] * half + low)[:, None] == jnp.arange(count * half, dtype=jnp.int32)[None, :]
    ).astype(jnp.bfloat16)
    keep = (
        (far_cslot // half)[:, None] == (jnp.arange(unknowns, dtype=jnp.int32) // directions)[None, :]
    ).astype(jnp.bfloat16)
    couple = jnp.transpose(far_coupling, (2, 1, 0))

    coef, pick, keep, couple, starts, block_at, position, column_row, shards[-1] = (
        lax.optimization_barrier(
            (coef, pick, keep, couple, starts, block_at, position, column_row, shards[-1])
        )
    )
    coef_all = lax.all_gather(coef, "blk", axis=0, tiled=True)

    near_sums = []
    for j in range(NEAR):
        out = pl.pallas_call(
            functools.partial(near_kernel, dict(shards=count, subs=SUBS, at=j), 4),
            out_shape=[jax.ShapeDtypeStruct((size, directions, unknowns), jnp.bfloat16)] * SUBS
            + [jax.ShapeDtypeStruct((size, directions, unknowns), jnp.float32)] * SUBS,
            in_specs=[whole(pltpu.SMEM)] * 4 + [whole(pl.ANY)] * (count + 1),
            out_specs=[whole()] * (2 * SUBS),
            scratch_shapes=[
                pltpu.VMEM((count, clusters, directions, unknowns), jnp.bfloat16),
                pltpu.VMEM(near_blocks.shape, jnp.bfloat16),
                pltpu.VMEM((2 * SUBS * size + 1, directions, unknowns), jnp.float32),
                pltpu.SemaphoreType.DMA((count + 1,)),
            ],
            compiler_params=pltpu.CompilerParams(vmem_limit_bytes=NEAR_VMEM),
            cost_estimate=pl.CostEstimate(
                flops=2 * stored * directions * unknowns * unknowns * 8,
                bytes_accessed=12 << 20,
                transcendentals=0,
            ),
            name="near",
        )(starts, block_at, position, column_row, *shards, near_blocks)
        near_sums += list(zip(out[:SUBS], out[SUBS:]))

    far = pl.pallas_call(
        far_kernel,
        out_shape=jax.ShapeDtypeStruct((clusters, directions, unknowns), jnp.float32),
        in_specs=[whole()] * 6,
        out_specs=whole(),
        compiler_params=pltpu.CompilerParams(vmem_limit_bytes=FAR_VMEM),
        cost_estimate=pl.CostEstimate(
            flops=4 * clusters * rank_k * pairs * rank_k * unknowns,
            bytes_accessed=8 << 20,
            transcendentals=0,
        ),
        name="far",
    )(coef_all, couple, far_slot.reshape(1, pairs), pick, keep, basis_out)

    core = [(i, i ^ 1) for i in range(count)]
    side = [(i, i ^ 2) for i in range(count)]
    quarter = depth * per
    fields = []
    for j, (send, own) in enumerate(near_sums):
        total = own + lax.ppermute(send, "blk", core).astype(jnp.float32)
        got = lax.ppermute(total[quarter:].astype(jnp.bfloat16), "blk", side)
        total = total[:quarter] + got.astype(jnp.float32)
        field = total[:per] + far[j * per : (j + 1) * per]
        for k in range(1, depth):
            field = field + lax.ppermute(
                total[k * per : (k + 1) * per].astype(jnp.bfloat16),
                "blk",
                [(i, (i + 4 * k) % count) for i in range(count)],
            ).astype(jnp.float32)
        fields.append(field.astype(jnp.bfloat16))
    return jnp.concatenate(fields, axis=0)


def on_device(*args):
    rhs = args[0]
    count = lax.axis_size("blk")
    if count % 4 == 0 and count * rhs.size * 4 <= DENSE_BYTES:
        return stationary(*args)
    return routed(*args)


def solution(mesh):
    placed = (
        P(("groups", "blk"), None, None),
        P(("groups", "blk"), None, None),
        P(("groups", "blk"), None),
        P(("groups", "blk")),
        P(("groups", "blk")),
        P(("groups", "blk"), None, None),
        P(("groups", "blk")),
        P(("groups", "blk"), None),
        P(("groups", "blk")),
        P(("groups", "blk"), None, None),
        P(("groups", "blk"), None, None),
    )
    return jax.shard_map(
        on_device,
        mesh=mesh,
        in_specs=placed,
        out_specs=P(("groups", "blk"), None, None),
        check_vma=False,
    )
```

```python
import functools

import jax
import jax.numpy as jnp
from jax import lax
from jax.experimental import pallas as pl
from jax.experimental.pallas import tpu as pltpu
from jax.sharding import PartitionSpec as P

DENSE_BYTES = 16 << 20
NEAR_VMEM = 46 << 20
FAR_VMEM = 16 << 20


def with_halo(cells, sides, width):
    for axis, dim in sides:
        count = lax.axis_size(axis)
        head = lax.slice_in_dim(cells, 0, width, axis=dim)
        tail = lax.slice_in_dim(cells, cells.shape[dim] - width, cells.shape[dim], axis=dim)
        cells = jnp.concatenate(
            [
                lax.ppermute(tail, axis, [(i, (i + 1) % count) for i in range(count)]),
                cells,
                lax.ppermute(head, axis, [((i + 1) % count, i) for i in range(count)]),
            ],
            axis=dim,
        )
    return cells


def place_ranks(targets, count):
    onehot = (targets[:, None] == jnp.arange(count, dtype=jnp.int32)[None, :]).astype(jnp.int32)
    before = jnp.cumsum(onehot, axis=0) - onehot
    return jnp.sum(before * onehot, axis=1)


def routed(
    rhs,
    near_blocks,
    near_owner,
    near_slot,
    near_offset,
    far_coupling,
    far_slot,
    far_dev,
    far_cslot,
    basis_out,
    basis_in,
):
    clusters = rhs.shape[0]
    directions = rhs.shape[1]
    unknowns = rhs.shape[2]
    cycle_size = lax.axis_size("blk")
    stored = near_blocks.shape[0]
    capacity = max(2, 2 * stored // cycle_size)
    owners = near_owner[:, 0]
    target = owners * capacity + place_ranks(owners, cycle_size)
    outbox = (
        jnp.zeros((cycle_size * capacity, unknowns, unknowns), near_blocks.dtype)
        .at[target]
        .set(near_blocks)
    )
    labels = (
        jnp.zeros((cycle_size * capacity, 2), jnp.int32)
        .at[target]
        .set(jnp.stack([near_slot, near_offset], axis=1))
    )
    window = with_halo(rhs, (("blk", 0),), clusters)
    inbox, in_labels = (
        lax.all_to_all(outbox, "blk", split_axis=0, concat_axis=0, tiled=True),
        lax.all_to_all(labels, "blk", split_axis=0, concat_axis=0, tiled=True),
    )
    position = clusters + in_labels[:, 0] + in_labels[:, 1]
    columns = jnp.take(window, position, axis=0)
    products = jnp.einsum("srj,sij->sri", columns, inbox, preferred_element_type=jnp.float32)
    selector = (in_labels[:, 0][None, :] == jnp.arange(clusters, dtype=jnp.int32)[:, None]).astype(
        jnp.float32
    )
    near_sum = jnp.dot(
        selector,
        products.reshape(products.shape[0], -1),
        precision=lax.Precision.HIGHEST,
        preferred_element_type=jnp.float32,
    ).reshape(clusters, directions, unknowns)
    coef_local = jnp.einsum(
        "ckj,crj->crk", basis_in, rhs, preferred_element_type=jnp.float32
    ).astype(jnp.bfloat16)
    rank_k = basis_in.shape[1]
    coef_local = coef_local.reshape(clusters, directions * rank_k)
    pairs = far_slot.shape[0]
    wanted = far_dev[:, 0] * clusters + far_cslot
    piece = lax.all_gather(coef_local, "blk", axis=0, tiled=True)
    chosen = jnp.take(piece, wanted, axis=0)
    coupled = jnp.einsum(
        "pkq,prq->prk",
        far_coupling,
        chosen.reshape(pairs, directions, rank_k),
        preferred_element_type=jnp.float32,
    )
    row_pick = (far_slot[None, :] == jnp.arange(clusters, dtype=jnp.int32)[:, None]).astype(
        jnp.float32
    )
    gathered = jnp.dot(
        row_pick,
        coupled.reshape(pairs, -1),
        precision=lax.Precision.HIGHEST,
        preferred_element_type=jnp.float32,
    )
    gathered = gathered.astype(jnp.bfloat16).reshape(clusters, directions, rank_k)
    far_sum = jnp.einsum("crk,ckb->crb", gathered, basis_out, preferred_element_type=jnp.float32)
    return (near_sum + far_sum).astype(jnp.bfloat16)


def whole(space=pltpu.VMEM):
    return pl.BlockSpec(memory_space=space)


def coef_kernel(rhs_ref, basis_ref, out_ref, copy_ref):
    copy_ref[...] = rhs_ref[...]
    clusters = rhs_ref.shape[0]
    rank_k = basis_ref.shape[1]
    half = clusters // 2
    rows = []
    for c in range(half):
        parts = [
            lax.dot_general(
                basis_ref[e],
                rhs_ref[e],
                (((1,), (1,)), ((), ())),
                preferred_element_type=jnp.float32,
            )
            for e in (c, c + half)
        ]
        rows.append(jnp.concatenate(parts, axis=1))
    for q in range(rank_k):
        out_ref[q * half : (q + 1) * half, :] = jnp.concatenate(
            [row[q : q + 1] for row in rows], axis=0
        )


def near_kernel(part, batch, starts_ref, block_ref, pos_ref, row_ref, *rest):
    shards, rest = rest[: part["shards"]], rest[part["shards"] :]
    blocks_hbm, rest = rest[0], rest[1:]
    send_ref, keep_ref, columns, blocks, acc, sems = rest
    directions, unknowns = acc.shape[1:]
    load = pltpu.make_async_copy(blocks_hbm, blocks, sems.at[len(shards)])
    load.start()
    copies = [
        pltpu.make_async_copy(shard, columns.at[k], sems.at[k]) for k, shard in enumerate(shards)
    ]
    for copy in copies:
        copy.start()
    acc[...] = jnp.zeros_like(acc)
    for copy in copies:
        copy.wait()
    load.wait()
    begin, end = starts_ref[part["at"]], starts_ref[part["at"] + 1]
    last = blocks.shape[0] - 1
    dummy = acc.shape[0] - 1

    def body(step, carry):
        first = begin + step * batch
        products = []
        for k in range(batch):
            at = jnp.minimum(first + k, last)
            row = row_ref[at]
            products.append(
                lax.dot_general(
                    columns[row // columns.shape[1], row % columns.shape[1]],
                    blocks[block_ref[at]],
                    (((1,), (1,)), ((), ())),
                    preferred_element_type=jnp.float32,
                )
            )
        for k in range(batch):
            at = jnp.where(first + k < end, pos_ref[jnp.minimum(first + k, last)], dummy)
            acc[at] = acc[at] + products[k]
        return carry

    lax.fori_loop(0, (end - begin + batch - 1) // batch, body, 0)
    size = send_ref.shape[0]
    keep_ref[...] = acc[0:size]
    send_ref[...] = acc[size : 2 * size].astype(send_ref.dtype)


def far_kernel(*refs):
    coef_refs, (couple_ref, slot_ref, pick_ref, half_ref, basis_ref, out_ref) = refs[:4], refs[4:]
    clusters, rank_k, unknowns = basis_ref.shape
    pairs = couple_ref.shape[2]
    directions = out_ref.shape[1]
    half = clusters // 2
    coef = jnp.concatenate([ref[...].astype(jnp.float32) for ref in coef_refs], axis=0)
    coef = coef.reshape(-1, rank_k, half, unknowns)
    count = coef.shape[0]
    hot = (
        lax.broadcasted_iota(jnp.int32, (clusters, pairs), 0)
        == jnp.broadcast_to(slot_ref[...], (clusters, pairs))
    ).astype(jnp.float32).astype(jnp.bfloat16)
    pick = pick_ref[...]
    keep = half_ref[...]
    total = jnp.zeros((clusters * rank_k, unknowns), jnp.float32)
    for q in range(rank_k):
        table = coef[:, q].reshape(count * half, unknowns).astype(jnp.bfloat16)
        chosen = jnp.dot(pick, table, preferred_element_type=jnp.float32).astype(jnp.bfloat16)
        chosen = chosen * keep
        couple = couple_ref[q]
        weight = jnp.concatenate([couple * hot[s : s + 1] for s in range(clusters)], axis=0)
        total = total + jnp.dot(weight, chosen, preferred_element_type=jnp.float32)
    total = total + pltpu.roll(total, unknowns // 2, axis=1)
    gathered = jnp.transpose(total)[0:directions, :].astype(jnp.bfloat16).astype(jnp.float32)
    lane = lax.broadcasted_iota(jnp.int32, gathered.shape, 1) // rank_k
    basis = basis_ref[...].reshape(clusters * rank_k, unknowns)
    for s in range(clusters):
        own = jnp.where(lane == s, gathered, 0.0).astype(jnp.bfloat16)
        out_ref[s] = jnp.dot(own, basis, preferred_element_type=jnp.float32)


def ring_device(place, core, chips):
    depth = chips // 2
    place = place % chips
    z, y = (place, 0) if place < depth else (chips - 1 - place, 1)
    return (z * 2 + y) * 2 + core


def ring_pairs(count):
    chips = count // 2
    cores = [(p, c) for p in range(chips) for c in range(2)]
    ahead = [(ring_device(p, c, chips), ring_device(p + 1 - 2 * c, c, chips)) for p, c in cores]
    cross = [
        (ring_device(p, c, chips), ring_device(p - 1 + 2 * c, 1 - c, chips)) for p, c in cores
    ]
    return ahead, cross


def ring_place(device, chips):
    z, y = device >> 2, (device >> 1) & 1
    return jnp.where(y == 0, z, chips - 1 - z)


def gather_slot(device, me, count):
    chips = count // 2
    back = (1 - 2 * (me & 1)) * (ring_place(me, chips) - ring_place(device, chips))
    return 2 * ((back + chips) % chips) + ((device ^ me) & 1)


def scatter_place(device, me, count):
    chips = count // 2
    half = chips // 2
    ahead = (ring_place(device, chips) - ring_place(me, chips) + chips) % chips
    core = device & 1
    handler = jnp.where(ahead % half == 0, core, (ahead > half).astype(jnp.int32))
    steps = jnp.where(handler == 0, ahead, (chips - ahead) % chips)
    return handler, steps, core ^ handler


def stationary(
    rhs,
    near_blocks,
    near_owner,
    near_slot,
    near_offset,
    far_coupling,
    far_slot,
    far_dev,
    far_cslot,
    basis_out,
    basis_in,
):
    clusters, directions, unknowns = rhs.shape
    rank_k = basis_in.shape[1]
    count = lax.axis_size("blk")
    chips = count // 2
    depth = chips // 2
    me = lax.axis_index("blk")
    stored = near_blocks.shape[0]
    pairs = far_slot.shape[0]
    half = clusters // 2
    ahead, cross = ring_pairs(count)
    mate = [(i, i ^ 1) for i in range(count)]
    side = [(i, i ^ 2) for i in range(count)]

    def move(values, where):
        return lax.ppermute(values, "blk", where)

    coef, here_rhs = pl.pallas_call(
        coef_kernel,
        out_shape=[
            jax.ShapeDtypeStruct((half * rank_k, unknowns), jnp.float32),
            jax.ShapeDtypeStruct(rhs.shape, rhs.dtype),
        ],
        in_specs=[whole(), whole()],
        out_specs=[whole(), whole()],
        name="coef",
    )(rhs, basis_in)
    coef = coef.astype(jnp.bfloat16)

    owner = near_owner[:, 0]
    handler, steps, other = scatter_place(owner, me, count)
    group = (steps < depth - 1).astype(jnp.int32)
    sizes = (3, 2 * (depth - 2) + 1)
    shard_at = jnp.where(
        group == 0,
        jnp.where(steps == depth, 0, 1 + other),
        jnp.where(steps == 0, 2 * (depth - 2), 2 * (depth - 2 - steps) + other),
    )
    shard_at = shard_at + jnp.where(
        handler == (me & 1), 0, jnp.where(group == 0, sizes[0], sizes[1])
    )
    position = shard_at * clusters + near_slot
    column = (owner * clusters + near_slot + near_offset) % (count * clusters)
    column_row = gather_slot(column // clusters, me, count) * clusters + column % clusters
    index = jnp.arange(stored, dtype=jnp.int32)
    before = (group[None, :] < group[:, None]) | (
        (group[None, :] == group[:, None]) & (index[None, :] < index[:, None])
    )
    rank = jnp.sum(before.astype(jnp.int32), axis=1)
    here = rank[None, :] == index[:, None]
    block_at, position, column_row = [
        jnp.sum(jnp.where(here, values[None, :], 0), axis=1)
        for values in (index, position, column_row)
    ]
    starts = jnp.sum(
        (group[None, :] < jnp.arange(3, dtype=jnp.int32)[:, None]).astype(jnp.int32), axis=1
    )

    far_at = far_dev[:, 0]
    far_at = (
        ((far_at ^ me) & 1) * (2 * depth)
        + (((far_at ^ me) >> 1) & 1) * depth
        + ((me >> 2) - (far_at >> 2) + depth) % depth
    )
    pick = (
        (far_at * half + far_cslot % half)[:, None]
        == jnp.arange(count * half, dtype=jnp.int32)[None, :]
    ).astype(jnp.bfloat16)
    keep = (
        (far_cslot // half)[:, None] == (jnp.arange(unknowns, dtype=jnp.int32) // directions)[None, :]
    ).astype(jnp.bfloat16)
    couple = jnp.transpose(far_coupling, (2, 1, 0))

    slots = {0: here_rhs}
    flow = [move(rhs, ahead), move(rhs, cross)]
    slots[1] = move(rhs, mate)
    for t in range(1, depth + 1):
        if t == 2:
            flow[0], coef, starts, block_at, position, column_row = lax.optimization_barrier(
                (flow[0], coef, starts, block_at, position, column_row)
            )
            coefs = [coef] + [
                move(coef, [(i, (i + 4 * k) % count) for i in range(count)])
                for k in range(1, depth)
            ]
        if t == 3:
            flow[0], couple, pick, keep = lax.optimization_barrier((flow[0], couple, pick, keep))
        if t == 4:
            flow[0], coefs = lax.optimization_barrier((flow[0], jnp.concatenate(coefs, axis=0)))
            coefs = [coefs, move(coefs, side)]
        for x in range(2 if t < depth else 1):
            slots[2 * t + x] = flow[x]
            slots[2 * (chips - t) + 1 - x] = move(flow[x], mate)
            if t + x < depth:
                flow[x] = move(flow[x], ahead)

    sums = []
    for j, size in enumerate(sizes):
        if j == 1:
            starts, coefs = lax.optimization_barrier((starts, coefs))
            coefs = coefs + [move(part, mate) for part in coefs]
        sums.append(
            pl.pallas_call(
                functools.partial(near_kernel, dict(shards=count, at=j), 4),
                out_shape=[
                    jax.ShapeDtypeStruct((size * clusters, directions, unknowns), jnp.bfloat16),
                    jax.ShapeDtypeStruct((size * clusters, directions, unknowns), jnp.float32),
                ],
                in_specs=[whole(pltpu.SMEM)] * 4
                + [whole(pl.ANY)] * (count + 1),
                out_specs=[whole()] * 2,
                scratch_shapes=[
                    pltpu.VMEM((count, clusters, directions, unknowns), jnp.bfloat16),
                    pltpu.VMEM(near_blocks.shape, jnp.bfloat16),
                    pltpu.VMEM((2 * size * clusters + 1, directions, unknowns), jnp.float32),
                    pltpu.SemaphoreType.DMA((count + 1,)),
                ],
                compiler_params=pltpu.CompilerParams(vmem_limit_bytes=NEAR_VMEM),
                cost_estimate=pl.CostEstimate(
                    flops=2 * stored * directions * unknowns * unknowns * 8,
                    bytes_accessed=12 << 20,
                    transcendentals=0,
                ),
                name="near",
            )(
                starts,
                block_at,
                position,
                column_row,
                *[slots[k] for k in range(count)],
                near_blocks,
            )
        )

    far = pl.pallas_call(
        far_kernel,
        out_shape=jax.ShapeDtypeStruct((clusters, directions, unknowns), jnp.float32),
        in_specs=[whole()] * 9,
        out_specs=whole(),
        compiler_params=pltpu.CompilerParams(vmem_limit_bytes=FAR_VMEM),
        cost_estimate=pl.CostEstimate(
            flops=4 * clusters * rank_k * pairs * rank_k * unknowns,
            bytes_accessed=8 << 20,
            transcendentals=0,
        ),
        name="far",
    )(*coefs, couple, far_slot.reshape(1, pairs), pick, keep, basis_out)

    own = [kept for _, kept in sums]
    mates = [move(sent, mate) for sent, _ in sums]

    def term(j, k):
        at = slice(k * clusters, (k + 1) * clusters)
        return own[j][at] + mates[j][at].astype(jnp.float32)

    def add(flow, j, k):
        step = (flow.astype(jnp.float32) + term(j, k)).astype(jnp.bfloat16)
        step, mates[j] = lax.optimization_barrier((step, mates[j]))
        return step

    flow = lax.optimization_barrier(
        [term(0, 0).astype(jnp.bfloat16), term(0, 2).astype(jnp.bfloat16)]
    )
    for t in range(depth - 1, -1, -1):
        flow = [move(part, ahead) for part in flow]
        if t == 0:
            break
        flow[0] = add(flow[0], 0, 1) if t == depth - 1 else add(flow[0], 1, 2 * (depth - 2 - t))
        if t > 1:
            flow[1] = add(flow[1], 1, 2 * (depth - 1 - t) + 1)
        else:
            last = move(flow[1], mate)
            flow = flow[:1]
    total = far + term(1, 2 * (depth - 2)) + last.astype(jnp.float32) + flow[0].astype(jnp.float32)
    return total.astype(jnp.bfloat16)


def on_device(*args):
    rhs = args[0]
    count = lax.axis_size("blk")
    if count % 4 == 0 and count >= 16 and count * rhs.size * 4 <= DENSE_BYTES:
        return stationary(*args)
    return routed(*args)


def solution(mesh):
    placed = (
        P(("groups", "blk"), None, None),
        P(("groups", "blk"), None, None),
        P(("groups", "blk"), None),
        P(("groups", "blk")),
        P(("groups", "blk")),
        P(("groups", "blk"), None, None),
        P(("groups", "blk")),
        P(("groups", "blk"), None),
        P(("groups", "blk")),
        P(("groups", "blk"), None, None),
        P(("groups", "blk"), None, None),
    )
    return jax.shard_map(
        on_device,
        mesh=mesh,
        in_specs=placed,
        out_specs=P(("groups", "blk"), None, None),
        check_vma=False,
    )
```

```python
import functools

import jax
import jax.numpy as jnp
from jax import lax
from jax.experimental import pallas as pl
from jax.experimental.pallas import tpu as pltpu
from jax.sharding import PartitionSpec as P

DENSE_BYTES = 16 << 20
NEAR_VMEM = 46 << 20
FAR_VMEM = 16 << 20


def with_halo(cells, sides, width):
    for axis, dim in sides:
        count = lax.axis_size(axis)
        head = lax.slice_in_dim(cells, 0, width, axis=dim)
        tail = lax.slice_in_dim(cells, cells.shape[dim] - width, cells.shape[dim], axis=dim)
        cells = jnp.concatenate(
            [
                lax.ppermute(tail, axis, [(i, (i + 1) % count) for i in range(count)]),
                cells,
                lax.ppermute(head, axis, [((i + 1) % count, i) for i in range(count)]),
            ],
            axis=dim,
        )
    return cells


def place_ranks(targets, count):
    onehot = (targets[:, None] == jnp.arange(count, dtype=jnp.int32)[None, :]).astype(jnp.int32)
    before = jnp.cumsum(onehot, axis=0) - onehot
    return jnp.sum(before * onehot, axis=1)


def routed(
    rhs,
    near_blocks,
    near_owner,
    near_slot,
    near_offset,
    far_coupling,
    far_slot,
    far_dev,
    far_cslot,
    basis_out,
    basis_in,
):
    clusters = rhs.shape[0]
    directions = rhs.shape[1]
    unknowns = rhs.shape[2]
    cycle_size = lax.axis_size("blk")
    stored = near_blocks.shape[0]
    capacity = max(2, 2 * stored // cycle_size)
    owners = near_owner[:, 0]
    target = owners * capacity + place_ranks(owners, cycle_size)
    outbox = (
        jnp.zeros((cycle_size * capacity, unknowns, unknowns), near_blocks.dtype)
        .at[target]
        .set(near_blocks)
    )
    labels = (
        jnp.zeros((cycle_size * capacity, 2), jnp.int32)
        .at[target]
        .set(jnp.stack([near_slot, near_offset], axis=1))
    )
    window = with_halo(rhs, (("blk", 0),), clusters)
    inbox, in_labels = (
        lax.all_to_all(outbox, "blk", split_axis=0, concat_axis=0, tiled=True),
        lax.all_to_all(labels, "blk", split_axis=0, concat_axis=0, tiled=True),
    )
    position = clusters + in_labels[:, 0] + in_labels[:, 1]
    columns = jnp.take(window, position, axis=0)
    products = jnp.einsum("srj,sij->sri", columns, inbox, preferred_element_type=jnp.float32)
    selector = (in_labels[:, 0][None, :] == jnp.arange(clusters, dtype=jnp.int32)[:, None]).astype(
        jnp.float32
    )
    near_sum = jnp.dot(
        selector,
        products.reshape(products.shape[0], -1),
        precision=lax.Precision.HIGHEST,
        preferred_element_type=jnp.float32,
    ).reshape(clusters, directions, unknowns)
    coef_local = jnp.einsum(
        "ckj,crj->crk", basis_in, rhs, preferred_element_type=jnp.float32
    ).astype(jnp.bfloat16)
    rank_k = basis_in.shape[1]
    coef_local = coef_local.reshape(clusters, directions * rank_k)
    pairs = far_slot.shape[0]
    wanted = far_dev[:, 0] * clusters + far_cslot
    piece = lax.all_gather(coef_local, "blk", axis=0, tiled=True)
    chosen = jnp.take(piece, wanted, axis=0)
    coupled = jnp.einsum(
        "pkq,prq->prk",
        far_coupling,
        chosen.reshape(pairs, directions, rank_k),
        preferred_element_type=jnp.float32,
    )
    row_pick = (far_slot[None, :] == jnp.arange(clusters, dtype=jnp.int32)[:, None]).astype(
        jnp.float32
    )
    gathered = jnp.dot(
        row_pick,
        coupled.reshape(pairs, -1),
        precision=lax.Precision.HIGHEST,
        preferred_element_type=jnp.float32,
    )
    gathered = gathered.astype(jnp.bfloat16).reshape(clusters, directions, rank_k)
    far_sum = jnp.einsum("crk,ckb->crb", gathered, basis_out, preferred_element_type=jnp.float32)
    return (near_sum + far_sum).astype(jnp.bfloat16)


def whole(space=pltpu.VMEM):
    return pl.BlockSpec(memory_space=space)


def prologue_kernel(
    count, me_ref, owner_ref, slot_ref, offset_ref, rhs_ref, basis_ref, coef_ref, copy_ref, list_ref
):
    clusters = rhs_ref.shape[0]
    rank_k = basis_ref.shape[1]
    stored = owner_ref.shape[1]
    half = clusters // 2
    copy_ref[...] = rhs_ref[...]
    rows = []
    for c in range(half):
        parts = [
            lax.dot_general(
                basis_ref[e],
                rhs_ref[e],
                (((1,), (1,)), ((), ())),
                preferred_element_type=jnp.float32,
            )
            for e in (c, c + half)
        ]
        rows.append(jnp.concatenate(parts, axis=1))
    coef_ref[...] = jnp.concatenate(
        [row[q : q + 1] for q in range(rank_k) for row in rows], axis=0
    ).astype(coef_ref.dtype)

    me, owner, slot = me_ref[0], owner_ref[...], slot_ref[...]
    chips = count // 2
    depth = chips // 2
    handler, steps, other = scatter_place(owner, me, count)
    early = steps >= depth - 1
    shard_at = jnp.where(
        early,
        jnp.where(steps == depth, 0, 2 - other),
        jnp.where(steps == 0, 2 * (depth - 2), 2 * (depth - 2 - steps) + 1 - other),
    )
    shard_at = shard_at + jnp.where(handler == (me & 1), 0, jnp.where(early, 3, 2 * depth - 3))
    column = (owner * clusters + slot + offset_ref[...]) & (count * clusters - 1)
    column_slot = gather_slot(column // clusters, me, count)
    column_row = column_slot * clusters + (column & (clusters - 1))
    square = (stored, stored)
    group = jnp.broadcast_to(jnp.where(early, 0.0, 1.0), square)
    group_of_row = jnp.transpose(group)
    row_at = lax.broadcasted_iota(jnp.int32, square, 0)
    lane_at = lax.broadcasted_iota(jnp.int32, square, 1)
    before = (group_of_row < group) | ((group_of_row == group) & (row_at < lane_at))
    rank = jnp.sum(jnp.where(before, 1.0, 0.0), axis=0, keepdims=True)
    rank = jnp.transpose(jnp.broadcast_to(rank, square))
    here = jnp.where(rank == lane_at.astype(jnp.float32), 1.0, 0.0).astype(jnp.bfloat16)
    first = stored - jnp.sum(group[0:1], axis=1, keepdims=True)
    values = jnp.concatenate(
        [
            lane_at[0:1].astype(jnp.float32),
            (shard_at * clusters + slot).astype(jnp.float32),
            column_row.astype(jnp.float32),
            jnp.broadcast_to(first, (1, stored)),
            jnp.zeros((4, stored), jnp.float32),
        ],
        axis=0,
    )
    ordered = jnp.dot(values.astype(jnp.bfloat16), here, preferred_element_type=jnp.float32)
    list_ref[...] = ordered.astype(jnp.int32)


def near_kernel(late, batch, count, list_ref, *rest):
    shards, blocks_hbm, rest = rest[:count], rest[count], rest[count + 1 :]
    sends, (keep_ref, columns, blocks, acc, sems) = rest[:-5], rest[-5:]
    directions, unknowns = acc.shape[1:]
    load = pltpu.make_async_copy(blocks_hbm, blocks, sems.at[len(shards)])
    load.start()
    copies = [
        pltpu.make_async_copy(shard, columns.at[k], sems.at[k]) for k, shard in enumerate(shards)
    ]
    for copy in copies:
        copy.start()
    acc[...] = jnp.zeros_like(acc)
    for copy in copies:
        copy.wait()
    load.wait()
    begin = list_ref[3, 0] if late else 0
    end = blocks.shape[0] if late else list_ref[3, 0]
    last = blocks.shape[0] - 1
    dummy = acc.shape[0] - 1

    def body(step, carry):
        first = begin + step * batch
        products = []
        for k in range(batch):
            at = jnp.minimum(first + k, last)
            row = list_ref[2, at]
            products.append(
                lax.dot_general(
                    columns[row // columns.shape[1], row % columns.shape[1]],
                    blocks[list_ref[0, at]],
                    (((1,), (1,)), ((), ())),
                    preferred_element_type=jnp.float32,
                )
            )
        for k in range(batch):
            at = jnp.where(first + k < end, list_ref[1, jnp.minimum(first + k, last)], dummy)
            acc[at] = acc[at] + products[k]
        return carry

    lax.fori_loop(0, (end - begin + batch - 1) // batch, body, 0)
    at = keep_ref.shape[0]
    keep_ref[...] = acc[0:at]
    for send_ref in sends:
        size = send_ref.shape[0]
        send_ref[...] = acc[at : at + size].astype(send_ref.dtype)
        at += size


def far_kernel(*refs):
    coef_refs = refs[:4]
    me_ref, couple_ref, slot_ref, dev_ref, cslot_ref, basis_ref, out_ref = refs[4:]
    clusters, rank_k, unknowns = basis_ref.shape
    pairs = couple_ref.shape[2]
    directions = out_ref.shape[1]
    half = clusters // 2
    coef = jnp.concatenate([ref[...].astype(jnp.float32) for ref in coef_refs], axis=0)
    coef = coef.reshape(-1, rank_k, half, unknowns)
    count = coef.shape[0]
    hot = (
        lax.broadcasted_iota(jnp.int32, (clusters, pairs), 0)
        == jnp.broadcast_to(slot_ref[...], (clusters, pairs))
    ).astype(jnp.float32).astype(jnp.bfloat16)
    away = dev_ref[...] ^ me_ref[0]
    away = (away & 1) * (count // 2) + ((away >> 1) & 1) * (count // 4) + (away >> 2)
    cslot = cslot_ref[...]
    high = (cslot >= half).astype(jnp.int32)
    at = away * half + cslot - high * half
    table_rows = (count * half, pairs)
    pick = jnp.where(
        lax.broadcasted_iota(jnp.int32, table_rows, 0) == jnp.broadcast_to(at, table_rows), 1.0, 0.0
    )
    pick = jnp.transpose(pick).astype(jnp.bfloat16)
    lanes = (unknowns, pairs)
    keep = jnp.where(
        lax.broadcasted_iota(jnp.int32, lanes, 0) // directions == jnp.broadcast_to(high, lanes),
        1.0,
        0.0,
    )
    keep = jnp.transpose(keep).astype(jnp.bfloat16)
    total = jnp.zeros((clusters * rank_k, unknowns), jnp.float32)
    for q in range(rank_k):
        table = coef[:, q].reshape(count * half, unknowns).astype(jnp.bfloat16)
        chosen = jnp.dot(pick, table, preferred_element_type=jnp.float32).astype(jnp.bfloat16)
        chosen = chosen * keep
        couple = couple_ref[q]
        weight = jnp.concatenate([couple * hot[s : s + 1] for s in range(clusters)], axis=0)
        total = total + jnp.dot(weight, chosen, preferred_element_type=jnp.float32)
    total = total + pltpu.roll(total, unknowns // 2, axis=1)
    gathered = jnp.transpose(total)[0:directions, :].astype(jnp.bfloat16).astype(jnp.float32)
    lane = lax.broadcasted_iota(jnp.int32, gathered.shape, 1) // rank_k
    basis = basis_ref[...].reshape(clusters * rank_k, unknowns)
    for s in range(clusters):
        own = jnp.where(lane == s, gathered, 0.0).astype(jnp.bfloat16)
        out_ref[s] = jnp.dot(own, basis, preferred_element_type=jnp.float32)


def ring_device(place, core, chips):
    depth = chips // 2
    place = place % chips
    z, y = (place, 0) if place < depth else (chips - 1 - place, 1)
    return (z * 2 + y) * 2 + core


def ring_pairs(count):
    chips = count // 2
    cores = [(p, c) for p in range(chips) for c in range(2)]
    ahead = [(ring_device(p, c, chips), ring_device(p + 1 - 2 * c, c, chips)) for p, c in cores]
    cross = [
        (ring_device(p, c, chips), ring_device(p - 1 + 2 * c, 1 - c, chips)) for p, c in cores
    ]
    return ahead, cross


def ring_place(device, chips):
    z, y = device >> 2, (device >> 1) & 1
    return jnp.where(y == 0, z, chips - 1 - z)


def gather_slot(device, me, count):
    chips = count // 2
    back = (1 - 2 * (me & 1)) * (ring_place(me, chips) - ring_place(device, chips))
    return 2 * ((back + chips) % chips) + ((device ^ me) & 1)


def scatter_place(device, me, count):
    chips = count // 2
    half = chips // 2
    ahead = (ring_place(device, chips) - ring_place(me, chips) + chips) % chips
    core = device & 1
    handler = jnp.where(ahead % half == 0, core, (ahead > half).astype(jnp.int32))
    steps = jnp.where(handler == 0, ahead, (chips - ahead) % chips)
    return handler, steps, core ^ handler


def stationary(
    rhs,
    near_blocks,
    near_owner,
    near_slot,
    near_offset,
    far_coupling,
    far_slot,
    far_dev,
    far_cslot,
    basis_out,
    basis_in,
):
    clusters, directions, unknowns = rhs.shape
    rank_k = basis_in.shape[1]
    count = lax.axis_size("blk")
    chips = count // 2
    depth = chips // 2
    me = lax.axis_index("blk")
    stored = near_blocks.shape[0]
    pairs = far_slot.shape[0]
    half = clusters // 2
    assert stored == unknowns and 2 * directions == unknowns
    ahead, cross = ring_pairs(count)
    mate = [(i, i ^ 1) for i in range(count)]
    side = [(i, i ^ 2) for i in range(count)]

    def move(values, where):
        return lax.ppermute(values, "blk", where)

    def after(values, *others):
        return lax.optimization_barrier((values, *others))[0]

    flow = [move(rhs, ahead), move(rhs, cross)]
    here = me.astype(jnp.int32).reshape(1)
    coef, here_rhs, lists = pl.pallas_call(
        functools.partial(prologue_kernel, count),
        out_shape=[
            jax.ShapeDtypeStruct((half * rank_k, unknowns), jnp.bfloat16),
            jax.ShapeDtypeStruct(rhs.shape, rhs.dtype),
            jax.ShapeDtypeStruct((8, stored), jnp.int32),
        ],
        in_specs=[whole(pltpu.SMEM)] + [whole()] * 5,
        out_specs=[whole()] * 3,
        name="prologue",
    )(
        here,
        near_owner.reshape(1, stored),
        near_slot.reshape(1, stored),
        near_offset.reshape(1, stored),
        rhs,
        basis_in,
    )
    slots = {0: here_rhs, 1: move(rhs, mate)}
    coefs, level = coef, 1
    waits = [[coef, here_rhs, lists], []]
    for t in range(1, depth + 1):
        for x in range(2 if t < depth else 1):
            flow[x] = after(flow[x], *waits[x])
            slots[2 * t + x] = flow[x]
            opposite = 2 * (chips - t) + 1 - x
            if t + x < depth:
                moving = move(flow[x], ahead)
            slots[opposite] = move(flow[x], mate)
            waits[x] = [slots[opposite]]
            if t + x < depth:
                flow[x] = moving
            if x == 0 and level < depth:
                got = move(coefs, [(i, i ^ (4 * level)) for i in range(count)])
                coefs, level = jnp.concatenate([coefs, got], axis=0), 2 * level
                waits[1].append(coefs)
    coefs = [coefs, move(coefs, side)]
    couple = jnp.transpose(far_coupling, (2, 1, 0))

    def near(late, lists):
        parts = [1, 2 * depth - 4] if late else [1, 1, 1]
        size = sum(parts) * clusters
        *sends, kept = pl.pallas_call(
            functools.partial(near_kernel, late, 4, count),
            out_shape=[
                jax.ShapeDtypeStruct((part * clusters, directions, unknowns), jnp.bfloat16)
                for part in parts
            ]
            + [jax.ShapeDtypeStruct((size, directions, unknowns), jnp.float32)],
            in_specs=[whole(pltpu.SMEM)] + [whole(pl.ANY)] * (count + 1),
            out_specs=[whole()] * (len(parts) + 1),
            scratch_shapes=[
                pltpu.VMEM((count, clusters, directions, unknowns), jnp.bfloat16),
                pltpu.VMEM(near_blocks.shape, jnp.bfloat16),
                pltpu.VMEM((2 * size + 1, directions, unknowns), jnp.float32),
                pltpu.SemaphoreType.DMA((count + 1,)),
            ],
            compiler_params=pltpu.CompilerParams(vmem_limit_bytes=NEAR_VMEM),
            cost_estimate=pl.CostEstimate(
                flops=2 * stored * directions * unknowns * unknowns * 8,
                bytes_accessed=12 << 20,
                transcendentals=0,
            ),
            name="near",
        )(lists, *[slots[k] for k in range(count)], near_blocks)
        return [move(send, mate) for send in sends], kept

    own, mates = [None, None], [None, None]

    def term(late, k):
        part, skip = (min(k, 1), min(k, 1)) if late else (k, k)
        at = slice(k * clusters, (k + 1) * clusters)
        got = mates[late][part][(k - skip) * clusters : (k - skip + 1) * clusters]
        return own[late][at] + got.astype(jnp.float32)

    def add(flow, late, k, *others):
        step = (flow.astype(jnp.float32) + term(late, k)).astype(jnp.bfloat16)
        step, mates[late], *_ = lax.optimization_barrier((step, mates[late], *others))
        return step

    mates[0], own[0] = near(False, lists)
    flow = [term(0, 0).astype(jnp.bfloat16), term(0, 1).astype(jnp.bfloat16)]
    *flow, lists, coefs[0], coefs[1] = lax.optimization_barrier((*flow, lists, *coefs))
    flow = [move(part, ahead) for part in flow]
    coefs = coefs + [move(part, mate) for part in coefs]
    mates[1], own[1] = near(True, lists)
    far = pl.pallas_call(
        far_kernel,
        out_shape=jax.ShapeDtypeStruct((clusters, directions, unknowns), jnp.float32),
        in_specs=[whole()] * 4 + [whole(pltpu.SMEM)] + [whole()] * 5,
        out_specs=whole(),
        compiler_params=pltpu.CompilerParams(vmem_limit_bytes=FAR_VMEM),
        cost_estimate=pl.CostEstimate(
            flops=4 * clusters * rank_k * pairs * rank_k * unknowns,
            bytes_accessed=8 << 20,
            transcendentals=0,
        ),
        name="far",
    )(
        *coefs,
        here,
        couple,
        far_slot.reshape(1, pairs),
        far_dev.reshape(1, pairs),
        far_cslot.reshape(1, pairs),
        basis_out,
    )
    for t in range(depth - 1, 0, -1):
        if t == depth - 1:
            flow[0] = add(flow[0], 0, 2)
        elif t > 1:
            flow[0] = add(flow[0], 1, 2 * (depth - 2 - t) + 1)
        else:
            flow[0] = add(flow[0], 1, 2 * (depth - 2 - t) + 1, far)
        flow[0] = move(flow[0], ahead)
        if t > 1:
            flow[1] = move(add(flow[1], 1, 2 * (depth - 1 - t)), ahead)
        else:
            flow[1] = move(flow[1], mate)
    total = far + term(1, 2 * (depth - 2)) + flow[1].astype(jnp.float32)
    return (total + flow[0].astype(jnp.float32)).astype(jnp.bfloat16)


def on_device(*args):
    rhs = args[0]
    count = lax.axis_size("blk")
    if count % 4 == 0 and count >= 16 and count * rhs.size * 4 <= DENSE_BYTES:
        return stationary(*args)
    return routed(*args)


def solution(mesh):
    placed = (
        P(("groups", "blk"), None, None),
        P(("groups", "blk"), None, None),
        P(("groups", "blk"), None),
        P(("groups", "blk")),
        P(("groups", "blk")),
        P(("groups", "blk"), None, None),
        P(("groups", "blk")),
        P(("groups", "blk"), None),
        P(("groups", "blk")),
        P(("groups", "blk"), None, None),
        P(("groups", "blk"), None, None),
    )
    return jax.shard_map(
        on_device,
        mesh=mesh,
        in_specs=placed,
        out_specs=P(("groups", "blk"), None, None),
        check_vma=False,
    )
```

```python
import functools

import jax
import jax.numpy as jnp
from jax import lax
from jax.experimental import pallas as pl
from jax.experimental.pallas import tpu as pltpu
from jax.sharding import PartitionSpec as P

NEAR_VMEM = 16 << 20
FAR_VMEM = 16 << 20


def with_halo(cells, sides, width):
    for axis, dim in sides:
        count = lax.axis_size(axis)
        head = lax.slice_in_dim(cells, 0, width, axis=dim)
        tail = lax.slice_in_dim(cells, cells.shape[dim] - width, cells.shape[dim], axis=dim)
        cells = jnp.concatenate(
            [
                lax.ppermute(tail, axis, [(i, (i + 1) % count) for i in range(count)]),
                cells,
                lax.ppermute(head, axis, [((i + 1) % count, i) for i in range(count)]),
            ],
            axis=dim,
        )
    return cells


def place_ranks(targets, count):
    onehot = (targets[:, None] == jnp.arange(count, dtype=jnp.int32)[None, :]).astype(jnp.int32)
    before = jnp.cumsum(onehot, axis=0) - onehot
    return jnp.sum(before * onehot, axis=1)


def routed(
    rhs,
    near_blocks,
    near_owner,
    near_slot,
    near_offset,
    far_coupling,
    far_slot,
    far_dev,
    far_cslot,
    basis_out,
    basis_in,
):
    clusters = rhs.shape[0]
    directions = rhs.shape[1]
    unknowns = rhs.shape[2]
    cycle_size = lax.axis_size("blk")
    stored = near_blocks.shape[0]
    capacity = max(2, 2 * stored // cycle_size)
    owners = near_owner[:, 0]
    target = owners * capacity + place_ranks(owners, cycle_size)
    outbox = (
        jnp.zeros((cycle_size * capacity, unknowns, unknowns), near_blocks.dtype)
        .at[target]
        .set(near_blocks)
    )
    labels = (
        jnp.zeros((cycle_size * capacity, 2), jnp.int32)
        .at[target]
        .set(jnp.stack([near_slot, near_offset], axis=1))
    )
    window = with_halo(rhs, (("blk", 0),), clusters)
    inbox, in_labels = (
        lax.all_to_all(outbox, "blk", split_axis=0, concat_axis=0, tiled=True),
        lax.all_to_all(labels, "blk", split_axis=0, concat_axis=0, tiled=True),
    )
    position = clusters + in_labels[:, 0] + in_labels[:, 1]
    columns = jnp.take(window, position, axis=0)
    products = jnp.einsum("srj,sij->sri", columns, inbox, preferred_element_type=jnp.float32)
    selector = (in_labels[:, 0][None, :] == jnp.arange(clusters, dtype=jnp.int32)[:, None]).astype(
        jnp.float32
    )
    near_sum = jnp.dot(
        selector,
        products.reshape(products.shape[0], -1),
        precision=lax.Precision.HIGHEST,
        preferred_element_type=jnp.float32,
    ).reshape(clusters, directions, unknowns)
    coef_local = jnp.einsum(
        "ckj,crj->crk", basis_in, rhs, preferred_element_type=jnp.float32
    ).astype(jnp.bfloat16)
    rank_k = basis_in.shape[1]
    coef_local = coef_local.reshape(clusters, directions * rank_k)
    pairs = far_slot.shape[0]
    wanted = far_dev[:, 0] * clusters + far_cslot
    piece = lax.all_gather(coef_local, "blk", axis=0, tiled=True)
    chosen = jnp.take(piece, wanted, axis=0)
    coupled = jnp.einsum(
        "pkq,prq->prk",
        far_coupling,
        chosen.reshape(pairs, directions, rank_k),
        preferred_element_type=jnp.float32,
    )
    row_pick = (far_slot[None, :] == jnp.arange(clusters, dtype=jnp.int32)[:, None]).astype(
        jnp.float32
    )
    gathered = jnp.dot(
        row_pick,
        coupled.reshape(pairs, -1),
        precision=lax.Precision.HIGHEST,
        preferred_element_type=jnp.float32,
    )
    gathered = gathered.astype(jnp.bfloat16).reshape(clusters, directions, rank_k)
    far_sum = jnp.einsum("crk,ckb->crb", gathered, basis_out, preferred_element_type=jnp.float32)
    return (near_sum + far_sum).astype(jnp.bfloat16)


def whole(space=pltpu.VMEM):
    return pl.BlockSpec(memory_space=space)


def prologue_kernel(
    count, me_ref, own_ref, mate_ref, rhs_ref, basis_ref, blocks_ref, *outs
):
    clusters = rhs_ref.shape[0]
    rank_k = basis_ref.shape[1]
    half = clusters // 2
    coef_ref, copy_ref, list_ref, held_ref, sem = outs
    hold = pltpu.make_async_copy(blocks_ref, held_ref, sem)
    hold.start()
    copy_ref[...] = rhs_ref[...]
    rows = []
    for c in range(half):
        parts = [
            lax.dot_general(
                basis_ref[e],
                rhs_ref[e],
                (((1,), (1,)), ((), ())),
                preferred_element_type=jnp.float32,
            )
            for e in (c, c + half)
        ]
        rows.append(jnp.concatenate(parts, axis=1))
    coef_ref[...] = jnp.concatenate(
        [row[q : q + 1] for q in range(rank_k) for row in rows], axis=0
    ).astype(coef_ref.dtype)

    lists = [ordered_blocks(ref[...], me_ref[0], count, clusters) for ref in (own_ref, mate_ref)]
    list_ref[...] = jnp.concatenate(lists, axis=0).astype(jnp.int32)
    hold.wait()


def ordered_blocks(labels, me, count, clusters):
    stored = labels.shape[1]
    owner, slot, offset = labels[0:1], labels[1:2], labels[2:3]
    place = scatter_place(owner, me, count) * clusters + slot
    column = (owner * clusters + slot + offset) & (count * clusters - 1)
    shard = gather_place(column // clusters, me, count).astype(jnp.float32)
    square = (stored, stored)
    shard = jnp.broadcast_to(shard, square)
    shard_of_row = jnp.transpose(shard)
    row_at = lax.broadcasted_iota(jnp.int32, square, 0)
    lane_at = lax.broadcasted_iota(jnp.int32, square, 1)
    lane = lane_at.astype(jnp.float32)
    before = (shard_of_row < shard) | ((shard_of_row == shard) & (row_at < lane_at))
    rank = jnp.sum(jnp.where(before, 1.0, 0.0), axis=0, keepdims=True)
    rank = jnp.transpose(jnp.broadcast_to(rank, square))
    here = jnp.where(rank == lane, 1.0, 0.0).astype(jnp.bfloat16)
    starts = jnp.sum(jnp.where(shard_of_row < lane, 1.0, 0.0), axis=0, keepdims=True)
    values = jnp.concatenate(
        [lane[0:1], place.astype(jnp.float32), (column & (clusters - 1)).astype(jnp.float32)]
        + [jnp.zeros((5, stored), jnp.float32)],
        axis=0,
    )
    values = jnp.dot(values.astype(jnp.bfloat16), here, preferred_element_type=jnp.float32)
    return jnp.concatenate([values[0:3], starts], axis=0)


def near_kernel(k, batch, sends, list_ref, column_ref, own_ref, mate_ref, *rest):
    sum_ref = rest[-1 - sends]
    if k == 0:
        sum_ref[...] = jnp.zeros_like(sum_ref)
    last = own_ref.shape[0] - 1
    dummy = sum_ref.shape[0] - 1
    for base, blocks_ref in ((0, own_ref), (4, mate_ref)):
        begin, end = list_ref[base + 3, k], list_ref[base + 3, k + 1]

        def body(step, carry, base=base, blocks_ref=blocks_ref, begin=begin, end=end):
            first = begin + step * batch
            products = []
            for i in range(batch):
                at = jnp.minimum(first + i, last)
                products.append(
                    lax.dot_general(
                        column_ref[list_ref[base + 2, at]],
                        blocks_ref[list_ref[base, at]],
                        (((1,), (1,)), ((), ())),
                        preferred_element_type=jnp.float32,
                    )
                )
            for i in range(batch):
                at = jnp.minimum(first + i, last)
                at = jnp.where(first + i < end, list_ref[base + 1, at], dummy)
                sum_ref[at] = sum_ref[at] + products[i]
            return carry

        lax.fori_loop(0, (end - begin + batch - 1) // batch, body, 0)
    at = dummy // 2
    for send_ref in rest[len(rest) - sends :]:
        size = send_ref.shape[0]
        send_ref[...] = sum_ref[at : at + size].astype(send_ref.dtype)
        at += size


def far_kernel(*refs):
    coef_refs = refs[:4]
    me_ref, couple_ref, slot_ref, dev_ref, cslot_ref, basis_ref, out_ref = refs[4:]
    clusters, rank_k, unknowns = basis_ref.shape
    pairs = couple_ref.shape[2]
    directions = out_ref.shape[1]
    half = clusters // 2
    coef = jnp.concatenate([ref[...].astype(jnp.float32) for ref in coef_refs], axis=0)
    coef = coef.reshape(-1, rank_k, half, unknowns)
    count = coef.shape[0]
    hot = (
        lax.broadcasted_iota(jnp.int32, (clusters, pairs), 0)
        == jnp.broadcast_to(slot_ref[...], (clusters, pairs))
    ).astype(jnp.float32).astype(jnp.bfloat16)
    away = dev_ref[...] ^ me_ref[0]
    away = (away & 1) * (count // 2) + ((away >> 1) & 1) * (count // 4) + (away >> 2)
    cslot = cslot_ref[...]
    high = (cslot >= half).astype(jnp.int32)
    at = away * half + cslot - high * half
    table_rows = (count * half, pairs)
    pick = jnp.where(
        lax.broadcasted_iota(jnp.int32, table_rows, 0) == jnp.broadcast_to(at, table_rows), 1.0, 0.0
    )
    pick = jnp.transpose(pick).astype(jnp.bfloat16)
    lanes = (unknowns, pairs)
    keep = jnp.where(
        lax.broadcasted_iota(jnp.int32, lanes, 0) // directions == jnp.broadcast_to(high, lanes),
        1.0,
        0.0,
    )
    keep = jnp.transpose(keep).astype(jnp.bfloat16)
    total = jnp.zeros((clusters * rank_k, unknowns), jnp.float32)
    for q in range(rank_k):
        table = coef[:, q].reshape(count * half, unknowns).astype(jnp.bfloat16)
        chosen = jnp.dot(pick, table, preferred_element_type=jnp.float32).astype(jnp.bfloat16)
        chosen = chosen * keep
        couple = couple_ref[q]
        weight = jnp.concatenate([couple * hot[s : s + 1] for s in range(clusters)], axis=0)
        total = total + jnp.dot(weight, chosen, preferred_element_type=jnp.float32)
    total = total + pltpu.roll(total, unknowns // 2, axis=1)
    gathered = jnp.transpose(total)[0:directions, :].astype(jnp.bfloat16).astype(jnp.float32)
    lane = lax.broadcasted_iota(jnp.int32, gathered.shape, 1) // rank_k
    basis = basis_ref[...].reshape(clusters * rank_k, unknowns)
    for s in range(clusters):
        own = jnp.where(lane == s, gathered, 0.0).astype(jnp.bfloat16)
        out_ref[s] = jnp.dot(own, basis, preferred_element_type=jnp.float32)


def ring_device(place, core, chips):
    depth = chips // 2
    place = place % chips
    z, y = (place, 0) if place < depth else (chips - 1 - place, 1)
    return (z * 2 + y) * 2 + core


def ring_pairs(count):
    chips = count // 2
    cores = [(p, c) for p in range(chips) for c in range(2)]
    ahead = [(ring_device(p, c, chips), ring_device(p + 1 - 2 * c, c, chips)) for p, c in cores]
    cross = [
        (ring_device(p, c, chips), ring_device(p - 1 + 2 * c, 1 - c, chips)) for p, c in cores
    ]
    return ahead, cross


def ring_place(device, chips):
    z, y = device >> 2, (device >> 1) & 1
    return jnp.where(y == 0, z, chips - 1 - z)


def gather_place(device, me, count):
    chips = count // 2
    depth = chips // 2
    back = (1 - 2 * (me & 1)) * (ring_place(me, chips) - ring_place(device, chips))
    back = (back + chips) & (chips - 1)
    other = (device ^ me) & 1
    here = (back < depth) & (back > 0) | ((back & (depth - 1)) == 0) & (other == 0)
    return jnp.where(here, jnp.where(back == 0, 0, 2 * back - 1 + other), chips)


def scatter_place(device, me, count):
    chips = count // 2
    depth = chips // 2
    ahead = (ring_place(device, chips) - ring_place(me, chips) + chips) & (chips - 1)
    core = device & 1
    handler = jnp.where((ahead & (depth - 1)) == 0, core, (ahead > depth).astype(jnp.int32))
    steps = jnp.where(handler == 0, ahead, (chips - ahead) & (chips - 1))
    place = jnp.where(
        steps == depth,
        0,
        jnp.where(steps == 0, chips - 1, 2 * (depth - steps) - (core ^ handler)),
    )
    return place + jnp.where(handler == (me & 1), 0, chips)


def stationary(
    rhs,
    near_blocks,
    near_owner,
    near_slot,
    near_offset,
    far_coupling,
    far_slot,
    far_dev,
    far_cslot,
    basis_out,
    basis_in,
):
    clusters, directions, unknowns = rhs.shape
    rank_k = basis_in.shape[1]
    count = lax.axis_size("blk")
    chips = count // 2
    depth = chips // 2
    me = lax.axis_index("blk")
    stored = near_blocks.shape[0]
    pairs = far_slot.shape[0]
    half = clusters // 2
    ahead, cross = ring_pairs(count)
    mate = [(i, i ^ 1) for i in range(count)]
    side = [(i, i ^ 2) for i in range(count)]

    def move(values, where):
        return lax.ppermute(values, "blk", where)

    def after(values, *others):
        return lax.optimization_barrier((values, *others))[0]

    def after(values, *others):
        return lax.optimization_barrier((values, *others))[0]

    flow = [move(rhs, ahead), move(rhs, cross)]
    labels = jnp.stack([near_owner[:, 0], near_slot, near_offset], axis=0)
    mate_labels = move(labels, mate)
    mate_blocks = move(near_blocks, mate)
    here = me.astype(jnp.int32).reshape(1)
    coef, here_rhs, lists, own_blocks = pl.pallas_call(
        functools.partial(prologue_kernel, count),
        out_shape=[
            jax.ShapeDtypeStruct((half * rank_k, unknowns), jnp.bfloat16),
            jax.ShapeDtypeStruct(rhs.shape, rhs.dtype),
            jax.ShapeDtypeStruct((8, stored), jnp.int32),
            jax.ShapeDtypeStruct(near_blocks.shape, near_blocks.dtype),
        ],
        in_specs=[whole(pltpu.SMEM)] + [whole()] * 4 + [whole(pl.ANY)],
        out_specs=[whole()] * 4,
        scratch_shapes=[pltpu.SemaphoreType.DMA],
        name="prologue",
    )(here, labels, mate_labels, rhs, basis_in, near_blocks)
    got = move(coef, [(i, i ^ 4) for i in range(count)])

    pieces = [1, 1, chips - 2]

    def near(k, shard, sums):
        sends = pieces if k == chips - 1 else []
        sum_shape = jax.ShapeDtypeStruct((count * clusters + 1, directions, unknowns), jnp.float32)
        return pl.pallas_call(
            functools.partial(near_kernel, k, 4, len(sends)),
            out_shape=[sum_shape]
            + [
                jax.ShapeDtypeStruct((part * clusters, directions, unknowns), jnp.bfloat16)
                for part in sends
            ],
            in_specs=[whole(pltpu.SMEM)] + [whole()] * (3 + len(sums)),
            out_specs=[whole()] * (1 + len(sends)),
            input_output_aliases={4: 0} if sums else {},
            compiler_params=pltpu.CompilerParams(vmem_limit_bytes=NEAR_VMEM),
            cost_estimate=pl.CostEstimate(
                flops=2 * stored * directions * unknowns * unknowns,
                bytes_accessed=2 << 20,
                transcendentals=0,
            ),
            name="near",
        )(lists, shard, own_blocks, mate_blocks, *sums)

    sums, passed = near(0, here_rhs, []), None
    waits = [coef, here_rhs, lists]
    for k in range(1, chips):
        x = 1 - k % 2
        shard = after(flow[x], *waits)
        if k < chips - 2:
            flow[x] = move(shard, ahead)
        waits = [sums[0], got] if k == depth else [sums[0]]
        sums = near(k, shard, sums)
    sums, *sends = sums
    couple = jnp.transpose(far_coupling, (2, 1, 0))

    mates = [move(part, mate) for part in sends]

    def term(k):
        part = min(k, 2)
        got = mates[part][(k - part) * clusters : (k - part + 1) * clusters]
        return sums[k * clusters : (k + 1) * clusters] + got.astype(jnp.float32)

    def tied(values, *others):
        values, mates[2], *others = lax.optimization_barrier((values, mates[2], *others))
        return values, *others

    def add(flow, k):
        return (flow.astype(jnp.float32) + term(k)).astype(jnp.bfloat16)

    flow = [term(0).astype(jnp.bfloat16), term(1).astype(jnp.bfloat16)]
    *flow, coef, got = lax.optimization_barrier((*flow, coef, got))
    flow = [move(part, ahead) for part in flow]
    coefs = jnp.concatenate([coef, got], axis=0)
    got = move(coefs, [(i, i ^ 8) for i in range(count)])
    flow[0] = move(tied(add(flow[0], 2))[0], ahead)
    flow[1], coefs, got = tied(add(flow[1], 3), coefs, got)
    flow[1] = move(flow[1], ahead)
    coefs = jnp.concatenate([coefs, got], axis=0)
    got = move(coefs, side)
    flow[0], coefs, got = tied(add(flow[0], 4), coefs, got)
    flow[0] = move(flow[0], ahead)
    coefs = [coefs, got, move(coefs, mate), move(got, mate)]
    flow[1] = move(tied(add(flow[1], 5))[0], ahead)
    far = pl.pallas_call(
        far_kernel,
        out_shape=jax.ShapeDtypeStruct((clusters, directions, unknowns), jnp.float32),
        in_specs=[whole()] * 4 + [whole(pltpu.SMEM)] + [whole()] * 5,
        out_specs=whole(),
        compiler_params=pltpu.CompilerParams(vmem_limit_bytes=FAR_VMEM),
        cost_estimate=pl.CostEstimate(
            flops=4 * clusters * rank_k * pairs * rank_k * unknowns,
            bytes_accessed=8 << 20,
            transcendentals=0,
        ),
        name="far",
    )(
        *coefs,
        here,
        couple,
        far_slot.reshape(1, pairs),
        far_dev.reshape(1, pairs),
        far_cslot.reshape(1, pairs),
        basis_out,
    )
    flow[0] = move(tied(add(flow[0], 6), far)[0], ahead)
    flow[1] = move(flow[1], mate)
    total = far + term(chips - 1) + flow[1].astype(jnp.float32)
    return (total + flow[0].astype(jnp.float32)).astype(jnp.bfloat16)


def on_device(*args):
    rhs, near_blocks = args[0], args[1]
    clusters, directions, unknowns = rhs.shape
    small = lax.axis_size("blk") == 16 and clusters == 16
    if small and near_blocks.shape[0] == unknowns and 2 * directions == unknowns:
        return stationary(*args)
    return routed(*args)


def solution(mesh):
    placed = (
        P(("groups", "blk"), None, None),
        P(("groups", "blk"), None, None),
        P(("groups", "blk"), None),
        P(("groups", "blk")),
        P(("groups", "blk")),
        P(("groups", "blk"), None, None),
        P(("groups", "blk")),
        P(("groups", "blk"), None),
        P(("groups", "blk")),
        P(("groups", "blk"), None, None),
        P(("groups", "blk"), None, None),
    )
    return jax.shard_map(
        on_device,
        mesh=mesh,
        in_specs=placed,
        out_specs=P(("groups", "blk"), None, None),
        check_vma=False,
    )
```

```python
import functools

import jax
import jax.numpy as jnp
from jax import lax
from jax.experimental import pallas as pl
from jax.experimental.pallas import tpu as pltpu
from jax.sharding import PartitionSpec as P

CHUNKS = 4
BATCH = 8
PROLOGUE_VMEM = 16 << 20
NEAR_VMEM = 44 << 20
FAR_VMEM = 16 << 20


def with_halo(cells, sides, width):
    for axis, dim in sides:
        count = lax.axis_size(axis)
        head = lax.slice_in_dim(cells, 0, width, axis=dim)
        tail = lax.slice_in_dim(cells, cells.shape[dim] - width, cells.shape[dim], axis=dim)
        cells = jnp.concatenate(
            [
                lax.ppermute(tail, axis, [(i, (i + 1) % count) for i in range(count)]),
                cells,
                lax.ppermute(head, axis, [((i + 1) % count, i) for i in range(count)]),
            ],
            axis=dim,
        )
    return cells


def place_ranks(targets, count):
    onehot = (targets[:, None] == jnp.arange(count, dtype=jnp.int32)[None, :]).astype(jnp.int32)
    before = jnp.cumsum(onehot, axis=0) - onehot
    return jnp.sum(before * onehot, axis=1)


def routed(
    rhs,
    near_blocks,
    near_owner,
    near_slot,
    near_offset,
    far_coupling,
    far_slot,
    far_dev,
    far_cslot,
    basis_out,
    basis_in,
):
    clusters = rhs.shape[0]
    directions = rhs.shape[1]
    unknowns = rhs.shape[2]
    cycle_size = lax.axis_size("blk")
    stored = near_blocks.shape[0]
    capacity = max(2, 2 * stored // cycle_size)
    owners = near_owner[:, 0]
    target = owners * capacity + place_ranks(owners, cycle_size)
    outbox = (
        jnp.zeros((cycle_size * capacity, unknowns, unknowns), near_blocks.dtype)
        .at[target]
        .set(near_blocks)
    )
    labels = (
        jnp.zeros((cycle_size * capacity, 2), jnp.int32)
        .at[target]
        .set(jnp.stack([near_slot, near_offset], axis=1))
    )
    window = with_halo(rhs, (("blk", 0),), clusters)
    inbox, in_labels = (
        lax.all_to_all(outbox, "blk", split_axis=0, concat_axis=0, tiled=True),
        lax.all_to_all(labels, "blk", split_axis=0, concat_axis=0, tiled=True),
    )
    position = clusters + in_labels[:, 0] + in_labels[:, 1]
    columns = jnp.take(window, position, axis=0)
    products = jnp.einsum("srj,sij->sri", columns, inbox, preferred_element_type=jnp.float32)
    selector = (in_labels[:, 0][None, :] == jnp.arange(clusters, dtype=jnp.int32)[:, None]).astype(
        jnp.float32
    )
    near_sum = jnp.dot(
        selector,
        products.reshape(products.shape[0], -1),
        precision=lax.Precision.HIGHEST,
        preferred_element_type=jnp.float32,
    ).reshape(clusters, directions, unknowns)
    coef_local = jnp.einsum(
        "ckj,crj->crk", basis_in, rhs, preferred_element_type=jnp.float32
    ).astype(jnp.bfloat16)
    rank_k = basis_in.shape[1]
    coef_local = coef_local.reshape(clusters, directions * rank_k)
    pairs = far_slot.shape[0]
    wanted = far_dev[:, 0] * clusters + far_cslot
    piece = lax.all_gather(coef_local, "blk", axis=0, tiled=True)
    chosen = jnp.take(piece, wanted, axis=0)
    coupled = jnp.einsum(
        "pkq,prq->prk",
        far_coupling,
        chosen.reshape(pairs, directions, rank_k),
        preferred_element_type=jnp.float32,
    )
    row_pick = (far_slot[None, :] == jnp.arange(clusters, dtype=jnp.int32)[:, None]).astype(
        jnp.float32
    )
    gathered = jnp.dot(
        row_pick,
        coupled.reshape(pairs, -1),
        precision=lax.Precision.HIGHEST,
        preferred_element_type=jnp.float32,
    )
    gathered = gathered.astype(jnp.bfloat16).reshape(clusters, directions, rank_k)
    far_sum = jnp.einsum("crk,ckb->crb", gathered, basis_out, preferred_element_type=jnp.float32)
    return (near_sum + far_sum).astype(jnp.bfloat16)


def whole(space=pltpu.VMEM):
    return pl.BlockSpec(memory_space=space)


def prologue_kernel(
    count, me_ref, owner_ref, slot_ref, offset_ref, rhs_ref, basis_ref, coef_ref, list_ref
):
    clusters = rhs_ref.shape[0]
    rank_k = basis_ref.shape[1]
    half = clusters // 2
    rows = []
    for c in range(half):
        parts = [
            lax.dot_general(
                basis_ref[e],
                rhs_ref[e],
                (((1,), (1,)), ((), ())),
                preferred_element_type=jnp.float32,
            )
            for e in (c, c + half)
        ]
        rows.append(jnp.concatenate(parts, axis=1))
    coef_ref[...] = jnp.concatenate(
        [row[q : q + 1] for q in range(rank_k) for row in rows], axis=0
    ).astype(coef_ref.dtype)

    me, owner, slot = me_ref[0], owner_ref[...], slot_ref[...]
    stored = owner.shape[1]
    place = scatter_place(owner, me, count) * clusters + slot
    column = (owner * clusters + slot + offset_ref[...]) & (count * clusters - 1)
    shard = gather_place(column // clusters, me, count)
    theirs = shard == count // 2
    shard = jnp.where(theirs, gather_place(column // clusters, me ^ 1, count), shard)
    column_place = shard * clusters + (column & (clusters - 1))
    square = (stored, stored)
    late = jnp.broadcast_to(jnp.where(theirs, 1.0, 0.0), square)
    late_of_row = jnp.transpose(late)
    row_at = lax.broadcasted_iota(jnp.int32, square, 0)
    lane_at = lax.broadcasted_iota(jnp.int32, square, 1)
    lane = lane_at.astype(jnp.float32)
    before = (late_of_row < late) | ((late_of_row == late) & (row_at < lane_at))
    rank = jnp.sum(jnp.where(before, 1.0, 0.0), axis=0, keepdims=True)
    rank = jnp.transpose(jnp.broadcast_to(rank, square))
    here = jnp.where(rank == lane, 1.0, 0.0).astype(jnp.bfloat16)
    chunk = row_at < lane_at * (stored // CHUNKS)
    mine = jnp.sum(jnp.where(chunk, 1.0 - late_of_row, 0.0), axis=0, keepdims=True)
    other = jnp.sum(jnp.where(chunk, late_of_row, 0.0), axis=0, keepdims=True)
    other = other + (stored - jnp.sum(late[0:1], axis=1, keepdims=True))
    values = jnp.concatenate(
        [lane[0:1], place.astype(jnp.float32), column_place.astype(jnp.float32)]
        + [jnp.zeros((5, stored), jnp.float32)],
        axis=0,
    )
    values = jnp.dot(values.astype(jnp.bfloat16), here, preferred_element_type=jnp.float32)
    values = jnp.concatenate([values[0:3], mine, other, values[5:8]], axis=0)
    list_ref[...] = values.astype(jnp.int32)


def near_kernel(batch, shards, sends, list_ref, mate_list_ref, *refs):
    shard_refs, (own_hbm, mate_hbm) = refs[:shards], refs[shards : shards + 2]
    keep_ref, refs = refs[shards + 2], refs[shards + 3 :]
    send_refs, (columns, blocks, sums, column_sem, block_sem) = refs[:sends], refs[sends:]
    clusters = shard_refs[0].shape[0]
    chunk = blocks.shape[1] // CHUNKS

    def load(source, half, c):
        at = pl.ds(c * chunk, chunk)
        return pltpu.make_async_copy(
            source.at[at], blocks.at[half, at], block_sem.at[half * CHUNKS + c]
        )

    copies = [
        pltpu.make_async_copy(ref, columns.at[pl.ds(k * clusters, clusters)], column_sem.at[k])
        for k, ref in enumerate(shard_refs)
    ]
    for copy in copies:
        copy.start()
    for half, source in enumerate((own_hbm, mate_hbm)):
        for c in range(CHUNKS):
            load(source, half, c).start()

    dummy = sums.shape[0] - 1

    def clear(i, carry):
        sums[i] = jnp.zeros(sums.shape[1:], sums.dtype)
        return carry

    lax.fori_loop(0, dummy, clear, 0)
    for copy in copies:
        copy.wait()
    for half, (source, ref) in enumerate(((own_hbm, list_ref), (mate_hbm, mate_list_ref))):
        swap = half * (dummy // 2)

        def run(c, carry, half=half, source=source, ref=ref, swap=swap):
            load(source, half, c).wait()
            begin, end = ref[3 + half, c], ref[3 + half, c + 1]

            def body(step, carry):
                first = begin + step * batch
                products = []
                for i in range(batch):
                    at = jnp.minimum(first + i, end - 1)
                    products.append(
                        lax.dot_general(
                            columns[ref[2, at]],
                            blocks[half, ref[0, at]],
                            (((1,), (1,)), ((), ())),
                            preferred_element_type=jnp.float32,
                        )
                    )
                for i in range(batch):
                    at = jnp.minimum(first + i, end - 1)
                    at = jnp.where(first + i < end, ref[1, at] ^ swap, dummy)
                    sums[at] = sums[at] + products[i]
                return carry

            return lax.fori_loop(0, (end - begin + batch - 1) // batch, body, carry)

        lax.fori_loop(0, CHUNKS, run, 0)

    def keep(i, carry):
        keep_ref[i] = sums[i]
        return carry

    lax.fori_loop(0, dummy // 2, keep, 0, unroll=2)
    at = dummy // 2
    for send_ref in send_refs:

        def pack(i, carry, at=at, send_ref=send_ref):
            send_ref[i] = sums[at + i].astype(send_ref.dtype)
            return carry

        lax.fori_loop(0, send_ref.shape[0], pack, 0, unroll=2)
        at += send_ref.shape[0]


def far_kernel(*refs):
    coef_refs = refs[:4]
    me_ref, couple_ref, slot_ref, dev_ref, cslot_ref, basis_ref, out_ref = refs[4:]
    clusters, rank_k, unknowns = basis_ref.shape
    pairs = couple_ref.shape[2]
    directions = out_ref.shape[1]
    half = clusters // 2
    coef = jnp.concatenate([ref[...].astype(jnp.float32) for ref in coef_refs], axis=0)
    coef = coef.reshape(-1, rank_k, half, unknowns)
    count = coef.shape[0]
    hot = (
        lax.broadcasted_iota(jnp.int32, (clusters, pairs), 0)
        == jnp.broadcast_to(slot_ref[...], (clusters, pairs))
    ).astype(jnp.float32).astype(jnp.bfloat16)
    away = dev_ref[...] ^ me_ref[0]
    away = (away & 1) * (count // 2) + ((away >> 1) & 1) * (count // 4) + (away >> 2)
    cslot = cslot_ref[...]
    high = (cslot >= half).astype(jnp.int32)
    at = away * half + cslot - high * half
    table_rows = (count * half, pairs)
    pick = jnp.where(
        lax.broadcasted_iota(jnp.int32, table_rows, 0) == jnp.broadcast_to(at, table_rows), 1.0, 0.0
    )
    pick = jnp.transpose(pick).astype(jnp.bfloat16)
    lanes = (unknowns, pairs)
    keep = jnp.where(
        lax.broadcasted_iota(jnp.int32, lanes, 0) // directions == jnp.broadcast_to(high, lanes),
        1.0,
        0.0,
    )
    keep = jnp.transpose(keep).astype(jnp.bfloat16)
    total = jnp.zeros((clusters * rank_k, unknowns), jnp.float32)
    for q in range(rank_k):
        table = coef[:, q].reshape(count * half, unknowns).astype(jnp.bfloat16)
        chosen = jnp.dot(pick, table, preferred_element_type=jnp.float32).astype(jnp.bfloat16)
        chosen = chosen * keep
        couple = couple_ref[q]
        weight = jnp.concatenate([couple * hot[s : s + 1] for s in range(clusters)], axis=0)
        total = total + jnp.dot(weight, chosen, preferred_element_type=jnp.float32)
    total = total + pltpu.roll(total, unknowns // 2, axis=1)
    gathered = jnp.transpose(total)[0:directions, :].astype(jnp.bfloat16).astype(jnp.float32)
    lane = lax.broadcasted_iota(jnp.int32, gathered.shape, 1) // rank_k
    basis = basis_ref[...].reshape(clusters * rank_k, unknowns)
    for s in range(clusters):
        own = jnp.where(lane == s, gathered, 0.0).astype(jnp.bfloat16)
        out_ref[s] = jnp.dot(own, basis, preferred_element_type=jnp.float32)


def ring_device(place, core, chips):
    depth = chips // 2
    place = place % chips
    z, y = (place, 0) if place < depth else (chips - 1 - place, 1)
    return (z * 2 + y) * 2 + core


def ring_pairs(count):
    chips = count // 2
    cores = [(p, c) for p in range(chips) for c in range(2)]
    ahead = [(ring_device(p, c, chips), ring_device(p + 1 - 2 * c, c, chips)) for p, c in cores]
    cross = [
        (ring_device(p, c, chips), ring_device(p - 1 + 2 * c, 1 - c, chips)) for p, c in cores
    ]
    return ahead, cross


def ring_place(device, chips):
    z, y = device >> 2, (device >> 1) & 1
    return jnp.where(y == 0, z, chips - 1 - z)


def gather_place(device, me, count):
    chips = count // 2
    depth = chips // 2
    back = (1 - 2 * (me & 1)) * (ring_place(me, chips) - ring_place(device, chips))
    back = (back + chips) & (chips - 1)
    other = (device ^ me) & 1
    here = (back < depth) & (back > 0) | ((back & (depth - 1)) == 0) & (other == 0)
    return jnp.where(here, jnp.where(back == 0, 0, 2 * back - 1 + other), chips)


def scatter_place(device, me, count):
    chips = count // 2
    depth = chips // 2
    ahead = (ring_place(device, chips) - ring_place(me, chips) + chips) & (chips - 1)
    core = device & 1
    handler = jnp.where((ahead & (depth - 1)) == 0, core, (ahead > depth).astype(jnp.int32))
    steps = jnp.where(handler == 0, ahead, (chips - ahead) & (chips - 1))
    place = jnp.where(
        steps == depth,
        0,
        jnp.where(steps == 0, chips - 1, 2 * (depth - steps) - (core ^ handler)),
    )
    return place + jnp.where(handler == (me & 1), 0, chips)


def stationary(
    rhs,
    near_blocks,
    near_owner,
    near_slot,
    near_offset,
    far_coupling,
    far_slot,
    far_dev,
    far_cslot,
    basis_out,
    basis_in,
):
    clusters, directions, unknowns = rhs.shape
    rank_k = basis_in.shape[1]
    count = lax.axis_size("blk")
    chips = count // 2
    depth = chips // 2
    me = lax.axis_index("blk")
    stored = near_blocks.shape[0]
    pairs = far_slot.shape[0]
    half = clusters // 2
    ahead, cross = ring_pairs(count)
    mate = [(i, i ^ 1) for i in range(count)]
    side = [(i, i ^ 2) for i in range(count)]

    def move(values, where):
        return lax.ppermute(values, "blk", where)

    def after(values, *others):
        return lax.optimization_barrier((values, *others))[0]

    flow = [move(rhs, ahead), move(rhs, cross)]
    mate_blocks = move(near_blocks, mate)
    here = me.astype(jnp.int32).reshape(1)
    coef, lists = pl.pallas_call(
        functools.partial(prologue_kernel, count),
        out_shape=[
            jax.ShapeDtypeStruct((half * rank_k, unknowns), jnp.bfloat16),
            jax.ShapeDtypeStruct((8, stored), jnp.int32),
        ],
        in_specs=[whole(pltpu.SMEM)] + [whole()] * 5,
        out_specs=[whole()] * 2,
        compiler_params=pltpu.CompilerParams(vmem_limit_bytes=PROLOGUE_VMEM),
        name="prologue",
    )(
        here,
        near_owner.reshape(1, stored),
        near_slot.reshape(1, stored),
        near_offset.reshape(1, stored),
        rhs,
        basis_in,
    )
    got = move(coef, [(i, i ^ 4) for i in range(count)])
    flow[0] = after(flow[0], coef, lists)
    shards = [rhs]
    for k in range(1, chips):
        x = 1 - k % 2
        if k == 3:
            flow[x], mate_blocks, lists = lax.optimization_barrier((flow[x], mate_blocks, lists))
        shards.append(flow[x])
        if k < chips - 2:
            flow[x] = move(flow[x], ahead)
        if k == 1:
            mate_lists = move(lists, mate)
        if k == 2:
            coef = jnp.concatenate([coef, after(got, shards[k])], axis=0)
            got = move(coef, [(i, i ^ 8) for i in range(count)])
        if k == 3:
            couple = after(jnp.transpose(far_coupling, (2, 1, 0)), shards[k])
        if k == 4:
            coef = jnp.concatenate([coef, after(got, shards[k])], axis=0)
            got = move(coef, side)
    coefs = [coef, got, move(coef, mate), move(got, mate)]
    lists = after(lists, couple, *coefs)

    pieces = [1, 1, chips - 2]
    kept, *sends = pl.pallas_call(
        functools.partial(near_kernel, BATCH, chips, len(pieces)),
        out_shape=[jax.ShapeDtypeStruct((chips * clusters, directions, unknowns), jnp.float32)]
        + [
            jax.ShapeDtypeStruct((part * clusters, directions, unknowns), jnp.bfloat16)
            for part in pieces
        ],
        in_specs=[whole(pltpu.SMEM)] * 2 + [whole(pl.ANY)] * (chips + 2),
        out_specs=[whole()] * (1 + len(pieces)),
        scratch_shapes=[
            pltpu.VMEM((chips * clusters, directions, unknowns), jnp.bfloat16),
            pltpu.VMEM((2, *near_blocks.shape), jnp.bfloat16),
            pltpu.VMEM((count * clusters + 1, directions, unknowns), jnp.float32),
            pltpu.SemaphoreType.DMA((chips,)),
            pltpu.SemaphoreType.DMA((2 * CHUNKS,)),
        ],
        compiler_params=pltpu.CompilerParams(vmem_limit_bytes=NEAR_VMEM),
        cost_estimate=pl.CostEstimate(
            flops=16 * stored * directions * unknowns * unknowns,
            bytes_accessed=16 << 20,
            transcendentals=0,
        ),
        name="near",
    )(lists, mate_lists, *shards, near_blocks, mate_blocks)

    mates = [move(part, mate) for part in sends]

    def term(k):
        part = min(k, 2)
        got = mates[part][(k - part) * clusters : (k - part + 1) * clusters]
        return kept[k * clusters : (k + 1) * clusters] + got.astype(jnp.float32)

    def tied(values, *others):
        values, mates[2], *others = lax.optimization_barrier((values, mates[2], *others))
        return values

    def add(flow, k):
        return (flow.astype(jnp.float32) + term(k)).astype(jnp.bfloat16)

    flow = lax.optimization_barrier([term(0).astype(jnp.bfloat16), term(1).astype(jnp.bfloat16)])
    couple = after(couple, *flow)
    flow = [move(part, ahead) for part in flow]
    far = pl.pallas_call(
        far_kernel,
        out_shape=jax.ShapeDtypeStruct((clusters, directions, unknowns), jnp.float32),
        in_specs=[whole()] * 4 + [whole(pltpu.SMEM)] + [whole()] * 5,
        out_specs=whole(),
        compiler_params=pltpu.CompilerParams(vmem_limit_bytes=FAR_VMEM),
        cost_estimate=pl.CostEstimate(
            flops=4 * clusters * rank_k * pairs * rank_k * unknowns,
            bytes_accessed=8 << 20,
            transcendentals=0,
        ),
        name="far",
    )(
        *coefs,
        here,
        couple,
        far_slot.reshape(1, pairs),
        far_dev.reshape(1, pairs),
        far_cslot.reshape(1, pairs),
        basis_out,
    )
    for k in range(2, chips - 1):
        x = k % 2
        flow[x] = move(tied(add(flow[x], k), *([far] if k == 2 else [])), ahead)
    flow[1] = move(flow[1], mate)
    total = far + term(chips - 1) + flow[1].astype(jnp.float32)
    return (total + flow[0].astype(jnp.float32)).astype(jnp.bfloat16)


def on_device(*args):
    rhs, near_blocks = args[0], args[1]
    clusters, directions, unknowns = rhs.shape
    small = lax.axis_size("blk") == 16 and clusters == 16
    if small and near_blocks.shape[0] == unknowns and 2 * directions == unknowns:
        return stationary(*args)
    return routed(*args)


def solution(mesh):
    placed = (
        P(("groups", "blk"), None, None),
        P(("groups", "blk"), None, None),
        P(("groups", "blk"), None),
        P(("groups", "blk")),
        P(("groups", "blk")),
        P(("groups", "blk"), None, None),
        P(("groups", "blk")),
        P(("groups", "blk"), None),
        P(("groups", "blk")),
        P(("groups", "blk"), None, None),
        P(("groups", "blk"), None, None),
    )
    return jax.shard_map(
        on_device,
        mesh=mesh,
        in_specs=placed,
        out_specs=P(("groups", "blk"), None, None),
        check_vma=False,
    )
```

```python
import functools

import jax
import jax.numpy as jnp
from jax import lax
from jax.experimental import pallas as pl
from jax.experimental.pallas import tpu as pltpu
from jax.sharding import PartitionSpec as P

CHUNKS = 4
BATCH = 8
PROLOGUE_VMEM = 58 << 20
NEAR_VMEM = 44 << 20
FAR_VMEM = 16 << 20


def with_halo(cells, sides, width):
    for axis, dim in sides:
        count = lax.axis_size(axis)
        head = lax.slice_in_dim(cells, 0, width, axis=dim)
        tail = lax.slice_in_dim(cells, cells.shape[dim] - width, cells.shape[dim], axis=dim)
        cells = jnp.concatenate(
            [
                lax.ppermute(tail, axis, [(i, (i + 1) % count) for i in range(count)]),
                cells,
                lax.ppermute(head, axis, [((i + 1) % count, i) for i in range(count)]),
            ],
            axis=dim,
        )
    return cells


def place_ranks(targets, count):
    onehot = (targets[:, None] == jnp.arange(count, dtype=jnp.int32)[None, :]).astype(jnp.int32)
    before = jnp.cumsum(onehot, axis=0) - onehot
    return jnp.sum(before * onehot, axis=1)


def routed(
    rhs,
    near_blocks,
    near_owner,
    near_slot,
    near_offset,
    far_coupling,
    far_slot,
    far_dev,
    far_cslot,
    basis_out,
    basis_in,
):
    clusters = rhs.shape[0]
    directions = rhs.shape[1]
    unknowns = rhs.shape[2]
    cycle_size = lax.axis_size("blk")
    stored = near_blocks.shape[0]
    capacity = max(2, 2 * stored // cycle_size)
    owners = near_owner[:, 0]
    target = owners * capacity + place_ranks(owners, cycle_size)
    outbox = (
        jnp.zeros((cycle_size * capacity, unknowns, unknowns), near_blocks.dtype)
        .at[target]
        .set(near_blocks)
    )
    labels = (
        jnp.zeros((cycle_size * capacity, 2), jnp.int32)
        .at[target]
        .set(jnp.stack([near_slot, near_offset], axis=1))
    )
    window = with_halo(rhs, (("blk", 0),), clusters)
    inbox, in_labels = (
        lax.all_to_all(outbox, "blk", split_axis=0, concat_axis=0, tiled=True),
        lax.all_to_all(labels, "blk", split_axis=0, concat_axis=0, tiled=True),
    )
    position = clusters + in_labels[:, 0] + in_labels[:, 1]
    columns = jnp.take(window, position, axis=0)
    products = jnp.einsum("srj,sij->sri", columns, inbox, preferred_element_type=jnp.float32)
    selector = (in_labels[:, 0][None, :] == jnp.arange(clusters, dtype=jnp.int32)[:, None]).astype(
        jnp.float32
    )
    near_sum = jnp.dot(
        selector,
        products.reshape(products.shape[0], -1),
        precision=lax.Precision.HIGHEST,
        preferred_element_type=jnp.float32,
    ).reshape(clusters, directions, unknowns)
    coef_local = jnp.einsum(
        "ckj,crj->crk", basis_in, rhs, preferred_element_type=jnp.float32
    ).astype(jnp.bfloat16)
    rank_k = basis_in.shape[1]
    coef_local = coef_local.reshape(clusters, directions * rank_k)
    pairs = far_slot.shape[0]
    wanted = far_dev[:, 0] * clusters + far_cslot
    piece = lax.all_gather(coef_local, "blk", axis=0, tiled=True)
    chosen = jnp.take(piece, wanted, axis=0)
    coupled = jnp.einsum(
        "pkq,prq->prk",
        far_coupling,
        chosen.reshape(pairs, directions, rank_k),
        preferred_element_type=jnp.float32,
    )
    row_pick = (far_slot[None, :] == jnp.arange(clusters, dtype=jnp.int32)[:, None]).astype(
        jnp.float32
    )
    gathered = jnp.dot(
        row_pick,
        coupled.reshape(pairs, -1),
        precision=lax.Precision.HIGHEST,
        preferred_element_type=jnp.float32,
    )
    gathered = gathered.astype(jnp.bfloat16).reshape(clusters, directions, rank_k)
    far_sum = jnp.einsum("crk,ckb->crb", gathered, basis_out, preferred_element_type=jnp.float32)
    return (near_sum + far_sum).astype(jnp.bfloat16)


def whole(space=pltpu.VMEM):
    return pl.BlockSpec(memory_space=space)


def prologue_kernel(
    count, me_ref, owner_ref, slot_ref, offset_ref, rhs_ref, basis_ref, payload_ref, list_ref
):
    clusters, directions, unknowns = rhs_ref.shape
    base = clusters * directions
    payload_ref[0:base, :] = rhs_ref[...].reshape(base, unknowns)
    rank_k = basis_ref.shape[1]
    half = clusters // 2
    rows = []
    for c in range(half):
        parts = [
            lax.dot_general(
                basis_ref[e],
                rhs_ref[e],
                (((1,), (1,)), ((), ())),
                preferred_element_type=jnp.float32,
            )
            for e in (c, c + half)
        ]
        rows.append(jnp.concatenate(parts, axis=1))
    payload_ref[base:, :] = jnp.concatenate(
        [row[q : q + 1] for q in range(rank_k) for row in rows], axis=0
    ).astype(payload_ref.dtype)

    me, owner, slot = me_ref[0], owner_ref[...], slot_ref[...]
    stored = owner.shape[1]
    place = scatter_place(owner, me, count) * clusters + slot
    column = (owner * clusters + slot + offset_ref[...]) & (count * clusters - 1)
    shard = gather_place(column // clusters, me, count)
    theirs = shard == count // 2
    shard = jnp.where(theirs, gather_place(column // clusters, me ^ 1, count), shard)
    column_place = shard * clusters + (column & (clusters - 1))
    square = (stored, stored)
    late = jnp.broadcast_to(jnp.where(theirs, 1.0, 0.0), square)
    late_of_row = jnp.transpose(late)
    row_at = lax.broadcasted_iota(jnp.int32, square, 0)
    lane_at = lax.broadcasted_iota(jnp.int32, square, 1)
    lane = lane_at.astype(jnp.float32)
    before = (late_of_row < late) | ((late_of_row == late) & (row_at < lane_at))
    rank = jnp.sum(jnp.where(before, 1.0, 0.0), axis=0, keepdims=True)
    rank = jnp.transpose(jnp.broadcast_to(rank, square))
    here = jnp.where(rank == lane, 1.0, 0.0).astype(jnp.bfloat16)
    chunk = row_at < lane_at * (stored // CHUNKS)
    mine = jnp.sum(jnp.where(chunk, 1.0 - late_of_row, 0.0), axis=0, keepdims=True)
    other = jnp.sum(jnp.where(chunk, late_of_row, 0.0), axis=0, keepdims=True)
    other = other + (stored - jnp.sum(late[0:1], axis=1, keepdims=True))
    values = jnp.concatenate(
        [lane[0:1], place.astype(jnp.float32), column_place.astype(jnp.float32)]
        + [jnp.zeros((5, stored), jnp.float32)],
        axis=0,
    )
    values = jnp.dot(values.astype(jnp.bfloat16), here, preferred_element_type=jnp.float32)
    values = jnp.concatenate([values[0:3], mine, other, values[5:8]], axis=0)
    list_ref[...] = values.astype(jnp.int32)


def near_kernel(batch, shards, sends, list_ref, mate_list_ref, *refs):
    shard_refs, (own_hbm, mate_hbm) = refs[:shards], refs[shards : shards + 2]
    keep_ref, coef_ref, refs = refs[shards + 2], refs[shards + 3], refs[shards + 4 :]
    send_refs, (columns, blocks, sums, column_sem, coef_sem, block_sem) = refs[:sends], refs[sends:]
    directions = sums.shape[1]
    span = columns.shape[0] // shards
    tail = coef_ref.shape[0] // shards
    chunk = blocks.shape[1] // CHUNKS

    def load(source, half, c):
        at = pl.ds(c * chunk, chunk)
        return pltpu.make_async_copy(
            source.at[at], blocks.at[half, at], block_sem.at[half * CHUNKS + c]
        )

    copies = [
        pltpu.make_async_copy(
            ref.at[pl.ds(0, span)], columns.at[pl.ds(k * span, span)], column_sem.at[k]
        )
        for k, ref in enumerate(shard_refs)
    ]
    for copy in copies:
        copy.start()
    tails = [
        pltpu.make_async_copy(
            ref.at[pl.ds(span, tail)], coef_ref.at[pl.ds(k * tail, tail)], coef_sem.at[k]
        )
        for k, ref in enumerate(shard_refs)
    ]
    for copy in tails:
        copy.start()
    for half, source in enumerate((own_hbm, mate_hbm)):
        for c in range(CHUNKS):
            load(source, half, c).start()

    dummy = sums.shape[0] - 1

    def clear(i, carry):
        sums[i] = jnp.zeros(sums.shape[1:], sums.dtype)
        return carry

    lax.fori_loop(0, dummy, clear, 0)
    for copy in copies:
        copy.wait()
    for half, (source, ref) in enumerate(((own_hbm, list_ref), (mate_hbm, mate_list_ref))):
        swap = half * (dummy // 2)

        def run(c, carry, half=half, source=source, ref=ref, swap=swap):
            load(source, half, c).wait()
            begin, end = ref[3 + half, c], ref[3 + half, c + 1]

            def body(step, carry):
                first = begin + step * batch
                products = []
                for i in range(batch):
                    at = jnp.minimum(first + i, end - 1)
                    products.append(
                        lax.dot_general(
                            columns[
                                pl.ds(pl.multiple_of(ref[2, at] * directions, directions), directions)
                            ],
                            blocks[half, ref[0, at]],
                            (((1,), (1,)), ((), ())),
                            preferred_element_type=jnp.float32,
                        )
                    )
                for i in range(batch):
                    at = jnp.minimum(first + i, end - 1)
                    at = jnp.where(first + i < end, ref[1, at] ^ swap, dummy)
                    sums[at] = sums[at] + products[i]
                return carry

            return lax.fori_loop(0, (end - begin + batch - 1) // batch, body, carry)

        lax.fori_loop(0, CHUNKS, run, 0)

    def keep(i, carry):
        keep_ref[i] = sums[i]
        return carry

    lax.fori_loop(0, dummy // 2, keep, 0, unroll=2)
    at = dummy // 2
    for send_ref in send_refs:

        def pack(i, carry, at=at, send_ref=send_ref):
            send_ref[i] = sums[at + i].astype(send_ref.dtype)
            return carry

        lax.fori_loop(0, send_ref.shape[0], pack, 0, unroll=2)
        at += send_ref.shape[0]
    for copy in tails:
        copy.wait()


def far_kernel(*refs):
    coef_refs = refs[:2]
    me_ref, couple_ref, slot_ref, dev_ref, cslot_ref, basis_ref, out_ref = refs[2:]
    clusters, rank_k, unknowns = basis_ref.shape
    pairs = couple_ref.shape[2]
    directions = out_ref.shape[1]
    half = clusters // 2
    coef = jnp.concatenate([ref[...].astype(jnp.float32) for ref in coef_refs], axis=0)
    coef = coef.reshape(-1, rank_k, half, unknowns)
    count = coef.shape[0]
    hot = (
        lax.broadcasted_iota(jnp.int32, (clusters, pairs), 0)
        == jnp.broadcast_to(slot_ref[...], (clusters, pairs))
    ).astype(jnp.float32).astype(jnp.bfloat16)
    away = gather_place(dev_ref[...], me_ref[0], count)
    theirs = count // 2 + gather_place(dev_ref[...], me_ref[0] ^ 1, count)
    away = jnp.where(away == count // 2, theirs, away)
    cslot = cslot_ref[...]
    high = (cslot >= half).astype(jnp.int32)
    at = away * half + cslot - high * half
    table_rows = (count * half, pairs)
    pick = jnp.where(
        lax.broadcasted_iota(jnp.int32, table_rows, 0) == jnp.broadcast_to(at, table_rows), 1.0, 0.0
    )
    pick = jnp.transpose(pick).astype(jnp.bfloat16)
    lanes = (unknowns, pairs)
    keep = jnp.where(
        lax.broadcasted_iota(jnp.int32, lanes, 0) // directions == jnp.broadcast_to(high, lanes),
        1.0,
        0.0,
    )
    keep = jnp.transpose(keep).astype(jnp.bfloat16)
    total = jnp.zeros((clusters * rank_k, unknowns), jnp.float32)
    for q in range(rank_k):
        table = coef[:, q].reshape(count * half, unknowns).astype(jnp.bfloat16)
        chosen = jnp.dot(pick, table, preferred_element_type=jnp.float32).astype(jnp.bfloat16)
        chosen = chosen * keep
        couple = couple_ref[q]
        weight = jnp.concatenate([couple * hot[s : s + 1] for s in range(clusters)], axis=0)
        total = total + jnp.dot(weight, chosen, preferred_element_type=jnp.float32)
    total = total + pltpu.roll(total, unknowns // 2, axis=1)
    gathered = jnp.transpose(total)[0:directions, :].astype(jnp.bfloat16).astype(jnp.float32)
    lane = lax.broadcasted_iota(jnp.int32, gathered.shape, 1) // rank_k
    basis = basis_ref[...].reshape(clusters * rank_k, unknowns)
    for s in range(clusters):
        own = jnp.where(lane == s, gathered, 0.0).astype(jnp.bfloat16)
        out_ref[s] = jnp.dot(own, basis, preferred_element_type=jnp.float32)


def ring_device(place, core, chips):
    depth = chips // 2
    place = place % chips
    z, y = (place, 0) if place < depth else (chips - 1 - place, 1)
    return (z * 2 + y) * 2 + core


def ring_pairs(count):
    chips = count // 2
    cores = [(p, c) for p in range(chips) for c in range(2)]
    ahead = [(ring_device(p, c, chips), ring_device(p + 1 - 2 * c, c, chips)) for p, c in cores]
    cross = [
        (ring_device(p, c, chips), ring_device(p - 1 + 2 * c, 1 - c, chips)) for p, c in cores
    ]
    return ahead, cross


def ring_place(device, chips):
    z, y = device >> 2, (device >> 1) & 1
    return jnp.where(y == 0, z, chips - 1 - z)


def gather_place(device, me, count):
    chips = count // 2
    depth = chips // 2
    back = (1 - 2 * (me & 1)) * (ring_place(me, chips) - ring_place(device, chips))
    back = (back + chips) & (chips - 1)
    other = (device ^ me) & 1
    here = (back < depth) & (back > 0) | ((back & (depth - 1)) == 0) & (other == 0)
    return jnp.where(here, jnp.where(back == 0, 0, 2 * back - 1 + other), chips)


def scatter_place(device, me, count):
    chips = count // 2
    depth = chips // 2
    ahead = (ring_place(device, chips) - ring_place(me, chips) + chips) & (chips - 1)
    core = device & 1
    handler = jnp.where((ahead & (depth - 1)) == 0, core, (ahead > depth).astype(jnp.int32))
    steps = jnp.where(handler == 0, ahead, (chips - ahead) & (chips - 1))
    place = jnp.where(
        steps == depth,
        0,
        jnp.where(steps == 0, chips - 1, 2 * (depth - steps) - (core ^ handler)),
    )
    return place + jnp.where(handler == (me & 1), 0, chips)


def stationary(
    rhs,
    near_blocks,
    near_owner,
    near_slot,
    near_offset,
    far_coupling,
    far_slot,
    far_dev,
    far_cslot,
    basis_out,
    basis_in,
):
    clusters, directions, unknowns = rhs.shape
    rank_k = basis_in.shape[1]
    count = lax.axis_size("blk")
    chips = count // 2
    depth = chips // 2
    me = lax.axis_index("blk")
    stored = near_blocks.shape[0]
    pairs = far_slot.shape[0]
    half = clusters // 2
    ahead, cross = ring_pairs(count)
    mate = [(i, i ^ 1) for i in range(count)]
    side = [(i, i ^ 2) for i in range(count)]

    def move(values, where):
        return lax.ppermute(values, "blk", where)

    def after(values, *others):
        return lax.optimization_barrier((values, *others))[0]

    mate_blocks = move(near_blocks, mate)
    here = me.astype(jnp.int32).reshape(1)
    base = clusters * directions
    payload, lists = pl.pallas_call(
        functools.partial(prologue_kernel, count),
        out_shape=[
            jax.ShapeDtypeStruct((base + half * rank_k, unknowns), jnp.bfloat16),
            jax.ShapeDtypeStruct((8, stored), jnp.int32),
        ],
        in_specs=[whole(pltpu.SMEM)] + [whole()] * 5,
        out_specs=[whole()] * 2,
        compiler_params=pltpu.CompilerParams(vmem_limit_bytes=PROLOGUE_VMEM),
        name="prologue",
    )(
        here,
        near_owner.reshape(1, stored),
        near_slot.reshape(1, stored),
        near_offset.reshape(1, stored),
        rhs,
        basis_in,
    )
    flow = [move(payload, ahead), move(payload, cross)]
    mate_lists = move(lists, mate)
    couple = after(jnp.transpose(far_coupling, (2, 1, 0)), payload)
    shards = [payload]
    for k in range(1, chips):
        x = 1 - k % 2
        if k == 3:
            flow[x], mate_blocks, lists, mate_lists, couple = lax.optimization_barrier(
                (flow[x], mate_blocks, lists, mate_lists, couple)
            )
        shards.append(flow[x])
        if k < chips - 2:
            flow[x] = move(flow[x], ahead)

    pieces = [1, 1, chips - 2]
    kept, coef, *sends = pl.pallas_call(
        functools.partial(near_kernel, BATCH, chips, len(pieces)),
        out_shape=[
            jax.ShapeDtypeStruct((chips * clusters, directions, unknowns), jnp.float32),
            jax.ShapeDtypeStruct((chips * half * rank_k, unknowns), jnp.bfloat16),
        ]
        + [
            jax.ShapeDtypeStruct((part * clusters, directions, unknowns), jnp.bfloat16)
            for part in pieces
        ],
        in_specs=[whole(pltpu.SMEM)] * 2 + [whole(pl.ANY)] * (chips + 2),
        out_specs=[whole()] * (2 + len(pieces)),
        scratch_shapes=[
            pltpu.VMEM((chips * base, unknowns), jnp.bfloat16),
            pltpu.VMEM((2, *near_blocks.shape), jnp.bfloat16),
            pltpu.VMEM((count * clusters + 1, directions, unknowns), jnp.float32),
            pltpu.SemaphoreType.DMA((chips,)),
            pltpu.SemaphoreType.DMA((chips,)),
            pltpu.SemaphoreType.DMA((2 * CHUNKS,)),
        ],
        compiler_params=pltpu.CompilerParams(vmem_limit_bytes=NEAR_VMEM),
        cost_estimate=pl.CostEstimate(
            flops=16 * stored * directions * unknowns * unknowns,
            bytes_accessed=16 << 20,
            transcendentals=0,
        ),
        name="near",
    )(lists, mate_lists, *shards, near_blocks, mate_blocks)

    mates = [move(sends[0], mate), move(sends[1], mate)]
    coefs = [coef, move(coef, mate)]

    def term(k):
        part = min(k, 2)
        got = mates[part][(k - part) * clusters : (k - part + 1) * clusters]
        return kept[k * clusters : (k + 1) * clusters] + got.astype(jnp.float32)

    def tied(values, *others):
        values, mates[2], *others = lax.optimization_barrier((values, mates[2], *others))
        return values

    def add(flow, k):
        return (flow.astype(jnp.float32) + term(k)).astype(jnp.bfloat16)

    flow = lax.optimization_barrier([term(0).astype(jnp.bfloat16), term(1).astype(jnp.bfloat16)])
    couple, sends[2] = after(couple, *flow), after(sends[2], *flow)
    flow = [move(part, ahead) for part in flow]
    mates.append(move(sends[2], mate))
    far = pl.pallas_call(
        far_kernel,
        out_shape=jax.ShapeDtypeStruct((clusters, directions, unknowns), jnp.float32),
        in_specs=[whole()] * 2 + [whole(pltpu.SMEM)] + [whole()] * 5,
        out_specs=whole(),
        compiler_params=pltpu.CompilerParams(vmem_limit_bytes=FAR_VMEM),
        cost_estimate=pl.CostEstimate(
            flops=4 * clusters * rank_k * pairs * rank_k * unknowns,
            bytes_accessed=8 << 20,
            transcendentals=0,
        ),
        name="far",
    )(
        *coefs,
        here,
        couple,
        far_slot.reshape(1, pairs),
        far_dev.reshape(1, pairs),
        far_cslot.reshape(1, pairs),
        basis_out,
    )
    for k in range(2, chips - 1):
        x = k % 2
        flow[x] = move(tied(add(flow[x], k), *([far] if k == 2 else [])), ahead)
    flow[1] = move(flow[1], mate)
    total = far + term(chips - 1) + flow[0].astype(jnp.float32)
    total = lax.optimization_barrier(total)
    return (total + flow[1].astype(jnp.float32)).astype(jnp.bfloat16)


def on_device(*args):
    rhs, near_blocks = args[0], args[1]
    clusters, directions, unknowns = rhs.shape
    small = lax.axis_size("blk") == 16 and clusters == 16
    if small and near_blocks.shape[0] == unknowns and 2 * directions == unknowns:
        return stationary(*args)
    return routed(*args)


def solution(mesh):
    placed = (
        P(("groups", "blk"), None, None),
        P(("groups", "blk"), None, None),
        P(("groups", "blk"), None),
        P(("groups", "blk")),
        P(("groups", "blk")),
        P(("groups", "blk"), None, None),
        P(("groups", "blk")),
        P(("groups", "blk"), None),
        P(("groups", "blk")),
        P(("groups", "blk"), None, None),
        P(("groups", "blk"), None, None),
    )
    return jax.shard_map(
        on_device,
        mesh=mesh,
        in_specs=placed,
        out_specs=P(("groups", "blk"), None, None),
        check_vma=False,
    )
```

```python
import functools

import jax
import jax.numpy as jnp
from jax import lax
from jax.experimental import pallas as pl
from jax.experimental.pallas import tpu as pltpu
from jax.sharding import PartitionSpec as P

CHUNKS = 4
BATCH = 16
LAG = 4
PROLOGUE_VMEM = 58 << 20
NEAR_VMEM = 48 << 20
FAR_VMEM = 16 << 20


def with_halo(cells, sides, width):
    for axis, dim in sides:
        count = lax.axis_size(axis)
        head = lax.slice_in_dim(cells, 0, width, axis=dim)
        tail = lax.slice_in_dim(cells, cells.shape[dim] - width, cells.shape[dim], axis=dim)
        cells = jnp.concatenate(
            [
                lax.ppermute(tail, axis, [(i, (i + 1) % count) for i in range(count)]),
                cells,
                lax.ppermute(head, axis, [((i + 1) % count, i) for i in range(count)]),
            ],
            axis=dim,
        )
    return cells


def place_ranks(targets, count):
    onehot = (targets[:, None] == jnp.arange(count, dtype=jnp.int32)[None, :]).astype(jnp.int32)
    before = jnp.cumsum(onehot, axis=0) - onehot
    return jnp.sum(before * onehot, axis=1)


def routed(
    rhs,
    near_blocks,
    near_owner,
    near_slot,
    near_offset,
    far_coupling,
    far_slot,
    far_dev,
    far_cslot,
    basis_out,
    basis_in,
):
    clusters = rhs.shape[0]
    directions = rhs.shape[1]
    unknowns = rhs.shape[2]
    cycle_size = lax.axis_size("blk")
    stored = near_blocks.shape[0]
    capacity = max(2, 2 * stored // cycle_size)
    owners = near_owner[:, 0]
    target = owners * capacity + place_ranks(owners, cycle_size)
    outbox = (
        jnp.zeros((cycle_size * capacity, unknowns, unknowns), near_blocks.dtype)
        .at[target]
        .set(near_blocks)
    )
    labels = (
        jnp.zeros((cycle_size * capacity, 2), jnp.int32)
        .at[target]
        .set(jnp.stack([near_slot, near_offset], axis=1))
    )
    window = with_halo(rhs, (("blk", 0),), clusters)
    inbox, in_labels = (
        lax.all_to_all(outbox, "blk", split_axis=0, concat_axis=0, tiled=True),
        lax.all_to_all(labels, "blk", split_axis=0, concat_axis=0, tiled=True),
    )
    position = clusters + in_labels[:, 0] + in_labels[:, 1]
    columns = jnp.take(window, position, axis=0)
    products = jnp.einsum("srj,sij->sri", columns, inbox, preferred_element_type=jnp.float32)
    selector = (in_labels[:, 0][None, :] == jnp.arange(clusters, dtype=jnp.int32)[:, None]).astype(
        jnp.float32
    )
    near_sum = jnp.dot(
        selector,
        products.reshape(products.shape[0], -1),
        precision=lax.Precision.HIGHEST,
        preferred_element_type=jnp.float32,
    ).reshape(clusters, directions, unknowns)
    coef_local = jnp.einsum(
        "ckj,crj->crk", basis_in, rhs, preferred_element_type=jnp.float32
    ).astype(jnp.bfloat16)
    rank_k = basis_in.shape[1]
    coef_local = coef_local.reshape(clusters, directions * rank_k)
    pairs = far_slot.shape[0]
    wanted = far_dev[:, 0] * clusters + far_cslot
    piece = lax.all_gather(coef_local, "blk", axis=0, tiled=True)
    chosen = jnp.take(piece, wanted, axis=0)
    coupled = jnp.einsum(
        "pkq,prq->prk",
        far_coupling,
        chosen.reshape(pairs, directions, rank_k),
        preferred_element_type=jnp.float32,
    )
    row_pick = (far_slot[None, :] == jnp.arange(clusters, dtype=jnp.int32)[:, None]).astype(
        jnp.float32
    )
    gathered = jnp.dot(
        row_pick,
        coupled.reshape(pairs, -1),
        precision=lax.Precision.HIGHEST,
        preferred_element_type=jnp.float32,
    )
    gathered = gathered.astype(jnp.bfloat16).reshape(clusters, directions, rank_k)
    far_sum = jnp.einsum("crk,ckb->crb", gathered, basis_out, preferred_element_type=jnp.float32)
    return (near_sum + far_sum).astype(jnp.bfloat16)


def whole(space=pltpu.VMEM):
    return pl.BlockSpec(memory_space=space)


def prologue_kernel(
    count, me_ref, owner_ref, slot_ref, offset_ref, rhs_ref, basis_ref, payload_ref, list_ref
):
    clusters, directions, unknowns = rhs_ref.shape
    base = clusters * directions
    payload_ref[0:base, :] = rhs_ref[...].reshape(base, unknowns)
    rank_k = basis_ref.shape[1]
    half = clusters // 2
    rows = []
    for c in range(half):
        parts = [
            lax.dot_general(
                basis_ref[e],
                rhs_ref[e],
                (((1,), (1,)), ((), ())),
                preferred_element_type=jnp.float32,
            )
            for e in (c, c + half)
        ]
        rows.append(jnp.concatenate(parts, axis=1))
    payload_ref[base:, :] = jnp.concatenate(
        [row[q : q + 1] for q in range(rank_k) for row in rows], axis=0
    ).astype(payload_ref.dtype)

    me, owner, slot = me_ref[0], owner_ref[...], slot_ref[...]
    stored = owner.shape[1]
    place = scatter_place(owner, me, count) * clusters + slot
    column = (owner * clusters + slot + offset_ref[...]) & (count * clusters - 1)
    shard = gather_place(column // clusters, me, count)
    theirs = shard == count // 2
    shard = jnp.where(theirs, gather_place(column // clusters, me ^ 1, count), shard)
    column_place = shard * clusters + (column & (clusters - 1))
    square = (stored, stored)
    late = jnp.broadcast_to(jnp.where(theirs, 1.0, 0.0), square)
    late_of_row = jnp.transpose(late)
    row_at = lax.broadcasted_iota(jnp.int32, square, 0)
    lane_at = lax.broadcasted_iota(jnp.int32, square, 1)
    lane = lane_at.astype(jnp.float32)
    before = (late_of_row < late) | ((late_of_row == late) & (row_at < lane_at))
    rank = jnp.sum(jnp.where(before, 1.0, 0.0), axis=0, keepdims=True)
    rank = jnp.transpose(jnp.broadcast_to(rank, square))
    here = jnp.where(rank == lane, 1.0, 0.0).astype(jnp.bfloat16)
    chunk = row_at < lane_at * (stored // CHUNKS)
    mine = jnp.sum(jnp.where(chunk, 1.0 - late_of_row, 0.0), axis=0, keepdims=True)
    other = jnp.sum(jnp.where(chunk, late_of_row, 0.0), axis=0, keepdims=True)
    other = other + (stored - jnp.sum(late[0:1], axis=1, keepdims=True))
    values = jnp.concatenate(
        [lane[0:1], place.astype(jnp.float32), column_place.astype(jnp.float32)]
        + [jnp.zeros((5, stored), jnp.float32)],
        axis=0,
    )
    values = jnp.dot(values.astype(jnp.bfloat16), here, preferred_element_type=jnp.float32)
    values = jnp.concatenate([values[0:3], mine, other, values[5:8]], axis=0)
    list_ref[...] = values.astype(jnp.int32)


def near_kernel(batch, lag, shards, sends, list_ref, *refs):
    shard_refs, (own_hbm, mate_hbm, sums, coef_ref) = refs[:shards], refs[shards : shards + 4]
    refs = refs[shards + 4 :]
    send_refs, (columns, blocks, column_sem, coef_sem, block_sem) = refs[:sends], refs[sends:]
    directions = sums.shape[1]
    span = columns.shape[0] // shards
    tail = coef_ref.shape[0] // shards
    stored = blocks.shape[1]
    chunk = stored // CHUNKS
    dummy = sums.shape[0] - 1

    copies = [
        pltpu.make_async_copy(
            ref.at[pl.ds(0, span)], columns.at[pl.ds(k * span, span)], column_sem.at[k]
        )
        for k, ref in enumerate(shard_refs)
    ]
    for copy in copies:
        copy.start()
    for half, source in enumerate((own_hbm, mate_hbm)):
        for c in range(CHUNKS):
            at = pl.ds(c * chunk, chunk)
            pltpu.make_async_copy(
                source.at[at], blocks.at[half, at], block_sem.at[half * CHUNKS + c]
            ).start()
    tails = [
        pltpu.make_async_copy(
            ref.at[pl.ds(span, tail)], coef_ref.at[pl.ds(k * tail, tail)], coef_sem.at[k]
        )
        for k, ref in enumerate(shard_refs)
    ]
    for copy in tails:
        copy.start()

    def clear(i, carry):
        sums[i] = jnp.zeros(sums.shape[1:], sums.dtype)
        return carry

    lax.fori_loop(0, dummy, clear, 0)
    for copy in copies:
        copy.wait()

    here = list_ref[3, CHUNKS]
    there = list_ref[8 + 4, 0]
    total = here + stored - there

    def entry(j):
        j = jnp.minimum(j, total - 1)
        half = (j >= here).astype(jnp.int32)
        return half, half * 8, j + half * (there - here)

    def wait(c, carry):
        at = pl.ds(0, chunk)
        pltpu.make_async_copy(own_hbm.at[at], blocks.at[0, at], block_sem.at[c]).wait()
        return carry

    def body(step, ready):
        first = step * batch
        half, row, at = entry(first + batch - 1)
        needed = half * CHUNKS + list_ref[row, at] // chunk + 1
        lax.fori_loop(ready, needed, wait, 0)
        products = []

        def add(i):
            half, row, at = entry(first + i)
            place = list_ref[row + 1, at] ^ (half * (dummy // 2))
            place = jnp.where(first + i < total, place, dummy)
            sums[place] = sums[place] + products[i]

        for i in range(batch):
            half, row, at = entry(first + i)
            start = pl.multiple_of(list_ref[row + 2, at] * directions, directions)
            products.append(
                lax.dot_general(
                    columns[pl.ds(start, directions)],
                    blocks[half, list_ref[row, at]],
                    (((1,), (1,)), ((), ())),
                    preferred_element_type=jnp.float32,
                )
            )
            if i >= lag:
                add(i - lag)
        for i in range(batch - lag, batch):
            add(i)
        return jnp.maximum(ready, needed)

    ready = lax.fori_loop(0, (total + batch - 1) // batch, body, 0)
    lax.fori_loop(ready, 2 * CHUNKS, wait, 0)
    at = dummy // 2
    for send_ref in send_refs:

        def pack(i, carry, at=at, send_ref=send_ref):
            send_ref[i] = sums[at + i].astype(send_ref.dtype)
            return carry

        lax.fori_loop(0, send_ref.shape[0], pack, 0, unroll=2)
        at += send_ref.shape[0]
    for copy in tails:
        copy.wait()


def far_kernel(*refs):
    coef_refs = refs[:2]
    me_ref, couple_ref, slot_ref, dev_ref, cslot_ref, basis_ref, out_ref = refs[2:]
    clusters, rank_k, unknowns = basis_ref.shape
    pairs = couple_ref.shape[2]
    directions = out_ref.shape[1]
    half = clusters // 2
    coef = jnp.concatenate([ref[...].astype(jnp.float32) for ref in coef_refs], axis=0)
    coef = coef.reshape(-1, rank_k, half, unknowns)
    count = coef.shape[0]
    hot = (
        lax.broadcasted_iota(jnp.int32, (clusters, pairs), 0)
        == jnp.broadcast_to(slot_ref[...], (clusters, pairs))
    ).astype(jnp.float32).astype(jnp.bfloat16)
    away = gather_place(dev_ref[...], me_ref[0], count)
    theirs = count // 2 + gather_place(dev_ref[...], me_ref[0] ^ 1, count)
    away = jnp.where(away == count // 2, theirs, away)
    cslot = cslot_ref[...]
    high = (cslot >= half).astype(jnp.int32)
    at = away * half + cslot - high * half
    table_rows = (count * half, pairs)
    pick = jnp.where(
        lax.broadcasted_iota(jnp.int32, table_rows, 0) == jnp.broadcast_to(at, table_rows), 1.0, 0.0
    )
    pick = jnp.transpose(pick).astype(jnp.bfloat16)
    lanes = (unknowns, pairs)
    keep = jnp.where(
        lax.broadcasted_iota(jnp.int32, lanes, 0) // directions == jnp.broadcast_to(high, lanes),
        1.0,
        0.0,
    )
    keep = jnp.transpose(keep).astype(jnp.bfloat16)
    total = jnp.zeros((clusters * rank_k, unknowns), jnp.float32)
    for q in range(rank_k):
        table = coef[:, q].reshape(count * half, unknowns).astype(jnp.bfloat16)
        chosen = jnp.dot(pick, table, preferred_element_type=jnp.float32).astype(jnp.bfloat16)
        chosen = chosen * keep
        couple = couple_ref[q]
        weight = jnp.concatenate([couple * hot[s : s + 1] for s in range(clusters)], axis=0)
        total = total + jnp.dot(weight, chosen, preferred_element_type=jnp.float32)
    total = total + pltpu.roll(total, unknowns // 2, axis=1)
    gathered = jnp.transpose(total)[0:directions, :].astype(jnp.bfloat16).astype(jnp.float32)
    lane = lax.broadcasted_iota(jnp.int32, gathered.shape, 1) // rank_k
    basis = basis_ref[...].reshape(clusters * rank_k, unknowns)
    for s in range(clusters):
        own = jnp.where(lane == s, gathered, 0.0).astype(jnp.bfloat16)
        out_ref[s] = jnp.dot(own, basis, preferred_element_type=jnp.float32)


def ring_device(place, core, chips):
    depth = chips // 2
    place = place % chips
    z, y = (place, 0) if place < depth else (chips - 1 - place, 1)
    return (z * 2 + y) * 2 + core


def ring_pairs(count):
    chips = count // 2
    cores = [(p, c) for p in range(chips) for c in range(2)]
    ahead = [(ring_device(p, c, chips), ring_device(p - 1 + 2 * c, c, chips)) for p, c in cores]
    cross = [
        (ring_device(p, c, chips), ring_device(p + 1 - 2 * c, 1 - c, chips)) for p, c in cores
    ]
    return ahead, cross


def ring_place(device, chips):
    z, y = device >> 2, (device >> 1) & 1
    return jnp.where(y == 0, z, chips - 1 - z)


def gather_place(device, me, count):
    chips = count // 2
    depth = chips // 2
    back = (2 * (me & 1) - 1) * (ring_place(me, chips) - ring_place(device, chips))
    back = (back + chips) & (chips - 1)
    other = (device ^ me) & 1
    here = (back < depth) & (back > 0) | (back == 0) & (other == 1) | (back == depth) & (other == 0)
    return jnp.where(here, jnp.where(back == 0, 0, 2 * back - 1 + other), chips)


def scatter_place(device, me, count):
    chips = count // 2
    depth = chips // 2
    ahead = (ring_place(me, chips) - ring_place(device, chips) + chips) & (chips - 1)
    core = device & 1
    handler = jnp.where((ahead & (depth - 1)) == 0, core, (ahead > depth).astype(jnp.int32))
    steps = jnp.where(handler == 0, ahead, (chips - ahead) & (chips - 1))
    place = jnp.where(
        steps == depth,
        0,
        jnp.where(steps == 0, chips - 1, 2 * (depth - steps) - (core ^ handler)),
    )
    return place + jnp.where(handler == (me & 1), 0, chips)


def stationary(
    rhs,
    near_blocks,
    near_owner,
    near_slot,
    near_offset,
    far_coupling,
    far_slot,
    far_dev,
    far_cslot,
    basis_out,
    basis_in,
):
    clusters, directions, unknowns = rhs.shape
    rank_k = basis_in.shape[1]
    count = lax.axis_size("blk")
    chips = count // 2
    depth = chips // 2
    me = lax.axis_index("blk")
    stored = near_blocks.shape[0]
    pairs = far_slot.shape[0]
    half = clusters // 2
    ahead, cross = ring_pairs(count)
    mate = [(i, i ^ 1) for i in range(count)]
    side = [(i, i ^ 2) for i in range(count)]

    def move(values, where):
        return lax.ppermute(values, "blk", where)

    def after(values, *others):
        return lax.optimization_barrier((values, *others))[0]

    mate_blocks = move(near_blocks, mate)
    here = me.astype(jnp.int32).reshape(1)
    base = clusters * directions
    payload, lists = pl.pallas_call(
        functools.partial(prologue_kernel, count),
        out_shape=[
            jax.ShapeDtypeStruct((base + half * rank_k, unknowns), jnp.bfloat16),
            jax.ShapeDtypeStruct((8, stored), jnp.int32),
        ],
        in_specs=[whole(pltpu.SMEM)] + [whole()] * 5,
        out_specs=[whole()] * 2,
        compiler_params=pltpu.CompilerParams(vmem_limit_bytes=PROLOGUE_VMEM),
        name="prologue",
    )(
        here,
        near_owner.reshape(1, stored),
        near_slot.reshape(1, stored),
        near_offset.reshape(1, stored),
        rhs,
        basis_in,
    )
    flow = [move(payload, ahead), move(payload, cross)]
    shards = [move(payload, mate)]
    lists = jnp.concatenate([lists, move(lists, mate)], axis=0)
    couple = after(jnp.transpose(far_coupling, (2, 1, 0)), payload)
    for k in range(1, chips):
        x = 1 - k % 2
        if k == 3:
            flow[x], mate_blocks, shards[0], lists, couple = lax.optimization_barrier(
                (flow[x], mate_blocks, shards[0], lists, couple)
            )
        shards.append(flow[x])
        if k < chips - 2:
            flow[x] = move(flow[x], ahead)

    pieces = [1, 1, chips - 2]
    kept, coef, *sends = pl.pallas_call(
        functools.partial(near_kernel, BATCH, LAG, chips, len(pieces)),
        out_shape=[
            jax.ShapeDtypeStruct((count * clusters + 1, directions, unknowns), jnp.float32),
            jax.ShapeDtypeStruct((chips * half * rank_k, unknowns), jnp.bfloat16),
        ]
        + [
            jax.ShapeDtypeStruct((part * clusters, directions, unknowns), jnp.bfloat16)
            for part in pieces
        ],
        in_specs=[whole(pltpu.SMEM)] + [whole(pl.ANY)] * (chips + 2),
        out_specs=[whole()] * (2 + len(pieces)),
        scratch_shapes=[
            pltpu.VMEM((chips * base, unknowns), jnp.bfloat16),
            pltpu.VMEM((2, *near_blocks.shape), jnp.bfloat16),
            pltpu.SemaphoreType.DMA((chips,)),
            pltpu.SemaphoreType.DMA((chips,)),
            pltpu.SemaphoreType.DMA((2 * CHUNKS,)),
        ],
        compiler_params=pltpu.CompilerParams(vmem_limit_bytes=NEAR_VMEM),
        cost_estimate=pl.CostEstimate(
            flops=16 * stored * directions * unknowns * unknowns,
            bytes_accessed=16 << 20,
            transcendentals=0,
        ),
        name="near",
    )(lists, *shards, near_blocks, mate_blocks)

    mates = [move(sends[0], mate), move(sends[1], mate)]
    coefs = [coef, move(coef, mate)]

    def term(k):
        part = min(k, 2)
        got = mates[part][(k - part) * clusters : (k - part + 1) * clusters]
        return kept[k * clusters : (k + 1) * clusters] + got.astype(jnp.float32)

    def tied(values, *others):
        values, mates[2], *others = lax.optimization_barrier((values, mates[2], *others))
        return values

    def add(flow, k):
        return (flow.astype(jnp.float32) + term(k)).astype(jnp.bfloat16)

    flow = lax.optimization_barrier([term(0).astype(jnp.bfloat16), term(1).astype(jnp.bfloat16)])
    couple, sends[2] = after(couple, *flow), after(sends[2], *flow)
    flow = [move(part, ahead) for part in flow]
    mates.append(move(sends[2], mate))
    far = pl.pallas_call(
        far_kernel,
        out_shape=jax.ShapeDtypeStruct((clusters, directions, unknowns), jnp.float32),
        in_specs=[whole()] * 2 + [whole(pltpu.SMEM)] + [whole()] * 5,
        out_specs=whole(),
        compiler_params=pltpu.CompilerParams(vmem_limit_bytes=FAR_VMEM),
        cost_estimate=pl.CostEstimate(
            flops=4 * clusters * rank_k * pairs * rank_k * unknowns,
            bytes_accessed=8 << 20,
            transcendentals=0,
        ),
        name="far",
    )(
        *coefs,
        here,
        couple,
        far_slot.reshape(1, pairs),
        far_dev.reshape(1, pairs),
        far_cslot.reshape(1, pairs),
        basis_out,
    )
    for k in range(2, chips - 1):
        x = k % 2
        flow[x] = move(tied(add(flow[x], k), *([far] if k == 2 else [])), ahead)
    flow[1] = move(flow[1], mate)
    total = far + term(chips - 1) + flow[0].astype(jnp.float32)
    total = lax.optimization_barrier(total)
    return (total + flow[1].astype(jnp.float32)).astype(jnp.bfloat16)


def on_device(*args):
    rhs, near_blocks = args[0], args[1]
    clusters, directions, unknowns = rhs.shape
    small = lax.axis_size("blk") == 16 and clusters == 16
    if small and near_blocks.shape[0] == unknowns and 2 * directions == unknowns:
        return stationary(*args)
    return routed(*args)


def solution(mesh):
    placed = (
        P(("groups", "blk"), None, None),
        P(("groups", "blk"), None, None),
        P(("groups", "blk"), None),
        P(("groups", "blk")),
        P(("groups", "blk")),
        P(("groups", "blk"), None, None),
        P(("groups", "blk")),
        P(("groups", "blk"), None),
        P(("groups", "blk")),
        P(("groups", "blk"), None, None),
        P(("groups", "blk"), None, None),
    )
    return jax.shard_map(
        on_device,
        mesh=mesh,
        in_specs=placed,
        out_specs=P(("groups", "blk"), None, None),
        check_vma=False,
    )
```

```python
import functools

import jax
import jax.numpy as jnp
from jax import lax
from jax.experimental import pallas as pl
from jax.experimental.pallas import tpu as pltpu
from jax.sharding import PartitionSpec as P

CHUNKS = 4
BATCH = 16
LAG = 4
PROLOGUE_VMEM = 58 << 20
NEAR_VMEM = 48 << 20
FAR_VMEM = 16 << 20


def with_halo(cells, sides, width):
    for axis, dim in sides:
        count = lax.axis_size(axis)
        head = lax.slice_in_dim(cells, 0, width, axis=dim)
        tail = lax.slice_in_dim(cells, cells.shape[dim] - width, cells.shape[dim], axis=dim)
        cells = jnp.concatenate(
            [
                lax.ppermute(tail, axis, [(i, (i + 1) % count) for i in range(count)]),
                cells,
                lax.ppermute(head, axis, [((i + 1) % count, i) for i in range(count)]),
            ],
            axis=dim,
        )
    return cells


def place_ranks(targets, count):
    onehot = (targets[:, None] == jnp.arange(count, dtype=jnp.int32)[None, :]).astype(jnp.int32)
    before = jnp.cumsum(onehot, axis=0) - onehot
    return jnp.sum(before * onehot, axis=1)


def routed(
    rhs,
    near_blocks,
    near_owner,
    near_slot,
    near_offset,
    far_coupling,
    far_slot,
    far_dev,
    far_cslot,
    basis_out,
    basis_in,
):
    clusters = rhs.shape[0]
    directions = rhs.shape[1]
    unknowns = rhs.shape[2]
    cycle_size = lax.axis_size("blk")
    stored = near_blocks.shape[0]
    capacity = max(2, 2 * stored // cycle_size)
    owners = near_owner[:, 0]
    target = owners * capacity + place_ranks(owners, cycle_size)
    outbox = (
        jnp.zeros((cycle_size * capacity, unknowns, unknowns), near_blocks.dtype)
        .at[target]
        .set(near_blocks)
    )
    labels = (
        jnp.zeros((cycle_size * capacity, 2), jnp.int32)
        .at[target]
        .set(jnp.stack([near_slot, near_offset], axis=1))
    )
    window = with_halo(rhs, (("blk", 0),), clusters)
    inbox, in_labels = (
        lax.all_to_all(outbox, "blk", split_axis=0, concat_axis=0, tiled=True),
        lax.all_to_all(labels, "blk", split_axis=0, concat_axis=0, tiled=True),
    )
    position = clusters + in_labels[:, 0] + in_labels[:, 1]
    columns = jnp.take(window, position, axis=0)
    products = jnp.einsum("srj,sij->sri", columns, inbox, preferred_element_type=jnp.float32)
    selector = (in_labels[:, 0][None, :] == jnp.arange(clusters, dtype=jnp.int32)[:, None]).astype(
        jnp.float32
    )
    near_sum = jnp.dot(
        selector,
        products.reshape(products.shape[0], -1),
        precision=lax.Precision.HIGHEST,
        preferred_element_type=jnp.float32,
    ).reshape(clusters, directions, unknowns)
    coef_local = jnp.einsum(
        "ckj,crj->crk", basis_in, rhs, preferred_element_type=jnp.float32
    ).astype(jnp.bfloat16)
    rank_k = basis_in.shape[1]
    coef_local = coef_local.reshape(clusters, directions * rank_k)
    pairs = far_slot.shape[0]
    wanted = far_dev[:, 0] * clusters + far_cslot
    piece = lax.all_gather(coef_local, "blk", axis=0, tiled=True)
    chosen = jnp.take(piece, wanted, axis=0)
    coupled = jnp.einsum(
        "pkq,prq->prk",
        far_coupling,
        chosen.reshape(pairs, directions, rank_k),
        preferred_element_type=jnp.float32,
    )
    row_pick = (far_slot[None, :] == jnp.arange(clusters, dtype=jnp.int32)[:, None]).astype(
        jnp.float32
    )
    gathered = jnp.dot(
        row_pick,
        coupled.reshape(pairs, -1),
        precision=lax.Precision.HIGHEST,
        preferred_element_type=jnp.float32,
    )
    gathered = gathered.astype(jnp.bfloat16).reshape(clusters, directions, rank_k)
    far_sum = jnp.einsum("crk,ckb->crb", gathered, basis_out, preferred_element_type=jnp.float32)
    return (near_sum + far_sum).astype(jnp.bfloat16)


def whole(space=pltpu.VMEM):
    return pl.BlockSpec(memory_space=space)


def prologue_kernel(
    count, me_ref, owner_ref, slot_ref, offset_ref, rhs_ref, basis_ref, payload_ref, list_ref
):
    clusters, directions, unknowns = rhs_ref.shape
    base = clusters * directions
    payload_ref[0:base, :] = rhs_ref[...].reshape(base, unknowns)
    rank_k = basis_ref.shape[1]
    half = clusters // 2
    rows = []
    for c in range(half):
        parts = [
            lax.dot_general(
                basis_ref[e],
                rhs_ref[e],
                (((1,), (1,)), ((), ())),
                preferred_element_type=jnp.float32,
            )
            for e in (c, c + half)
        ]
        rows.append(jnp.concatenate(parts, axis=1))
    payload_ref[base:, :] = jnp.concatenate(
        [row[q : q + 1] for q in range(rank_k) for row in rows], axis=0
    ).astype(payload_ref.dtype)

    me, owner, slot = me_ref[0], owner_ref[...], slot_ref[...]
    stored = owner.shape[1]
    place = scatter_place(owner, me, count)
    quarter = count // 4
    late = (place // quarter) & 1
    place = (place // (2 * quarter) * quarter + (place & (quarter - 1))) * clusters + slot
    column = (owner * clusters + slot + offset_ref[...]) & (count * clusters - 1)
    shard = gather_place(column // clusters, me, count)
    theirs = (shard == count // 2).astype(jnp.int32)
    shard = jnp.where(theirs == 1, gather_place(column // clusters, me ^ 1, count), shard)
    column_place = shard * clusters + (column & (clusters - 1))
    square = (stored, stored)
    group = jnp.broadcast_to((2 * theirs + late).astype(jnp.float32), square)
    group_of_row = jnp.transpose(group)
    row_at = lax.broadcasted_iota(jnp.int32, square, 0)
    lane_at = lax.broadcasted_iota(jnp.int32, square, 1)
    lane = lane_at.astype(jnp.float32)
    before = (group_of_row < group) | ((group_of_row == group) & (row_at < lane_at))
    rank = jnp.sum(jnp.where(before, 1.0, 0.0), axis=0, keepdims=True)
    rank = jnp.transpose(jnp.broadcast_to(rank, square))
    here = jnp.where(rank == lane, 1.0, 0.0).astype(jnp.bfloat16)
    starts = jnp.sum(jnp.where(group_of_row < lane, 1.0, 0.0), axis=0, keepdims=True)
    values = jnp.concatenate(
        [lane[0:1], place.astype(jnp.float32), column_place.astype(jnp.float32)]
        + [jnp.zeros((5, stored), jnp.float32)],
        axis=0,
    )
    values = jnp.dot(values.astype(jnp.bfloat16), here, preferred_element_type=jnp.float32)
    values = jnp.concatenate([values[0:3], starts, values[4:8]], axis=0)
    list_ref[...] = values.astype(jnp.int32)


def near_kernel(late, batch, lag, shards, sends, list_ref, *refs):
    shard_refs, (own_hbm, mate_hbm, keep_ref) = refs[:shards], refs[shards : shards + 3]
    send_refs, refs = refs[shards + 3 : shards + 3 + sends], refs[shards + 3 + sends :]
    if not late:
        coef_ref, refs = refs[0], refs[1:]
    columns, blocks, sums, column_sem, coef_sem, block_sem = refs
    directions = sums.shape[1]
    span = columns.shape[0] // shards
    stored = blocks.shape[1]
    chunk = stored // CHUNKS
    dummy = sums.shape[0] - 1

    copies = [
        pltpu.make_async_copy(
            ref.at[pl.ds(0, span)], columns.at[pl.ds(k * span, span)], column_sem.at[k]
        )
        for k, ref in enumerate(shard_refs)
    ]
    for copy in copies:
        copy.start()
    for half, source in enumerate((own_hbm, mate_hbm)):
        for c in range(CHUNKS):
            at = pl.ds(c * chunk, chunk)
            pltpu.make_async_copy(
                source.at[at], blocks.at[half, at], block_sem.at[half * CHUNKS + c]
            ).start()
    tails = []
    if not late:
        tail = coef_ref.shape[0] // shards
        tails = [
            pltpu.make_async_copy(
                ref.at[pl.ds(span, tail)], coef_ref.at[pl.ds(k * tail, tail)], coef_sem.at[k]
            )
            for k, ref in enumerate(shard_refs)
        ]
    for copy in tails:
        copy.start()

    def clear(i, carry):
        sums[i] = jnp.zeros(sums.shape[1:], sums.dtype)
        return carry

    lax.fori_loop(0, dummy, clear, 0)
    for copy in copies:
        copy.wait()

    begin, begin_there = list_ref[3, late], list_ref[11, 2 + late]
    here = list_ref[3, late + 1] - begin
    total = here + list_ref[11, 3 + late] - begin_there

    def entry(j):
        j = jnp.minimum(j, total - 1)
        half = (j >= here).astype(jnp.int32)
        return half, half * 8, j + jnp.where(half == 1, begin_there - here, begin)

    def wait(c, carry):
        at = pl.ds(0, chunk)
        pltpu.make_async_copy(own_hbm.at[at], blocks.at[0, at], block_sem.at[c]).wait()
        return carry

    def body(step, ready):
        first = step * batch
        half, row, at = entry(first + batch - 1)
        needed = half * CHUNKS + list_ref[row, at] // chunk + 1
        lax.fori_loop(ready, needed, wait, 0)
        products = []

        def add(i):
            half, row, at = entry(first + i)
            place = list_ref[row + 1, at] ^ (half * (dummy // 2))
            place = jnp.where(first + i < total, place, dummy)
            sums[place] = sums[place] + products[i]

        for i in range(batch):
            half, row, at = entry(first + i)
            start = pl.multiple_of(list_ref[row + 2, at] * directions, directions)
            products.append(
                lax.dot_general(
                    columns[pl.ds(start, directions)],
                    blocks[half, list_ref[row, at]],
                    (((1,), (1,)), ((), ())),
                    preferred_element_type=jnp.float32,
                )
            )
            if i >= lag:
                add(i - lag)
        for i in range(batch - lag, batch):
            add(i)
        return jnp.maximum(ready, needed)

    ready = lax.fori_loop(0, (total + batch - 1) // batch, body, 0)
    lax.fori_loop(ready, 2 * CHUNKS, wait, 0)

    def keep(i, carry):
        keep_ref[i] = sums[i]
        return carry

    lax.fori_loop(0, dummy // 2, keep, 0, unroll=2)
    at = dummy // 2
    for send_ref in send_refs:

        def pack(i, carry, at=at, send_ref=send_ref):
            send_ref[i] = sums[at + i].astype(send_ref.dtype)
            return carry

        lax.fori_loop(0, send_ref.shape[0], pack, 0, unroll=2)
        at += send_ref.shape[0]
    for copy in tails:
        copy.wait()


def far_kernel(*refs):
    coef_refs = refs[:2]
    me_ref, couple_ref, slot_ref, dev_ref, cslot_ref, basis_ref, out_ref = refs[2:]
    clusters, rank_k, unknowns = basis_ref.shape
    pairs = couple_ref.shape[2]
    directions = out_ref.shape[1]
    half = clusters // 2
    coef = jnp.concatenate([ref[...].astype(jnp.float32) for ref in coef_refs], axis=0)
    coef = coef.reshape(-1, rank_k, half, unknowns)
    count = coef.shape[0]
    hot = (
        lax.broadcasted_iota(jnp.int32, (clusters, pairs), 0)
        == jnp.broadcast_to(slot_ref[...], (clusters, pairs))
    ).astype(jnp.float32).astype(jnp.bfloat16)
    away = gather_place(dev_ref[...], me_ref[0], count)
    theirs = count // 2 + gather_place(dev_ref[...], me_ref[0] ^ 1, count)
    away = jnp.where(away == count // 2, theirs, away)
    cslot = cslot_ref[...]
    high = (cslot >= half).astype(jnp.int32)
    at = away * half + cslot - high * half
    table_rows = (count * half, pairs)
    pick = jnp.where(
        lax.broadcasted_iota(jnp.int32, table_rows, 0) == jnp.broadcast_to(at, table_rows), 1.0, 0.0
    )
    pick = jnp.transpose(pick).astype(jnp.bfloat16)
    lanes = (unknowns, pairs)
    keep = jnp.where(
        lax.broadcasted_iota(jnp.int32, lanes, 0) // directions == jnp.broadcast_to(high, lanes),
        1.0,
        0.0,
    )
    keep = jnp.transpose(keep).astype(jnp.bfloat16)
    total = jnp.zeros((clusters * rank_k, unknowns), jnp.float32)
    for q in range(rank_k):
        table = coef[:, q].reshape(count * half, unknowns).astype(jnp.bfloat16)
        chosen = jnp.dot(pick, table, preferred_element_type=jnp.float32).astype(jnp.bfloat16)
        chosen = chosen * keep
        couple = couple_ref[q]
        weight = jnp.concatenate([couple * hot[s : s + 1] for s in range(clusters)], axis=0)
        total = total + jnp.dot(weight, chosen, preferred_element_type=jnp.float32)
    total = total + pltpu.roll(total, unknowns // 2, axis=1)
    gathered = jnp.transpose(total)[0:directions, :].astype(jnp.bfloat16).astype(jnp.float32)
    lane = lax.broadcasted_iota(jnp.int32, gathered.shape, 1) // rank_k
    basis = basis_ref[...].reshape(clusters * rank_k, unknowns)
    for s in range(clusters):
        own = jnp.where(lane == s, gathered, 0.0).astype(jnp.bfloat16)
        out_ref[s] = jnp.dot(own, basis, preferred_element_type=jnp.float32)


def ring_device(place, core, chips):
    depth = chips // 2
    place = place % chips
    z, y = (place, 0) if place < depth else (chips - 1 - place, 1)
    return (z * 2 + y) * 2 + core


def ring_pairs(count):
    chips = count // 2
    cores = [(p, c) for p in range(chips) for c in range(2)]
    ahead = [(ring_device(p, c, chips), ring_device(p + 1 - 2 * c, c, chips)) for p, c in cores]
    cross = [
        (ring_device(p, c, chips), ring_device(p - 1 + 2 * c, 1 - c, chips)) for p, c in cores
    ]
    return ahead, cross


def ring_place(device, chips):
    z, y = device >> 2, (device >> 1) & 1
    return jnp.where(y == 0, z, chips - 1 - z)


def gather_place(device, me, count):
    chips = count // 2
    depth = chips // 2
    back = (1 - 2 * (me & 1)) * (ring_place(me, chips) - ring_place(device, chips))
    back = (back + chips) & (chips - 1)
    other = (device ^ me) & 1
    here = (back < depth) & (back > 0) | (back == 0) & (other == 1) | (back == depth) & (other == 0)
    return jnp.where(here, jnp.where(back == 0, 0, 2 * back - 1 + other), chips)


def scatter_place(device, me, count):
    chips = count // 2
    depth = chips // 2
    ahead = (ring_place(device, chips) - ring_place(me, chips) + chips) & (chips - 1)
    core = device & 1
    handler = jnp.where((ahead & (depth - 1)) == 0, core, (ahead > depth).astype(jnp.int32))
    steps = jnp.where(handler == 0, ahead, (chips - ahead) & (chips - 1))
    place = jnp.where(
        steps == depth,
        0,
        jnp.where(steps == 0, chips - 1, 2 * (depth - steps) - (core ^ handler)),
    )
    return place + jnp.where(handler == (me & 1), 0, chips)


def stationary(
    rhs,
    near_blocks,
    near_owner,
    near_slot,
    near_offset,
    far_coupling,
    far_slot,
    far_dev,
    far_cslot,
    basis_out,
    basis_in,
):
    clusters, directions, unknowns = rhs.shape
    rank_k = basis_in.shape[1]
    count = lax.axis_size("blk")
    chips = count // 2
    depth = chips // 2
    me = lax.axis_index("blk")
    stored = near_blocks.shape[0]
    pairs = far_slot.shape[0]
    half = clusters // 2
    ahead, cross = ring_pairs(count)
    mate = [(i, i ^ 1) for i in range(count)]
    side = [(i, i ^ 2) for i in range(count)]

    def move(values, where):
        return lax.ppermute(values, "blk", where)

    def after(values, *others):
        return lax.optimization_barrier((values, *others))[0]

    mate_blocks = move(near_blocks, mate)
    here = me.astype(jnp.int32).reshape(1)
    base = clusters * directions
    payload, lists = pl.pallas_call(
        functools.partial(prologue_kernel, count),
        out_shape=[
            jax.ShapeDtypeStruct((base + half * rank_k, unknowns), jnp.bfloat16),
            jax.ShapeDtypeStruct((8, stored), jnp.int32),
        ],
        in_specs=[whole(pltpu.SMEM)] + [whole()] * 5,
        out_specs=[whole()] * 2,
        compiler_params=pltpu.CompilerParams(vmem_limit_bytes=PROLOGUE_VMEM),
        name="prologue",
    )(
        here,
        near_owner.reshape(1, stored),
        near_slot.reshape(1, stored),
        near_offset.reshape(1, stored),
        rhs,
        basis_in,
    )
    flow = [move(payload, ahead), move(payload, cross)]
    shards = [move(payload, mate)]
    lists = jnp.concatenate([lists, move(lists, mate)], axis=0)
    couple = after(jnp.transpose(far_coupling, (2, 1, 0)), payload)
    for k in range(1, chips):
        x = 1 - k % 2
        if k == 3:
            flow[x], mate_blocks, shards[0], lists, couple = lax.optimization_barrier(
                (flow[x], mate_blocks, shards[0], lists, couple)
            )
        shards.append(flow[x])
        if k < chips - 2:
            flow[x] = move(flow[x], ahead)

    quarter = chips // 2

    def near(late, lists):
        pieces = [1] * quarter
        kept, *sends = pl.pallas_call(
            functools.partial(near_kernel, late, BATCH, LAG, chips, len(pieces)),
            out_shape=[
                jax.ShapeDtypeStruct((quarter * clusters, directions, unknowns), jnp.float32)
            ]
            + [
                jax.ShapeDtypeStruct((part * clusters, directions, unknowns), jnp.bfloat16)
                for part in pieces
            ]
            + [jax.ShapeDtypeStruct((chips * half * rank_k, unknowns), jnp.bfloat16)] * (1 - late),
            in_specs=[whole(pltpu.SMEM)] + [whole(pl.ANY)] * (chips + 2),
            out_specs=[whole()] * (2 + len(pieces) - late),
            scratch_shapes=[
                pltpu.VMEM((chips * base, unknowns), jnp.bfloat16),
                pltpu.VMEM((2, *near_blocks.shape), jnp.bfloat16),
                pltpu.VMEM((2 * quarter * clusters + 1, directions, unknowns), jnp.float32),
                pltpu.SemaphoreType.DMA((chips,)),
                pltpu.SemaphoreType.DMA((chips,)),
                pltpu.SemaphoreType.DMA((2 * CHUNKS,)),
            ],
            compiler_params=pltpu.CompilerParams(vmem_limit_bytes=NEAR_VMEM),
            cost_estimate=pl.CostEstimate(
                flops=16 * stored * directions * unknowns * unknowns,
                bytes_accessed=16 << 20,
                transcendentals=0,
            ),
            name="near",
        )(lists, *shards, near_blocks, mate_blocks)
        return kept, sends

    early, (*sends, coef) = near(0, lists)
    mates = [move(sends[0], mate), move(sends[1], mate)]
    coefs = [coef, move(coef, mate)]
    kept = [early]

    def term(k):
        at = k % quarter * clusters
        return kept[k // quarter][at : at + clusters] + mates[k].astype(jnp.float32)

    def tied(values, k, *others):
        values, mates[k + 1], *others = lax.optimization_barrier((values, mates[k + 1], *others))
        return values

    def add(flow, k):
        return (flow.astype(jnp.float32) + term(k)).astype(jnp.bfloat16)

    flow = lax.optimization_barrier([term(0).astype(jnp.bfloat16), term(1).astype(jnp.bfloat16)])
    lists, couple = after(lists, *flow), after(couple, *flow)
    mates += [move(after(send, *flow), mate) for send in sends[2:]]
    flow = [move(part, ahead) for part in flow]
    late, sends = near(1, lists)
    kept.append(late)
    mates += [move(send, mate) for send in sends]
    far = pl.pallas_call(
        far_kernel,
        out_shape=jax.ShapeDtypeStruct((clusters, directions, unknowns), jnp.float32),
        in_specs=[whole()] * 2 + [whole(pltpu.SMEM)] + [whole()] * 5,
        out_specs=whole(),
        compiler_params=pltpu.CompilerParams(vmem_limit_bytes=FAR_VMEM),
        cost_estimate=pl.CostEstimate(
            flops=4 * clusters * rank_k * pairs * rank_k * unknowns,
            bytes_accessed=8 << 20,
            transcendentals=0,
        ),
        name="far",
    )(
        *coefs,
        here,
        couple,
        far_slot.reshape(1, pairs),
        far_dev.reshape(1, pairs),
        far_cslot.reshape(1, pairs),
        basis_out,
    )
    for k in range(2, chips - 1):
        x = k % 2
        flow[x] = move(tied(add(flow[x], k), k, *([far] if k == chips - 3 else [])), ahead)
    flow[1] = move(flow[1], mate)
    total = far + term(chips - 1) + flow[0].astype(jnp.float32)
    total = lax.optimization_barrier(total)
    return (total + flow[1].astype(jnp.float32)).astype(jnp.bfloat16)


def on_device(*args):
    rhs, near_blocks = args[0], args[1]
    clusters, directions, unknowns = rhs.shape
    small = lax.axis_size("blk") == 16 and clusters == 16
    if small and near_blocks.shape[0] == unknowns and 2 * directions == unknowns:
        return stationary(*args)
    return routed(*args)


def solution(mesh):
    placed = (
        P(("groups", "blk"), None, None),
        P(("groups", "blk"), None, None),
        P(("groups", "blk"), None),
        P(("groups", "blk")),
        P(("groups", "blk")),
        P(("groups", "blk"), None, None),
        P(("groups", "blk")),
        P(("groups", "blk"), None),
        P(("groups", "blk")),
        P(("groups", "blk"), None, None),
        P(("groups", "blk"), None, None),
    )
    return jax.shard_map(
        on_device,
        mesh=mesh,
        in_specs=placed,
        out_specs=P(("groups", "blk"), None, None),
        check_vma=False,
    )
```

```python
import functools

import jax
import jax.numpy as jnp
from jax import lax
from jax.experimental import pallas as pl
from jax.experimental.pallas import tpu as pltpu
from jax.sharding import PartitionSpec as P

CHUNKS = 4
BATCH = 16
LAG = 4
PROLOGUE_VMEM = 58 << 20
NEAR_VMEM = 48 << 20
FAR_VMEM = 16 << 20


def with_halo(cells, sides, width):
    for axis, dim in sides:
        count = lax.axis_size(axis)
        head = lax.slice_in_dim(cells, 0, width, axis=dim)
        tail = lax.slice_in_dim(cells, cells.shape[dim] - width, cells.shape[dim], axis=dim)
        cells = jnp.concatenate(
            [
                lax.ppermute(tail, axis, [(i, (i + 1) % count) for i in range(count)]),
                cells,
                lax.ppermute(head, axis, [((i + 1) % count, i) for i in range(count)]),
            ],
            axis=dim,
        )
    return cells


def place_ranks(targets, count):
    onehot = (targets[:, None] == jnp.arange(count, dtype=jnp.int32)[None, :]).astype(jnp.int32)
    before = jnp.cumsum(onehot, axis=0) - onehot
    return jnp.sum(before * onehot, axis=1)


def routed(
    rhs,
    near_blocks,
    near_owner,
    near_slot,
    near_offset,
    far_coupling,
    far_slot,
    far_dev,
    far_cslot,
    basis_out,
    basis_in,
):
    clusters = rhs.shape[0]
    directions = rhs.shape[1]
    unknowns = rhs.shape[2]
    cycle_size = lax.axis_size("blk")
    stored = near_blocks.shape[0]
    capacity = max(2, 2 * stored // cycle_size)
    owners = near_owner[:, 0]
    target = owners * capacity + place_ranks(owners, cycle_size)
    outbox = (
        jnp.zeros((cycle_size * capacity, unknowns, unknowns), near_blocks.dtype)
        .at[target]
        .set(near_blocks)
    )
    labels = (
        jnp.zeros((cycle_size * capacity, 2), jnp.int32)
        .at[target]
        .set(jnp.stack([near_slot, near_offset], axis=1))
    )
    window = with_halo(rhs, (("blk", 0),), clusters)
    inbox, in_labels = (
        lax.all_to_all(outbox, "blk", split_axis=0, concat_axis=0, tiled=True),
        lax.all_to_all(labels, "blk", split_axis=0, concat_axis=0, tiled=True),
    )
    position = clusters + in_labels[:, 0] + in_labels[:, 1]
    columns = jnp.take(window, position, axis=0)
    products = jnp.einsum("srj,sij->sri", columns, inbox, preferred_element_type=jnp.float32)
    selector = (in_labels[:, 0][None, :] == jnp.arange(clusters, dtype=jnp.int32)[:, None]).astype(
        jnp.float32
    )
    near_sum = jnp.dot(
        selector,
        products.reshape(products.shape[0], -1),
        precision=lax.Precision.HIGHEST,
        preferred_element_type=jnp.float32,
    ).reshape(clusters, directions, unknowns)
    coef_local = jnp.einsum(
        "ckj,crj->crk", basis_in, rhs, preferred_element_type=jnp.float32
    ).astype(jnp.bfloat16)
    rank_k = basis_in.shape[1]
    coef_local = coef_local.reshape(clusters, directions * rank_k)
    pairs = far_slot.shape[0]
    wanted = far_dev[:, 0] * clusters + far_cslot
    piece = lax.all_gather(coef_local, "blk", axis=0, tiled=True)
    chosen = jnp.take(piece, wanted, axis=0)
    coupled = jnp.einsum(
        "pkq,prq->prk",
        far_coupling,
        chosen.reshape(pairs, directions, rank_k),
        preferred_element_type=jnp.float32,
    )
    row_pick = (far_slot[None, :] == jnp.arange(clusters, dtype=jnp.int32)[:, None]).astype(
        jnp.float32
    )
    gathered = jnp.dot(
        row_pick,
        coupled.reshape(pairs, -1),
        precision=lax.Precision.HIGHEST,
        preferred_element_type=jnp.float32,
    )
    gathered = gathered.astype(jnp.bfloat16).reshape(clusters, directions, rank_k)
    far_sum = jnp.einsum("crk,ckb->crb", gathered, basis_out, preferred_element_type=jnp.float32)
    return (near_sum + far_sum).astype(jnp.bfloat16)


def whole(space=pltpu.VMEM):
    return pl.BlockSpec(memory_space=space)


def prologue_kernel(
    count, me_ref, owner_ref, slot_ref, offset_ref, rhs_ref, basis_ref, payload_ref, list_ref
):
    clusters, directions, unknowns = rhs_ref.shape
    base = clusters * directions
    payload_ref[0:base, :] = rhs_ref[...].reshape(base, unknowns)
    rank_k = basis_ref.shape[1]
    half = clusters // 2
    rows = []
    for c in range(half):
        parts = [
            lax.dot_general(
                basis_ref[e],
                rhs_ref[e],
                (((1,), (1,)), ((), ())),
                preferred_element_type=jnp.float32,
            )
            for e in (c, c + half)
        ]
        rows.append(jnp.concatenate(parts, axis=1))
    payload_ref[base:, :] = jnp.concatenate(
        [row[q : q + 1] for q in range(rank_k) for row in rows], axis=0
    ).astype(payload_ref.dtype)

    me, owner, slot = me_ref[0], owner_ref[...], slot_ref[...]
    stored = owner.shape[1]
    place = scatter_place(owner, me, count)
    quarter = count // 4
    late = (place // quarter) & 1
    place = (place // (2 * quarter) * quarter + (place & (quarter - 1))) * clusters + slot
    column = (owner * clusters + slot + offset_ref[...]) & (count * clusters - 1)
    shard = gather_place(column // clusters, me, count)
    theirs = (shard == count // 2).astype(jnp.int32)
    shard = jnp.where(theirs == 1, gather_place(column // clusters, me ^ 1, count), shard)
    column_place = shard * clusters + (column & (clusters - 1))
    square = (stored, stored)
    group = jnp.broadcast_to((2 * theirs + late).astype(jnp.float32), square)
    group_of_row = jnp.transpose(group)
    row_at = lax.broadcasted_iota(jnp.int32, square, 0)
    lane_at = lax.broadcasted_iota(jnp.int32, square, 1)
    lane = lane_at.astype(jnp.float32)
    before = (group_of_row < group) | ((group_of_row == group) & (row_at < lane_at))
    rank = jnp.sum(jnp.where(before, 1.0, 0.0), axis=0, keepdims=True)
    rank = jnp.transpose(jnp.broadcast_to(rank, square))
    here = jnp.where(rank == lane, 1.0, 0.0).astype(jnp.bfloat16)
    starts = jnp.sum(jnp.where(group_of_row < lane, 1.0, 0.0), axis=0, keepdims=True)
    values = jnp.concatenate(
        [lane[0:1], place.astype(jnp.float32), column_place.astype(jnp.float32)]
        + [jnp.zeros((5, stored), jnp.float32)],
        axis=0,
    )
    values = jnp.dot(values.astype(jnp.bfloat16), here, preferred_element_type=jnp.float32)
    values = jnp.concatenate([values[0:3], starts, values[4:8]], axis=0)
    list_ref[...] = values.astype(jnp.int32)


def near_kernel(late, batch, lag, shards, sends, list_ref, *refs):
    shard_refs, (own_hbm, mate_hbm, keep_ref) = refs[:shards], refs[shards : shards + 3]
    send_refs, refs = refs[shards + 3 : shards + 3 + sends], refs[shards + 3 + sends :]
    if not late:
        coef_ref, refs = refs[0], refs[1:]
    columns, blocks, sums, column_sem, coef_sem, block_sem = refs
    directions = sums.shape[1]
    span = columns.shape[0] // shards
    stored = blocks.shape[1]
    chunk = stored // CHUNKS
    dummy = sums.shape[0] - 1

    copies = [
        pltpu.make_async_copy(
            ref.at[pl.ds(0, span)], columns.at[pl.ds(k * span, span)], column_sem.at[k]
        )
        for k, ref in enumerate(shard_refs)
    ]
    for copy in copies:
        copy.start()
    for half, source in enumerate((own_hbm, mate_hbm)):
        for c in range(CHUNKS):
            at = pl.ds(c * chunk, chunk)
            pltpu.make_async_copy(
                source.at[at], blocks.at[half, at], block_sem.at[half * CHUNKS + c]
            ).start()
    tails = []
    if not late:
        tail = coef_ref.shape[0] // shards
        tails = [
            pltpu.make_async_copy(
                ref.at[pl.ds(span, tail)], coef_ref.at[pl.ds(k * tail, tail)], coef_sem.at[k]
            )
            for k, ref in enumerate(shard_refs)
        ]
    for copy in tails:
        copy.start()

    def clear(i, carry):
        sums[i] = jnp.zeros(sums.shape[1:], sums.dtype)
        return carry

    lax.fori_loop(0, dummy, clear, 0)
    for copy in copies:
        copy.wait()

    begin, begin_there = list_ref[3, late], list_ref[11, 2 + late]
    here = list_ref[3, late + 1] - begin
    total = here + list_ref[11, 3 + late] - begin_there

    def entry(j):
        j = jnp.minimum(j, total - 1)
        half = (j >= here).astype(jnp.int32)
        return half, half * 8, j + jnp.where(half == 1, begin_there - here, begin)

    def wait(c, carry):
        at = pl.ds(0, chunk)
        pltpu.make_async_copy(own_hbm.at[at], blocks.at[0, at], block_sem.at[c]).wait()
        return carry

    def body(step, ready):
        first = step * batch
        half, row, at = entry(first + batch - 1)
        needed = half * CHUNKS + list_ref[row, at] // chunk + 1
        lax.fori_loop(ready, needed, wait, 0)
        products = []

        def add(i):
            half, row, at = entry(first + i)
            place = list_ref[row + 1, at] ^ (half * (dummy // 2))
            place = jnp.where(first + i < total, place, dummy)
            sums[place] = sums[place] + products[i]

        for i in range(batch):
            half, row, at = entry(first + i)
            start = pl.multiple_of(list_ref[row + 2, at] * directions, directions)
            products.append(
                lax.dot_general(
                    columns[pl.ds(start, directions)],
                    blocks[half, list_ref[row, at]],
                    (((1,), (1,)), ((), ())),
                    preferred_element_type=jnp.float32,
                )
            )
            if i >= lag:
                add(i - lag)
        for i in range(batch - lag, batch):
            add(i)
        return jnp.maximum(ready, needed)

    ready = lax.fori_loop(0, (total + batch - 1) // batch, body, 0)
    lax.fori_loop(ready, 2 * CHUNKS, wait, 0)

    def keep(i, carry):
        keep_ref[i] = sums[i]
        return carry

    lax.fori_loop(0, dummy // 2, keep, 0, unroll=2)
    at = dummy // 2
    for send_ref in send_refs:

        def pack(i, carry, at=at, send_ref=send_ref):
            send_ref[i] = sums[at + i].astype(send_ref.dtype)
            return carry

        lax.fori_loop(0, send_ref.shape[0], pack, 0, unroll=2)
        at += send_ref.shape[0]
    for copy in tails:
        copy.wait()


def far_kernel(*refs):
    coef_refs = refs[:2]
    me_ref, couple_ref, slot_ref, dev_ref, cslot_ref, basis_ref, out_ref = refs[2:]
    clusters, rank_k, unknowns = basis_ref.shape
    pairs = couple_ref.shape[2]
    directions = out_ref.shape[1]
    half = clusters // 2
    coef = jnp.concatenate([ref[...].astype(jnp.float32) for ref in coef_refs], axis=0)
    coef = coef.reshape(-1, rank_k, half, unknowns)
    count = coef.shape[0]
    hot = (
        lax.broadcasted_iota(jnp.int32, (clusters, pairs), 0)
        == jnp.broadcast_to(slot_ref[...], (clusters, pairs))
    ).astype(jnp.float32).astype(jnp.bfloat16)
    away = gather_place(dev_ref[...], me_ref[0], count)
    theirs = count // 2 + gather_place(dev_ref[...], me_ref[0] ^ 1, count)
    away = jnp.where(away == count // 2, theirs, away)
    cslot = cslot_ref[...]
    high = (cslot >= half).astype(jnp.int32)
    at = away * half + cslot - high * half
    table_rows = (count * half, pairs)
    pick = jnp.where(
        lax.broadcasted_iota(jnp.int32, table_rows, 0) == jnp.broadcast_to(at, table_rows), 1.0, 0.0
    )
    pick = jnp.transpose(pick).astype(jnp.bfloat16)
    lanes = (unknowns, pairs)
    keep = jnp.where(
        lax.broadcasted_iota(jnp.int32, lanes, 0) // directions == jnp.broadcast_to(high, lanes),
        1.0,
        0.0,
    )
    keep = jnp.transpose(keep).astype(jnp.bfloat16)
    total = jnp.zeros((clusters * rank_k, unknowns), jnp.float32)
    for q in range(rank_k):
        table = coef[:, q].reshape(count * half, unknowns).astype(jnp.bfloat16)
        chosen = jnp.dot(pick, table, preferred_element_type=jnp.float32).astype(jnp.bfloat16)
        chosen = chosen * keep
        couple = couple_ref[q]
        weight = jnp.concatenate([couple * hot[s : s + 1] for s in range(clusters)], axis=0)
        total = total + jnp.dot(weight, chosen, preferred_element_type=jnp.float32)
    total = total + pltpu.roll(total, unknowns // 2, axis=1)
    gathered = jnp.transpose(total)[0:directions, :].astype(jnp.bfloat16).astype(jnp.float32)
    lane = lax.broadcasted_iota(jnp.int32, gathered.shape, 1) // rank_k
    basis = basis_ref[...].reshape(clusters * rank_k, unknowns)
    for s in range(clusters):
        own = jnp.where(lane == s, gathered, 0.0).astype(jnp.bfloat16)
        out_ref[s] = jnp.dot(own, basis, preferred_element_type=jnp.float32)


def ring_device(place, core, chips):
    depth = chips // 2
    place = place % chips
    z, y = (place, 0) if place < depth else (chips - 1 - place, 1)
    return (z * 2 + y) * 2 + core


def ring_pairs(count):
    chips = count // 2
    cores = [(p, c) for p in range(chips) for c in range(2)]
    ahead = [(ring_device(p, c, chips), ring_device(p + 1 - 2 * c, c, chips)) for p, c in cores]
    behind = [(target, source) for source, target in ahead]
    return ahead, behind


def ring_place(device, chips):
    z, y = device >> 2, (device >> 1) & 1
    return jnp.where(y == 0, z, chips - 1 - z)


def gather_place(device, me, count):
    chips = count // 2
    depth = chips // 2
    back = (1 - 2 * (me & 1)) * (ring_place(me, chips) - ring_place(device, chips))
    back = (back + chips) & (chips - 1)
    other = (device ^ me) & 1
    arrival = jnp.where(back <= depth, 2 * back - 1, 2 * (chips - back))
    arrival = jnp.where(back == 0, 0, arrival)
    return jnp.where((other == 1) == (back == 0), arrival, chips)


def scatter_place(device, me, count):
    chips = count // 2
    depth = chips // 2
    away = (1 - 2 * (device & 1)) * (ring_place(device, chips) - ring_place(me, chips))
    away = (away + chips) & (chips - 1)
    hop = jnp.where(away > depth, 2 * (away - depth) - 1, 2 * (depth - away))
    hop = jnp.where(away == 0, chips - 1, hop)
    return hop + chips * ((device ^ me) & 1)


def stationary(
    rhs,
    near_blocks,
    near_owner,
    near_slot,
    near_offset,
    far_coupling,
    far_slot,
    far_dev,
    far_cslot,
    basis_out,
    basis_in,
):
    clusters, directions, unknowns = rhs.shape
    rank_k = basis_in.shape[1]
    count = lax.axis_size("blk")
    chips = count // 2
    depth = chips // 2
    me = lax.axis_index("blk")
    stored = near_blocks.shape[0]
    pairs = far_slot.shape[0]
    half = clusters // 2
    ways = ring_pairs(count)
    mate = [(i, i ^ 1) for i in range(count)]
    side = [(i, i ^ 2) for i in range(count)]

    def move(values, where):
        return lax.ppermute(values, "blk", where)

    def after(values, *others):
        return lax.optimization_barrier((values, *others))[0]

    mate_blocks = move(near_blocks, mate)
    here = me.astype(jnp.int32).reshape(1)
    base = clusters * directions
    payload, lists = pl.pallas_call(
        functools.partial(prologue_kernel, count),
        out_shape=[
            jax.ShapeDtypeStruct((base + half * rank_k, unknowns), jnp.bfloat16),
            jax.ShapeDtypeStruct((8, stored), jnp.int32),
        ],
        in_specs=[whole(pltpu.SMEM)] + [whole()] * 5,
        out_specs=[whole()] * 2,
        compiler_params=pltpu.CompilerParams(vmem_limit_bytes=PROLOGUE_VMEM),
        name="prologue",
    )(
        here,
        near_owner.reshape(1, stored),
        near_slot.reshape(1, stored),
        near_offset.reshape(1, stored),
        rhs,
        basis_in,
    )
    flow = [move(payload, way) for way in ways]
    shards = [move(payload, mate)]
    lists = jnp.concatenate([lists, move(lists, mate)], axis=0)
    couple = after(jnp.transpose(far_coupling, (2, 1, 0)), payload)
    for k in range(1, chips):
        x = 1 - k % 2
        if k == 3:
            flow[x], mate_blocks, shards[0], lists, couple = lax.optimization_barrier(
                (flow[x], mate_blocks, shards[0], lists, couple)
            )
        shards.append(flow[x])
        if k < chips - 2:
            flow[x] = move(flow[x], ways[x])

    quarter = chips // 2

    def near(late, lists):
        pieces = [1] * quarter
        kept, *sends = pl.pallas_call(
            functools.partial(near_kernel, late, BATCH, LAG, chips, len(pieces)),
            out_shape=[
                jax.ShapeDtypeStruct((quarter * clusters, directions, unknowns), jnp.float32)
            ]
            + [
                jax.ShapeDtypeStruct((part * clusters, directions, unknowns), jnp.bfloat16)
                for part in pieces
            ]
            + [jax.ShapeDtypeStruct((chips * half * rank_k, unknowns), jnp.bfloat16)] * (1 - late),
            in_specs=[whole(pltpu.SMEM)] + [whole(pl.ANY)] * (chips + 2),
            out_specs=[whole()] * (2 + len(pieces) - late),
            scratch_shapes=[
                pltpu.VMEM((chips * base, unknowns), jnp.bfloat16),
                pltpu.VMEM((2, *near_blocks.shape), jnp.bfloat16),
                pltpu.VMEM((2 * quarter * clusters + 1, directions, unknowns), jnp.float32),
                pltpu.SemaphoreType.DMA((chips,)),
                pltpu.SemaphoreType.DMA((chips,)),
                pltpu.SemaphoreType.DMA((2 * CHUNKS,)),
            ],
            compiler_params=pltpu.CompilerParams(vmem_limit_bytes=NEAR_VMEM),
            cost_estimate=pl.CostEstimate(
                flops=16 * stored * directions * unknowns * unknowns,
                bytes_accessed=16 << 20,
                transcendentals=0,
            ),
            name="near",
        )(lists, *shards, near_blocks, mate_blocks)
        return kept, sends

    def far_field(couple):
        return pl.pallas_call(
            far_kernel,
            out_shape=jax.ShapeDtypeStruct((clusters, directions, unknowns), jnp.float32),
            in_specs=[whole()] * 2 + [whole(pltpu.SMEM)] + [whole()] * 5,
            out_specs=whole(),
            compiler_params=pltpu.CompilerParams(vmem_limit_bytes=FAR_VMEM),
            cost_estimate=pl.CostEstimate(
                flops=4 * clusters * rank_k * pairs * rank_k * unknowns,
                bytes_accessed=8 << 20,
                transcendentals=0,
            ),
            name="far",
        )(
            *coefs,
            here,
            couple,
            far_slot.reshape(1, pairs),
            far_dev.reshape(1, pairs),
            far_cslot.reshape(1, pairs),
            basis_out,
        )

    early, (*sends, coef) = near(0, lists)
    mates = [move(sends[0], mate), move(sends[1], mate)]
    coefs = [coef, move(coef, mate)]
    kept = [early]

    def term(k):
        at = k % quarter * clusters
        return kept[k // quarter][at : at + clusters] + mates[k].astype(jnp.float32)

    def tied(values, k, *others):
        values, mates[k + 1], *others = lax.optimization_barrier((values, mates[k + 1], *others))
        return values

    def add(flow, k):
        return (flow.astype(jnp.float32) + term(k)).astype(jnp.bfloat16)

    flow = lax.optimization_barrier([term(0).astype(jnp.bfloat16), term(1).astype(jnp.bfloat16)])
    lists = after(lists, *flow)
    mates += [move(after(send, *flow), mate) for send in sends[2:]]
    flow = [move(part, way) for part, way in zip(flow, ways)]
    late, sends = near(1, lists)
    kept.append(late)
    mates += [move(send, mate) for send in sends]
    for k in range(2, chips - 1):
        x = k % 2
        flow[x] = tied(add(flow[x], k), k)
        if k == chips - 2:
            couple = after(couple, flow[x])
        flow[x] = move(flow[x], ways[x])
    far = far_field(couple)
    total = far + term(chips - 1) + flow[1].astype(jnp.float32)
    return (total + flow[0].astype(jnp.float32)).astype(jnp.bfloat16)


def on_device(*args):
    rhs, near_blocks = args[0], args[1]
    clusters, directions, unknowns = rhs.shape
    small = lax.axis_size("blk") == 16 and clusters == 16
    if small and near_blocks.shape[0] == unknowns and 2 * directions == unknowns:
        return stationary(*args)
    return routed(*args)


def solution(mesh):
    placed = (
        P(("groups", "blk"), None, None),
        P(("groups", "blk"), None, None),
        P(("groups", "blk"), None),
        P(("groups", "blk")),
        P(("groups", "blk")),
        P(("groups", "blk"), None, None),
        P(("groups", "blk")),
        P(("groups", "blk"), None),
        P(("groups", "blk")),
        P(("groups", "blk"), None, None),
        P(("groups", "blk"), None, None),
    )
    return jax.shard_map(
        on_device,
        mesh=mesh,
        in_specs=placed,
        out_specs=P(("groups", "blk"), None, None),
        check_vma=False,
    )
```

```python
import functools

import jax
import jax.numpy as jnp
from jax import lax
from jax.experimental import pallas as pl
from jax.experimental.pallas import tpu as pltpu
from jax.sharding import PartitionSpec as P

CHUNKS = 4
BATCH = 16
LAG = 4
PROLOGUE_VMEM = 58 << 20
NEAR_VMEM = 48 << 20
FAR_VMEM = 16 << 20


def with_halo(cells, sides, width):
    for axis, dim in sides:
        count = lax.axis_size(axis)
        head = lax.slice_in_dim(cells, 0, width, axis=dim)
        tail = lax.slice_in_dim(cells, cells.shape[dim] - width, cells.shape[dim], axis=dim)
        cells = jnp.concatenate(
            [
                lax.ppermute(tail, axis, [(i, (i + 1) % count) for i in range(count)]),
                cells,
                lax.ppermute(head, axis, [((i + 1) % count, i) for i in range(count)]),
            ],
            axis=dim,
        )
    return cells


def place_ranks(targets, count):
    onehot = (targets[:, None] == jnp.arange(count, dtype=jnp.int32)[None, :]).astype(jnp.int32)
    before = jnp.cumsum(onehot, axis=0) - onehot
    return jnp.sum(before * onehot, axis=1)


def routed(
    rhs,
    near_blocks,
    near_owner,
    near_slot,
    near_offset,
    far_coupling,
    far_slot,
    far_dev,
    far_cslot,
    basis_out,
    basis_in,
):
    clusters = rhs.shape[0]
    directions = rhs.shape[1]
    unknowns = rhs.shape[2]
    cycle_size = lax.axis_size("blk")
    stored = near_blocks.shape[0]
    capacity = max(2, 2 * stored // cycle_size)
    owners = near_owner[:, 0]
    target = owners * capacity + place_ranks(owners, cycle_size)
    outbox = (
        jnp.zeros((cycle_size * capacity, unknowns, unknowns), near_blocks.dtype)
        .at[target]
        .set(near_blocks)
    )
    labels = (
        jnp.zeros((cycle_size * capacity, 2), jnp.int32)
        .at[target]
        .set(jnp.stack([near_slot, near_offset], axis=1))
    )
    window = with_halo(rhs, (("blk", 0),), clusters)
    inbox, in_labels = (
        lax.all_to_all(outbox, "blk", split_axis=0, concat_axis=0, tiled=True),
        lax.all_to_all(labels, "blk", split_axis=0, concat_axis=0, tiled=True),
    )
    position = clusters + in_labels[:, 0] + in_labels[:, 1]
    columns = jnp.take(window, position, axis=0)
    products = jnp.einsum("srj,sij->sri", columns, inbox, preferred_element_type=jnp.float32)
    selector = (in_labels[:, 0][None, :] == jnp.arange(clusters, dtype=jnp.int32)[:, None]).astype(
        jnp.float32
    )
    near_sum = jnp.dot(
        selector,
        products.reshape(products.shape[0], -1),
        precision=lax.Precision.HIGHEST,
        preferred_element_type=jnp.float32,
    ).reshape(clusters, directions, unknowns)
    coef_local = jnp.einsum(
        "ckj,crj->crk", basis_in, rhs, preferred_element_type=jnp.float32
    ).astype(jnp.bfloat16)
    rank_k = basis_in.shape[1]
    coef_local = coef_local.reshape(clusters, directions * rank_k)
    pairs = far_slot.shape[0]
    wanted = far_dev[:, 0] * clusters + far_cslot
    piece = lax.all_gather(coef_local, "blk", axis=0, tiled=True)
    chosen = jnp.take(piece, wanted, axis=0)
    coupled = jnp.einsum(
        "pkq,prq->prk",
        far_coupling,
        chosen.reshape(pairs, directions, rank_k),
        preferred_element_type=jnp.float32,
    )
    row_pick = (far_slot[None, :] == jnp.arange(clusters, dtype=jnp.int32)[:, None]).astype(
        jnp.float32
    )
    gathered = jnp.dot(
        row_pick,
        coupled.reshape(pairs, -1),
        precision=lax.Precision.HIGHEST,
        preferred_element_type=jnp.float32,
    )
    gathered = gathered.astype(jnp.bfloat16).reshape(clusters, directions, rank_k)
    far_sum = jnp.einsum("crk,ckb->crb", gathered, basis_out, preferred_element_type=jnp.float32)
    return (near_sum + far_sum).astype(jnp.bfloat16)


def whole(space=pltpu.VMEM):
    return pl.BlockSpec(memory_space=space)


def prologue_kernel(
    count, me_ref, owner_ref, slot_ref, offset_ref, rhs_ref, basis_ref, payload_ref, list_ref
):
    clusters, directions, unknowns = rhs_ref.shape
    base = clusters * directions
    payload_ref[0:base, :] = rhs_ref[...].reshape(base, unknowns)
    rank_k = basis_ref.shape[1]
    half = clusters // 2
    rows = []
    for c in range(half):
        parts = [
            lax.dot_general(
                basis_ref[e],
                rhs_ref[e],
                (((1,), (1,)), ((), ())),
                preferred_element_type=jnp.float32,
            )
            for e in (c, c + half)
        ]
        rows.append(jnp.concatenate(parts, axis=1))
    payload_ref[base:, :] = jnp.concatenate(
        [row[q : q + 1] for q in range(rank_k) for row in rows], axis=0
    ).astype(payload_ref.dtype)

    me, owner, slot = me_ref[0], owner_ref[...], slot_ref[...]
    stored = owner.shape[1]
    place = scatter_place(owner, me, count)
    quarter = count // 4
    late = (place // quarter) & 1
    place = (place // (2 * quarter) * quarter + (place & (quarter - 1))) * clusters + slot
    column = (owner * clusters + slot + offset_ref[...]) & (count * clusters - 1)
    shard = gather_place(column // clusters, me, count)
    theirs = (shard == count // 2).astype(jnp.int32)
    shard = jnp.where(theirs == 1, gather_place(column // clusters, me ^ 1, count), shard)
    column_place = shard * clusters + (column & (clusters - 1))
    square = (stored, stored)
    group = jnp.broadcast_to((2 * theirs + late).astype(jnp.float32), square)
    group_of_row = jnp.transpose(group)
    row_at = lax.broadcasted_iota(jnp.int32, square, 0)
    lane_at = lax.broadcasted_iota(jnp.int32, square, 1)
    lane = lane_at.astype(jnp.float32)
    before = (group_of_row < group) | ((group_of_row == group) & (row_at < lane_at))
    rank = jnp.sum(jnp.where(before, 1.0, 0.0), axis=0, keepdims=True)
    rank = jnp.transpose(jnp.broadcast_to(rank, square))
    here = jnp.where(rank == lane, 1.0, 0.0).astype(jnp.bfloat16)
    starts = jnp.sum(jnp.where(group_of_row < lane, 1.0, 0.0), axis=0, keepdims=True)
    values = jnp.concatenate(
        [lane[0:1], place.astype(jnp.float32), column_place.astype(jnp.float32)]
        + [jnp.zeros((5, stored), jnp.float32)],
        axis=0,
    )
    values = jnp.dot(values.astype(jnp.bfloat16), here, preferred_element_type=jnp.float32)
    values = jnp.concatenate([values[0:3], starts, values[4:8]], axis=0)
    list_ref[...] = values.astype(jnp.int32)


def near_kernel(late, batch, lag, shards, sends, list_ref, *refs):
    shard_refs, (own_hbm, mate_hbm, keep_ref) = refs[:shards], refs[shards : shards + 3]
    send_refs, refs = refs[shards + 3 : shards + 3 + sends], refs[shards + 3 + sends :]
    if not late:
        coef_ref, refs = refs[0], refs[1:]
    columns, blocks, sums, column_sem, coef_sem, block_sem = refs
    directions = sums.shape[1]
    span = columns.shape[0] // shards
    stored = blocks.shape[1]
    chunk = stored // CHUNKS
    dummy = sums.shape[0] - 1

    copies = [
        pltpu.make_async_copy(
            ref.at[pl.ds(0, span)], columns.at[pl.ds(k * span, span)], column_sem.at[k]
        )
        for k, ref in enumerate(shard_refs)
    ]
    for copy in copies:
        copy.start()
    for half, source in enumerate((own_hbm, mate_hbm)):
        for c in range(CHUNKS):
            at = pl.ds(c * chunk, chunk)
            pltpu.make_async_copy(
                source.at[at], blocks.at[half, at], block_sem.at[half * CHUNKS + c]
            ).start()
    tails = []
    if not late:
        tail = coef_ref.shape[0] // shards
        tails = [
            pltpu.make_async_copy(
                ref.at[pl.ds(span, tail)], coef_ref.at[pl.ds(k * tail, tail)], coef_sem.at[k]
            )
            for k, ref in enumerate(shard_refs)
        ]
    for copy in tails:
        copy.start()

    def clear(i, carry):
        sums[i] = jnp.zeros(sums.shape[1:], sums.dtype)
        return carry

    lax.fori_loop(0, dummy, clear, 0)
    for copy in copies:
        copy.wait()

    begin, begin_there = list_ref[3, late], list_ref[11, 2 + late]
    here = list_ref[3, late + 1] - begin
    total = here + list_ref[11, 3 + late] - begin_there

    def entry(j):
        j = jnp.minimum(j, total - 1)
        half = (j >= here).astype(jnp.int32)
        return half, half * 8, j + jnp.where(half == 1, begin_there - here, begin)

    def wait(c, carry):
        at = pl.ds(0, chunk)
        pltpu.make_async_copy(own_hbm.at[at], blocks.at[0, at], block_sem.at[c]).wait()
        return carry

    def body(step, ready):
        first = step * batch
        half, row, at = entry(first + batch - 1)
        needed = half * CHUNKS + list_ref[row, at] // chunk + 1
        lax.fori_loop(ready, needed, wait, 0)
        products = []

        def add(i):
            half, row, at = entry(first + i)
            place = list_ref[row + 1, at] ^ (half * (dummy // 2))
            place = jnp.where(first + i < total, place, dummy)
            sums[place] = sums[place] + products[i]

        for i in range(batch):
            half, row, at = entry(first + i)
            start = pl.multiple_of(list_ref[row + 2, at] * directions, directions)
            products.append(
                lax.dot_general(
                    columns[pl.ds(start, directions)],
                    blocks[half, list_ref[row, at]],
                    (((1,), (1,)), ((), ())),
                    preferred_element_type=jnp.float32,
                )
            )
            if i >= lag:
                add(i - lag)
        for i in range(batch - lag, batch):
            add(i)
        return jnp.maximum(ready, needed)

    ready = lax.fori_loop(0, (total + batch - 1) // batch, body, 0)
    lax.fori_loop(ready, 2 * CHUNKS, wait, 0)

    def keep(i, carry):
        keep_ref[i] = sums[i]
        return carry

    lax.fori_loop(0, dummy // 2, keep, 0, unroll=2)
    at = dummy // 2
    for send_ref in send_refs:

        def pack(i, carry, at=at, send_ref=send_ref):
            send_ref[i] = sums[at + i].astype(send_ref.dtype)
            return carry

        lax.fori_loop(0, send_ref.shape[0], pack, 0, unroll=2)
        at += send_ref.shape[0]
    for copy in tails:
        copy.wait()


def far_kernel(*refs):
    coef_refs = refs[:2]
    me_ref, couple_ref, slot_ref, dev_ref, cslot_ref, basis_ref, out_ref = refs[2:]
    clusters, rank_k, unknowns = basis_ref.shape
    pairs = couple_ref.shape[2]
    directions = out_ref.shape[1]
    half = clusters // 2
    coef = jnp.concatenate([ref[...].astype(jnp.float32) for ref in coef_refs], axis=0)
    coef = coef.reshape(-1, rank_k, half, unknowns)
    count = coef.shape[0]
    hot = (
        lax.broadcasted_iota(jnp.int32, (clusters, pairs), 0)
        == jnp.broadcast_to(slot_ref[...], (clusters, pairs))
    ).astype(jnp.float32).astype(jnp.bfloat16)
    away = gather_place(dev_ref[...], me_ref[0], count)
    theirs = count // 2 + gather_place(dev_ref[...], me_ref[0] ^ 1, count)
    away = jnp.where(away == count // 2, theirs, away)
    cslot = cslot_ref[...]
    high = (cslot >= half).astype(jnp.int32)
    at = away * half + cslot - high * half
    table_rows = (count * half, pairs)
    pick = jnp.where(
        lax.broadcasted_iota(jnp.int32, table_rows, 0) == jnp.broadcast_to(at, table_rows), 1.0, 0.0
    )
    pick = jnp.transpose(pick).astype(jnp.bfloat16)
    lanes = (unknowns, pairs)
    keep = jnp.where(
        lax.broadcasted_iota(jnp.int32, lanes, 0) // directions == jnp.broadcast_to(high, lanes),
        1.0,
        0.0,
    )
    keep = jnp.transpose(keep).astype(jnp.bfloat16)
    total = jnp.zeros((clusters * rank_k, unknowns), jnp.float32)
    for q in range(rank_k):
        table = coef[:, q].reshape(count * half, unknowns).astype(jnp.bfloat16)
        chosen = jnp.dot(pick, table, preferred_element_type=jnp.float32).astype(jnp.bfloat16)
        chosen = chosen * keep
        couple = couple_ref[q]
        weight = jnp.concatenate([couple * hot[s : s + 1] for s in range(clusters)], axis=0)
        total = total + jnp.dot(weight, chosen, preferred_element_type=jnp.float32)
    total = total + pltpu.roll(total, unknowns // 2, axis=1)
    gathered = jnp.transpose(total)[0:directions, :].astype(jnp.bfloat16).astype(jnp.float32)
    lane = lax.broadcasted_iota(jnp.int32, gathered.shape, 1) // rank_k
    basis = basis_ref[...].reshape(clusters * rank_k, unknowns)
    for s in range(clusters):
        own = jnp.where(lane == s, gathered, 0.0).astype(jnp.bfloat16)
        out_ref[s] = jnp.dot(own, basis, preferred_element_type=jnp.float32)


def ring_device(place, core, chips):
    depth = chips // 2
    place = place % chips
    z, y = (place, 0) if place < depth else (chips - 1 - place, 1)
    return (z * 2 + y) * 2 + core


def ring_pairs(count):
    chips = count // 2
    cores = [(p, c) for p in range(chips) for c in range(2)]
    ahead = [(ring_device(p, c, chips), ring_device(p + 1 - 2 * c, c, chips)) for p, c in cores]
    return ahead


def ring_place(device, chips):
    z, y = device >> 2, (device >> 1) & 1
    return jnp.where(y == 0, z, chips - 1 - z)


def gather_place(device, me, count):
    chips = count // 2
    depth = chips // 2
    back = (1 - 2 * (me & 1)) * (ring_place(me, chips) - ring_place(device, chips))
    back = (back + chips) & (chips - 1)
    other = (device ^ me) & 1
    here = (back < depth) & (back > 0) | (back == 0) & (other == 1) | (back == depth) & (other == 0)
    return jnp.where(here, jnp.where(back == 0, 0, 2 * back - 1 + other), chips)


def scatter_place(device, me, count):
    chips = count // 2
    depth = chips // 2
    ahead = (ring_place(device, chips) - ring_place(me, chips) + chips) & (chips - 1)
    core = device & 1
    handler = jnp.where((ahead & (depth - 1)) == 0, core, (ahead > depth).astype(jnp.int32))
    steps = jnp.where(handler == 0, ahead, (chips - ahead) & (chips - 1))
    place = jnp.where(
        steps == depth,
        0,
        jnp.where(steps == 0, chips - 1, 2 * (depth - steps) - (core ^ handler)),
    )
    return place + jnp.where(handler == (me & 1), 0, chips)


def stationary(
    rhs,
    near_blocks,
    near_owner,
    near_slot,
    near_offset,
    far_coupling,
    far_slot,
    far_dev,
    far_cslot,
    basis_out,
    basis_in,
):
    clusters, directions, unknowns = rhs.shape
    rank_k = basis_in.shape[1]
    count = lax.axis_size("blk")
    chips = count // 2
    depth = chips // 2
    me = lax.axis_index("blk")
    stored = near_blocks.shape[0]
    pairs = far_slot.shape[0]
    half = clusters // 2
    ahead = ring_pairs(count)
    mate = [(i, i ^ 1) for i in range(count)]
    side = [(i, i ^ 2) for i in range(count)]

    def move(values, where):
        return lax.ppermute(values, "blk", where)

    def after(values, *others):
        return lax.optimization_barrier((values, *others))[0]

    here = me.astype(jnp.int32).reshape(1)
    base = clusters * directions
    payload, lists = pl.pallas_call(
        functools.partial(prologue_kernel, count),
        out_shape=[
            jax.ShapeDtypeStruct((base + half * rank_k, unknowns), jnp.bfloat16),
            jax.ShapeDtypeStruct((8, stored), jnp.int32),
        ],
        in_specs=[whole(pltpu.SMEM)] + [whole()] * 5,
        out_specs=[whole()] * 2,
        compiler_params=pltpu.CompilerParams(vmem_limit_bytes=PROLOGUE_VMEM),
        name="prologue",
    )(
        here,
        near_owner.reshape(1, stored),
        near_slot.reshape(1, stored),
        near_offset.reshape(1, stored),
        rhs,
        basis_in,
    )
    shards = [move(payload, mate)]
    flow = [move(payload, ahead), move(shards[0], ahead)]
    mate_blocks = move(after(near_blocks, shards[0]), mate)
    lists = jnp.concatenate([lists, move(lists, mate)], axis=0)
    couple = after(jnp.transpose(far_coupling, (2, 1, 0)), payload)
    for k in range(1, chips):
        x = 1 - k % 2
        if k == 3:
            flow[x], mate_blocks, shards[0], lists, couple = lax.optimization_barrier(
                (flow[x], mate_blocks, shards[0], lists, couple)
            )
        shards.append(flow[x])
        if k < chips - 2:
            flow[x] = move(flow[x], ahead)

    quarter = chips // 2

    def near(late, lists):
        pieces = [1] * quarter
        kept, *sends = pl.pallas_call(
            functools.partial(near_kernel, late, BATCH, LAG, chips, len(pieces)),
            out_shape=[
                jax.ShapeDtypeStruct((quarter * clusters, directions, unknowns), jnp.float32)
            ]
            + [
                jax.ShapeDtypeStruct((part * clusters, directions, unknowns), jnp.bfloat16)
                for part in pieces
            ]
            + [jax.ShapeDtypeStruct((chips * half * rank_k, unknowns), jnp.bfloat16)] * (1 - late),
            in_specs=[whole(pltpu.SMEM)] + [whole(pl.ANY)] * (chips + 2),
            out_specs=[whole()] * (2 + len(pieces) - late),
            scratch_shapes=[
                pltpu.VMEM((chips * base, unknowns), jnp.bfloat16),
                pltpu.VMEM((2, *near_blocks.shape), jnp.bfloat16),
                pltpu.VMEM((2 * quarter * clusters + 1, directions, unknowns), jnp.float32),
                pltpu.SemaphoreType.DMA((chips,)),
                pltpu.SemaphoreType.DMA((chips,)),
                pltpu.SemaphoreType.DMA((2 * CHUNKS,)),
            ],
            compiler_params=pltpu.CompilerParams(vmem_limit_bytes=NEAR_VMEM),
            cost_estimate=pl.CostEstimate(
                flops=16 * stored * directions * unknowns * unknowns,
                bytes_accessed=16 << 20,
                transcendentals=0,
            ),
            name="near",
        )(lists, *shards, near_blocks, mate_blocks)
        return kept, sends

    def far_field(couple):
        return pl.pallas_call(
            far_kernel,
            out_shape=jax.ShapeDtypeStruct((clusters, directions, unknowns), jnp.float32),
            in_specs=[whole()] * 2 + [whole(pltpu.SMEM)] + [whole()] * 5,
            out_specs=whole(),
            compiler_params=pltpu.CompilerParams(vmem_limit_bytes=FAR_VMEM),
            cost_estimate=pl.CostEstimate(
                flops=4 * clusters * rank_k * pairs * rank_k * unknowns,
                bytes_accessed=8 << 20,
                transcendentals=0,
            ),
            name="far",
        )(
            *coefs,
            here,
            couple,
            far_slot.reshape(1, pairs),
            far_dev.reshape(1, pairs),
            far_cslot.reshape(1, pairs),
            basis_out,
        )

    early, (*sends, coef) = near(0, lists)
    mates = [move(sends[0], mate), move(sends[1], mate)]
    coefs = [coef, move(coef, mate)]
    kept = [early]

    def term(k):
        at = k % quarter * clusters
        return kept[k // quarter][at : at + clusters] + mates[k].astype(jnp.float32)

    def tied(values, k, *others):
        values, mates[k + 1], *others = lax.optimization_barrier((values, mates[k + 1], *others))
        return values

    def add(flow, k):
        return (flow.astype(jnp.float32) + term(k)).astype(jnp.bfloat16)

    flow = lax.optimization_barrier([term(0).astype(jnp.bfloat16), term(1).astype(jnp.bfloat16)])
    lists = after(lists, *flow)
    mates += [move(after(send, *flow), mate) for send in sends[2:]]
    flow = [move(part, ahead) for part in flow]
    late, sends = near(1, lists)
    kept.append(late)
    mates += [move(send, mate) for send in sends]
    for k in range(2, chips - 1):
        x = k % 2
        flow[x] = tied(add(flow[x], k), k)
        if k == chips - 2:
            couple = after(couple, flow[x])
        flow[x] = move(flow[x], ahead)
    flow[1] = move(flow[1], mate)
    total = far_field(couple) + term(chips - 1) + flow[0].astype(jnp.float32)
    total = lax.optimization_barrier(total)
    return (total + flow[1].astype(jnp.float32)).astype(jnp.bfloat16)


def on_device(*args):
    rhs, near_blocks = args[0], args[1]
    clusters, directions, unknowns = rhs.shape
    small = lax.axis_size("blk") == 16 and clusters == 16
    if small and near_blocks.shape[0] == unknowns and 2 * directions == unknowns:
        return stationary(*args)
    return routed(*args)


def solution(mesh):
    placed = (
        P(("groups", "blk"), None, None),
        P(("groups", "blk"), None, None),
        P(("groups", "blk"), None),
        P(("groups", "blk")),
        P(("groups", "blk")),
        P(("groups", "blk"), None, None),
        P(("groups", "blk")),
        P(("groups", "blk"), None),
        P(("groups", "blk")),
        P(("groups", "blk"), None, None),
        P(("groups", "blk"), None, None),
    )
    return jax.shard_map(
        on_device,
        mesh=mesh,
        in_specs=placed,
        out_specs=P(("groups", "blk"), None, None),
        check_vma=False,
    )
```

```python
import functools

import jax
import jax.numpy as jnp
from jax import lax
from jax.experimental import pallas as pl
from jax.experimental.pallas import tpu as pltpu
from jax.sharding import PartitionSpec as P

BATCH = 16
LAG = 4
PROLOGUE_VMEM = 58 << 20
NEAR_VMEM = 48 << 20
FAR_VMEM = 16 << 20


def with_halo(cells, sides, width):
    for axis, dim in sides:
        count = lax.axis_size(axis)
        head = lax.slice_in_dim(cells, 0, width, axis=dim)
        tail = lax.slice_in_dim(cells, cells.shape[dim] - width, cells.shape[dim], axis=dim)
        cells = jnp.concatenate(
            [
                lax.ppermute(tail, axis, [(i, (i + 1) % count) for i in range(count)]),
                cells,
                lax.ppermute(head, axis, [((i + 1) % count, i) for i in range(count)]),
            ],
            axis=dim,
        )
    return cells


def place_ranks(targets, count):
    onehot = (targets[:, None] == jnp.arange(count, dtype=jnp.int32)[None, :]).astype(jnp.int32)
    before = jnp.cumsum(onehot, axis=0) - onehot
    return jnp.sum(before * onehot, axis=1)


def routed(
    rhs,
    near_blocks,
    near_owner,
    near_slot,
    near_offset,
    far_coupling,
    far_slot,
    far_dev,
    far_cslot,
    basis_out,
    basis_in,
):
    clusters = rhs.shape[0]
    directions = rhs.shape[1]
    unknowns = rhs.shape[2]
    cycle_size = lax.axis_size("blk")
    stored = near_blocks.shape[0]
    capacity = max(2, 2 * stored // cycle_size)
    owners = near_owner[:, 0]
    target = owners * capacity + place_ranks(owners, cycle_size)
    outbox = (
        jnp.zeros((cycle_size * capacity, unknowns, unknowns), near_blocks.dtype)
        .at[target]
        .set(near_blocks)
    )
    labels = (
        jnp.zeros((cycle_size * capacity, 2), jnp.int32)
        .at[target]
        .set(jnp.stack([near_slot, near_offset], axis=1))
    )
    window = with_halo(rhs, (("blk", 0),), clusters)
    inbox, in_labels = (
        lax.all_to_all(outbox, "blk", split_axis=0, concat_axis=0, tiled=True),
        lax.all_to_all(labels, "blk", split_axis=0, concat_axis=0, tiled=True),
    )
    position = clusters + in_labels[:, 0] + in_labels[:, 1]
    columns = jnp.take(window, position, axis=0)
    products = jnp.einsum("srj,sij->sri", columns, inbox, preferred_element_type=jnp.float32)
    selector = (in_labels[:, 0][None, :] == jnp.arange(clusters, dtype=jnp.int32)[:, None]).astype(
        jnp.float32
    )
    near_sum = jnp.dot(
        selector,
        products.reshape(products.shape[0], -1),
        precision=lax.Precision.HIGHEST,
        preferred_element_type=jnp.float32,
    ).reshape(clusters, directions, unknowns)
    coef_local = jnp.einsum(
        "ckj,crj->crk", basis_in, rhs, preferred_element_type=jnp.float32
    ).astype(jnp.bfloat16)
    rank_k = basis_in.shape[1]
    coef_local = coef_local.reshape(clusters, directions * rank_k)
    pairs = far_slot.shape[0]
    wanted = far_dev[:, 0] * clusters + far_cslot
    piece = lax.all_gather(coef_local, "blk", axis=0, tiled=True)
    chosen = jnp.take(piece, wanted, axis=0)
    coupled = jnp.einsum(
        "pkq,prq->prk",
        far_coupling,
        chosen.reshape(pairs, directions, rank_k),
        preferred_element_type=jnp.float32,
    )
    row_pick = (far_slot[None, :] == jnp.arange(clusters, dtype=jnp.int32)[:, None]).astype(
        jnp.float32
    )
    gathered = jnp.dot(
        row_pick,
        coupled.reshape(pairs, -1),
        precision=lax.Precision.HIGHEST,
        preferred_element_type=jnp.float32,
    )
    gathered = gathered.astype(jnp.bfloat16).reshape(clusters, directions, rank_k)
    far_sum = jnp.einsum("crk,ckb->crb", gathered, basis_out, preferred_element_type=jnp.float32)
    return (near_sum + far_sum).astype(jnp.bfloat16)


def whole(space=pltpu.VMEM):
    return pl.BlockSpec(memory_space=space)


def prologue_kernel(
    count, me_ref, owner_ref, slot_ref, offset_ref, rhs_ref, basis_ref, payload_ref, list_ref
):
    clusters, directions, unknowns = rhs_ref.shape
    base = clusters * directions
    payload_ref[0:base, :] = rhs_ref[...].reshape(base, unknowns)
    rank_k = basis_ref.shape[1]
    half = clusters // 2
    rows = []
    for c in range(half):
        parts = [
            lax.dot_general(
                basis_ref[e],
                rhs_ref[e],
                (((1,), (1,)), ((), ())),
                preferred_element_type=jnp.float32,
            )
            for e in (c, c + half)
        ]
        rows.append(jnp.concatenate(parts, axis=1))
    payload_ref[base:, :] = jnp.concatenate(
        [row[q : q + 1] for q in range(rank_k) for row in rows], axis=0
    ).astype(payload_ref.dtype)

    me, owner, slot = me_ref[0], owner_ref[...], slot_ref[...]
    stored = owner.shape[1]
    place = scatter_place(owner, me, count)
    quarter = count // 4
    late = (place // quarter) & 1
    place = (place // (2 * quarter) * quarter + (place & (quarter - 1))) * clusters + slot
    column = (owner * clusters + slot + offset_ref[...]) & (count * clusters - 1)
    shard = gather_place(column // clusters, me, count)
    theirs = (shard == count // 2).astype(jnp.int32)
    shard = jnp.where(theirs == 1, gather_place(column // clusters, me ^ 1, count), shard)
    column_place = shard * clusters + (column & (clusters - 1))
    square = (stored, stored)
    group = jnp.broadcast_to((2 * theirs + late).astype(jnp.float32), square)
    group_of_row = jnp.transpose(group)
    row_at = lax.broadcasted_iota(jnp.int32, square, 0)
    lane_at = lax.broadcasted_iota(jnp.int32, square, 1)
    lane = lane_at.astype(jnp.float32)
    before = (group_of_row < group) | ((group_of_row == group) & (row_at < lane_at))
    rank = jnp.sum(jnp.where(before, 1.0, 0.0), axis=0, keepdims=True)
    rank = jnp.transpose(jnp.broadcast_to(rank, square))
    here = jnp.where(rank == lane, 1.0, 0.0).astype(jnp.bfloat16)
    starts = jnp.sum(jnp.where(group_of_row < lane, 1.0, 0.0), axis=0, keepdims=True)
    values = jnp.concatenate(
        [lane[0:1], place.astype(jnp.float32), column_place.astype(jnp.float32)]
        + [jnp.zeros((5, stored), jnp.float32)],
        axis=0,
    )
    values = jnp.dot(values.astype(jnp.bfloat16), here, preferred_element_type=jnp.float32)
    values = jnp.concatenate([values[0:3], starts, values[4:8]], axis=0)
    list_ref[...] = values.astype(jnp.int32)


def near_kernel(late, batch, lag, shards, sends, list_ref, *refs):
    shard_refs, (own_hbm, mate_hbm, keep_ref) = refs[:shards], refs[shards : shards + 3]
    send_refs, refs = refs[shards + 3 : shards + 3 + sends], refs[shards + 3 + sends :]
    if not late:
        coef_ref, refs = refs[0], refs[1:]
    columns, blocks, sums, column_sem, coef_sem, block_sem = refs
    directions = sums.shape[1]
    span = columns.shape[0] // shards
    dummy = sums.shape[0] - 1

    copies = [
        pltpu.make_async_copy(
            ref.at[pl.ds(0, span)], columns.at[pl.ds(k * span, span)], column_sem.at[k]
        )
        for k, ref in enumerate(shard_refs)
    ]
    for copy in copies:
        copy.start()
    tails = []
    if not late:
        tail = coef_ref.shape[0] // shards
        tails = [
            pltpu.make_async_copy(
                ref.at[pl.ds(span, tail)], coef_ref.at[pl.ds(k * tail, tail)], coef_sem.at[k]
            )
            for k, ref in enumerate(shard_refs)
        ]
    for copy in tails:
        copy.start()

    begin, begin_there = list_ref[3, late], list_ref[11, 2 + late]
    here = list_ref[3, late + 1] - begin
    total = here + list_ref[11, 3 + late] - begin_there

    def entry(j):
        j = jnp.minimum(j, total - 1)
        half = (j >= here).astype(jnp.int32)
        return half, half * 8, j + jnp.where(half == 1, begin_there - here, begin)

    def fetch(j, carry):
        half, row, at = entry(j)

        for side, source in enumerate((own_hbm, mate_hbm)):

            @pl.when(half == side)
            def _():
                pltpu.make_async_copy(
                    source.at[list_ref[row, at]], blocks.at[j], block_sem.at[j // batch]
                ).start()

        return carry

    steps = (total + batch - 1) // batch
    lax.fori_loop(0, steps * batch, fetch, 0)

    def clear(i, carry):
        sums[i] = jnp.zeros(sums.shape[1:], sums.dtype)
        return carry

    lax.fori_loop(0, dummy, clear, 0)
    for copy in copies:
        copy.wait()

    def body(step, carry):
        first = step * batch
        here_blocks = pl.ds(first, batch)
        pltpu.make_async_copy(
            own_hbm.at[pl.ds(0, batch)], blocks.at[here_blocks], block_sem.at[step]
        ).wait()
        products = []

        def add(i):
            half, row, at = entry(first + i)
            place = list_ref[row + 1, at] ^ (half * (dummy // 2))
            place = jnp.where(first + i < total, place, dummy)
            sums[place] = sums[place] + products[i]

        for i in range(batch):
            half, row, at = entry(first + i)
            start = pl.multiple_of(list_ref[row + 2, at] * directions, directions)
            products.append(
                lax.dot_general(
                    columns[pl.ds(start, directions)],
                    blocks[first + i],
                    (((1,), (1,)), ((), ())),
                    preferred_element_type=jnp.float32,
                )
            )
            if i >= lag:
                add(i - lag)
        for i in range(batch - lag, batch):
            add(i)
        return carry

    lax.fori_loop(0, steps, body, 0)

    def keep(i, carry):
        keep_ref[i] = sums[i]
        return carry

    lax.fori_loop(0, dummy // 2, keep, 0, unroll=2)
    at = dummy // 2
    for send_ref in send_refs:

        def pack(i, carry, at=at, send_ref=send_ref):
            send_ref[i] = sums[at + i].astype(send_ref.dtype)
            return carry

        lax.fori_loop(0, send_ref.shape[0], pack, 0, unroll=2)
        at += send_ref.shape[0]
    for copy in tails:
        copy.wait()


def far_kernel(*refs):
    coef_refs = refs[:2]
    me_ref, couple_ref, slot_ref, dev_ref, cslot_ref, basis_ref, out_ref = refs[2:]
    clusters, rank_k, unknowns = basis_ref.shape
    pairs = couple_ref.shape[2]
    directions = out_ref.shape[1]
    half = clusters // 2
    coef = jnp.concatenate([ref[...].astype(jnp.float32) for ref in coef_refs], axis=0)
    coef = coef.reshape(-1, rank_k, half, unknowns)
    count = coef.shape[0]
    hot = (
        lax.broadcasted_iota(jnp.int32, (clusters, pairs), 0)
        == jnp.broadcast_to(slot_ref[...], (clusters, pairs))
    ).astype(jnp.float32).astype(jnp.bfloat16)
    away = gather_place(dev_ref[...], me_ref[0], count)
    theirs = count // 2 + gather_place(dev_ref[...], me_ref[0] ^ 1, count)
    away = jnp.where(away == count // 2, theirs, away)
    cslot = cslot_ref[...]
    high = (cslot >= half).astype(jnp.int32)
    at = away * half + cslot - high * half
    table_rows = (count * half, pairs)
    pick = jnp.where(
        lax.broadcasted_iota(jnp.int32, table_rows, 0) == jnp.broadcast_to(at, table_rows), 1.0, 0.0
    )
    pick = jnp.transpose(pick).astype(jnp.bfloat16)
    lanes = (unknowns, pairs)
    keep = jnp.where(
        lax.broadcasted_iota(jnp.int32, lanes, 0) // directions == jnp.broadcast_to(high, lanes),
        1.0,
        0.0,
    )
    keep = jnp.transpose(keep).astype(jnp.bfloat16)
    total = jnp.zeros((clusters * rank_k, unknowns), jnp.float32)
    for q in range(rank_k):
        table = coef[:, q].reshape(count * half, unknowns).astype(jnp.bfloat16)
        chosen = jnp.dot(pick, table, preferred_element_type=jnp.float32).astype(jnp.bfloat16)
        chosen = chosen * keep
        couple = couple_ref[q]
        weight = jnp.concatenate([couple * hot[s : s + 1] for s in range(clusters)], axis=0)
        total = total + jnp.dot(weight, chosen, preferred_element_type=jnp.float32)
    total = total + pltpu.roll(total, unknowns // 2, axis=1)
    gathered = jnp.transpose(total)[0:directions, :].astype(jnp.bfloat16).astype(jnp.float32)
    lane = lax.broadcasted_iota(jnp.int32, gathered.shape, 1) // rank_k
    basis = basis_ref[...].reshape(clusters * rank_k, unknowns)
    for s in range(clusters):
        own = jnp.where(lane == s, gathered, 0.0).astype(jnp.bfloat16)
        out_ref[s] = jnp.dot(own, basis, preferred_element_type=jnp.float32)


def ring_device(place, core, chips):
    depth = chips // 2
    place = place % chips
    z, y = (place, 0) if place < depth else (chips - 1 - place, 1)
    return (z * 2 + y) * 2 + core


def ring_pairs(count):
    chips = count // 2
    cores = [(p, c) for p in range(chips) for c in range(2)]
    ahead = [(ring_device(p, c, chips), ring_device(p + 1 - 2 * c, c, chips)) for p, c in cores]
    cross = [
        (ring_device(p, c, chips), ring_device(p - 1 + 2 * c, 1 - c, chips)) for p, c in cores
    ]
    return ahead, cross


def ring_place(device, chips):
    z, y = device >> 2, (device >> 1) & 1
    return jnp.where(y == 0, z, chips - 1 - z)


def gather_place(device, me, count):
    chips = count // 2
    depth = chips // 2
    back = (1 - 2 * (me & 1)) * (ring_place(me, chips) - ring_place(device, chips))
    back = (back + chips) & (chips - 1)
    other = (device ^ me) & 1
    here = (back < depth) & (back > 0) | (back == 0) & (other == 1) | (back == depth) & (other == 0)
    return jnp.where(here, jnp.where(back == 0, 0, 2 * back - 1 + other), chips)


def scatter_place(device, me, count):
    chips = count // 2
    depth = chips // 2
    ahead = (ring_place(device, chips) - ring_place(me, chips) + chips) & (chips - 1)
    core = device & 1
    handler = jnp.where((ahead & (depth - 1)) == 0, core, (ahead > depth).astype(jnp.int32))
    steps = jnp.where(handler == 0, ahead, (chips - ahead) & (chips - 1))
    place = jnp.where(
        steps == depth,
        0,
        jnp.where(steps == 0, chips - 1, 2 * (depth - steps) - (core ^ handler)),
    )
    return place + jnp.where(handler == (me & 1), 0, chips)


def stationary(
    rhs,
    near_blocks,
    near_owner,
    near_slot,
    near_offset,
    far_coupling,
    far_slot,
    far_dev,
    far_cslot,
    basis_out,
    basis_in,
):
    clusters, directions, unknowns = rhs.shape
    rank_k = basis_in.shape[1]
    count = lax.axis_size("blk")
    chips = count // 2
    depth = chips // 2
    me = lax.axis_index("blk")
    stored = near_blocks.shape[0]
    pairs = far_slot.shape[0]
    half = clusters // 2
    ahead, cross = ring_pairs(count)
    mate = [(i, i ^ 1) for i in range(count)]
    side = [(i, i ^ 2) for i in range(count)]

    def move(values, where):
        return lax.ppermute(values, "blk", where)

    def after(values, *others):
        return lax.optimization_barrier((values, *others))[0]

    here = me.astype(jnp.int32).reshape(1)
    base = clusters * directions
    payload, lists = pl.pallas_call(
        functools.partial(prologue_kernel, count),
        out_shape=[
            jax.ShapeDtypeStruct((base + half * rank_k, unknowns), jnp.bfloat16),
            jax.ShapeDtypeStruct((8, stored), jnp.int32),
        ],
        in_specs=[whole(pltpu.SMEM)] + [whole()] * 5,
        out_specs=[whole()] * 2,
        compiler_params=pltpu.CompilerParams(vmem_limit_bytes=PROLOGUE_VMEM),
        name="prologue",
    )(
        here,
        near_owner.reshape(1, stored),
        near_slot.reshape(1, stored),
        near_offset.reshape(1, stored),
        rhs,
        basis_in,
    )
    flow = [move(payload, ahead)]
    mate_blocks = move(near_blocks, mate)
    lists = jnp.concatenate([lists, move(lists, mate)], axis=0)
    couple = jnp.transpose(far_coupling, (2, 1, 0))
    flow.append(move(after(payload, couple), cross))
    shards = [move(payload, mate)]
    for k in range(1, chips):
        x = 1 - k % 2
        if k == 3:
            flow[x], mate_blocks, shards[0], lists = lax.optimization_barrier(
                (flow[x], mate_blocks, shards[0], lists)
            )
        shards.append(flow[x])
        if k < chips - 2:
            flow[x] = move(flow[x], ahead)

    quarter = chips // 2

    def near(late, lists):
        pieces = [1] * quarter
        kept, *sends = pl.pallas_call(
            functools.partial(near_kernel, late, BATCH, LAG, chips, len(pieces)),
            out_shape=[
                jax.ShapeDtypeStruct((quarter * clusters, directions, unknowns), jnp.float32)
            ]
            + [
                jax.ShapeDtypeStruct((part * clusters, directions, unknowns), jnp.bfloat16)
                for part in pieces
            ]
            + [jax.ShapeDtypeStruct((chips * half * rank_k, unknowns), jnp.bfloat16)] * (1 - late),
            in_specs=[whole(pltpu.SMEM)] + [whole(pl.ANY)] * (chips + 2),
            out_specs=[whole()] * (2 + len(pieces) - late),
            scratch_shapes=[
                pltpu.VMEM((chips * base, unknowns), jnp.bfloat16),
                pltpu.VMEM((2 * stored, unknowns, unknowns), jnp.bfloat16),
                pltpu.VMEM((2 * quarter * clusters + 1, directions, unknowns), jnp.float32),
                pltpu.SemaphoreType.DMA((chips,)),
                pltpu.SemaphoreType.DMA((chips,)),
                pltpu.SemaphoreType.DMA((2 * stored // BATCH,)),
            ],
            compiler_params=pltpu.CompilerParams(vmem_limit_bytes=NEAR_VMEM),
            cost_estimate=pl.CostEstimate(
                flops=16 * stored * directions * unknowns * unknowns,
                bytes_accessed=16 << 20,
                transcendentals=0,
            ),
            name="near",
        )(lists, *shards, near_blocks, mate_blocks)
        return kept, sends

    def far_field(couple):
        return pl.pallas_call(
            far_kernel,
            out_shape=jax.ShapeDtypeStruct((clusters, directions, unknowns), jnp.float32),
            in_specs=[whole()] * 2 + [whole(pltpu.SMEM)] + [whole()] * 5,
            out_specs=whole(),
            compiler_params=pltpu.CompilerParams(vmem_limit_bytes=FAR_VMEM),
            cost_estimate=pl.CostEstimate(
                flops=4 * clusters * rank_k * pairs * rank_k * unknowns,
                bytes_accessed=8 << 20,
                transcendentals=0,
            ),
            name="far",
        )(
            *coefs,
            here,
            couple,
            far_slot.reshape(1, pairs),
            far_dev.reshape(1, pairs),
            far_cslot.reshape(1, pairs),
            basis_out,
        )

    early, (*sends, coef) = near(0, lists)
    mates = [move(sends[0], mate), move(sends[1], mate)]
    coefs = [coef, move(coef, mate)]
    kept = [early]

    def term(k):
        at = k % quarter * clusters
        return kept[k // quarter][at : at + clusters] + mates[k].astype(jnp.float32)

    def tied(values, k, *others):
        values, mates[k + 1], *others = lax.optimization_barrier((values, mates[k + 1], *others))
        return values

    def add(flow, k):
        return (flow.astype(jnp.float32) + term(k)).astype(jnp.bfloat16)

    flow = lax.optimization_barrier([term(0).astype(jnp.bfloat16), term(1).astype(jnp.bfloat16)])
    lists = after(lists, *flow)
    mates += [move(after(send, *flow), mate) for send in sends[2:]]
    flow = [move(part, ahead) for part in flow]
    late, sends = near(1, lists)
    kept.append(late)
    mates += [move(send, mate) for send in sends]
    for k in range(2, chips - 1):
        x = k % 2
        flow[x] = tied(add(flow[x], k), k)
        if k == chips - 2:
            couple = after(couple, flow[x])
        flow[x] = move(flow[x], ahead)
    flow[1] = move(flow[1], mate)
    total = far_field(couple) + term(chips - 1) + flow[0].astype(jnp.float32)
    total = lax.optimization_barrier(total)
    return (total + flow[1].astype(jnp.float32)).astype(jnp.bfloat16)


def on_device(*args):
    rhs, near_blocks = args[0], args[1]
    clusters, directions, unknowns = rhs.shape
    small = lax.axis_size("blk") == 16 and clusters == 16
    if small and near_blocks.shape[0] == unknowns and 2 * directions == unknowns:
        return stationary(*args)
    return routed(*args)


def solution(mesh):
    placed = (
        P(("groups", "blk"), None, None),
        P(("groups", "blk"), None, None),
        P(("groups", "blk"), None),
        P(("groups", "blk")),
        P(("groups", "blk")),
        P(("groups", "blk"), None, None),
        P(("groups", "blk")),
        P(("groups", "blk"), None),
        P(("groups", "blk")),
        P(("groups", "blk"), None, None),
        P(("groups", "blk"), None, None),
    )
    return jax.shard_map(
        on_device,
        mesh=mesh,
        in_specs=placed,
        out_specs=P(("groups", "blk"), None, None),
        check_vma=False,
    )
```

```python
import functools

import jax
import jax.numpy as jnp
from jax import lax
from jax.experimental import pallas as pl
from jax.experimental.pallas import tpu as pltpu
from jax.sharding import PartitionSpec as P

BATCH = 16
LAG = 4
PROLOGUE_VMEM = 58 << 20
NEAR_VMEM = 48 << 20
FAR_VMEM = 16 << 20


def with_halo(cells, sides, width):
    for axis, dim in sides:
        count = lax.axis_size(axis)
        head = lax.slice_in_dim(cells, 0, width, axis=dim)
        tail = lax.slice_in_dim(cells, cells.shape[dim] - width, cells.shape[dim], axis=dim)
        cells = jnp.concatenate(
            [
                lax.ppermute(tail, axis, [(i, (i + 1) % count) for i in range(count)]),
                cells,
                lax.ppermute(head, axis, [((i + 1) % count, i) for i in range(count)]),
            ],
            axis=dim,
        )
    return cells


def place_ranks(targets, count):
    onehot = (targets[:, None] == jnp.arange(count, dtype=jnp.int32)[None, :]).astype(jnp.int32)
    before = jnp.cumsum(onehot, axis=0) - onehot
    return jnp.sum(before * onehot, axis=1)


def routed(
    rhs,
    near_blocks,
    near_owner,
    near_slot,
    near_offset,
    far_coupling,
    far_slot,
    far_dev,
    far_cslot,
    basis_out,
    basis_in,
):
    clusters = rhs.shape[0]
    directions = rhs.shape[1]
    unknowns = rhs.shape[2]
    cycle_size = lax.axis_size("blk")
    stored = near_blocks.shape[0]
    capacity = max(2, 2 * stored // cycle_size)
    owners = near_owner[:, 0]
    target = owners * capacity + place_ranks(owners, cycle_size)
    outbox = (
        jnp.zeros((cycle_size * capacity, unknowns, unknowns), near_blocks.dtype)
        .at[target]
        .set(near_blocks)
    )
    labels = (
        jnp.zeros((cycle_size * capacity, 2), jnp.int32)
        .at[target]
        .set(jnp.stack([near_slot, near_offset], axis=1))
    )
    window = with_halo(rhs, (("blk", 0),), clusters)
    inbox, in_labels = (
        lax.all_to_all(outbox, "blk", split_axis=0, concat_axis=0, tiled=True),
        lax.all_to_all(labels, "blk", split_axis=0, concat_axis=0, tiled=True),
    )
    position = clusters + in_labels[:, 0] + in_labels[:, 1]
    columns = jnp.take(window, position, axis=0)
    products = jnp.einsum("srj,sij->sri", columns, inbox, preferred_element_type=jnp.float32)
    selector = (in_labels[:, 0][None, :] == jnp.arange(clusters, dtype=jnp.int32)[:, None]).astype(
        jnp.float32
    )
    near_sum = jnp.dot(
        selector,
        products.reshape(products.shape[0], -1),
        precision=lax.Precision.HIGHEST,
        preferred_element_type=jnp.float32,
    ).reshape(clusters, directions, unknowns)
    coef_local = jnp.einsum(
        "ckj,crj->crk", basis_in, rhs, preferred_element_type=jnp.float32
    ).astype(jnp.bfloat16)
    rank_k = basis_in.shape[1]
    coef_local = coef_local.reshape(clusters, directions * rank_k)
    pairs = far_slot.shape[0]
    wanted = far_dev[:, 0] * clusters + far_cslot
    piece = lax.all_gather(coef_local, "blk", axis=0, tiled=True)
    chosen = jnp.take(piece, wanted, axis=0)
    coupled = jnp.einsum(
        "pkq,prq->prk",
        far_coupling,
        chosen.reshape(pairs, directions, rank_k),
        preferred_element_type=jnp.float32,
    )
    row_pick = (far_slot[None, :] == jnp.arange(clusters, dtype=jnp.int32)[:, None]).astype(
        jnp.float32
    )
    gathered = jnp.dot(
        row_pick,
        coupled.reshape(pairs, -1),
        precision=lax.Precision.HIGHEST,
        preferred_element_type=jnp.float32,
    )
    gathered = gathered.astype(jnp.bfloat16).reshape(clusters, directions, rank_k)
    far_sum = jnp.einsum("crk,ckb->crb", gathered, basis_out, preferred_element_type=jnp.float32)
    return (near_sum + far_sum).astype(jnp.bfloat16)


def whole(space=pltpu.VMEM):
    return pl.BlockSpec(memory_space=space)


def prologue_kernel(
    count, me_ref, owner_ref, slot_ref, offset_ref, rhs_ref, basis_ref, payload_ref, list_ref
):
    clusters, directions, unknowns = rhs_ref.shape
    rank_k = basis_ref.shape[1]
    half = clusters // 2
    base = clusters * directions
    rows = []
    for c in range(half):
        pair = jnp.concatenate([rhs_ref[c], rhs_ref[c + half]], axis=0).astype(jnp.float32)
        tile = jnp.transpose(pair).astype(payload_ref.dtype)
        payload_ref[c * unknowns : (c + 1) * unknowns, :] = tile
        parts = [
            jnp.dot(basis_ref[e], tile, preferred_element_type=jnp.float32) for e in (c, c + half)
        ]
        lane = lax.broadcasted_iota(jnp.int32, parts[0].shape, 1)
        rows.append(jnp.where(lane < directions, *parts))
    payload_ref[base:, :] = jnp.concatenate(
        [row[q : q + 1] for q in range(rank_k) for row in rows], axis=0
    ).astype(payload_ref.dtype)

    me, owner, slot = me_ref[0], owner_ref[...], slot_ref[...]
    stored = owner.shape[1]
    place = scatter_place(owner, me, count)
    quarter = count // 4
    late = (place // quarter) & 1
    place = (place // (2 * quarter) * quarter + (place & (quarter - 1))) * clusters + slot
    column = (owner * clusters + slot + offset_ref[...]) & (count * clusters - 1)
    shard = gather_place(column // clusters, me, count)
    theirs = (shard == count // 2).astype(jnp.int32)
    shard = jnp.where(theirs == 1, gather_place(column // clusters, me ^ 1, count), shard)
    column_place = shard * clusters + (column & (clusters - 1))
    square = (stored, stored)
    group = jnp.broadcast_to((2 * theirs + late).astype(jnp.float32), square)
    group_of_row = jnp.transpose(group)
    row_at = lax.broadcasted_iota(jnp.int32, square, 0)
    lane_at = lax.broadcasted_iota(jnp.int32, square, 1)
    lane = lane_at.astype(jnp.float32)
    before = (group_of_row < group) | ((group_of_row == group) & (row_at < lane_at))
    rank = jnp.sum(jnp.where(before, 1.0, 0.0), axis=0, keepdims=True)
    rank = jnp.transpose(jnp.broadcast_to(rank, square))
    here = jnp.where(rank == lane, 1.0, 0.0).astype(jnp.bfloat16)
    starts = jnp.sum(jnp.where(group_of_row < lane, 1.0, 0.0), axis=0, keepdims=True)
    values = jnp.concatenate(
        [lane[0:1], place.astype(jnp.float32), column_place.astype(jnp.float32)]
        + [jnp.zeros((5, stored), jnp.float32)],
        axis=0,
    )
    values = jnp.dot(values.astype(jnp.bfloat16), here, preferred_element_type=jnp.float32)
    values = jnp.concatenate([values[0:3], starts, values[4:8]], axis=0)
    list_ref[...] = values.astype(jnp.int32)


def near_kernel(late, batch, lag, shards, kept, sends, list_ref, *refs):
    shard_refs, (own_hbm, mate_hbm), refs = refs[:shards], refs[shards : shards + 2], refs[shards + 2 :]
    keep_refs, send_refs, refs = refs[:kept], refs[kept : kept + sends], refs[kept + sends :]
    if not late:
        coef_ref, refs = refs[0], refs[1:]
    columns, blocks, sums, entries, column_sem, coef_sem, block_sem = refs
    unknowns, width = sums.shape[1:]
    span = columns.shape[0] // shards
    dummy = sums.shape[0] - 1
    pairs = span // unknowns

    copies = [
        pltpu.make_async_copy(
            ref.at[pl.ds(0, span)], columns.at[pl.ds(k * span, span)], column_sem.at[k]
        )
        for k, ref in enumerate(shard_refs)
    ]
    for copy in copies:
        copy.start()
    tails = []
    if not late:
        tail = coef_ref.shape[0] // shards
        tails = [
            pltpu.make_async_copy(
                ref.at[pl.ds(span, tail)], coef_ref.at[pl.ds(k * tail, tail)], coef_sem.at[k]
            )
            for k, ref in enumerate(shard_refs)
        ]

    begin, begin_there = list_ref[3, late], list_ref[11, 2 + late]
    here = list_ref[3, late + 1] - begin
    total = here + list_ref[11, 3 + late] - begin_there
    steps = (total + batch - 1) // batch

    def fetch(source, row, shift, swap):
        def one(j, carry):
            at = j + shift
            place, column = list_ref[row + 1, at], list_ref[row + 2, at]
            slot, cluster = place & (2 * pairs - 1), column & (2 * pairs - 1)
            entries[0, j] = (((place // (2 * pairs)) * pairs) ^ swap) + (slot & (pairs - 1))
            entries[1, j] = (
                (column // (2 * pairs)) * pairs + (cluster & (pairs - 1))
            ) * unknowns
            entries[2, j] = slot // pairs
            entries[3, j] = ((slot // pairs) ^ (cluster // pairs)) * (width // 2)
            pltpu.make_async_copy(
                source.at[list_ref[row, at]], blocks.at[j], block_sem.at[j // batch]
            ).start()
            return carry

        return one

    def fill(j, carry):
        entries[0, j] = dummy
        entries[1, j] = 0
        entries[2, j] = 0
        entries[3, j] = 0
        pltpu.make_async_copy(own_hbm.at[0], blocks.at[j], block_sem.at[j // batch]).start()
        return carry

    lax.fori_loop(0, here, fetch(own_hbm, 0, begin, 0), 0)
    lax.fori_loop(here, total, fetch(mate_hbm, 8, begin_there - here, dummy // 2), 0)
    lax.fori_loop(total, steps * batch, fill, 0)
    for copy in tails:
        copy.start()

    def clear(i, carry):
        sums[i] = jnp.zeros(sums.shape[1:], sums.dtype)
        return carry

    lax.fori_loop(0, dummy, clear, 0)
    for copy in copies:
        copy.wait()
    lane_half = lax.broadcasted_iota(jnp.int32, (unknowns, width), 1) // (width // 2)

    def body(step, carry):
        first = step * batch
        pltpu.make_async_copy(
            own_hbm.at[pl.ds(0, batch)], blocks.at[pl.ds(first, batch)], block_sem.at[step]
        ).wait()
        products = []

        def add(i):
            product = pltpu.roll(products[i], entries[3, first + i], axis=1)
            place = entries[0, first + i]
            sums[place] = sums[place] + jnp.where(lane_half == entries[2, first + i], product, 0.0)

        for i in range(batch):
            start = pl.multiple_of(entries[1, first + i], unknowns)
            products.append(
                jnp.dot(
                    blocks[first + i],
                    columns[pl.ds(start, unknowns)],
                    preferred_element_type=jnp.float32,
                )
            )
            if i >= lag:
                add(i - lag)
        for i in range(batch - lag, batch):
            add(i)
        return carry

    lax.fori_loop(0, steps, body, 0)
    at = 0
    for out_ref in (*keep_refs, *send_refs):

        def pack(i, carry, at=at, out_ref=out_ref):
            out_ref[i] = sums[at + i].astype(out_ref.dtype)
            return carry

        lax.fori_loop(0, out_ref.shape[0], pack, 0)
        at += out_ref.shape[0]
    for copy in tails:
        copy.wait()


def last_kernel(first_ref, second_ref, rest_ref, out_ref):
    pairs, unknowns, width = first_ref.shape
    for p in range(pairs):
        tile = first_ref[p].astype(jnp.float32) + second_ref[p].astype(jnp.float32)
        tile = jnp.transpose(tile)
        for h in range(2):
            c = h * pairs + p
            part = tile[h * (width // 2) : (h + 1) * (width // 2)]
            out_ref[c] = (part + rest_ref[c]).astype(out_ref.dtype)


def far_kernel(*refs):
    coef_refs = refs[:2]
    me_ref, couple_ref, slot_ref, dev_ref, cslot_ref, basis_ref = refs[2:8]
    own_ref, mate_ref, out_ref = refs[8:]
    clusters, rank_k, unknowns = basis_ref.shape
    pairs = couple_ref.shape[2]
    directions = out_ref.shape[1]
    half = clusters // 2
    coef = jnp.concatenate([ref[...].astype(jnp.float32) for ref in coef_refs], axis=0)
    coef = coef.reshape(-1, rank_k, half, unknowns)
    count = coef.shape[0]
    hot = (
        lax.broadcasted_iota(jnp.int32, (clusters, pairs), 0)
        == jnp.broadcast_to(slot_ref[...], (clusters, pairs))
    ).astype(jnp.float32).astype(jnp.bfloat16)
    away = gather_place(dev_ref[...], me_ref[0], count)
    theirs = count // 2 + gather_place(dev_ref[...], me_ref[0] ^ 1, count)
    away = jnp.where(away == count // 2, theirs, away)
    cslot = cslot_ref[...]
    high = (cslot >= half).astype(jnp.int32)
    at = away * half + cslot - high * half
    table_rows = (count * half, pairs)
    pick = jnp.where(
        lax.broadcasted_iota(jnp.int32, table_rows, 0) == jnp.broadcast_to(at, table_rows), 1.0, 0.0
    )
    pick = jnp.transpose(pick).astype(jnp.bfloat16)
    lanes = (unknowns, pairs)
    keep = jnp.where(
        lax.broadcasted_iota(jnp.int32, lanes, 0) // directions == jnp.broadcast_to(high, lanes),
        1.0,
        0.0,
    )
    keep = jnp.transpose(keep).astype(jnp.bfloat16)
    total = jnp.zeros((clusters * rank_k, unknowns), jnp.float32)
    for q in range(rank_k):
        table = coef[:, q].reshape(count * half, unknowns).astype(jnp.bfloat16)
        chosen = jnp.dot(pick, table, preferred_element_type=jnp.float32).astype(jnp.bfloat16)
        chosen = chosen * keep
        couple = couple_ref[q]
        weight = jnp.concatenate([couple * hot[s : s + 1] for s in range(clusters)], axis=0)
        total = total + jnp.dot(weight, chosen, preferred_element_type=jnp.float32)
    total = total + pltpu.roll(total, unknowns // 2, axis=1)
    gathered = jnp.transpose(total)[0:directions, :].astype(jnp.bfloat16).astype(jnp.float32)
    lane = lax.broadcasted_iota(jnp.int32, gathered.shape, 1) // rank_k
    basis = basis_ref[...].reshape(clusters * rank_k, unknowns)
    for p in range(half):
        near = jnp.transpose(own_ref[p] + mate_ref[p].astype(jnp.float32))
        for h in range(2):
            s = h * half + p
            own = jnp.where(lane == s, gathered, 0.0).astype(jnp.bfloat16)
            out_ref[s] = near[h * directions : (h + 1) * directions] + jnp.dot(
                own, basis, preferred_element_type=jnp.float32
            )


def ring_device(place, core, chips):
    depth = chips // 2
    place = place % chips
    z, y = (place, 0) if place < depth else (chips - 1 - place, 1)
    return (z * 2 + y) * 2 + core


def ring_pairs(count):
    chips = count // 2
    cores = [(p, c) for p in range(chips) for c in range(2)]
    ahead = [(ring_device(p, c, chips), ring_device(p + 1 - 2 * c, c, chips)) for p, c in cores]
    cross = [
        (ring_device(p, c, chips), ring_device(p - 1 + 2 * c, 1 - c, chips)) for p, c in cores
    ]
    return ahead, cross


def ring_place(device, chips):
    z, y = device >> 2, (device >> 1) & 1
    return jnp.where(y == 0, z, chips - 1 - z)


def gather_place(device, me, count):
    chips = count // 2
    depth = chips // 2
    back = (1 - 2 * (me & 1)) * (ring_place(me, chips) - ring_place(device, chips))
    back = (back + chips) & (chips - 1)
    other = (device ^ me) & 1
    here = (back < depth) & (back > 0) | (back == 0) & (other == 1) | (back == depth) & (other == 0)
    return jnp.where(here, jnp.where(back == 0, 0, 2 * back - 1 + other), chips)


def scatter_place(device, me, count):
    chips = count // 2
    depth = chips // 2
    ahead = (ring_place(device, chips) - ring_place(me, chips) + chips) & (chips - 1)
    core = device & 1
    handler = jnp.where((ahead & (depth - 1)) == 0, core, (ahead > depth).astype(jnp.int32))
    steps = jnp.where(handler == 0, ahead, (chips - ahead) & (chips - 1))
    place = jnp.where(
        steps == depth,
        0,
        jnp.where(steps == 0, chips - 1, 2 * (depth - steps) - (core ^ handler)),
    )
    return place + jnp.where(handler == (me & 1), 0, chips)


def stationary(
    rhs,
    near_blocks,
    near_owner,
    near_slot,
    near_offset,
    far_coupling,
    far_slot,
    far_dev,
    far_cslot,
    basis_out,
    basis_in,
):
    clusters, directions, unknowns = rhs.shape
    rank_k = basis_in.shape[1]
    count = lax.axis_size("blk")
    chips = count // 2
    depth = chips // 2
    me = lax.axis_index("blk")
    stored = near_blocks.shape[0]
    pairs = far_slot.shape[0]
    half = clusters // 2
    ahead, cross = ring_pairs(count)
    mate = [(i, i ^ 1) for i in range(count)]
    side = [(i, i ^ 2) for i in range(count)]

    def move(values, where):
        return lax.ppermute(values, "blk", where)

    def after(values, *others):
        return lax.optimization_barrier((values, *others))[0]

    here = me.astype(jnp.int32).reshape(1)
    base = clusters * directions
    payload, lists = pl.pallas_call(
        functools.partial(prologue_kernel, count),
        out_shape=[
            jax.ShapeDtypeStruct((base + half * rank_k, unknowns), jnp.bfloat16),
            jax.ShapeDtypeStruct((8, stored), jnp.int32),
        ],
        in_specs=[whole(pltpu.SMEM)] + [whole()] * 5,
        out_specs=[whole()] * 2,
        compiler_params=pltpu.CompilerParams(vmem_limit_bytes=PROLOGUE_VMEM),
        name="prologue",
    )(
        here,
        near_owner.reshape(1, stored),
        near_slot.reshape(1, stored),
        near_offset.reshape(1, stored),
        rhs,
        basis_in,
    )
    flow = [move(payload, ahead)]
    mate_blocks = move(near_blocks, mate)
    lists = jnp.concatenate([lists, move(lists, mate)], axis=0)
    couple = jnp.transpose(far_coupling, (2, 1, 0))
    flow.append(move(after(payload, couple), cross))
    shards = [move(payload, mate)]
    for k in range(1, chips):
        x = 1 - k % 2
        if k == 3:
            flow[x], mate_blocks, shards[0], lists = lax.optimization_barrier(
                (flow[x], mate_blocks, shards[0], lists)
            )
        shards.append(flow[x])
        if k < chips - 2:
            flow[x] = move(flow[x], ahead)

    quarter = chips // 2

    def near(late, lists):
        keeps = [quarter - 1, 1] if late else [quarter]
        sends = [1] * quarter
        outs = pl.pallas_call(
            functools.partial(near_kernel, late, BATCH, LAG, chips, len(keeps), len(sends)),
            out_shape=[
                jax.ShapeDtypeStruct((part * half, unknowns, 2 * directions), jnp.float32)
                for part in keeps
            ]
            + [
                jax.ShapeDtypeStruct((part * half, unknowns, 2 * directions), jnp.bfloat16)
                for part in sends
            ]
            + [jax.ShapeDtypeStruct((chips * half * rank_k, unknowns), jnp.bfloat16)] * (1 - late),
            in_specs=[whole(pltpu.SMEM)] + [whole(pl.ANY)] * (chips + 2),
            out_specs=[whole()] * (len(keeps) + len(sends) + 1 - late),
            scratch_shapes=[
                pltpu.VMEM((chips * base, unknowns), jnp.bfloat16),
                pltpu.VMEM((2 * stored, unknowns, unknowns), jnp.bfloat16),
                pltpu.VMEM((2 * quarter * half + 1, unknowns, 2 * directions), jnp.float32),
                pltpu.SMEM((4, 2 * stored), jnp.int32),
                pltpu.SemaphoreType.DMA((chips,)),
                pltpu.SemaphoreType.DMA((chips,)),
                pltpu.SemaphoreType.DMA((2 * stored // BATCH,)),
            ],
            compiler_params=pltpu.CompilerParams(vmem_limit_bytes=NEAR_VMEM),
            cost_estimate=pl.CostEstimate(
                flops=16 * stored * directions * unknowns * unknowns,
                bytes_accessed=16 << 20,
                transcendentals=0,
            ),
            name="near",
        )(lists, *shards, near_blocks, mate_blocks)
        return outs[: len(keeps)], outs[len(keeps) :]

    def far_field(couple, own, got):
        return pl.pallas_call(
            far_kernel,
            out_shape=jax.ShapeDtypeStruct((clusters, directions, unknowns), jnp.float32),
            in_specs=[whole()] * 2 + [whole(pltpu.SMEM)] + [whole()] * 7,
            out_specs=whole(),
            compiler_params=pltpu.CompilerParams(vmem_limit_bytes=FAR_VMEM),
            cost_estimate=pl.CostEstimate(
                flops=4 * clusters * rank_k * pairs * rank_k * unknowns,
                bytes_accessed=8 << 20,
                transcendentals=0,
            ),
            name="far",
        )(
            *coefs,
            here,
            couple,
            far_slot.reshape(1, pairs),
            far_dev.reshape(1, pairs),
            far_cslot.reshape(1, pairs),
            basis_out,
            own,
            got,
        )

    kept, (*sends, coef) = near(0, lists)
    mates = [move(sends[0], mate), move(sends[1], mate)]
    coefs = [coef, move(coef, mate)]

    def term(k):
        at = k % quarter * half
        return kept[k // quarter][at : at + half] + mates[k].astype(jnp.float32)

    def tied(values, k, *others):
        values, mates[k + 1], *others = lax.optimization_barrier((values, mates[k + 1], *others))
        return values

    def add(flow, k):
        return (flow.astype(jnp.float32) + term(k)).astype(jnp.bfloat16)

    flow = lax.optimization_barrier([term(0).astype(jnp.bfloat16), term(1).astype(jnp.bfloat16)])
    lists = after(lists, *flow)
    mates += [move(after(send, *flow), mate) for send in sends[2:]]
    flow = [move(part, ahead) for part in flow]
    late, sends = near(1, lists)
    kept += late
    mates += [move(send, mate) for send in sends]
    for k in range(2, chips - 1):
        x = k % 2
        flow[x] = tied(add(flow[x], k), k)
        if k == chips - 2:
            couple = after(couple, flow[x])
        flow[x] = move(flow[x], ahead)
    flow[1] = move(flow[1], mate)
    rest = far_field(couple, kept[-1], mates[-1])
    return pl.pallas_call(
        last_kernel,
        out_shape=jax.ShapeDtypeStruct(rhs.shape, jnp.bfloat16),
        in_specs=[whole()] * 3,
        out_specs=whole(),
        name="last",
    )(*flow, rest)


def on_device(*args):
    rhs, near_blocks = args[0], args[1]
    clusters, directions, unknowns = rhs.shape
    small = lax.axis_size("blk") == 16 and clusters == 16
    if small and near_blocks.shape[0] == unknowns and 2 * directions == unknowns:
        return stationary(*args)
    return routed(*args)


def solution(mesh):
    placed = (
        P(("groups", "blk"), None, None),
        P(("groups", "blk"), None, None),
        P(("groups", "blk"), None),
        P(("groups", "blk")),
        P(("groups", "blk")),
        P(("groups", "blk"), None, None),
        P(("groups", "blk")),
        P(("groups", "blk"), None),
        P(("groups", "blk")),
        P(("groups", "blk"), None, None),
        P(("groups", "blk"), None, None),
    )
    return jax.shard_map(
        on_device,
        mesh=mesh,
        in_specs=placed,
        out_specs=P(("groups", "blk"), None, None),
        check_vma=False,
    )
```

```python
import functools

import jax
import jax.numpy as jnp
from jax import lax
from jax.experimental import pallas as pl
from jax.experimental.pallas import tpu as pltpu
from jax.sharding import PartitionSpec as P

BATCH = 16
LAG = 4
PROLOGUE_VMEM = 58 << 20
NEAR_VMEM = 48 << 20
FAR_VMEM = 16 << 20


def with_halo(cells, sides, width):
    for axis, dim in sides:
        count = lax.axis_size(axis)
        head = lax.slice_in_dim(cells, 0, width, axis=dim)
        tail = lax.slice_in_dim(cells, cells.shape[dim] - width, cells.shape[dim], axis=dim)
        cells = jnp.concatenate(
            [
                lax.ppermute(tail, axis, [(i, (i + 1) % count) for i in range(count)]),
                cells,
                lax.ppermute(head, axis, [((i + 1) % count, i) for i in range(count)]),
            ],
            axis=dim,
        )
    return cells


def place_ranks(targets, count):
    onehot = (targets[:, None] == jnp.arange(count, dtype=jnp.int32)[None, :]).astype(jnp.int32)
    before = jnp.cumsum(onehot, axis=0) - onehot
    return jnp.sum(before * onehot, axis=1)


def routed(
    rhs,
    near_blocks,
    near_owner,
    near_slot,
    near_offset,
    far_coupling,
    far_slot,
    far_dev,
    far_cslot,
    basis_out,
    basis_in,
):
    clusters = rhs.shape[0]
    directions = rhs.shape[1]
    unknowns = rhs.shape[2]
    cycle_size = lax.axis_size("blk")
    stored = near_blocks.shape[0]
    capacity = max(2, 2 * stored // cycle_size)
    owners = near_owner[:, 0]
    target = owners * capacity + place_ranks(owners, cycle_size)
    outbox = (
        jnp.zeros((cycle_size * capacity, unknowns, unknowns), near_blocks.dtype)
        .at[target]
        .set(near_blocks)
    )
    labels = (
        jnp.zeros((cycle_size * capacity, 2), jnp.int32)
        .at[target]
        .set(jnp.stack([near_slot, near_offset], axis=1))
    )
    window = with_halo(rhs, (("blk", 0),), clusters)
    inbox, in_labels = (
        lax.all_to_all(outbox, "blk", split_axis=0, concat_axis=0, tiled=True),
        lax.all_to_all(labels, "blk", split_axis=0, concat_axis=0, tiled=True),
    )
    position = clusters + in_labels[:, 0] + in_labels[:, 1]
    columns = jnp.take(window, position, axis=0)
    products = jnp.einsum("srj,sij->sri", columns, inbox, preferred_element_type=jnp.float32)
    selector = (in_labels[:, 0][None, :] == jnp.arange(clusters, dtype=jnp.int32)[:, None]).astype(
        jnp.float32
    )
    near_sum = jnp.dot(
        selector,
        products.reshape(products.shape[0], -1),
        precision=lax.Precision.HIGHEST,
        preferred_element_type=jnp.float32,
    ).reshape(clusters, directions, unknowns)
    coef_local = jnp.einsum(
        "ckj,crj->crk", basis_in, rhs, preferred_element_type=jnp.float32
    ).astype(jnp.bfloat16)
    rank_k = basis_in.shape[1]
    coef_local = coef_local.reshape(clusters, directions * rank_k)
    pairs = far_slot.shape[0]
    wanted = far_dev[:, 0] * clusters + far_cslot
    piece = lax.all_gather(coef_local, "blk", axis=0, tiled=True)
    chosen = jnp.take(piece, wanted, axis=0)
    coupled = jnp.einsum(
        "pkq,prq->prk",
        far_coupling,
        chosen.reshape(pairs, directions, rank_k),
        preferred_element_type=jnp.float32,
    )
    row_pick = (far_slot[None, :] == jnp.arange(clusters, dtype=jnp.int32)[:, None]).astype(
        jnp.float32
    )
    gathered = jnp.dot(
        row_pick,
        coupled.reshape(pairs, -1),
        precision=lax.Precision.HIGHEST,
        preferred_element_type=jnp.float32,
    )
    gathered = gathered.astype(jnp.bfloat16).reshape(clusters, directions, rank_k)
    far_sum = jnp.einsum("crk,ckb->crb", gathered, basis_out, preferred_element_type=jnp.float32)
    return (near_sum + far_sum).astype(jnp.bfloat16)


def whole(space=pltpu.VMEM):
    return pl.BlockSpec(memory_space=space)


def prologue_kernel(
    count, me_ref, owner_ref, slot_ref, offset_ref, rhs_ref, basis_ref, payload_ref, list_ref
):
    clusters, directions, unknowns = rhs_ref.shape
    base = clusters * directions
    payload_ref[0:base, :] = rhs_ref[...].reshape(base, unknowns)
    rank_k = basis_ref.shape[1]
    half = clusters // 2
    rows = []
    for c in range(half):
        parts = [
            lax.dot_general(
                basis_ref[e],
                rhs_ref[e],
                (((1,), (1,)), ((), ())),
                preferred_element_type=jnp.float32,
            )
            for e in (c, c + half)
        ]
        rows.append(jnp.concatenate(parts, axis=1))
    payload_ref[base:, :] = jnp.concatenate(
        [row[q : q + 1] for q in range(rank_k) for row in rows], axis=0
    ).astype(payload_ref.dtype)

    me, owner, slot = me_ref[0], owner_ref[...], slot_ref[...]
    stored = owner.shape[1]
    place = scatter_place(owner, me, count)
    quarter = count // 4
    late = (place // quarter) & 1
    place = (place // (2 * quarter) * quarter + (place & (quarter - 1))) * clusters + slot
    column = (owner * clusters + slot + offset_ref[...]) & (count * clusters - 1)
    shard = gather_place(column // clusters, me, count)
    theirs = (shard == count // 2).astype(jnp.int32)
    shard = jnp.where(theirs == 1, gather_place(column // clusters, me ^ 1, count), shard)
    column_place = shard * clusters + (column & (clusters - 1))
    square = (stored, stored)
    group = jnp.broadcast_to((2 * theirs + late).astype(jnp.float32), square)
    group_of_row = jnp.transpose(group)
    row_at = lax.broadcasted_iota(jnp.int32, square, 0)
    lane_at = lax.broadcasted_iota(jnp.int32, square, 1)
    lane = lane_at.astype(jnp.float32)
    before = (group_of_row < group) | ((group_of_row == group) & (row_at < lane_at))
    rank = jnp.sum(jnp.where(before, 1.0, 0.0), axis=0, keepdims=True)
    rank = jnp.transpose(jnp.broadcast_to(rank, square))
    here = jnp.where(rank == lane, 1.0, 0.0).astype(jnp.bfloat16)
    starts = jnp.sum(jnp.where(group_of_row < lane, 1.0, 0.0), axis=0, keepdims=True)
    values = jnp.concatenate(
        [lane[0:1], place.astype(jnp.float32), column_place.astype(jnp.float32)]
        + [jnp.zeros((5, stored), jnp.float32)],
        axis=0,
    )
    values = jnp.dot(values.astype(jnp.bfloat16), here, preferred_element_type=jnp.float32)
    values = jnp.concatenate([values[0:3], starts, values[4:8]], axis=0)
    list_ref[...] = values.astype(jnp.int32)


def near_kernel(late, batch, lag, shards, sends, list_ref, *refs):
    shard_refs, (own_hbm, mate_hbm, keep_ref) = refs[:shards], refs[shards : shards + 3]
    send_refs, refs = refs[shards + 3 : shards + 3 + sends], refs[shards + 3 + sends :]
    if not late:
        coef_ref, refs = refs[0], refs[1:]
    columns, blocks, sums, entries, block_sem = refs
    directions = sums.shape[1]
    span = columns.shape[0] // shards
    dummy = sums.shape[0] - 1

    begin, begin_there = list_ref[3, late], list_ref[11, 2 + late]
    here = list_ref[3, late + 1] - begin
    total = here + list_ref[11, 3 + late] - begin_there
    steps = (total + batch - 1) // batch

    def fetch(source, row, shift, swap):
        def one(j, carry):
            at = j + shift
            pltpu.make_async_copy(
                source.at[list_ref[row, at]], blocks.at[j], block_sem.at[j // batch]
            ).start()
            entries[0, j] = list_ref[row + 1, at] ^ swap
            entries[1, j] = list_ref[row + 2, at] * directions
            return carry

        return one

    def fill(j, carry):
        pltpu.make_async_copy(own_hbm.at[0], blocks.at[j], block_sem.at[j // batch]).start()
        entries[0, j] = dummy
        entries[1, j] = 0
        return carry

    lax.fori_loop(0, here, fetch(own_hbm, 0, begin, 0), 0)
    lax.fori_loop(here, total, fetch(mate_hbm, 8, begin_there - here, dummy // 2), 0)
    lax.fori_loop(total, steps * batch, fill, 0)

    for k, ref in enumerate(shard_refs):

        def gather(i, carry, k=k, ref=ref):
            at = pl.multiple_of(i * directions, directions)
            columns[pl.ds(pl.multiple_of(k * span + at, directions), directions)] = ref[
                pl.ds(at, directions)
            ]
            return carry

        lax.fori_loop(0, span // directions, gather, 0, unroll=4)
        if not late:
            tail = coef_ref.shape[0] // shards
            coef_ref[k * tail : (k + 1) * tail] = ref[span : span + tail]

    def clear(i, carry):
        sums[i] = jnp.zeros(sums.shape[1:], sums.dtype)
        return carry

    lax.fori_loop(0, dummy, clear, 0)

    def body(step, carry):
        first = step * batch
        pltpu.make_async_copy(
            own_hbm.at[pl.ds(0, batch)], blocks.at[pl.ds(first, batch)], block_sem.at[step]
        ).wait()
        products = []

        def add(i):
            place = entries[0, first + i]
            sums[place] = sums[place] + products[i]

        for i in range(batch):
            start = pl.multiple_of(entries[1, first + i], directions)
            products.append(
                lax.dot_general(
                    columns[pl.ds(start, directions)],
                    blocks[first + i],
                    (((1,), (1,)), ((), ())),
                    preferred_element_type=jnp.float32,
                )
            )
            if i >= lag:
                add(i - lag)
        for i in range(batch - lag, batch):
            add(i)
        return carry

    lax.fori_loop(0, steps, body, 0)

    def keep(i, carry):
        keep_ref[i] = sums[i]
        return carry

    lax.fori_loop(0, dummy // 2, keep, 0, unroll=2)
    at = dummy // 2
    for send_ref in send_refs:

        def pack(i, carry, at=at, send_ref=send_ref):
            send_ref[i] = sums[at + i].astype(send_ref.dtype)
            return carry

        lax.fori_loop(0, send_ref.shape[0], pack, 0, unroll=2)
        at += send_ref.shape[0]


def far_kernel(*refs):
    coef_refs = refs[:2]
    me_ref, couple_ref, slot_ref, dev_ref, cslot_ref, basis_ref, out_ref = refs[2:]
    clusters, rank_k, unknowns = basis_ref.shape
    pairs = couple_ref.shape[2]
    directions = out_ref.shape[1]
    half = clusters // 2
    coef = jnp.concatenate([ref[...].astype(jnp.float32) for ref in coef_refs], axis=0)
    coef = coef.reshape(-1, rank_k, half, unknowns)
    count = coef.shape[0]
    hot = (
        lax.broadcasted_iota(jnp.int32, (clusters, pairs), 0)
        == jnp.broadcast_to(slot_ref[...], (clusters, pairs))
    ).astype(jnp.float32).astype(jnp.bfloat16)
    away = gather_place(dev_ref[...], me_ref[0], count)
    theirs = count // 2 + gather_place(dev_ref[...], me_ref[0] ^ 1, count)
    away = jnp.where(away == count // 2, theirs, away)
    cslot = cslot_ref[...]
    high = (cslot >= half).astype(jnp.int32)
    at = away * half + cslot - high * half
    table_rows = (count * half, pairs)
    pick = jnp.where(
        lax.broadcasted_iota(jnp.int32, table_rows, 0) == jnp.broadcast_to(at, table_rows), 1.0, 0.0
    )
    pick = jnp.transpose(pick).astype(jnp.bfloat16)
    lanes = (unknowns, pairs)
    keep = jnp.where(
        lax.broadcasted_iota(jnp.int32, lanes, 0) // directions == jnp.broadcast_to(high, lanes),
        1.0,
        0.0,
    )
    keep = jnp.transpose(keep).astype(jnp.bfloat16)
    total = jnp.zeros((clusters * rank_k, unknowns), jnp.float32)
    for q in range(rank_k):
        table = coef[:, q].reshape(count * half, unknowns).astype(jnp.bfloat16)
        chosen = jnp.dot(pick, table, preferred_element_type=jnp.float32).astype(jnp.bfloat16)
        chosen = chosen * keep
        couple = couple_ref[q]
        weight = jnp.concatenate([couple * hot[s : s + 1] for s in range(clusters)], axis=0)
        total = total + jnp.dot(weight, chosen, preferred_element_type=jnp.float32)
    total = total + pltpu.roll(total, unknowns // 2, axis=1)
    gathered = jnp.transpose(total)[0:directions, :].astype(jnp.bfloat16).astype(jnp.float32)
    lane = lax.broadcasted_iota(jnp.int32, gathered.shape, 1) // rank_k
    basis = basis_ref[...].reshape(clusters * rank_k, unknowns)
    for s in range(clusters):
        own = jnp.where(lane == s, gathered, 0.0).astype(jnp.bfloat16)
        out_ref[s] = jnp.dot(own, basis, preferred_element_type=jnp.float32)


def ring_device(place, core, chips):
    depth = chips // 2
    place = place % chips
    z, y = (place, 0) if place < depth else (chips - 1 - place, 1)
    return (z * 2 + y) * 2 + core


def ring_pairs(count):
    chips = count // 2
    cores = [(p, c) for p in range(chips) for c in range(2)]
    ahead = [(ring_device(p, c, chips), ring_device(p + 1 - 2 * c, c, chips)) for p, c in cores]
    cross = [
        (ring_device(p, c, chips), ring_device(p - 1 + 2 * c, 1 - c, chips)) for p, c in cores
    ]
    return ahead, cross


def ring_place(device, chips):
    z, y = device >> 2, (device >> 1) & 1
    return jnp.where(y == 0, z, chips - 1 - z)


def gather_place(device, me, count):
    chips = count // 2
    depth = chips // 2
    back = (1 - 2 * (me & 1)) * (ring_place(me, chips) - ring_place(device, chips))
    back = (back + chips) & (chips - 1)
    other = (device ^ me) & 1
    here = (back < depth) & (back > 0) | (back == 0) & (other == 1) | (back == depth) & (other == 0)
    return jnp.where(here, jnp.where(back == 0, 0, 2 * back - 1 + other), chips)


def scatter_place(device, me, count):
    chips = count // 2
    depth = chips // 2
    ahead = (ring_place(device, chips) - ring_place(me, chips) + chips) & (chips - 1)
    core = device & 1
    handler = jnp.where((ahead & (depth - 1)) == 0, core, (ahead > depth).astype(jnp.int32))
    steps = jnp.where(handler == 0, ahead, (chips - ahead) & (chips - 1))
    place = jnp.where(
        steps == depth,
        0,
        jnp.where(steps == 0, chips - 1, 2 * (depth - steps) - (core ^ handler)),
    )
    return place + jnp.where(handler == (me & 1), 0, chips)


def stationary(
    rhs,
    near_blocks,
    near_owner,
    near_slot,
    near_offset,
    far_coupling,
    far_slot,
    far_dev,
    far_cslot,
    basis_out,
    basis_in,
):
    clusters, directions, unknowns = rhs.shape
    rank_k = basis_in.shape[1]
    count = lax.axis_size("blk")
    chips = count // 2
    depth = chips // 2
    me = lax.axis_index("blk")
    stored = near_blocks.shape[0]
    pairs = far_slot.shape[0]
    half = clusters // 2
    ahead, cross = ring_pairs(count)
    mate = [(i, i ^ 1) for i in range(count)]
    side = [(i, i ^ 2) for i in range(count)]

    def move(values, where):
        return lax.ppermute(values, "blk", where)

    def after(values, *others):
        return lax.optimization_barrier((values, *others))[0]

    here = me.astype(jnp.int32).reshape(1)
    base = clusters * directions
    payload, lists = pl.pallas_call(
        functools.partial(prologue_kernel, count),
        out_shape=[
            jax.ShapeDtypeStruct((base + half * rank_k, unknowns), jnp.bfloat16),
            jax.ShapeDtypeStruct((8, stored), jnp.int32),
        ],
        in_specs=[whole(pltpu.SMEM)] + [whole()] * 5,
        out_specs=[whole()] * 2,
        compiler_params=pltpu.CompilerParams(vmem_limit_bytes=PROLOGUE_VMEM),
        name="prologue",
    )(
        here,
        near_owner.reshape(1, stored),
        near_slot.reshape(1, stored),
        near_offset.reshape(1, stored),
        rhs,
        basis_in,
    )
    flow = [move(payload, ahead)]
    mate_blocks = move(near_blocks, mate)
    lists = jnp.concatenate([lists, move(lists, mate)], axis=0)
    couple = jnp.transpose(far_coupling, (2, 1, 0))
    flow.append(move(after(payload, couple), cross))
    shards = [move(payload, mate)]
    for k in range(1, chips):
        x = 1 - k % 2
        if k == 3:
            flow[x], mate_blocks, shards[0], lists = lax.optimization_barrier(
                (flow[x], mate_blocks, shards[0], lists)
            )
        shards.append(flow[x])
        if k < chips - 2:
            flow[x] = move(flow[x], ahead)

    quarter = chips // 2

    def near(late, lists):
        pieces = [1] * quarter
        kept, *sends = pl.pallas_call(
            functools.partial(near_kernel, late, BATCH, LAG, chips, len(pieces)),
            out_shape=[
                jax.ShapeDtypeStruct((quarter * clusters, directions, unknowns), jnp.float32)
            ]
            + [
                jax.ShapeDtypeStruct((part * clusters, directions, unknowns), jnp.bfloat16)
                for part in pieces
            ]
            + [jax.ShapeDtypeStruct((chips * half * rank_k, unknowns), jnp.bfloat16)] * (1 - late),
            in_specs=[whole(pltpu.SMEM)] + [whole()] * chips + [whole(pl.ANY)] * 2,
            out_specs=[whole()] * (2 + len(pieces) - late),
            scratch_shapes=[
                pltpu.VMEM((chips * base, unknowns), jnp.bfloat16),
                pltpu.VMEM((2 * stored, unknowns, unknowns), jnp.bfloat16),
                pltpu.VMEM((2 * quarter * clusters + 1, directions, unknowns), jnp.float32),
                pltpu.SMEM((2, 2 * stored), jnp.int32),
                pltpu.SemaphoreType.DMA((2 * stored // BATCH,)),
            ],
            compiler_params=pltpu.CompilerParams(vmem_limit_bytes=NEAR_VMEM),
            cost_estimate=pl.CostEstimate(
                flops=16 * stored * directions * unknowns * unknowns,
                bytes_accessed=16 << 20,
                transcendentals=0,
            ),
            name="near",
        )(lists, *shards, near_blocks, mate_blocks)
        return kept, sends

    def far_field(couple):
        return pl.pallas_call(
            far_kernel,
            out_shape=jax.ShapeDtypeStruct((clusters, directions, unknowns), jnp.float32),
            in_specs=[whole()] * 2 + [whole(pltpu.SMEM)] + [whole()] * 5,
            out_specs=whole(),
            compiler_params=pltpu.CompilerParams(vmem_limit_bytes=FAR_VMEM),
            cost_estimate=pl.CostEstimate(
                flops=4 * clusters * rank_k * pairs * rank_k * unknowns,
                bytes_accessed=8 << 20,
                transcendentals=0,
            ),
            name="far",
        )(
            *coefs,
            here,
            couple,
            far_slot.reshape(1, pairs),
            far_dev.reshape(1, pairs),
            far_cslot.reshape(1, pairs),
            basis_out,
        )

    early, (*sends, coef) = near(0, lists)
    mates = [move(sends[0], mate), move(sends[1], mate)]
    coefs = [coef, move(coef, mate)]
    kept = [early]

    def term(k):
        at = k % quarter * clusters
        return kept[k // quarter][at : at + clusters] + mates[k].astype(jnp.float32)

    def tied(values, k, *others):
        values, mates[k + 1], *others = lax.optimization_barrier((values, mates[k + 1], *others))
        return values

    def add(flow, k):
        return (flow.astype(jnp.float32) + term(k)).astype(jnp.bfloat16)

    flow = lax.optimization_barrier([term(0).astype(jnp.bfloat16), term(1).astype(jnp.bfloat16)])
    lists = after(lists, *flow)
    mates += [move(after(send, *flow), mate) for send in sends[2:]]
    flow = [move(part, ahead) for part in flow]
    late, sends = near(1, lists)
    kept.append(late)
    mates += [move(send, mate) for send in sends]
    for k in range(2, chips - 1):
        x = k % 2
        flow[x] = tied(add(flow[x], k), k)
        if k == chips - 2:
            couple = after(couple, flow[x])
        flow[x] = move(flow[x], ahead)
    flow[1] = move(flow[1], mate)
    total = far_field(couple) + term(chips - 1) + flow[0].astype(jnp.float32)
    total = lax.optimization_barrier(total)
    return (total + flow[1].astype(jnp.float32)).astype(jnp.bfloat16)


def on_device(*args):
    rhs, near_blocks = args[0], args[1]
    clusters, directions, unknowns = rhs.shape
    small = lax.axis_size("blk") == 16 and clusters == 16
    if small and near_blocks.shape[0] == unknowns and 2 * directions == unknowns:
        return stationary(*args)
    return routed(*args)


def solution(mesh):
    placed = (
        P(("groups", "blk"), None, None),
        P(("groups", "blk"), None, None),
        P(("groups", "blk"), None),
        P(("groups", "blk")),
        P(("groups", "blk")),
        P(("groups", "blk"), None, None),
        P(("groups", "blk")),
        P(("groups", "blk"), None),
        P(("groups", "blk")),
        P(("groups", "blk"), None, None),
        P(("groups", "blk"), None, None),
    )
    return jax.shard_map(
        on_device,
        mesh=mesh,
        in_specs=placed,
        out_specs=P(("groups", "blk"), None, None),
        check_vma=False,
    )
```

```python
import functools

import jax
import jax.numpy as jnp
from jax import lax
from jax.experimental import pallas as pl
from jax.experimental.pallas import tpu as pltpu
from jax.sharding import PartitionSpec as P

BATCH = 8
CHUNKS = 4
LATE = 2
LAG = 4
PROLOGUE_VMEM = 58 << 20
NEAR_VMEM = 20 << 20, 20 << 20
FAR_VMEM = 16 << 20


def with_halo(cells, sides, width):
    for axis, dim in sides:
        count = lax.axis_size(axis)
        head = lax.slice_in_dim(cells, 0, width, axis=dim)
        tail = lax.slice_in_dim(cells, cells.shape[dim] - width, cells.shape[dim], axis=dim)
        cells = jnp.concatenate(
            [
                lax.ppermute(tail, axis, [(i, (i + 1) % count) for i in range(count)]),
                cells,
                lax.ppermute(head, axis, [((i + 1) % count, i) for i in range(count)]),
            ],
            axis=dim,
        )
    return cells


def place_ranks(targets, count):
    onehot = (targets[:, None] == jnp.arange(count, dtype=jnp.int32)[None, :]).astype(jnp.int32)
    before = jnp.cumsum(onehot, axis=0) - onehot
    return jnp.sum(before * onehot, axis=1)


def routed(
    rhs,
    near_blocks,
    near_owner,
    near_slot,
    near_offset,
    far_coupling,
    far_slot,
    far_dev,
    far_cslot,
    basis_out,
    basis_in,
):
    clusters = rhs.shape[0]
    directions = rhs.shape[1]
    unknowns = rhs.shape[2]
    cycle_size = lax.axis_size("blk")
    stored = near_blocks.shape[0]
    capacity = max(2, 2 * stored // cycle_size)
    owners = near_owner[:, 0]
    target = owners * capacity + place_ranks(owners, cycle_size)
    outbox = (
        jnp.zeros((cycle_size * capacity, unknowns, unknowns), near_blocks.dtype)
        .at[target]
        .set(near_blocks)
    )
    labels = (
        jnp.zeros((cycle_size * capacity, 2), jnp.int32)
        .at[target]
        .set(jnp.stack([near_slot, near_offset], axis=1))
    )
    window = with_halo(rhs, (("blk", 0),), clusters)
    inbox, in_labels = (
        lax.all_to_all(outbox, "blk", split_axis=0, concat_axis=0, tiled=True),
        lax.all_to_all(labels, "blk", split_axis=0, concat_axis=0, tiled=True),
    )
    position = clusters + in_labels[:, 0] + in_labels[:, 1]
    columns = jnp.take(window, position, axis=0)
    products = jnp.einsum("srj,sij->sri", columns, inbox, preferred_element_type=jnp.float32)
    selector = (in_labels[:, 0][None, :] == jnp.arange(clusters, dtype=jnp.int32)[:, None]).astype(
        jnp.float32
    )
    near_sum = jnp.dot(
        selector,
        products.reshape(products.shape[0], -1),
        precision=lax.Precision.HIGHEST,
        preferred_element_type=jnp.float32,
    ).reshape(clusters, directions, unknowns)
    coef_local = jnp.einsum(
        "ckj,crj->crk", basis_in, rhs, preferred_element_type=jnp.float32
    ).astype(jnp.bfloat16)
    rank_k = basis_in.shape[1]
    coef_local = coef_local.reshape(clusters, directions * rank_k)
    pairs = far_slot.shape[0]
    wanted = far_dev[:, 0] * clusters + far_cslot
    piece = lax.all_gather(coef_local, "blk", axis=0, tiled=True)
    chosen = jnp.take(piece, wanted, axis=0)
    coupled = jnp.einsum(
        "pkq,prq->prk",
        far_coupling,
        chosen.reshape(pairs, directions, rank_k),
        preferred_element_type=jnp.float32,
    )
    row_pick = (far_slot[None, :] == jnp.arange(clusters, dtype=jnp.int32)[:, None]).astype(
        jnp.float32
    )
    gathered = jnp.dot(
        row_pick,
        coupled.reshape(pairs, -1),
        precision=lax.Precision.HIGHEST,
        preferred_element_type=jnp.float32,
    )
    gathered = gathered.astype(jnp.bfloat16).reshape(clusters, directions, rank_k)
    far_sum = jnp.einsum("crk,ckb->crb", gathered, basis_out, preferred_element_type=jnp.float32)
    return (near_sum + far_sum).astype(jnp.bfloat16)


def whole(space=pltpu.VMEM):
    return pl.BlockSpec(memory_space=space)


def prologue_kernel(
    count, me_ref, owner_ref, slot_ref, offset_ref, rhs_ref, basis_ref, payload_ref, list_ref
):
    clusters, directions, unknowns = rhs_ref.shape
    base = clusters * directions
    payload_ref[0:base, :] = rhs_ref[...].reshape(base, unknowns)
    rank_k = basis_ref.shape[1]
    half = clusters // 2
    rows = []
    for c in range(half):
        parts = [
            lax.dot_general(
                basis_ref[e],
                rhs_ref[e],
                (((1,), (1,)), ((), ())),
                preferred_element_type=jnp.float32,
            )
            for e in (c, c + half)
        ]
        rows.append(jnp.concatenate(parts, axis=1))
    payload_ref[base:, :] = jnp.concatenate(
        [row[q : q + 1] for q in range(rank_k) for row in rows], axis=0
    ).astype(payload_ref.dtype)

    me, owner, slot = me_ref[0], owner_ref[...], slot_ref[...]
    stored = owner.shape[1]
    place = scatter_place(owner, me, count) * clusters + slot
    column = (owner * clusters + slot + offset_ref[...]) & (count * clusters - 1)
    shard = gather_place(column // clusters, me, count)
    theirs = (shard == count // 2).astype(jnp.int32)
    shard = jnp.where(theirs == 1, gather_place(column // clusters, me ^ 1, count), shard)
    column_place = shard * clusters + (column & (clusters - 1))
    late = (shard >= count // 2 - LATE).astype(jnp.int32)
    square = (stored, stored)
    group = jnp.broadcast_to((2 * theirs + late).astype(jnp.float32), square)
    group_of_row = jnp.transpose(group)
    row_at = lax.broadcasted_iota(jnp.int32, square, 0)
    lane_at = lax.broadcasted_iota(jnp.int32, square, 1)
    lane = lane_at.astype(jnp.float32)
    before = (group_of_row < group) | ((group_of_row == group) & (row_at < lane_at))
    rank = jnp.sum(jnp.where(before, 1.0, 0.0), axis=0, keepdims=True)
    rank = jnp.transpose(jnp.broadcast_to(rank, square))
    here = jnp.where(rank == lane, 1.0, 0.0).astype(jnp.bfloat16)
    starts = jnp.sum(jnp.where(group_of_row < lane, 1.0, 0.0), axis=0, keepdims=True)
    values = jnp.concatenate(
        [lane[0:1], place.astype(jnp.float32), column_place.astype(jnp.float32)]
        + [jnp.zeros((5, stored), jnp.float32)],
        axis=0,
    )
    values = jnp.dot(values.astype(jnp.bfloat16), here, preferred_element_type=jnp.float32)
    values = jnp.concatenate([values[0:3], starts, values[4:8]], axis=0)
    list_ref[...] = values.astype(jnp.int32)


def near_kernel(late, batch, lag, shards, sends, list_ref, *refs):
    used = LATE if late else shards
    shard_refs, (own_ref, mate_hbm), refs = refs[:shards], refs[shards : shards + 2], refs[shards + 2 :]
    if late:
        sums, coef_ref, send_refs, refs = refs[1], refs[2], refs[3 : 3 + sends], refs[3 + sends :]
    else:
        sums, refs = refs[0], refs[1:]
    columns, blocks, block_sem = refs
    stored = blocks.shape[0]
    directions = sums.shape[1]
    span = columns.shape[0] // used
    dummy = sums.shape[0] - 1
    chunk = stored // CHUNKS

    begin, end = list_ref[3, late], list_ref[3, late + 1]
    begin_there, end_there = list_ref[11, 2 + late], list_ref[11, 3 + late]
    steps_there = (end_there - begin_there + batch - 1) // batch

    def fetch(j, carry):
        at = jnp.minimum(begin_there + j, end_there - 1)
        pltpu.make_async_copy(
            mate_hbm.at[list_ref[8, at]], blocks.at[j], block_sem.at[j // batch]
        ).start()
        return carry

    if late:
        lax.fori_loop(0, steps_there * batch, fetch, 0)
    else:
        for c in range(CHUNKS):
            at = pl.ds(c * chunk, chunk)
            pltpu.make_async_copy(mate_hbm.at[at], blocks.at[at], block_sem.at[c]).start()

    for k, ref in enumerate(shard_refs[shards - used :]):

        def gather(i, carry, k=k, ref=ref):
            at = pl.multiple_of(i * directions, directions)
            columns[pl.ds(pl.multiple_of(k * span + at, directions), directions)] = ref[
                pl.ds(at, directions)
            ]
            return carry

        lax.fori_loop(0, span // directions, gather, 0, unroll=4)
    if late:
        tail = coef_ref.shape[0] // shards
        for k, ref in enumerate(shard_refs):
            coef_ref[k * tail : (k + 1) * tail] = ref[span : span + tail]
    else:

        def clear(i, carry):
            sums[i] = jnp.zeros(sums.shape[1:], sums.dtype)
            return carry

        lax.fori_loop(0, dummy + 1, clear, 0)

    def run(begin, end, row, swap, block_of):
        def entry(j):
            return jnp.minimum(begin + j, end - 1)

        def body(step, carry):
            first = step * batch
            products = []

            def add(i):
                place = list_ref[row + 1, entry(first + i)] ^ swap
                place = jnp.where(begin + first + i < end, place, dummy)
                sums[place] = sums[place] + products[i]

            take, carry = block_of(first, entry, carry)
            for i in range(batch):
                start = list_ref[row + 2, entry(first + i)] * directions - (shards - used) * span
                products.append(
                    lax.dot_general(
                        columns[pl.ds(pl.multiple_of(start, directions), directions)],
                        take(i),
                        (((1,), (1,)), ((), ())),
                        preferred_element_type=jnp.float32,
                    )
                )
                if i >= lag:
                    add(i - lag)
            for i in range(batch - lag, batch):
                add(i)
            return carry

        return lax.fori_loop(0, (end - begin + batch - 1) // batch, body, 0)

    def own_blocks(first, entry, carry):
        return lambda i: own_ref[list_ref[0, entry(first + i)]], carry

    def wait(c, carry):
        at = pl.ds(0, chunk)
        pltpu.make_async_copy(mate_hbm.at[at], blocks.at[at], block_sem.at[c]).wait()
        return carry

    def mate_blocks(first, entry, ready):
        if late:
            pltpu.make_async_copy(
                mate_hbm.at[pl.ds(0, batch)],
                blocks.at[pl.ds(first, batch)],
                block_sem.at[first // batch],
            ).wait()
            return lambda i: blocks[first + i], ready
        needed = list_ref[8, entry(first + batch - 1)] // chunk + 1
        lax.fori_loop(ready, needed, wait, 0)
        return lambda i: blocks[list_ref[8, entry(first + i)]], jnp.maximum(ready, needed)

    run(begin, end, 0, 0, own_blocks)
    ready = run(begin_there, end_there, 8, dummy // 2, mate_blocks)
    if not late:
        lax.fori_loop(ready, CHUNKS, wait, 0)
        return
    at = dummy // 2
    for send_ref in send_refs:

        def pack(i, carry, at=at, send_ref=send_ref):
            send_ref[i] = sums[at + i].astype(send_ref.dtype)
            return carry

        lax.fori_loop(0, send_ref.shape[0], pack, 0, unroll=2)
        at += send_ref.shape[0]


def far_kernel(*refs):
    coef_refs = refs[:2]
    me_ref, couple_ref, slot_ref, dev_ref, cslot_ref, basis_ref, out_ref = refs[2:]
    clusters, rank_k, unknowns = basis_ref.shape
    pairs = couple_ref.shape[2]
    directions = out_ref.shape[1]
    half = clusters // 2
    coef = jnp.concatenate([ref[...].astype(jnp.float32) for ref in coef_refs], axis=0)
    coef = coef.reshape(-1, rank_k, half, unknowns)
    count = coef.shape[0]
    hot = (
        lax.broadcasted_iota(jnp.int32, (clusters, pairs), 0)
        == jnp.broadcast_to(slot_ref[...], (clusters, pairs))
    ).astype(jnp.float32).astype(jnp.bfloat16)
    away = gather_place(dev_ref[...], me_ref[0], count)
    theirs = count // 2 + gather_place(dev_ref[...], me_ref[0] ^ 1, count)
    away = jnp.where(away == count // 2, theirs, away)
    cslot = cslot_ref[...]
    high = (cslot >= half).astype(jnp.int32)
    at = away * half + cslot - high * half
    table_rows = (count * half, pairs)
    pick = jnp.where(
        lax.broadcasted_iota(jnp.int32, table_rows, 0) == jnp.broadcast_to(at, table_rows), 1.0, 0.0
    )
    pick = jnp.transpose(pick).astype(jnp.bfloat16)
    lanes = (unknowns, pairs)
    keep = jnp.where(
        lax.broadcasted_iota(jnp.int32, lanes, 0) // directions == jnp.broadcast_to(high, lanes),
        1.0,
        0.0,
    )
    keep = jnp.transpose(keep).astype(jnp.bfloat16)
    total = jnp.zeros((clusters * rank_k, unknowns), jnp.float32)
    for q in range(rank_k):
        table = coef[:, q].reshape(count * half, unknowns).astype(jnp.bfloat16)
        chosen = jnp.dot(pick, table, preferred_element_type=jnp.float32).astype(jnp.bfloat16)
        chosen = chosen * keep
        couple = couple_ref[q]
        weight = jnp.concatenate([couple * hot[s : s + 1] for s in range(clusters)], axis=0)
        total = total + jnp.dot(weight, chosen, preferred_element_type=jnp.float32)
    total = total + pltpu.roll(total, unknowns // 2, axis=1)
    gathered = jnp.transpose(total)[0:directions, :].astype(jnp.bfloat16).astype(jnp.float32)
    lane = lax.broadcasted_iota(jnp.int32, gathered.shape, 1) // rank_k
    basis = basis_ref[...].reshape(clusters * rank_k, unknowns)
    for s in range(clusters):
        own = jnp.where(lane == s, gathered, 0.0).astype(jnp.bfloat16)
        out_ref[s] = jnp.dot(own, basis, preferred_element_type=jnp.float32)


def ring_device(place, core, chips):
    depth = chips // 2
    place = place % chips
    z, y = (place, 0) if place < depth else (chips - 1 - place, 1)
    return (z * 2 + y) * 2 + core


def ring_pairs(count):
    chips = count // 2
    cores = [(p, c) for p in range(chips) for c in range(2)]
    ahead = [(ring_device(p, c, chips), ring_device(p + 1 - 2 * c, c, chips)) for p, c in cores]
    cross = [
        (ring_device(p, c, chips), ring_device(p - 1 + 2 * c, 1 - c, chips)) for p, c in cores
    ]
    return ahead, cross


def ring_place(device, chips):
    z, y = device >> 2, (device >> 1) & 1
    return jnp.where(y == 0, z, chips - 1 - z)


def gather_place(device, me, count):
    chips = count // 2
    depth = chips // 2
    back = (1 - 2 * (me & 1)) * (ring_place(me, chips) - ring_place(device, chips))
    back = (back + chips) & (chips - 1)
    other = (device ^ me) & 1
    here = (back < depth) & (back > 0) | (back == 0) & (other == 1) | (back == depth) & (other == 0)
    return jnp.where(here, jnp.where(back == 0, 0, 2 * back - 1 + other), chips)


def scatter_place(device, me, count):
    chips = count // 2
    depth = chips // 2
    ahead = (ring_place(device, chips) - ring_place(me, chips) + chips) & (chips - 1)
    core = device & 1
    handler = jnp.where((ahead & (depth - 1)) == 0, core, (ahead > depth).astype(jnp.int32))
    steps = jnp.where(handler == 0, ahead, (chips - ahead) & (chips - 1))
    place = jnp.where(
        steps == depth,
        0,
        jnp.where(steps == 0, chips - 1, 2 * (depth - steps) - (core ^ handler)),
    )
    return place + jnp.where(handler == (me & 1), 0, chips)


def stationary(
    rhs,
    near_blocks,
    near_owner,
    near_slot,
    near_offset,
    far_coupling,
    far_slot,
    far_dev,
    far_cslot,
    basis_out,
    basis_in,
):
    clusters, directions, unknowns = rhs.shape
    rank_k = basis_in.shape[1]
    count = lax.axis_size("blk")
    chips = count // 2
    depth = chips // 2
    me = lax.axis_index("blk")
    stored = near_blocks.shape[0]
    pairs = far_slot.shape[0]
    half = clusters // 2
    ahead, cross = ring_pairs(count)
    mate = [(i, i ^ 1) for i in range(count)]
    side = [(i, i ^ 2) for i in range(count)]

    def move(values, where):
        return lax.ppermute(values, "blk", where)

    def after(values, *others):
        return lax.optimization_barrier((values, *others))[0]

    here = me.astype(jnp.int32).reshape(1)
    base = clusters * directions
    payload, lists = pl.pallas_call(
        functools.partial(prologue_kernel, count),
        out_shape=[
            jax.ShapeDtypeStruct((base + half * rank_k, unknowns), jnp.bfloat16),
            jax.ShapeDtypeStruct((8, stored), jnp.int32),
        ],
        in_specs=[whole(pltpu.SMEM)] + [whole()] * 5,
        out_specs=[whole()] * 2,
        compiler_params=pltpu.CompilerParams(vmem_limit_bytes=PROLOGUE_VMEM),
        name="prologue",
    )(
        here,
        near_owner.reshape(1, stored),
        near_slot.reshape(1, stored),
        near_offset.reshape(1, stored),
        rhs,
        basis_in,
    )
    flow = [move(payload, ahead)]
    mate_blocks = move(near_blocks, mate)
    lists = jnp.concatenate([lists, move(lists, mate)], axis=0)
    couple = jnp.transpose(far_coupling, (2, 1, 0))
    flow.append(move(after(payload, couple), cross))
    shards = [move(payload, mate)]
    for k in range(1, chips):
        x = 1 - k % 2
        if k == 3:
            flow[x], mate_blocks, shards[0], lists = lax.optimization_barrier(
                (flow[x], mate_blocks, shards[0], lists)
            )
        shards.append(flow[x])
        if k < chips - 2:
            flow[x] = move(flow[x], ahead)

    pieces = [1, 1, chips - 2]
    sums_shape = jax.ShapeDtypeStruct((count * clusters + 1, directions, unknowns), jnp.float32)

    def near(late, shards, *sums):
        sends = pieces if late else []
        return pl.pallas_call(
            functools.partial(near_kernel, late, BATCH, LAG, len(shards), len(sends)),
            out_shape=[sums_shape]
            + [jax.ShapeDtypeStruct((chips * half * rank_k, unknowns), jnp.bfloat16)] * late
            + [
                jax.ShapeDtypeStruct((part * clusters, directions, unknowns), jnp.bfloat16)
                for part in sends
            ],
            in_specs=[whole(pltpu.SMEM)]
            + [whole()] * len(shards)
            + [whole(), whole(pl.ANY)]
            + [whole()] * late,
            out_specs=[whole()] * (1 + late + len(sends)),
            input_output_aliases={len(shards) + 3: 0} if late else {},
            scratch_shapes=[
                pltpu.VMEM(((LATE if late else len(shards)) * base, unknowns), jnp.bfloat16),
                pltpu.VMEM(near_blocks.shape, jnp.bfloat16),
                pltpu.SemaphoreType.DMA((max(CHUNKS, stored // BATCH),)),
            ],
            compiler_params=pltpu.CompilerParams(vmem_limit_bytes=NEAR_VMEM[late]),
            cost_estimate=pl.CostEstimate(
                flops=16 * stored * directions * unknowns * unknowns,
                bytes_accessed=16 << 20,
                transcendentals=0,
            ),
            name="near",
        )(lists, *shards, near_blocks, mate_blocks, *sums)

    def far_field(couple):
        return pl.pallas_call(
            far_kernel,
            out_shape=jax.ShapeDtypeStruct((clusters, directions, unknowns), jnp.float32),
            in_specs=[whole()] * 2 + [whole(pltpu.SMEM)] + [whole()] * 5,
            out_specs=whole(),
            compiler_params=pltpu.CompilerParams(vmem_limit_bytes=FAR_VMEM),
            cost_estimate=pl.CostEstimate(
                flops=4 * clusters * rank_k * pairs * rank_k * unknowns,
                bytes_accessed=8 << 20,
                transcendentals=0,
            ),
            name="far",
        )(
            *coefs,
            here,
            couple,
            far_slot.reshape(1, pairs),
            far_dev.reshape(1, pairs),
            far_cslot.reshape(1, pairs),
            basis_out,
        )

    (sums,) = near(0, shards[: chips - LATE])
    sums, coef, *sends = near(1, shards, sums)
    mates = [move(sends[0], mate), move(sends[1], mate)]
    coefs = [coef, move(coef, mate)]

    def term(k):
        part = min(k, 2)
        got = mates[part][(k - part) * clusters : (k - part + 1) * clusters]
        return sums[k * clusters : (k + 1) * clusters] + got.astype(jnp.float32)

    def tied(values, k, *others):
        values, mates[2], *others = lax.optimization_barrier((values, mates[2], *others))
        return values

    def add(flow, k):
        return (flow.astype(jnp.float32) + term(k)).astype(jnp.bfloat16)

    flow = lax.optimization_barrier([term(0).astype(jnp.bfloat16), term(1).astype(jnp.bfloat16)])
    mates.append(move(after(sends[2], *flow), mate))
    flow = [move(part, ahead) for part in flow]
    for k in range(2, chips - 1):
        x = k % 2
        flow[x] = tied(add(flow[x], k), k)
        if k == chips - 2:
            couple = after(couple, flow[x])
        flow[x] = move(flow[x], ahead)
    flow[1] = move(flow[1], mate)
    total = far_field(couple) + term(chips - 1) + flow[0].astype(jnp.float32)
    total = lax.optimization_barrier(total)
    return (total + flow[1].astype(jnp.float32)).astype(jnp.bfloat16)


def on_device(*args):
    rhs, near_blocks = args[0], args[1]
    clusters, directions, unknowns = rhs.shape
    small = lax.axis_size("blk") == 16 and clusters == 16
    if small and near_blocks.shape[0] == unknowns and 2 * directions == unknowns:
        return stationary(*args)
    return routed(*args)


def solution(mesh):
    placed = (
        P(("groups", "blk"), None, None),
        P(("groups", "blk"), None, None),
        P(("groups", "blk"), None),
        P(("groups", "blk")),
        P(("groups", "blk")),
        P(("groups", "blk"), None, None),
        P(("groups", "blk")),
        P(("groups", "blk"), None),
        P(("groups", "blk")),
        P(("groups", "blk"), None, None),
        P(("groups", "blk"), None, None),
    )
    return jax.shard_map(
        on_device,
        mesh=mesh,
        in_specs=placed,
        out_specs=P(("groups", "blk"), None, None),
        check_vma=False,
    )
```

```python
import functools

import jax
import jax.numpy as jnp
from jax import lax
from jax.experimental import pallas as pl
from jax.experimental.pallas import tpu as pltpu
from jax.sharding import PartitionSpec as P

BATCH = 8
CHUNKS = 4
LATE = 2
LAG = 4
PROLOGUE_VMEM = 58 << 20
NEAR_VMEM = 20 << 20
FAR_VMEM = 16 << 20


def with_halo(cells, sides, width):
    for axis, dim in sides:
        count = lax.axis_size(axis)
        head = lax.slice_in_dim(cells, 0, width, axis=dim)
        tail = lax.slice_in_dim(cells, cells.shape[dim] - width, cells.shape[dim], axis=dim)
        cells = jnp.concatenate(
            [
                lax.ppermute(tail, axis, [(i, (i + 1) % count) for i in range(count)]),
                cells,
                lax.ppermute(head, axis, [((i + 1) % count, i) for i in range(count)]),
            ],
            axis=dim,
        )
    return cells


def place_ranks(targets, count):
    onehot = (targets[:, None] == jnp.arange(count, dtype=jnp.int32)[None, :]).astype(jnp.int32)
    before = jnp.cumsum(onehot, axis=0) - onehot
    return jnp.sum(before * onehot, axis=1)


def routed(
    rhs,
    near_blocks,
    near_owner,
    near_slot,
    near_offset,
    far_coupling,
    far_slot,
    far_dev,
    far_cslot,
    basis_out,
    basis_in,
):
    clusters = rhs.shape[0]
    directions = rhs.shape[1]
    unknowns = rhs.shape[2]
    cycle_size = lax.axis_size("blk")
    stored = near_blocks.shape[0]
    capacity = max(2, 2 * stored // cycle_size)
    owners = near_owner[:, 0]
    target = owners * capacity + place_ranks(owners, cycle_size)
    outbox = (
        jnp.zeros((cycle_size * capacity, unknowns, unknowns), near_blocks.dtype)
        .at[target]
        .set(near_blocks)
    )
    labels = (
        jnp.zeros((cycle_size * capacity, 2), jnp.int32)
        .at[target]
        .set(jnp.stack([near_slot, near_offset], axis=1))
    )
    window = with_halo(rhs, (("blk", 0),), clusters)
    inbox, in_labels = (
        lax.all_to_all(outbox, "blk", split_axis=0, concat_axis=0, tiled=True),
        lax.all_to_all(labels, "blk", split_axis=0, concat_axis=0, tiled=True),
    )
    position = clusters + in_labels[:, 0] + in_labels[:, 1]
    columns = jnp.take(window, position, axis=0)
    products = jnp.einsum("srj,sij->sri", columns, inbox, preferred_element_type=jnp.float32)
    selector = (in_labels[:, 0][None, :] == jnp.arange(clusters, dtype=jnp.int32)[:, None]).astype(
        jnp.float32
    )
    near_sum = jnp.dot(
        selector,
        products.reshape(products.shape[0], -1),
        precision=lax.Precision.HIGHEST,
        preferred_element_type=jnp.float32,
    ).reshape(clusters, directions, unknowns)
    coef_local = jnp.einsum(
        "ckj,crj->crk", basis_in, rhs, preferred_element_type=jnp.float32
    ).astype(jnp.bfloat16)
    rank_k = basis_in.shape[1]
    coef_local = coef_local.reshape(clusters, directions * rank_k)
    pairs = far_slot.shape[0]
    wanted = far_dev[:, 0] * clusters + far_cslot
    piece = lax.all_gather(coef_local, "blk", axis=0, tiled=True)
    chosen = jnp.take(piece, wanted, axis=0)
    coupled = jnp.einsum(
        "pkq,prq->prk",
        far_coupling,
        chosen.reshape(pairs, directions, rank_k),
        preferred_element_type=jnp.float32,
    )
    row_pick = (far_slot[None, :] == jnp.arange(clusters, dtype=jnp.int32)[:, None]).astype(
        jnp.float32
    )
    gathered = jnp.dot(
        row_pick,
        coupled.reshape(pairs, -1),
        precision=lax.Precision.HIGHEST,
        preferred_element_type=jnp.float32,
    )
    gathered = gathered.astype(jnp.bfloat16).reshape(clusters, directions, rank_k)
    far_sum = jnp.einsum("crk,ckb->crb", gathered, basis_out, preferred_element_type=jnp.float32)
    return (near_sum + far_sum).astype(jnp.bfloat16)


def whole(space=pltpu.VMEM):
    return pl.BlockSpec(memory_space=space)


def prologue_kernel(
    count, me_ref, owner_ref, slot_ref, offset_ref, rhs_ref, basis_ref, payload_ref, list_ref
):
    clusters, directions, unknowns = rhs_ref.shape
    base = clusters * directions
    payload_ref[0:base, :] = rhs_ref[...].reshape(base, unknowns)
    rank_k = basis_ref.shape[1]
    half = clusters // 2
    rows = []
    for c in range(half):
        parts = [
            lax.dot_general(
                basis_ref[e],
                rhs_ref[e],
                (((1,), (1,)), ((), ())),
                preferred_element_type=jnp.float32,
            )
            for e in (c, c + half)
        ]
        rows.append(jnp.concatenate(parts, axis=1))
    payload_ref[base:, :] = jnp.concatenate(
        [row[q : q + 1] for q in range(rank_k) for row in rows], axis=0
    ).astype(payload_ref.dtype)

    me, owner, slot = me_ref[0], owner_ref[...], slot_ref[...]
    stored = owner.shape[1]
    place = scatter_place(owner, me, count) * clusters + slot
    column = (owner * clusters + slot + offset_ref[...]) & (count * clusters - 1)
    shard = gather_place(column // clusters, me, count)
    theirs = (shard == count // 2).astype(jnp.int32)
    shard = jnp.where(theirs == 1, gather_place(column // clusters, me ^ 1, count), shard)
    column_place = shard * clusters + (column & (clusters - 1))
    late = (shard >= count // 2 - LATE).astype(jnp.int32)
    square = (stored, stored)
    group = jnp.broadcast_to((2 * theirs + late).astype(jnp.float32), square)
    group_of_row = jnp.transpose(group)
    row_at = lax.broadcasted_iota(jnp.int32, square, 0)
    lane_at = lax.broadcasted_iota(jnp.int32, square, 1)
    lane = lane_at.astype(jnp.float32)
    before = (group_of_row < group) | ((group_of_row == group) & (row_at < lane_at))
    rank = jnp.sum(jnp.where(before, 1.0, 0.0), axis=0, keepdims=True)
    rank = jnp.transpose(jnp.broadcast_to(rank, square))
    here = jnp.where(rank == lane, 1.0, 0.0).astype(jnp.bfloat16)
    starts = jnp.sum(jnp.where(group_of_row < lane, 1.0, 0.0), axis=0, keepdims=True)
    values = jnp.concatenate(
        [lane[0:1], place.astype(jnp.float32), column_place.astype(jnp.float32)]
        + [jnp.zeros((5, stored), jnp.float32)],
        axis=0,
    )
    values = jnp.dot(values.astype(jnp.bfloat16), here, preferred_element_type=jnp.float32)
    values = jnp.concatenate([values[0:3], starts, values[4:8]], axis=0)
    list_ref[...] = values.astype(jnp.int32)


def near_kernel(part, batch, lag, shards, sends, list_ref, *refs):
    late = int(part == 2)
    used = LATE if late else shards
    shard_refs, refs = refs[:shards], refs[shards:]
    if part > 0:
        own_ref, refs = refs[0], refs[1:]
    if part != 1:
        mate_hbm, refs = refs[0], refs[1:]
    if part > 0:
        refs = refs[1:]
    sums, refs = refs[0], refs[1:]
    if late:
        coef_ref, send_refs, refs = refs[0], refs[1 : 1 + sends], refs[1 + sends :]
    columns, blocks, block_sem = refs
    stored = blocks.shape[0]
    directions = sums.shape[1]
    span = columns.shape[0] // used
    dummy = sums.shape[0] - 1
    chunk = stored // CHUNKS

    begin, end = list_ref[3, late], list_ref[3, late + 1]
    begin_there, end_there = list_ref[11, 2 + late], list_ref[11, 3 + late]
    steps_there = (end_there - begin_there + batch - 1) // batch

    def fetch(j, carry):
        at = jnp.minimum(begin_there + j, end_there - 1)
        pltpu.make_async_copy(
            mate_hbm.at[list_ref[8, at]], blocks.at[j], block_sem.at[j // batch]
        ).start()
        return carry

    if late:
        lax.fori_loop(0, steps_there * batch, fetch, 0)
    elif part == 0:
        for c in range(CHUNKS):
            at = pl.ds(c * chunk, chunk)
            pltpu.make_async_copy(mate_hbm.at[at], blocks.at[at], block_sem.at[c]).start()

    for k, ref in enumerate(shard_refs[shards - used :]):

        def gather(i, carry, k=k, ref=ref):
            at = pl.multiple_of(i * directions, directions)
            columns[pl.ds(pl.multiple_of(k * span + at, directions), directions)] = ref[
                pl.ds(at, directions)
            ]
            return carry

        lax.fori_loop(0, span // directions, gather, 0, unroll=4)
    if late:
        tail = coef_ref.shape[0] // shards
        for k, ref in enumerate(shard_refs):
            coef_ref[k * tail : (k + 1) * tail] = ref[span : span + tail]
    elif part == 0:

        def clear(i, carry):
            sums[i] = jnp.zeros(sums.shape[1:], sums.dtype)
            return carry

        lax.fori_loop(0, dummy + 1, clear, 0)

    def run(begin, end, row, swap, block_of):
        def entry(j):
            return jnp.minimum(begin + j, end - 1)

        def body(step, carry):
            first = step * batch
            products = []

            def add(i):
                place = list_ref[row + 1, entry(first + i)] ^ swap
                place = jnp.where(begin + first + i < end, place, dummy)
                sums[place] = sums[place] + products[i]

            take, carry = block_of(first, entry, carry)
            for i in range(batch):
                start = list_ref[row + 2, entry(first + i)] * directions - (shards - used) * span
                products.append(
                    lax.dot_general(
                        columns[pl.ds(pl.multiple_of(start, directions), directions)],
                        take(i),
                        (((1,), (1,)), ((), ())),
                        preferred_element_type=jnp.float32,
                    )
                )
                if i >= lag:
                    add(i - lag)
            for i in range(batch - lag, batch):
                add(i)
            return carry

        return lax.fori_loop(0, (end - begin + batch - 1) // batch, body, 0)

    def own_blocks(first, entry, carry):
        return lambda i: own_ref[list_ref[0, entry(first + i)]], carry

    def wait(c, carry):
        at = pl.ds(0, chunk)
        pltpu.make_async_copy(mate_hbm.at[at], blocks.at[at], block_sem.at[c]).wait()
        return carry

    def mate_blocks(first, entry, ready):
        if late:
            pltpu.make_async_copy(
                mate_hbm.at[pl.ds(0, batch)],
                blocks.at[pl.ds(first, batch)],
                block_sem.at[first // batch],
            ).wait()
            return lambda i: blocks[first + i], ready
        needed = list_ref[8, entry(first + batch - 1)] // chunk + 1
        lax.fori_loop(ready, needed, wait, 0)
        return lambda i: blocks[list_ref[8, entry(first + i)]], jnp.maximum(ready, needed)

    if part > 0:
        run(begin, end, 0, 0, own_blocks)
    if part != 1:
        ready = run(begin_there, end_there, 8, dummy // 2, mate_blocks)
    if part == 0:
        lax.fori_loop(ready, CHUNKS, wait, 0)
    if not late:
        return
    at = dummy // 2
    for send_ref in send_refs:

        def pack(i, carry, at=at, send_ref=send_ref):
            send_ref[i] = sums[at + i].astype(send_ref.dtype)
            return carry

        lax.fori_loop(0, send_ref.shape[0], pack, 0, unroll=2)
        at += send_ref.shape[0]


def far_kernel(*refs):
    coef_refs = refs[:2]
    me_ref, couple_ref, slot_ref, dev_ref, cslot_ref, basis_ref, out_ref = refs[2:]
    clusters, rank_k, unknowns = basis_ref.shape
    pairs = couple_ref.shape[2]
    directions = out_ref.shape[1]
    half = clusters // 2
    coef = jnp.concatenate([ref[...].astype(jnp.float32) for ref in coef_refs], axis=0)
    coef = coef.reshape(-1, rank_k, half, unknowns)
    count = coef.shape[0]
    hot = (
        lax.broadcasted_iota(jnp.int32, (clusters, pairs), 0)
        == jnp.broadcast_to(slot_ref[...], (clusters, pairs))
    ).astype(jnp.float32).astype(jnp.bfloat16)
    away = gather_place(dev_ref[...], me_ref[0], count)
    theirs = count // 2 + gather_place(dev_ref[...], me_ref[0] ^ 1, count)
    away = jnp.where(away == count // 2, theirs, away)
    cslot = cslot_ref[...]
    high = (cslot >= half).astype(jnp.int32)
    at = away * half + cslot - high * half
    table_rows = (count * half, pairs)
    pick = jnp.where(
        lax.broadcasted_iota(jnp.int32, table_rows, 0) == jnp.broadcast_to(at, table_rows), 1.0, 0.0
    )
    pick = jnp.transpose(pick).astype(jnp.bfloat16)
    lanes = (unknowns, pairs)
    keep = jnp.where(
        lax.broadcasted_iota(jnp.int32, lanes, 0) // directions == jnp.broadcast_to(high, lanes),
        1.0,
        0.0,
    )
    keep = jnp.transpose(keep).astype(jnp.bfloat16)
    total = jnp.zeros((clusters * rank_k, unknowns), jnp.float32)
    for q in range(rank_k):
        table = coef[:, q].reshape(count * half, unknowns).astype(jnp.bfloat16)
        chosen = jnp.dot(pick, table, preferred_element_type=jnp.float32).astype(jnp.bfloat16)
        chosen = chosen * keep
        couple = couple_ref[q]
        weight = jnp.concatenate([couple * hot[s : s + 1] for s in range(clusters)], axis=0)
        total = total + jnp.dot(weight, chosen, preferred_element_type=jnp.float32)
    total = total + pltpu.roll(total, unknowns // 2, axis=1)
    gathered = jnp.transpose(total)[0:directions, :].astype(jnp.bfloat16).astype(jnp.float32)
    lane = lax.broadcasted_iota(jnp.int32, gathered.shape, 1) // rank_k
    basis = basis_ref[...].reshape(clusters * rank_k, unknowns)
    for s in range(clusters):
        own = jnp.where(lane == s, gathered, 0.0).astype(jnp.bfloat16)
        out_ref[s] = jnp.dot(own, basis, preferred_element_type=jnp.float32)


def ring_device(place, core, chips):
    depth = chips // 2
    place = place % chips
    z, y = (place, 0) if place < depth else (chips - 1 - place, 1)
    return (z * 2 + y) * 2 + core


def ring_pairs(count):
    chips = count // 2
    cores = [(p, c) for p in range(chips) for c in range(2)]
    ahead = [(ring_device(p, c, chips), ring_device(p + 1 - 2 * c, c, chips)) for p, c in cores]
    cross = [
        (ring_device(p, c, chips), ring_device(p - 1 + 2 * c, 1 - c, chips)) for p, c in cores
    ]
    return ahead, cross


def ring_place(device, chips):
    z, y = device >> 2, (device >> 1) & 1
    return jnp.where(y == 0, z, chips - 1 - z)


def gather_place(device, me, count):
    chips = count // 2
    depth = chips // 2
    back = (1 - 2 * (me & 1)) * (ring_place(me, chips) - ring_place(device, chips))
    back = (back + chips) & (chips - 1)
    other = (device ^ me) & 1
    here = (back < depth) & (back > 0) | (back == 0) & (other == 1) | (back == depth) & (other == 0)
    return jnp.where(here, jnp.where(back == 0, 0, 2 * back - 1 + other), chips)


def scatter_place(device, me, count):
    chips = count // 2
    depth = chips // 2
    ahead = (ring_place(device, chips) - ring_place(me, chips) + chips) & (chips - 1)
    core = device & 1
    handler = jnp.where((ahead & (depth - 1)) == 0, core, (ahead > depth).astype(jnp.int32))
    steps = jnp.where(handler == 0, ahead, (chips - ahead) & (chips - 1))
    place = jnp.where(
        steps == depth,
        0,
        jnp.where(steps == 0, chips - 1, 2 * (depth - steps) - (core ^ handler)),
    )
    return place + jnp.where(handler == (me & 1), 0, chips)


def stationary(
    rhs,
    near_blocks,
    near_owner,
    near_slot,
    near_offset,
    far_coupling,
    far_slot,
    far_dev,
    far_cslot,
    basis_out,
    basis_in,
):
    clusters, directions, unknowns = rhs.shape
    rank_k = basis_in.shape[1]
    count = lax.axis_size("blk")
    chips = count // 2
    depth = chips // 2
    me = lax.axis_index("blk")
    stored = near_blocks.shape[0]
    pairs = far_slot.shape[0]
    half = clusters // 2
    ahead, cross = ring_pairs(count)
    mate = [(i, i ^ 1) for i in range(count)]
    side = [(i, i ^ 2) for i in range(count)]

    def move(values, where):
        return lax.ppermute(values, "blk", where)

    def after(values, *others):
        return lax.optimization_barrier((values, *others))[0]

    here = me.astype(jnp.int32).reshape(1)
    base = clusters * directions
    payload, lists = pl.pallas_call(
        functools.partial(prologue_kernel, count),
        out_shape=[
            jax.ShapeDtypeStruct((base + half * rank_k, unknowns), jnp.bfloat16),
            jax.ShapeDtypeStruct((8, stored), jnp.int32),
        ],
        in_specs=[whole(pltpu.SMEM)] + [whole()] * 5,
        out_specs=[whole()] * 2,
        compiler_params=pltpu.CompilerParams(vmem_limit_bytes=PROLOGUE_VMEM),
        name="prologue",
    )(
        here,
        near_owner.reshape(1, stored),
        near_slot.reshape(1, stored),
        near_offset.reshape(1, stored),
        rhs,
        basis_in,
    )
    flow = [move(payload, ahead)]
    mate_blocks = move(near_blocks, mate)
    mate_lists = move(lists, mate)
    couple = jnp.transpose(far_coupling, (2, 1, 0))
    flow.append(move(after(payload, couple), cross))
    shards = [move(payload, mate)]
    for k in range(1, chips):
        x = 1 - k % 2
        if k == 3:
            flow[x], mate_blocks, shards[0], mate_lists = lax.optimization_barrier(
                (flow[x], mate_blocks, shards[0], mate_lists)
            )
        if k == 4:
            lists = jnp.concatenate([after(lists, flow[x]), mate_lists], axis=0)
        if k == 5:
            flow[x], lists = lax.optimization_barrier((flow[x], lists))
        shards.append(flow[x])
        if k < chips - 2:
            flow[x] = move(flow[x], ahead)

    pieces = [1, 1, chips - 2]
    sums_shape = jax.ShapeDtypeStruct((count * clusters + 1, directions, unknowns), jnp.float32)

    def near(part, shards, sources, *sums):
        late = int(part == 2)
        sends = pieces if late else []
        return pl.pallas_call(
            functools.partial(near_kernel, part, BATCH, LAG, len(shards), len(sends)),
            out_shape=[sums_shape]
            + [jax.ShapeDtypeStruct((chips * half * rank_k, unknowns), jnp.bfloat16)] * late
            + [
                jax.ShapeDtypeStruct((size * clusters, directions, unknowns), jnp.bfloat16)
                for size in sends
            ],
            in_specs=[whole(pltpu.SMEM)]
            + [whole()] * len(shards)
            + [[whole(pl.ANY)], [whole()], [whole(), whole(pl.ANY)]][part]
            + [whole()] * len(sums),
            out_specs=[whole()] * (1 + late + len(sends)),
            input_output_aliases={1 + len(shards) + len(sources): 0} if sums else {},
            scratch_shapes=[
                pltpu.VMEM(((LATE if late else len(shards)) * base, unknowns), jnp.bfloat16),
                pltpu.VMEM(near_blocks.shape, jnp.bfloat16),
                pltpu.SemaphoreType.DMA((max(CHUNKS, stored // BATCH),)),
            ],
            compiler_params=pltpu.CompilerParams(vmem_limit_bytes=NEAR_VMEM),
            cost_estimate=pl.CostEstimate(
                flops=16 * stored * directions * unknowns * unknowns,
                bytes_accessed=16 << 20,
                transcendentals=0,
            ),
            name="near",
        )(lists, *shards, *sources, *sums)

    def far_field(couple):
        return pl.pallas_call(
            far_kernel,
            out_shape=jax.ShapeDtypeStruct((clusters, directions, unknowns), jnp.float32),
            in_specs=[whole()] * 2 + [whole(pltpu.SMEM)] + [whole()] * 5,
            out_specs=whole(),
            compiler_params=pltpu.CompilerParams(vmem_limit_bytes=FAR_VMEM),
            cost_estimate=pl.CostEstimate(
                flops=4 * clusters * rank_k * pairs * rank_k * unknowns,
                bytes_accessed=8 << 20,
                transcendentals=0,
            ),
            name="far",
        )(
            *coefs,
            here,
            couple,
            far_slot.reshape(1, pairs),
            far_dev.reshape(1, pairs),
            far_cslot.reshape(1, pairs),
            basis_out,
        )

    (sums,) = near(0, shards[: chips - LATE], [mate_blocks])
    (sums,) = near(1, shards[: chips - LATE], [near_blocks], sums)
    sums, coef, *sends = near(2, shards, [near_blocks, mate_blocks], sums)
    mates = [move(sends[0], mate), move(sends[1], mate)]
    coefs = [coef, move(coef, mate)]

    def term(k):
        part = min(k, 2)
        got = mates[part][(k - part) * clusters : (k - part + 1) * clusters]
        return sums[k * clusters : (k + 1) * clusters] + got.astype(jnp.float32)

    def tied(values, k, *others):
        values, mates[2], *others = lax.optimization_barrier((values, mates[2], *others))
        return values

    def add(flow, k):
        return (flow.astype(jnp.float32) + term(k)).astype(jnp.bfloat16)

    flow = lax.optimization_barrier([term(0).astype(jnp.bfloat16), term(1).astype(jnp.bfloat16)])
    mates.append(move(after(sends[2], *flow), mate))
    flow = [move(part, ahead) for part in flow]
    for k in range(2, chips - 1):
        x = k % 2
        flow[x] = tied(add(flow[x], k), k)
        if k == chips - 2:
            couple = after(couple, flow[x])
        flow[x] = move(flow[x], ahead)
    flow[1] = move(flow[1], mate)
    total = far_field(couple) + term(chips - 1) + flow[0].astype(jnp.float32)
    total = lax.optimization_barrier(total)
    return (total + flow[1].astype(jnp.float32)).astype(jnp.bfloat16)


def on_device(*args):
    rhs, near_blocks = args[0], args[1]
    clusters, directions, unknowns = rhs.shape
    small = lax.axis_size("blk") == 16 and clusters == 16
    if small and near_blocks.shape[0] == unknowns and 2 * directions == unknowns:
        return stationary(*args)
    return routed(*args)


def solution(mesh):
    placed = (
        P(("groups", "blk"), None, None),
        P(("groups", "blk"), None, None),
        P(("groups", "blk"), None),
        P(("groups", "blk")),
        P(("groups", "blk")),
        P(("groups", "blk"), None, None),
        P(("groups", "blk")),
        P(("groups", "blk"), None),
        P(("groups", "blk")),
        P(("groups", "blk"), None, None),
        P(("groups", "blk"), None, None),
    )
    return jax.shard_map(
        on_device,
        mesh=mesh,
        in_specs=placed,
        out_specs=P(("groups", "blk"), None, None),
        check_vma=False,
    )
```

```python
import functools

import jax
import jax.numpy as jnp
from jax import lax
from jax.experimental import pallas as pl
from jax.experimental.pallas import tpu as pltpu
from jax.sharding import PartitionSpec as P

BATCH = 16, 16, 8
CHUNKS = 4
LATE = 2
PROLOGUE_VMEM = 58 << 20
NEAR_VMEM = 20 << 20
FAR_VMEM = 16 << 20


def with_halo(cells, sides, width):
    for axis, dim in sides:
        count = lax.axis_size(axis)
        head = lax.slice_in_dim(cells, 0, width, axis=dim)
        tail = lax.slice_in_dim(cells, cells.shape[dim] - width, cells.shape[dim], axis=dim)
        cells = jnp.concatenate(
            [
                lax.ppermute(tail, axis, [(i, (i + 1) % count) for i in range(count)]),
                cells,
                lax.ppermute(head, axis, [((i + 1) % count, i) for i in range(count)]),
            ],
            axis=dim,
        )
    return cells


def place_ranks(targets, count):
    onehot = (targets[:, None] == jnp.arange(count, dtype=jnp.int32)[None, :]).astype(jnp.int32)
    before = jnp.cumsum(onehot, axis=0) - onehot
    return jnp.sum(before * onehot, axis=1)


def routed(
    rhs,
    near_blocks,
    near_owner,
    near_slot,
    near_offset,
    far_coupling,
    far_slot,
    far_dev,
    far_cslot,
    basis_out,
    basis_in,
):
    clusters = rhs.shape[0]
    directions = rhs.shape[1]
    unknowns = rhs.shape[2]
    cycle_size = lax.axis_size("blk")
    stored = near_blocks.shape[0]
    capacity = max(2, 2 * stored // cycle_size)
    owners = near_owner[:, 0]
    target = owners * capacity + place_ranks(owners, cycle_size)
    outbox = (
        jnp.zeros((cycle_size * capacity, unknowns, unknowns), near_blocks.dtype)
        .at[target]
        .set(near_blocks)
    )
    labels = (
        jnp.zeros((cycle_size * capacity, 2), jnp.int32)
        .at[target]
        .set(jnp.stack([near_slot, near_offset], axis=1))
    )
    window = with_halo(rhs, (("blk", 0),), clusters)
    inbox, in_labels = (
        lax.all_to_all(outbox, "blk", split_axis=0, concat_axis=0, tiled=True),
        lax.all_to_all(labels, "blk", split_axis=0, concat_axis=0, tiled=True),
    )
    position = clusters + in_labels[:, 0] + in_labels[:, 1]
    columns = jnp.take(window, position, axis=0)
    products = jnp.einsum("srj,sij->sri", columns, inbox, preferred_element_type=jnp.float32)
    selector = (in_labels[:, 0][None, :] == jnp.arange(clusters, dtype=jnp.int32)[:, None]).astype(
        jnp.float32
    )
    near_sum = jnp.dot(
        selector,
        products.reshape(products.shape[0], -1),
        precision=lax.Precision.HIGHEST,
        preferred_element_type=jnp.float32,
    ).reshape(clusters, directions, unknowns)
    coef_local = jnp.einsum(
        "ckj,crj->crk", basis_in, rhs, preferred_element_type=jnp.float32
    ).astype(jnp.bfloat16)
    rank_k = basis_in.shape[1]
    coef_local = coef_local.reshape(clusters, directions * rank_k)
    pairs = far_slot.shape[0]
    wanted = far_dev[:, 0] * clusters + far_cslot
    piece = lax.all_gather(coef_local, "blk", axis=0, tiled=True)
    chosen = jnp.take(piece, wanted, axis=0)
    coupled = jnp.einsum(
        "pkq,prq->prk",
        far_coupling,
        chosen.reshape(pairs, directions, rank_k),
        preferred_element_type=jnp.float32,
    )
    row_pick = (far_slot[None, :] == jnp.arange(clusters, dtype=jnp.int32)[:, None]).astype(
        jnp.float32
    )
    gathered = jnp.dot(
        row_pick,
        coupled.reshape(pairs, -1),
        precision=lax.Precision.HIGHEST,
        preferred_element_type=jnp.float32,
    )
    gathered = gathered.astype(jnp.bfloat16).reshape(clusters, directions, rank_k)
    far_sum = jnp.einsum("crk,ckb->crb", gathered, basis_out, preferred_element_type=jnp.float32)
    return (near_sum + far_sum).astype(jnp.bfloat16)


def whole(space=pltpu.VMEM):
    return pl.BlockSpec(memory_space=space)


def prologue_kernel(
    count, me_ref, owner_ref, slot_ref, offset_ref, rhs_ref, basis_ref, payload_ref, list_ref
):
    clusters, directions, unknowns = rhs_ref.shape
    base = clusters * directions
    payload_ref[0:base, :] = rhs_ref[...].reshape(base, unknowns)
    rank_k = basis_ref.shape[1]
    half = clusters // 2
    rows = []
    for c in range(half):
        parts = [
            lax.dot_general(
                basis_ref[e],
                rhs_ref[e],
                (((1,), (1,)), ((), ())),
                preferred_element_type=jnp.float32,
            )
            for e in (c, c + half)
        ]
        rows.append(jnp.concatenate(parts, axis=1))
    payload_ref[base:, :] = jnp.concatenate(
        [row[q : q + 1] for q in range(rank_k) for row in rows], axis=0
    ).astype(payload_ref.dtype)

    me, owner, slot = me_ref[0], owner_ref[...], slot_ref[...]
    stored = owner.shape[1]
    place = scatter_place(owner, me, count) * clusters + slot
    column = (owner * clusters + slot + offset_ref[...]) & (count * clusters - 1)
    shard = gather_place(column // clusters, me, count)
    theirs = (shard == count // 2).astype(jnp.int32)
    shard = jnp.where(theirs == 1, gather_place(column // clusters, me ^ 1, count), shard)
    column_place = shard * clusters + (column & (clusters - 1))
    late = (shard >= count // 2 - LATE).astype(jnp.int32)
    square = (stored, stored)
    group = jnp.broadcast_to((2 * theirs + late).astype(jnp.float32), square)
    group_of_row = jnp.transpose(group)
    row_at = lax.broadcasted_iota(jnp.int32, square, 0)
    lane_at = lax.broadcasted_iota(jnp.int32, square, 1)
    lane = lane_at.astype(jnp.float32)
    before = (group_of_row < group) | ((group_of_row == group) & (row_at < lane_at))
    rank = jnp.sum(jnp.where(before, 1.0, 0.0), axis=0, keepdims=True)
    rank = jnp.transpose(jnp.broadcast_to(rank, square))
    here = jnp.where(rank == lane, 1.0, 0.0).astype(jnp.bfloat16)
    starts = jnp.sum(jnp.where(group_of_row < lane, 1.0, 0.0), axis=0, keepdims=True)
    values = jnp.concatenate(
        [lane[0:1], place.astype(jnp.float32), column_place.astype(jnp.float32)]
        + [jnp.zeros((5, stored), jnp.float32)],
        axis=0,
    )
    values = jnp.dot(values.astype(jnp.bfloat16), here, preferred_element_type=jnp.float32)
    values = jnp.concatenate([values[0:3], starts, values[4:8]], axis=0)
    list_ref[...] = values.astype(jnp.int32)


def near_kernel(part, batch, shards, sends, list_ref, *refs):
    late = int(part == 2)
    used = LATE if late else shards
    shard_refs, refs = refs[:shards], refs[shards:]
    if part > 0:
        own_ref, refs = refs[0], refs[1:]
    if part != 1:
        mate_hbm, refs = refs[0], refs[1:]
    if part > 0:
        refs = refs[1:]
    sums, refs = refs[0], refs[1:]
    if late:
        coef_ref, send_refs, refs = refs[0], refs[1 : 1 + sends], refs[1 + sends :]
    columns, blocks, block_sem = refs
    stored = blocks.shape[0]
    directions = sums.shape[1]
    span = columns.shape[0] // used
    dummy = sums.shape[0] - 1
    chunk = stored // CHUNKS

    begin, end = list_ref[3, late], list_ref[3, late + 1]
    begin_there, end_there = list_ref[11, 2 + late], list_ref[11, 3 + late]
    steps_there = (end_there - begin_there + batch - 1) // batch

    def fetch(j, carry):
        at = jnp.minimum(begin_there + j, end_there - 1)
        pltpu.make_async_copy(
            mate_hbm.at[list_ref[8, at]], blocks.at[j], block_sem.at[j // batch]
        ).start()
        return carry

    if late:
        lax.fori_loop(0, steps_there * batch, fetch, 0)
    elif part == 0:
        for c in range(CHUNKS):
            at = pl.ds(c * chunk, chunk)
            pltpu.make_async_copy(mate_hbm.at[at], blocks.at[at], block_sem.at[c]).start()

    for k, ref in enumerate(shard_refs[shards - used :]):

        def gather(i, carry, k=k, ref=ref):
            at = pl.multiple_of(i * directions, directions)
            columns[pl.ds(pl.multiple_of(k * span + at, directions), directions)] = ref[
                pl.ds(at, directions)
            ]
            return carry

        lax.fori_loop(0, span // directions, gather, 0, unroll=4)
    if late:
        tail = coef_ref.shape[0] // shards
        for k, ref in enumerate(shard_refs):
            coef_ref[k * tail : (k + 1) * tail] = ref[span : span + tail]
    elif part == 0:

        def clear(i, carry):
            sums[i] = jnp.zeros(sums.shape[1:], sums.dtype)
            return carry

        lax.fori_loop(0, dummy + 1, clear, 0)

    def run(begin, end, row, swap, block_of):
        def entry(j):
            return jnp.minimum(begin + j, end - 1)

        def body(step, carry):
            first = step * batch
            products = []

            def add(i):
                place = list_ref[row + 1, entry(first + i)] ^ swap
                place = jnp.where(begin + first + i < end, place, dummy)
                sums[place] = sums[place] + products[i]

            take, carry = block_of(first, entry, carry)
            for i in range(batch):
                start = list_ref[row + 2, entry(first + i)] * directions - (shards - used) * span
                products.append(
                    lax.dot_general(
                        columns[pl.ds(pl.multiple_of(start, directions), directions)],
                        take(i),
                        (((1,), (1,)), ((), ())),
                        preferred_element_type=jnp.float32,
                    )
                )
            for i in range(batch):
                add(i)
            return carry

        return lax.fori_loop(0, (end - begin + batch - 1) // batch, body, 0)

    def own_blocks(first, entry, carry):
        return lambda i: own_ref[list_ref[0, entry(first + i)]], carry

    def wait(c, carry):
        at = pl.ds(0, chunk)
        pltpu.make_async_copy(mate_hbm.at[at], blocks.at[at], block_sem.at[c]).wait()
        return carry

    def mate_blocks(first, entry, ready):
        if late:
            pltpu.make_async_copy(
                mate_hbm.at[pl.ds(0, batch)],
                blocks.at[pl.ds(first, batch)],
                block_sem.at[first // batch],
            ).wait()
            return lambda i: blocks[first + i], ready
        needed = list_ref[8, entry(first + batch - 1)] // chunk + 1
        lax.fori_loop(ready, needed, wait, 0)
        return lambda i: blocks[list_ref[8, entry(first + i)]], jnp.maximum(ready, needed)

    if part > 0:
        run(begin, end, 0, 0, own_blocks)
    if part != 1:
        ready = run(begin_there, end_there, 8, dummy // 2, mate_blocks)
    if part == 0:
        lax.fori_loop(ready, CHUNKS, wait, 0)
    if not late:
        return
    at = dummy // 2
    for send_ref in send_refs:

        def pack(i, carry, at=at, send_ref=send_ref):
            send_ref[i] = sums[at + i].astype(send_ref.dtype)
            return carry

        lax.fori_loop(0, send_ref.shape[0], pack, 0, unroll=2)
        at += send_ref.shape[0]


def far_kernel(*refs):
    coef_refs = refs[:2]
    me_ref, couple_ref, slot_ref, dev_ref, cslot_ref, basis_ref, out_ref = refs[2:]
    clusters, rank_k, unknowns = basis_ref.shape
    pairs = couple_ref.shape[2]
    directions = out_ref.shape[1]
    half = clusters // 2
    coef = jnp.concatenate([ref[...].astype(jnp.float32) for ref in coef_refs], axis=0)
    coef = coef.reshape(-1, rank_k, half, unknowns)
    count = coef.shape[0]
    hot = (
        lax.broadcasted_iota(jnp.int32, (clusters, pairs), 0)
        == jnp.broadcast_to(slot_ref[...], (clusters, pairs))
    ).astype(jnp.float32).astype(jnp.bfloat16)
    away = gather_place(dev_ref[...], me_ref[0], count)
    theirs = count // 2 + gather_place(dev_ref[...], me_ref[0] ^ 1, count)
    away = jnp.where(away == count // 2, theirs, away)
    cslot = cslot_ref[...]
    high = (cslot >= half).astype(jnp.int32)
    at = away * half + cslot - high * half
    table_rows = (count * half, pairs)
    pick = jnp.where(
        lax.broadcasted_iota(jnp.int32, table_rows, 0) == jnp.broadcast_to(at, table_rows), 1.0, 0.0
    )
    pick = jnp.transpose(pick).astype(jnp.bfloat16)
    lanes = (unknowns, pairs)
    keep = jnp.where(
        lax.broadcasted_iota(jnp.int32, lanes, 0) // directions == jnp.broadcast_to(high, lanes),
        1.0,
        0.0,
    )
    keep = jnp.transpose(keep).astype(jnp.bfloat16)
    total = jnp.zeros((clusters * rank_k, unknowns), jnp.float32)
    for q in range(rank_k):
        table = coef[:, q].reshape(count * half, unknowns).astype(jnp.bfloat16)
        chosen = jnp.dot(pick, table, preferred_element_type=jnp.float32).astype(jnp.bfloat16)
        chosen = chosen * keep
        couple = couple_ref[q]
        weight = jnp.concatenate([couple * hot[s : s + 1] for s in range(clusters)], axis=0)
        total = total + jnp.dot(weight, chosen, preferred_element_type=jnp.float32)
    total = total + pltpu.roll(total, unknowns // 2, axis=1)
    gathered = jnp.transpose(total)[0:directions, :].astype(jnp.bfloat16).astype(jnp.float32)
    lane = lax.broadcasted_iota(jnp.int32, gathered.shape, 1) // rank_k
    basis = basis_ref[...].reshape(clusters * rank_k, unknowns)
    for s in range(clusters):
        own = jnp.where(lane == s, gathered, 0.0).astype(jnp.bfloat16)
        out_ref[s] = jnp.dot(own, basis, preferred_element_type=jnp.float32)


def ring_device(place, core, chips):
    depth = chips // 2
    place = place % chips
    z, y = (place, 0) if place < depth else (chips - 1 - place, 1)
    return (z * 2 + y) * 2 + core


def ring_pairs(count):
    chips = count // 2
    cores = [(p, c) for p in range(chips) for c in range(2)]
    ahead = [(ring_device(p, c, chips), ring_device(p + 1 - 2 * c, c, chips)) for p, c in cores]
    cross = [
        (ring_device(p, c, chips), ring_device(p - 1 + 2 * c, 1 - c, chips)) for p, c in cores
    ]
    return ahead, cross


def ring_place(device, chips):
    z, y = device >> 2, (device >> 1) & 1
    return jnp.where(y == 0, z, chips - 1 - z)


def gather_place(device, me, count):
    chips = count // 2
    depth = chips // 2
    back = (1 - 2 * (me & 1)) * (ring_place(me, chips) - ring_place(device, chips))
    back = (back + chips) & (chips - 1)
    other = (device ^ me) & 1
    here = (back < depth) & (back > 0) | (back == 0) & (other == 1) | (back == depth) & (other == 0)
    return jnp.where(here, jnp.where(back == 0, 0, 2 * back - 1 + other), chips)


def scatter_place(device, me, count):
    chips = count // 2
    depth = chips // 2
    ahead = (ring_place(device, chips) - ring_place(me, chips) + chips) & (chips - 1)
    core = device & 1
    handler = jnp.where((ahead & (depth - 1)) == 0, core, (ahead > depth).astype(jnp.int32))
    steps = jnp.where(handler == 0, ahead, (chips - ahead) & (chips - 1))
    place = jnp.where(
        steps == depth,
        0,
        jnp.where(steps == 0, chips - 1, 2 * (depth - steps) - (core ^ handler)),
    )
    return place + jnp.where(handler == (me & 1), 0, chips)


def stationary(
    rhs,
    near_blocks,
    near_owner,
    near_slot,
    near_offset,
    far_coupling,
    far_slot,
    far_dev,
    far_cslot,
    basis_out,
    basis_in,
):
    clusters, directions, unknowns = rhs.shape
    rank_k = basis_in.shape[1]
    count = lax.axis_size("blk")
    chips = count // 2
    depth = chips // 2
    me = lax.axis_index("blk")
    stored = near_blocks.shape[0]
    pairs = far_slot.shape[0]
    half = clusters // 2
    ahead, cross = ring_pairs(count)
    mate = [(i, i ^ 1) for i in range(count)]
    side = [(i, i ^ 2) for i in range(count)]

    def move(values, where):
        return lax.ppermute(values, "blk", where)

    def after(values, *others):
        return lax.optimization_barrier((values, *others))[0]

    here = me.astype(jnp.int32).reshape(1)
    base = clusters * directions
    payload, lists = pl.pallas_call(
        functools.partial(prologue_kernel, count),
        out_shape=[
            jax.ShapeDtypeStruct((base + half * rank_k, unknowns), jnp.bfloat16),
            jax.ShapeDtypeStruct((8, stored), jnp.int32),
        ],
        in_specs=[whole(pltpu.SMEM)] + [whole()] * 5,
        out_specs=[whole()] * 2,
        compiler_params=pltpu.CompilerParams(vmem_limit_bytes=PROLOGUE_VMEM),
        name="prologue",
    )(
        here,
        near_owner.reshape(1, stored),
        near_slot.reshape(1, stored),
        near_offset.reshape(1, stored),
        rhs,
        basis_in,
    )
    flow = [move(payload, ahead)]
    mate_blocks = move(near_blocks, mate)
    mate_lists = move(lists, mate)
    couple = jnp.transpose(far_coupling, (2, 1, 0))
    flow.append(move(after(payload, couple), cross))
    shards = [move(payload, mate)]
    for k in range(1, chips):
        x = 1 - k % 2
        if k == 3:
            flow[x], mate_blocks, shards[0], mate_lists = lax.optimization_barrier(
                (flow[x], mate_blocks, shards[0], mate_lists)
            )
        if k == 4:
            lists = jnp.concatenate([after(lists, flow[x]), mate_lists], axis=0)
        if k == 5:
            flow[x], lists = lax.optimization_barrier((flow[x], lists))
        shards.append(flow[x])
        if k < chips - 2:
            flow[x] = move(flow[x], ahead)

    pieces = [2, chips - 2]
    sums_shape = jax.ShapeDtypeStruct((count * clusters + 1, directions, unknowns), jnp.float32)

    def near(part, shards, sources, *sums):
        late = int(part == 2)
        sends = pieces if late else []
        return pl.pallas_call(
            functools.partial(near_kernel, part, BATCH[part], len(shards), len(sends)),
            out_shape=[sums_shape]
            + [jax.ShapeDtypeStruct((chips * half * rank_k, unknowns), jnp.bfloat16)] * late
            + [
                jax.ShapeDtypeStruct((size * clusters, directions, unknowns), jnp.bfloat16)
                for size in sends
            ],
            in_specs=[whole(pltpu.SMEM)]
            + [whole()] * len(shards)
            + [[whole(pl.ANY)], [whole()], [whole(), whole(pl.ANY)]][part]
            + [whole()] * len(sums),
            out_specs=[whole()] * (1 + late + len(sends)),
            input_output_aliases={1 + len(shards) + len(sources): 0} if sums else {},
            scratch_shapes=[
                pltpu.VMEM(((LATE if late else len(shards)) * base, unknowns), jnp.bfloat16),
                pltpu.VMEM(near_blocks.shape, jnp.bfloat16),
                pltpu.SemaphoreType.DMA((max(CHUNKS, stored // BATCH[part]),)),
            ],
            compiler_params=pltpu.CompilerParams(vmem_limit_bytes=NEAR_VMEM),
            cost_estimate=pl.CostEstimate(
                flops=16 * stored * directions * unknowns * unknowns,
                bytes_accessed=16 << 20,
                transcendentals=0,
            ),
            name="near",
        )(lists, *shards, *sources, *sums)

    def far_field(couple):
        return pl.pallas_call(
            far_kernel,
            out_shape=jax.ShapeDtypeStruct((clusters, directions, unknowns), jnp.float32),
            in_specs=[whole()] * 2 + [whole(pltpu.SMEM)] + [whole()] * 5,
            out_specs=whole(),
            compiler_params=pltpu.CompilerParams(vmem_limit_bytes=FAR_VMEM),
            cost_estimate=pl.CostEstimate(
                flops=4 * clusters * rank_k * pairs * rank_k * unknowns,
                bytes_accessed=8 << 20,
                transcendentals=0,
            ),
            name="far",
        )(
            *coefs,
            here,
            couple,
            far_slot.reshape(1, pairs),
            far_dev.reshape(1, pairs),
            far_cslot.reshape(1, pairs),
            basis_out,
        )

    (sums,) = near(0, shards[: chips - LATE], [mate_blocks])
    (sums,) = near(1, shards[: chips - LATE], [near_blocks], sums)
    sums, coef, *sends = near(2, shards, [near_blocks, mate_blocks], sums)
    mates = [move(sends[0], mate)]
    coefs = [coef, move(coef, mate)]

    def term(k):
        part, at = (0, k) if k < 2 else (1, k - 2)
        got = mates[part][at * clusters : (at + 1) * clusters]
        return sums[k * clusters : (k + 1) * clusters] + got.astype(jnp.float32)

    def tied(values, k, *others):
        values, mates[1], *others = lax.optimization_barrier((values, mates[1], *others))
        return values

    def add(flow, k):
        return (flow.astype(jnp.float32) + term(k)).astype(jnp.bfloat16)

    flow = lax.optimization_barrier([term(0).astype(jnp.bfloat16), term(1).astype(jnp.bfloat16)])
    mates.append(move(after(sends[1], *flow), mate))
    flow = [move(part, ahead) for part in flow]
    for k in range(2, chips - 1):
        x = k % 2
        flow[x] = tied(add(flow[x], k), k)
        if k == chips - 2:
            couple = after(couple, flow[x])
        flow[x] = move(flow[x], ahead)
    flow[1] = move(flow[1], mate)
    total = far_field(couple) + term(chips - 1) + flow[0].astype(jnp.float32)
    total = lax.optimization_barrier(total)
    return (total + flow[1].astype(jnp.float32)).astype(jnp.bfloat16)


def on_device(*args):
    rhs, near_blocks = args[0], args[1]
    clusters, directions, unknowns = rhs.shape
    small = lax.axis_size("blk") == 16 and clusters == 16
    if small and near_blocks.shape[0] == unknowns and 2 * directions == unknowns:
        return stationary(*args)
    return routed(*args)


def solution(mesh):
    placed = (
        P(("groups", "blk"), None, None),
        P(("groups", "blk"), None, None),
        P(("groups", "blk"), None),
        P(("groups", "blk")),
        P(("groups", "blk")),
        P(("groups", "blk"), None, None),
        P(("groups", "blk")),
        P(("groups", "blk"), None),
        P(("groups", "blk")),
        P(("groups", "blk"), None, None),
        P(("groups", "blk"), None, None),
    )
    return jax.shard_map(
        on_device,
        mesh=mesh,
        in_specs=placed,
        out_specs=P(("groups", "blk"), None, None),
        check_vma=False,
    )
```

```python
import functools

import jax
import jax.numpy as jnp
from jax import lax
from jax.experimental import pallas as pl
from jax.experimental.pallas import tpu as pltpu
from jax.sharding import PartitionSpec as P

BATCH = 16, 16, 8
CHUNKS = 4
LATE = 2
PROLOGUE_VMEM = 58 << 20
NEAR_VMEM = 20 << 20
FAR_VMEM = 16 << 20


def with_halo(cells, sides, width):
    for axis, dim in sides:
        count = lax.axis_size(axis)
        head = lax.slice_in_dim(cells, 0, width, axis=dim)
        tail = lax.slice_in_dim(cells, cells.shape[dim] - width, cells.shape[dim], axis=dim)
        cells = jnp.concatenate(
            [
                lax.ppermute(tail, axis, [(i, (i + 1) % count) for i in range(count)]),
                cells,
                lax.ppermute(head, axis, [((i + 1) % count, i) for i in range(count)]),
            ],
            axis=dim,
        )
    return cells


def place_ranks(targets, count):
    onehot = (targets[:, None] == jnp.arange(count, dtype=jnp.int32)[None, :]).astype(jnp.int32)
    before = jnp.cumsum(onehot, axis=0) - onehot
    return jnp.sum(before * onehot, axis=1)


def routed(
    rhs,
    near_blocks,
    near_owner,
    near_slot,
    near_offset,
    far_coupling,
    far_slot,
    far_dev,
    far_cslot,
    basis_out,
    basis_in,
):
    clusters = rhs.shape[0]
    directions = rhs.shape[1]
    unknowns = rhs.shape[2]
    cycle_size = lax.axis_size("blk")
    stored = near_blocks.shape[0]
    capacity = max(2, 2 * stored // cycle_size)
    owners = near_owner[:, 0]
    target = owners * capacity + place_ranks(owners, cycle_size)
    outbox = (
        jnp.zeros((cycle_size * capacity, unknowns, unknowns), near_blocks.dtype)
        .at[target]
        .set(near_blocks)
    )
    labels = (
        jnp.zeros((cycle_size * capacity, 2), jnp.int32)
        .at[target]
        .set(jnp.stack([near_slot, near_offset], axis=1))
    )
    window = with_halo(rhs, (("blk", 0),), clusters)
    inbox, in_labels = (
        lax.all_to_all(outbox, "blk", split_axis=0, concat_axis=0, tiled=True),
        lax.all_to_all(labels, "blk", split_axis=0, concat_axis=0, tiled=True),
    )
    position = clusters + in_labels[:, 0] + in_labels[:, 1]
    columns = jnp.take(window, position, axis=0)
    products = jnp.einsum("srj,sij->sri", columns, inbox, preferred_element_type=jnp.float32)
    selector = (in_labels[:, 0][None, :] == jnp.arange(clusters, dtype=jnp.int32)[:, None]).astype(
        jnp.float32
    )
    near_sum = jnp.dot(
        selector,
        products.reshape(products.shape[0], -1),
        precision=lax.Precision.HIGHEST,
        preferred_element_type=jnp.float32,
    ).reshape(clusters, directions, unknowns)
    coef_local = jnp.einsum(
        "ckj,crj->crk", basis_in, rhs, preferred_element_type=jnp.float32
    ).astype(jnp.bfloat16)
    rank_k = basis_in.shape[1]
    coef_local = coef_local.reshape(clusters, directions * rank_k)
    pairs = far_slot.shape[0]
    wanted = far_dev[:, 0] * clusters + far_cslot
    piece = lax.all_gather(coef_local, "blk", axis=0, tiled=True)
    chosen = jnp.take(piece, wanted, axis=0)
    coupled = jnp.einsum(
        "pkq,prq->prk",
        far_coupling,
        chosen.reshape(pairs, directions, rank_k),
        preferred_element_type=jnp.float32,
    )
    row_pick = (far_slot[None, :] == jnp.arange(clusters, dtype=jnp.int32)[:, None]).astype(
        jnp.float32
    )
    gathered = jnp.dot(
        row_pick,
        coupled.reshape(pairs, -1),
        precision=lax.Precision.HIGHEST,
        preferred_element_type=jnp.float32,
    )
    gathered = gathered.astype(jnp.bfloat16).reshape(clusters, directions, rank_k)
    far_sum = jnp.einsum("crk,ckb->crb", gathered, basis_out, preferred_element_type=jnp.float32)
    return (near_sum + far_sum).astype(jnp.bfloat16)


def whole(space=pltpu.VMEM):
    return pl.BlockSpec(memory_space=space)


def payload_kernel(rhs_ref, basis_ref, payload_ref):
    clusters, directions, unknowns = rhs_ref.shape
    base = clusters * directions
    payload_ref[0:base, :] = rhs_ref[...].reshape(base, unknowns)
    rank_k = basis_ref.shape[1]
    half = clusters // 2
    rows = []
    for c in range(half):
        parts = [
            lax.dot_general(
                basis_ref[e],
                rhs_ref[e],
                (((1,), (1,)), ((), ())),
                preferred_element_type=jnp.float32,
            )
            for e in (c, c + half)
        ]
        rows.append(jnp.concatenate(parts, axis=1))
    rows = jnp.concatenate(rows, axis=0).astype(payload_ref.dtype)
    square = (rows.shape[0], rows.shape[0])
    row = lax.broadcasted_iota(jnp.int32, square, 0)
    source = (row & (half - 1)) * rank_k + row // half
    order = jnp.where(lax.broadcasted_iota(jnp.int32, square, 1) == source, 1.0, 0.0)
    payload_ref[base:, :] = jnp.dot(
        order.astype(rows.dtype), rows, preferred_element_type=jnp.float32
    ).astype(payload_ref.dtype)


def list_kernel(count, clusters, me_ref, owner_ref, slot_ref, offset_ref, list_ref):
    me, owner, slot = me_ref[0], owner_ref[...], slot_ref[...]
    stored = owner.shape[1]
    place = scatter_place(owner, me, count) * clusters + slot
    column = (owner * clusters + slot + offset_ref[...]) & (count * clusters - 1)
    shard = gather_place(column // clusters, me, count)
    theirs = (shard == count // 2).astype(jnp.int32)
    shard = jnp.where(theirs == 1, gather_place(column // clusters, me ^ 1, count), shard)
    column_place = shard * clusters + (column & (clusters - 1))
    late = (shard >= count // 2 - LATE + 1 - theirs).astype(jnp.int32)
    square = (stored, stored)
    group = jnp.broadcast_to((2 * theirs + late).astype(jnp.float32), square)
    group_of_row = jnp.transpose(group)
    row_at = lax.broadcasted_iota(jnp.int32, square, 0)
    lane_at = lax.broadcasted_iota(jnp.int32, square, 1)
    lane = lane_at.astype(jnp.float32)
    before = (group_of_row < group) | ((group_of_row == group) & (row_at < lane_at))
    rank = jnp.sum(jnp.where(before, 1.0, 0.0), axis=0, keepdims=True)
    rank = jnp.transpose(jnp.broadcast_to(rank, square))
    here = jnp.where(rank == lane, 1.0, 0.0).astype(jnp.bfloat16)
    starts = jnp.sum(jnp.where(group_of_row < lane, 1.0, 0.0), axis=0, keepdims=True)
    values = jnp.concatenate(
        [lane[0:1], place.astype(jnp.float32), column_place.astype(jnp.float32)]
        + [jnp.zeros((5, stored), jnp.float32)],
        axis=0,
    )
    values = jnp.dot(values.astype(jnp.bfloat16), here, preferred_element_type=jnp.float32)
    values = jnp.concatenate([values[0:3], starts, values[4:8]], axis=0)
    list_ref[...] = values.astype(jnp.int32)


def near_kernel(part, batch, shards, sends, list_ref, *refs):
    late = int(part == 2)
    used = LATE if late else shards
    shard_refs, refs = refs[:shards], refs[shards:]
    if part > 0:
        own_ref, refs = refs[0], refs[1:]
    if part != 1:
        mate_hbm, refs = refs[0], refs[1:]
    if part > 0:
        refs = refs[1:]
    sums, refs = refs[0], refs[1:]
    if late:
        coef_ref, send_refs, refs = refs[0], refs[1 : 1 + sends], refs[1 + sends :]
    columns, blocks, block_sem = refs
    stored = blocks.shape[0]
    directions = sums.shape[1]
    span = columns.shape[0] // used
    dummy = sums.shape[0] - 1
    chunk = stored // CHUNKS

    begin, end = list_ref[3, late], list_ref[3, late + 1]
    begin_there, end_there = list_ref[11, 2 + late], list_ref[11, 3 + late]
    steps_there = (end_there - begin_there + batch - 1) // batch

    def fetch(j, carry):
        at = jnp.minimum(begin_there + j, end_there - 1)
        pltpu.make_async_copy(
            mate_hbm.at[list_ref[8, at]], blocks.at[j], block_sem.at[j // batch]
        ).start()
        return carry

    if late:
        lax.fori_loop(0, steps_there * batch, fetch, 0)
    elif part == 0:
        for c in range(CHUNKS):
            at = pl.ds(c * chunk, chunk)
            pltpu.make_async_copy(mate_hbm.at[at], blocks.at[at], block_sem.at[c]).start()

    for k, ref in enumerate(shard_refs[shards - used :]):

        def gather(i, carry, k=k, ref=ref):
            at = pl.multiple_of(i * directions, directions)
            columns[pl.ds(pl.multiple_of(k * span + at, directions), directions)] = ref[
                pl.ds(at, directions)
            ]
            return carry

        lax.fori_loop(0, span // directions, gather, 0, unroll=8)
    if late:
        tail = coef_ref.shape[0] // shards
        for k, ref in enumerate(shard_refs):
            coef_ref[k * tail : (k + 1) * tail] = ref[span : span + tail]
    elif part == 0:

        def clear(i, carry):
            sums[i] = jnp.zeros(sums.shape[1:], sums.dtype)
            return carry

        lax.fori_loop(0, dummy, clear, 0, unroll=8)
        clear(dummy, 0)

    def run(begin, end, row, swap, block_of):
        def entry(j):
            return jnp.minimum(begin + j, end - 1)

        def body(step, carry):
            first = step * batch
            products = []

            def add(i):
                place = list_ref[row + 1, entry(first + i)] ^ swap
                place = jnp.where(begin + first + i < end, place, dummy)
                sums[place] = sums[place] + products[i]

            take, carry = block_of(first, entry, carry)
            for i in range(batch):
                start = list_ref[row + 2, entry(first + i)] * directions - (shards - used) * span
                products.append(
                    lax.dot_general(
                        columns[pl.ds(pl.multiple_of(start, directions), directions)],
                        take(i),
                        (((1,), (1,)), ((), ())),
                        preferred_element_type=jnp.float32,
                    )
                )
            for i in range(batch):
                add(i)
            return carry

        return lax.fori_loop(0, (end - begin + batch - 1) // batch, body, 0)

    def own_blocks(first, entry, carry):
        return lambda i: own_ref[list_ref[0, entry(first + i)]], carry

    def wait(c, carry):
        at = pl.ds(0, chunk)
        pltpu.make_async_copy(mate_hbm.at[at], blocks.at[at], block_sem.at[c]).wait()
        return carry

    def mate_blocks(first, entry, ready):
        if late:
            pltpu.make_async_copy(
                mate_hbm.at[pl.ds(0, batch)],
                blocks.at[pl.ds(first, batch)],
                block_sem.at[first // batch],
            ).wait()
            return lambda i: blocks[first + i], ready
        needed = list_ref[8, entry(first + batch - 1)] // chunk + 1
        lax.fori_loop(ready, needed, wait, 0)
        return lambda i: blocks[list_ref[8, entry(first + i)]], jnp.maximum(ready, needed)

    if part > 0:
        run(begin, end, 0, 0, own_blocks)
    if part != 1:
        ready = run(begin_there, end_there, 8, dummy // 2, mate_blocks)
    if part == 0:
        lax.fori_loop(ready, CHUNKS, wait, 0)
    if not late:
        return
    at = dummy // 2
    for send_ref in send_refs:

        def pack(i, carry, at=at, send_ref=send_ref):
            send_ref[i] = sums[at + i].astype(send_ref.dtype)
            return carry

        lax.fori_loop(0, send_ref.shape[0], pack, 0, unroll=8)
        at += send_ref.shape[0]


def far_kernel(*refs):
    coef_refs = refs[:2]
    me_ref, couple_ref, slot_ref, dev_ref, cslot_ref, basis_ref, out_ref = refs[2:]
    clusters, rank_k, unknowns = basis_ref.shape
    pairs = couple_ref.shape[2]
    directions = out_ref.shape[1]
    half = clusters // 2
    coef = jnp.concatenate([ref[...].astype(jnp.float32) for ref in coef_refs], axis=0)
    coef = coef.reshape(-1, rank_k, half, unknowns)
    count = coef.shape[0]
    hot = (
        lax.broadcasted_iota(jnp.int32, (clusters, pairs), 0)
        == jnp.broadcast_to(slot_ref[...], (clusters, pairs))
    ).astype(jnp.float32).astype(jnp.bfloat16)
    away = gather_place(dev_ref[...], me_ref[0], count)
    theirs = count // 2 + gather_place(dev_ref[...], me_ref[0] ^ 1, count)
    away = jnp.where(away == count // 2, theirs, away)
    cslot = cslot_ref[...]
    high = (cslot >= half).astype(jnp.int32)
    at = away * half + cslot - high * half
    table_rows = (count * half, pairs)
    pick = jnp.where(
        lax.broadcasted_iota(jnp.int32, table_rows, 0) == jnp.broadcast_to(at, table_rows), 1.0, 0.0
    )
    pick = jnp.transpose(pick).astype(jnp.bfloat16)
    lanes = (unknowns, pairs)
    keep = jnp.where(
        lax.broadcasted_iota(jnp.int32, lanes, 0) // directions == jnp.broadcast_to(high, lanes),
        1.0,
        0.0,
    )
    keep = jnp.transpose(keep).astype(jnp.bfloat16)
    total = jnp.zeros((clusters * rank_k, unknowns), jnp.float32)
    for q in range(rank_k):
        table = coef[:, q].reshape(count * half, unknowns).astype(jnp.bfloat16)
        chosen = jnp.dot(pick, table, preferred_element_type=jnp.float32).astype(jnp.bfloat16)
        chosen = chosen * keep
        couple = couple_ref[q]
        weight = jnp.concatenate([couple * hot[s : s + 1] for s in range(clusters)], axis=0)
        total = total + jnp.dot(weight, chosen, preferred_element_type=jnp.float32)
    total = total + pltpu.roll(total, unknowns // 2, axis=1)
    gathered = jnp.transpose(total)[0:directions, :].astype(jnp.bfloat16).astype(jnp.float32)
    lane = lax.broadcasted_iota(jnp.int32, gathered.shape, 1) // rank_k
    basis = basis_ref[...].reshape(clusters * rank_k, unknowns)
    for s in range(clusters):
        own = jnp.where(lane == s, gathered, 0.0).astype(jnp.bfloat16)
        out_ref[s] = jnp.dot(own, basis, preferred_element_type=jnp.float32)


def ring_device(place, core, chips):
    depth = chips // 2
    place = place % chips
    z, y = (place, 0) if place < depth else (chips - 1 - place, 1)
    return (z * 2 + y) * 2 + core


def ring_pairs(count):
    chips = count // 2
    cores = [(p, c) for p in range(chips) for c in range(2)]
    ahead = [(ring_device(p, c, chips), ring_device(p + 1 - 2 * c, c, chips)) for p, c in cores]
    cross = [
        (ring_device(p, c, chips), ring_device(p - 1 + 2 * c, 1 - c, chips)) for p, c in cores
    ]
    return ahead, cross


def ring_place(device, chips):
    z, y = device >> 2, (device >> 1) & 1
    return jnp.where(y == 0, z, chips - 1 - z)


def gather_place(device, me, count):
    chips = count // 2
    depth = chips // 2
    back = (1 - 2 * (me & 1)) * (ring_place(me, chips) - ring_place(device, chips))
    back = (back + chips) & (chips - 1)
    other = (device ^ me) & 1
    here = (back < depth) & (back > 0) | (back == 0) & (other == 1) | (back == depth) & (other == 0)
    return jnp.where(here, jnp.where(back == 0, 0, 2 * back - 1 + other), chips)


def scatter_place(device, me, count):
    chips = count // 2
    depth = chips // 2
    ahead = (ring_place(device, chips) - ring_place(me, chips) + chips) & (chips - 1)
    core = device & 1
    handler = jnp.where((ahead & (depth - 1)) == 0, core, (ahead > depth).astype(jnp.int32))
    steps = jnp.where(handler == 0, ahead, (chips - ahead) & (chips - 1))
    place = jnp.where(
        steps == depth,
        0,
        jnp.where(steps == 0, chips - 1, 2 * (depth - steps) - (core ^ handler)),
    )
    return place + jnp.where(handler == (me & 1), 0, chips)


def stationary(
    rhs,
    near_blocks,
    near_owner,
    near_slot,
    near_offset,
    far_coupling,
    far_slot,
    far_dev,
    far_cslot,
    basis_out,
    basis_in,
):
    clusters, directions, unknowns = rhs.shape
    rank_k = basis_in.shape[1]
    count = lax.axis_size("blk")
    chips = count // 2
    depth = chips // 2
    me = lax.axis_index("blk")
    stored = near_blocks.shape[0]
    pairs = far_slot.shape[0]
    half = clusters // 2
    ahead, cross = ring_pairs(count)
    mate = [(i, i ^ 1) for i in range(count)]
    side = [(i, i ^ 2) for i in range(count)]

    def move(values, where):
        return lax.ppermute(values, "blk", where)

    def after(values, *others):
        return lax.optimization_barrier((values, *others))[0]

    here = me.astype(jnp.int32).reshape(1)
    base = clusters * directions
    params = pltpu.CompilerParams(vmem_limit_bytes=PROLOGUE_VMEM)
    payload = pl.pallas_call(
        payload_kernel,
        out_shape=jax.ShapeDtypeStruct((base + half * rank_k, unknowns), jnp.bfloat16),
        in_specs=[whole()] * 2,
        out_specs=whole(),
        compiler_params=params,
        name="payload",
    )(rhs, basis_in)
    lists = pl.pallas_call(
        functools.partial(list_kernel, count, clusters),
        out_shape=jax.ShapeDtypeStruct((8, stored), jnp.int32),
        in_specs=[whole(pltpu.SMEM)] + [whole()] * 3,
        out_specs=whole(),
        compiler_params=params,
        name="lists",
    )(
        after(here, payload),
        near_owner.reshape(1, stored),
        near_slot.reshape(1, stored),
        near_offset.reshape(1, stored),
    )
    flow = [move(payload, ahead)]
    mate_blocks = move(near_blocks, mate)
    mate_lists = move(lists, mate)
    couple = jnp.transpose(far_coupling, (2, 1, 0))
    flow.append(move(after(payload, couple, lists), cross))
    shards = [move(payload, mate)]
    for k in range(1, chips):
        x = 1 - k % 2
        if k == 3:
            flow[x], mate_blocks, shards[0], mate_lists = lax.optimization_barrier(
                (flow[x], mate_blocks, shards[0], mate_lists)
            )
        if k == 4:
            lists = jnp.concatenate([after(lists, flow[x]), mate_lists], axis=0)
        if k == 5:
            flow[x], lists = lax.optimization_barrier((flow[x], lists))
        shards.append(flow[x])
        if k < chips - 2:
            flow[x] = move(flow[x], ahead)

    pieces = [2, chips - 2]
    sums_shape = jax.ShapeDtypeStruct((count * clusters + 1, directions, unknowns), jnp.float32)

    def near(part, shards, sources, *sums):
        late = int(part == 2)
        sends = pieces if late else []
        return pl.pallas_call(
            functools.partial(near_kernel, part, BATCH[part], len(shards), len(sends)),
            out_shape=[sums_shape]
            + [jax.ShapeDtypeStruct((chips * half * rank_k, unknowns), jnp.bfloat16)] * late
            + [
                jax.ShapeDtypeStruct((size * clusters, directions, unknowns), jnp.bfloat16)
                for size in sends
            ],
            in_specs=[whole(pltpu.SMEM)]
            + [whole()] * len(shards)
            + [[whole(pl.ANY)], [whole()], [whole(), whole(pl.ANY)]][part]
            + [whole()] * len(sums),
            out_specs=[whole()] * (1 + late + len(sends)),
            input_output_aliases={1 + len(shards) + len(sources): 0} if sums else {},
            scratch_shapes=[
                pltpu.VMEM(((LATE if late else len(shards)) * base, unknowns), jnp.bfloat16),
                pltpu.VMEM(near_blocks.shape, jnp.bfloat16),
                pltpu.SemaphoreType.DMA((max(CHUNKS, stored // BATCH[part]),)),
            ],
            compiler_params=pltpu.CompilerParams(vmem_limit_bytes=NEAR_VMEM),
            cost_estimate=pl.CostEstimate(
                flops=16 * stored * directions * unknowns * unknowns,
                bytes_accessed=16 << 20,
                transcendentals=0,
            ),
            name="near",
        )(lists, *shards, *sources, *sums)

    def far_field(couple):
        return pl.pallas_call(
            far_kernel,
            out_shape=jax.ShapeDtypeStruct((clusters, directions, unknowns), jnp.float32),
            in_specs=[whole()] * 2 + [whole(pltpu.SMEM)] + [whole()] * 5,
            out_specs=whole(),
            compiler_params=pltpu.CompilerParams(vmem_limit_bytes=FAR_VMEM),
            cost_estimate=pl.CostEstimate(
                flops=4 * clusters * rank_k * pairs * rank_k * unknowns,
                bytes_accessed=8 << 20,
                transcendentals=0,
            ),
            name="far",
        )(
            *coefs,
            here,
            couple,
            far_slot.reshape(1, pairs),
            far_dev.reshape(1, pairs),
            far_cslot.reshape(1, pairs),
            basis_out,
        )

    (sums,) = near(0, shards[: chips - LATE], [mate_blocks])
    (sums,) = near(1, shards[: chips - LATE + 1], [near_blocks], sums)
    sums, coef, *sends = near(2, shards, [near_blocks, mate_blocks], sums)
    mates = [move(sends[0], mate)]
    coefs = [coef, move(coef, mate)]

    def term(k):
        part, at = (0, k) if k < 2 else (1, k - 2)
        got = mates[part][at * clusters : (at + 1) * clusters]
        return sums[k * clusters : (k + 1) * clusters] + got.astype(jnp.float32)

    def tied(values, k, *others):
        values, mates[1], *others = lax.optimization_barrier((values, mates[1], *others))
        return values

    def add(flow, k):
        return (flow.astype(jnp.float32) + term(k)).astype(jnp.bfloat16)

    flow = lax.optimization_barrier([term(0).astype(jnp.bfloat16), term(1).astype(jnp.bfloat16)])
    mates.append(move(after(sends[1], *flow), mate))
    flow = [move(part, ahead) for part in flow]
    for k in range(2, chips - 1):
        x = k % 2
        flow[x] = tied(add(flow[x], k), k)
        if k == chips - 2:
            couple = after(couple, flow[x])
        flow[x] = move(flow[x], ahead)
    flow[1] = move(flow[1], mate)
    total = far_field(couple) + term(chips - 1) + flow[0].astype(jnp.float32)
    total = lax.optimization_barrier(total)
    return (total + flow[1].astype(jnp.float32)).astype(jnp.bfloat16)


def on_device(*args):
    rhs, near_blocks = args[0], args[1]
    clusters, directions, unknowns = rhs.shape
    small = lax.axis_size("blk") == 16 and clusters == 16
    if small and near_blocks.shape[0] == unknowns and 2 * directions == unknowns:
        return stationary(*args)
    return routed(*args)


def solution(mesh):
    placed = (
        P(("groups", "blk"), None, None),
        P(("groups", "blk"), None, None),
        P(("groups", "blk"), None),
        P(("groups", "blk")),
        P(("groups", "blk")),
        P(("groups", "blk"), None, None),
        P(("groups", "blk")),
        P(("groups", "blk"), None),
        P(("groups", "blk")),
        P(("groups", "blk"), None, None),
        P(("groups", "blk"), None, None),
    )
    return jax.shard_map(
        on_device,
        mesh=mesh,
        in_specs=placed,
        out_specs=P(("groups", "blk"), None, None),
        check_vma=False,
    )
```

```python
import functools

import jax
import jax.numpy as jnp
from jax import lax
from jax.experimental import pallas as pl
from jax.experimental.pallas import tpu as pltpu
from jax.sharding import PartitionSpec as P

BATCH = 16, 16, 8
CHUNKS = 4
LATE = 2
UNITS = 1
PROLOGUE_VMEM = 58 << 20
NEAR_VMEM = 20 << 20
FAR_VMEM = 16 << 20


def with_halo(cells, sides, width):
    for axis, dim in sides:
        count = lax.axis_size(axis)
        head = lax.slice_in_dim(cells, 0, width, axis=dim)
        tail = lax.slice_in_dim(cells, cells.shape[dim] - width, cells.shape[dim], axis=dim)
        cells = jnp.concatenate(
            [
                lax.ppermute(tail, axis, [(i, (i + 1) % count) for i in range(count)]),
                cells,
                lax.ppermute(head, axis, [((i + 1) % count, i) for i in range(count)]),
            ],
            axis=dim,
        )
    return cells


def place_ranks(targets, count):
    onehot = (targets[:, None] == jnp.arange(count, dtype=jnp.int32)[None, :]).astype(jnp.int32)
    before = jnp.cumsum(onehot, axis=0) - onehot
    return jnp.sum(before * onehot, axis=1)


def routed(
    rhs,
    near_blocks,
    near_owner,
    near_slot,
    near_offset,
    far_coupling,
    far_slot,
    far_dev,
    far_cslot,
    basis_out,
    basis_in,
):
    clusters = rhs.shape[0]
    directions = rhs.shape[1]
    unknowns = rhs.shape[2]
    cycle_size = lax.axis_size("blk")
    stored = near_blocks.shape[0]
    capacity = max(2, 2 * stored // cycle_size)
    owners = near_owner[:, 0]
    target = owners * capacity + place_ranks(owners, cycle_size)
    outbox = (
        jnp.zeros((cycle_size * capacity, unknowns, unknowns), near_blocks.dtype)
        .at[target]
        .set(near_blocks)
    )
    labels = (
        jnp.zeros((cycle_size * capacity, 2), jnp.int32)
        .at[target]
        .set(jnp.stack([near_slot, near_offset], axis=1))
    )
    window = with_halo(rhs, (("blk", 0),), clusters)
    inbox, in_labels = (
        lax.all_to_all(outbox, "blk", split_axis=0, concat_axis=0, tiled=True),
        lax.all_to_all(labels, "blk", split_axis=0, concat_axis=0, tiled=True),
    )
    position = clusters + in_labels[:, 0] + in_labels[:, 1]
    columns = jnp.take(window, position, axis=0)
    products = jnp.einsum("srj,sij->sri", columns, inbox, preferred_element_type=jnp.float32)
    selector = (in_labels[:, 0][None, :] == jnp.arange(clusters, dtype=jnp.int32)[:, None]).astype(
        jnp.float32
    )
    near_sum = jnp.dot(
        selector,
        products.reshape(products.shape[0], -1),
        precision=lax.Precision.HIGHEST,
        preferred_element_type=jnp.float32,
    ).reshape(clusters, directions, unknowns)
    coef_local = jnp.einsum(
        "ckj,crj->crk", basis_in, rhs, preferred_element_type=jnp.float32
    ).astype(jnp.bfloat16)
    rank_k = basis_in.shape[1]
    coef_local = coef_local.reshape(clusters, directions * rank_k)
    pairs = far_slot.shape[0]
    wanted = far_dev[:, 0] * clusters + far_cslot
    piece = lax.all_gather(coef_local, "blk", axis=0, tiled=True)
    chosen = jnp.take(piece, wanted, axis=0)
    coupled = jnp.einsum(
        "pkq,prq->prk",
        far_coupling,
        chosen.reshape(pairs, directions, rank_k),
        preferred_element_type=jnp.float32,
    )
    row_pick = (far_slot[None, :] == jnp.arange(clusters, dtype=jnp.int32)[:, None]).astype(
        jnp.float32
    )
    gathered = jnp.dot(
        row_pick,
        coupled.reshape(pairs, -1),
        precision=lax.Precision.HIGHEST,
        preferred_element_type=jnp.float32,
    )
    gathered = gathered.astype(jnp.bfloat16).reshape(clusters, directions, rank_k)
    far_sum = jnp.einsum("crk,ckb->crb", gathered, basis_out, preferred_element_type=jnp.float32)
    return (near_sum + far_sum).astype(jnp.bfloat16)


def whole(space=pltpu.VMEM):
    return pl.BlockSpec(memory_space=space)


def prologue_kernel(
    count, me_ref, owner_ref, slot_ref, offset_ref, rhs_ref, basis_ref, payload_ref, list_ref
):
    clusters, directions, unknowns = rhs_ref.shape
    base = clusters * directions
    payload_ref[0:base, :] = rhs_ref[...].reshape(base, unknowns)
    rank_k = basis_ref.shape[1]
    half = clusters // 2
    rows = []
    for c in range(half):
        parts = [
            lax.dot_general(
                basis_ref[e],
                rhs_ref[e],
                (((1,), (1,)), ((), ())),
                preferred_element_type=jnp.float32,
            )
            for e in (c, c + half)
        ]
        rows.append(jnp.concatenate(parts, axis=1))
    rows = jnp.concatenate(rows, axis=0).astype(payload_ref.dtype)
    square = (rows.shape[0], rows.shape[0])
    row = lax.broadcasted_iota(jnp.int32, square, 0)
    source = (row & (half - 1)) * rank_k + row // half
    order = jnp.where(lax.broadcasted_iota(jnp.int32, square, 1) == source, 1.0, 0.0)
    payload_ref[base:, :] = jnp.dot(
        order.astype(rows.dtype), rows, preferred_element_type=jnp.float32
    ).astype(payload_ref.dtype)

    me, owner, slot = me_ref[0], owner_ref[...], slot_ref[...]
    stored = owner.shape[1]
    place = scatter_place(owner, me, count) * clusters + slot
    column = (owner * clusters + slot + offset_ref[...]) & (count * clusters - 1)
    shard = gather_place(column // clusters, me, count)
    theirs = (shard == count // 2).astype(jnp.int32)
    shard = jnp.where(theirs == 1, gather_place(column // clusters, me ^ 1, count), shard)
    column_place = shard * clusters + (column & (clusters - 1))
    late = (shard >= count // 2 - LATE + 1 - theirs).astype(jnp.int32)
    square = (stored, stored)
    group = jnp.broadcast_to((2 * theirs + late).astype(jnp.float32), square)
    group_of_row = jnp.transpose(group)
    row_at = lax.broadcasted_iota(jnp.int32, square, 0)
    lane_at = lax.broadcasted_iota(jnp.int32, square, 1)
    lane = lane_at.astype(jnp.float32)
    before = (group_of_row < group) | ((group_of_row == group) & (row_at < lane_at))
    rank = jnp.sum(jnp.where(before, 1.0, 0.0), axis=0, keepdims=True)
    rank = jnp.transpose(jnp.broadcast_to(rank, square))
    here = jnp.where(rank == lane, 1.0, 0.0).astype(jnp.bfloat16)
    starts = jnp.sum(jnp.where(group_of_row < lane, 1.0, 0.0), axis=0, keepdims=True)
    values = jnp.concatenate(
        [lane[0:1], place.astype(jnp.float32), column_place.astype(jnp.float32)]
        + [jnp.zeros((5, stored), jnp.float32)],
        axis=0,
    )
    values = jnp.dot(values.astype(jnp.bfloat16), here, preferred_element_type=jnp.float32)
    values = jnp.concatenate([values[0:3], starts, values[4:8]], axis=0)
    list_ref[...] = values.astype(jnp.int32)


def near_kernel(part, batch, shards, sends, list_ref, *refs):
    late = int(part == 2)
    used = LATE if late else shards
    shard_refs, refs = refs[:shards], refs[shards:]
    if part > 0:
        own_ref, refs = refs[0], refs[1:]
    if part != 1:
        mate_hbm, refs = refs[0], refs[1:]
    if part > 0:
        refs = refs[1:]
    sums, refs = refs[0], refs[1:]
    if late:
        coef_ref, send_refs, refs = refs[0], refs[1 : 1 + sends], refs[1 + sends :]
    columns, blocks, block_sem = refs
    stored = blocks.shape[0]
    directions = sums.shape[1]
    span = columns.shape[0] // used
    dummy = sums.shape[0] - 1
    chunk = stored // CHUNKS

    begin, end = list_ref[3, late], list_ref[3, late + 1]
    begin_there, end_there = list_ref[11, 2 + late], list_ref[11, 3 + late]
    steps_there = (end_there - begin_there + batch - 1) // batch

    def fetch(j, carry):
        at = jnp.minimum(begin_there + j, end_there - 1)
        pltpu.make_async_copy(
            mate_hbm.at[list_ref[8, at]], blocks.at[j], block_sem.at[j // batch]
        ).start()
        return carry

    if late:
        lax.fori_loop(0, steps_there * batch, fetch, 0)
    elif part == 0:
        for c in range(CHUNKS):
            at = pl.ds(c * chunk, chunk)
            pltpu.make_async_copy(mate_hbm.at[at], blocks.at[at], block_sem.at[c]).start()

    for k, ref in enumerate(shard_refs[shards - used :]):

        def gather(i, carry, k=k, ref=ref):
            at = pl.multiple_of(i * directions, directions)
            columns[pl.ds(pl.multiple_of(k * span + at, directions), directions)] = ref[
                pl.ds(at, directions)
            ]
            return carry

        lax.fori_loop(0, span // directions, gather, 0, unroll=8)
    if late:
        tail = coef_ref.shape[0] // shards
        for k, ref in enumerate(shard_refs):
            coef_ref[k * tail : (k + 1) * tail] = ref[span : span + tail]
    elif part == 0:

        def clear(i, carry):
            sums[i] = jnp.zeros(sums.shape[1:], sums.dtype)
            return carry

        lax.fori_loop(0, dummy, clear, 0, unroll=8)
        clear(dummy, 0)

    def run(begin, end, row, swap, block_of):
        def entry(j):
            return jnp.minimum(begin + j, end - 1)

        def body(step, carry):
            first = step * batch
            products = []

            def add(i):
                place = list_ref[row + 1, entry(first + i)] ^ swap
                place = jnp.where(begin + first + i < end, place, dummy)
                sums[place] = sums[place] + products[i]

            take, carry = block_of(first, entry, carry)
            for i in range(batch):
                start = list_ref[row + 2, entry(first + i)] * directions - (shards - used) * span
                products.append(
                    lax.dot_general(
                        columns[pl.ds(pl.multiple_of(start, directions), directions)],
                        take(i),
                        (((1,), (1,)), ((), ())),
                        preferred_element_type=jnp.float32,
                    )
                )
            for i in range(batch):
                add(i)
            return carry

        return lax.fori_loop(0, (end - begin + batch - 1) // batch, body, 0)

    def own_blocks(first, entry, carry):
        return lambda i: own_ref[list_ref[0, entry(first + i)]], carry

    def wait(c, carry):
        at = pl.ds(0, chunk)
        pltpu.make_async_copy(mate_hbm.at[at], blocks.at[at], block_sem.at[c]).wait()
        return carry

    def mate_blocks(first, entry, ready):
        if late:
            pltpu.make_async_copy(
                mate_hbm.at[pl.ds(0, batch)],
                blocks.at[pl.ds(first, batch)],
                block_sem.at[first // batch],
            ).wait()
            return lambda i: blocks[first + i], ready
        needed = list_ref[8, entry(first + batch - 1)] // chunk + 1
        lax.fori_loop(ready, needed, wait, 0)
        return lambda i: blocks[list_ref[8, entry(first + i)]], jnp.maximum(ready, needed)

    if part > 0:
        run(begin, end, 0, 0, own_blocks)
    if part != 1:
        ready = run(begin_there, end_there, 8, dummy // 2, mate_blocks)
    if part == 0:
        lax.fori_loop(ready, CHUNKS, wait, 0)
    if not late:
        return
    at = dummy // 2
    for send_ref in send_refs:

        def pack(i, carry, at=at, send_ref=send_ref):
            send_ref[i] = sums[at + i].astype(send_ref.dtype)
            return carry

        lax.fori_loop(0, send_ref.shape[0], pack, 0, unroll=8)
        at += send_ref.shape[0]


def far_kernel(*refs):
    coef_refs = refs[:2]
    me_ref, couple_ref, slot_ref, dev_ref, cslot_ref, basis_ref, out_ref = refs[2:]
    clusters, rank_k, unknowns = basis_ref.shape
    pairs = couple_ref.shape[2]
    directions = out_ref.shape[1]
    half = clusters // 2
    coef = jnp.concatenate([ref[...].astype(jnp.float32) for ref in coef_refs], axis=0)
    coef = coef.reshape(-1, rank_k, half, unknowns)
    count = coef.shape[0]
    hot = (
        lax.broadcasted_iota(jnp.int32, (clusters, pairs), 0)
        == jnp.broadcast_to(slot_ref[...], (clusters, pairs))
    ).astype(jnp.float32).astype(jnp.bfloat16)
    away = gather_place(dev_ref[...], me_ref[0], count)
    theirs = count // 2 + gather_place(dev_ref[...], me_ref[0] ^ 1, count)
    away = jnp.where(away == count // 2, theirs, away)
    cslot = cslot_ref[...]
    high = (cslot >= half).astype(jnp.int32)
    at = away * half + cslot - high * half
    table_rows = (count * half, pairs)
    pick = jnp.where(
        lax.broadcasted_iota(jnp.int32, table_rows, 0) == jnp.broadcast_to(at, table_rows), 1.0, 0.0
    )
    pick = jnp.transpose(pick).astype(jnp.bfloat16)
    lanes = (unknowns, pairs)
    keep = jnp.where(
        lax.broadcasted_iota(jnp.int32, lanes, 0) // directions == jnp.broadcast_to(high, lanes),
        1.0,
        0.0,
    )
    keep = jnp.transpose(keep).astype(jnp.bfloat16)
    total = jnp.zeros((clusters * rank_k, unknowns), jnp.float32)
    for q in range(rank_k):
        table = coef[:, q].reshape(count * half, unknowns).astype(jnp.bfloat16)
        chosen = jnp.dot(pick, table, preferred_element_type=jnp.float32).astype(jnp.bfloat16)
        chosen = chosen * keep
        couple = couple_ref[q]
        weight = jnp.concatenate([couple * hot[s : s + 1] for s in range(clusters)], axis=0)
        total = total + jnp.dot(weight, chosen, preferred_element_type=jnp.float32)
    total = total + pltpu.roll(total, unknowns // 2, axis=1)
    gathered = jnp.transpose(total)[0:directions, :].astype(jnp.bfloat16).astype(jnp.float32)
    lane = lax.broadcasted_iota(jnp.int32, gathered.shape, 1) // rank_k
    basis = basis_ref[...].reshape(clusters * rank_k, unknowns)
    for s in range(clusters):
        own = jnp.where(lane == s, gathered, 0.0).astype(jnp.bfloat16)
        out_ref[s] = jnp.dot(own, basis, preferred_element_type=jnp.float32)


def ring_device(place, core, chips):
    depth = chips // 2
    place = place % chips
    z, y = (place, 0) if place < depth else (chips - 1 - place, 1)
    return (z * 2 + y) * 2 + core


def ring_pairs(count):
    chips = count // 2
    cores = [(p, c) for p in range(chips) for c in range(2)]
    ahead = [(ring_device(p, c, chips), ring_device(p + 1 - 2 * c, c, chips)) for p, c in cores]
    cross = [
        (ring_device(p, c, chips), ring_device(p - 1 + 2 * c, 1 - c, chips)) for p, c in cores
    ]
    return ahead, cross


def ring_place(device, chips):
    z, y = device >> 2, (device >> 1) & 1
    return jnp.where(y == 0, z, chips - 1 - z)


def gather_place(device, me, count):
    chips = count // 2
    depth = chips // 2
    back = (1 - 2 * (me & 1)) * (ring_place(me, chips) - ring_place(device, chips))
    back = (back + chips) & (chips - 1)
    other = (device ^ me) & 1
    here = (back < depth) & (back > 0) | (back == 0) & (other == 1) | (back == depth) & (other == 0)
    return jnp.where(here, jnp.where(back == 0, 0, 2 * back - 1 + other), chips)


def scatter_place(device, me, count):
    chips = count // 2
    depth = chips // 2
    ahead = (ring_place(device, chips) - ring_place(me, chips) + chips) & (chips - 1)
    core = device & 1
    handler = jnp.where((ahead & (depth - 1)) == 0, core, (ahead > depth).astype(jnp.int32))
    steps = jnp.where(handler == 0, ahead, (chips - ahead) & (chips - 1))
    place = jnp.where(
        steps == depth,
        0,
        jnp.where(steps == 0, chips - 1, 2 * (depth - steps) - (core ^ handler)),
    )
    return place + jnp.where(handler == (me & 1), 0, chips)


def stationary(
    rhs,
    near_blocks,
    near_owner,
    near_slot,
    near_offset,
    far_coupling,
    far_slot,
    far_dev,
    far_cslot,
    basis_out,
    basis_in,
):
    clusters, directions, unknowns = rhs.shape
    rank_k = basis_in.shape[1]
    count = lax.axis_size("blk")
    chips = count // 2
    depth = chips // 2
    me = lax.axis_index("blk")
    stored = near_blocks.shape[0]
    pairs = far_slot.shape[0]
    half = clusters // 2
    ahead, cross = ring_pairs(count)
    mate = [(i, i ^ 1) for i in range(count)]
    side = [(i, i ^ 2) for i in range(count)]

    def move(values, where):
        return lax.ppermute(values, "blk", where)

    def after(values, *others):
        return lax.optimization_barrier((values, *others))[0]

    here = me.astype(jnp.int32).reshape(1)
    base = clusters * directions
    payload, lists = pl.pallas_call(
        functools.partial(prologue_kernel, count),
        out_shape=[
            jax.ShapeDtypeStruct((base + half * rank_k, unknowns), jnp.bfloat16),
            jax.ShapeDtypeStruct((8, stored), jnp.int32),
        ],
        in_specs=[whole(pltpu.SMEM)] + [whole()] * 5,
        out_specs=[whole()] * 2,
        compiler_params=pltpu.CompilerParams(vmem_limit_bytes=PROLOGUE_VMEM),
        name="prologue",
    )(
        here,
        near_owner.reshape(1, stored),
        near_slot.reshape(1, stored),
        near_offset.reshape(1, stored),
        rhs,
        basis_in,
    )
    flow = [move(payload, ahead)]
    mate_blocks = move(near_blocks, mate)
    mate_lists = move(lists, mate)
    couple = jnp.transpose(far_coupling, (2, 1, 0))
    flow.append(move(after(payload, couple), cross))
    shards = [move(payload, mate)]
    for k in range(1, chips):
        x = 1 - k % 2
        if k == 3:
            flow[x], mate_blocks, shards[0], mate_lists = lax.optimization_barrier(
                (flow[x], mate_blocks, shards[0], mate_lists)
            )
        if k == 4:
            lists = jnp.concatenate([after(lists, flow[x]), mate_lists], axis=0)
        if k == 5:
            flow[x], lists = lax.optimization_barrier((flow[x], lists))
        shards.append(flow[x])
        if k < chips - 2:
            flow[x] = move(flow[x], ahead)

    pieces = [2, chips - 2]
    sums_shape = jax.ShapeDtypeStruct((count * clusters + 1, directions, unknowns), jnp.float32)

    def near(part, shards, sources, *sums):
        late = int(part == 2)
        sends = pieces if late else []
        return pl.pallas_call(
            functools.partial(near_kernel, part, BATCH[part], len(shards), len(sends)),
            out_shape=[sums_shape]
            + [jax.ShapeDtypeStruct((chips * half * rank_k, unknowns), jnp.bfloat16)] * late
            + [
                jax.ShapeDtypeStruct((size * clusters, directions, unknowns), jnp.bfloat16)
                for size in sends
            ],
            in_specs=[whole(pltpu.SMEM)]
            + [whole()] * len(shards)
            + [[whole(pl.ANY)], [whole()], [whole(), whole(pl.ANY)]][part]
            + [whole()] * len(sums),
            out_specs=[whole()] * (1 + late + len(sends)),
            input_output_aliases={1 + len(shards) + len(sources): 0} if sums else {},
            scratch_shapes=[
                pltpu.VMEM(((LATE if late else len(shards)) * base, unknowns), jnp.bfloat16),
                pltpu.VMEM(near_blocks.shape, jnp.bfloat16),
                pltpu.SemaphoreType.DMA((max(CHUNKS, stored // BATCH[part]),)),
            ],
            compiler_params=pltpu.CompilerParams(vmem_limit_bytes=NEAR_VMEM),
            cost_estimate=pl.CostEstimate(
                flops=16 * stored * directions * unknowns * unknowns,
                bytes_accessed=16 << 20,
                transcendentals=0,
            ),
            name="near",
        )(lists, *shards, *sources, *sums)

    def far_field(couple):
        return pl.pallas_call(
            far_kernel,
            out_shape=jax.ShapeDtypeStruct((clusters, directions, unknowns), jnp.float32),
            in_specs=[whole()] * 2 + [whole(pltpu.SMEM)] + [whole()] * 5,
            out_specs=whole(),
            compiler_params=pltpu.CompilerParams(vmem_limit_bytes=FAR_VMEM),
            cost_estimate=pl.CostEstimate(
                flops=4 * clusters * rank_k * pairs * rank_k * unknowns,
                bytes_accessed=8 << 20,
                transcendentals=0,
            ),
            name="far",
        )(
            *coefs,
            here,
            couple,
            far_slot.reshape(1, pairs),
            far_dev.reshape(1, pairs),
            far_cslot.reshape(1, pairs),
            basis_out,
        )

    (sums,) = near(0, shards[: chips - LATE], [mate_blocks])
    (sums,) = near(1, shards[: chips - LATE + 1], [near_blocks], sums)
    sums, coef, *sends = near(2, shards, [near_blocks, mate_blocks], sums)
    mates = [move(sends[0], mate)]
    coefs = [coef, move(coef, mate)]

    piece = clusters // UNITS

    def term(k, h):
        part, at = (0, k) if k < 2 else (1, k - 2)
        got = mates[part][at * clusters + h * piece : at * clusters + (h + 1) * piece]
        at = k * clusters + h * piece
        return sums[at : at + piece] + got.astype(jnp.float32)

    flow = lax.optimization_barrier(
        [[term(k, h).astype(jnp.bfloat16) for h in range(UNITS)] for k in range(2)]
    )
    mates.append(move(after(sends[1], *flow[0], *flow[1]), mate))
    flow = [[move(unit, ahead) for unit in units] for units in flow]
    for k in range(2, chips - 1):
        for h in range(UNITS):
            unit = (flow[k % 2][h].astype(jnp.float32) + term(k, h)).astype(jnp.bfloat16)
            unit, mates[1] = lax.optimization_barrier((unit, mates[1]))
            if (k, h) == (chips - 2, UNITS - 1):
                couple = after(couple, unit)
            flow[k % 2][h] = move(unit, ahead)
    last = [move(unit, mate) for unit in flow[1]]
    own = sums[(chips - 1) * clusters : chips * clusters]
    total = far_field(couple) + own + mates[1][(chips - 3) * clusters :].astype(jnp.float32)
    total = total + jnp.concatenate(flow[0], axis=0).astype(jnp.float32)
    total = lax.optimization_barrier(total)
    return (total + jnp.concatenate(last, axis=0).astype(jnp.float32)).astype(jnp.bfloat16)


def on_device(*args):
    rhs, near_blocks = args[0], args[1]
    clusters, directions, unknowns = rhs.shape
    small = lax.axis_size("blk") == 16 and clusters == 16
    if small and near_blocks.shape[0] == unknowns and 2 * directions == unknowns:
        return stationary(*args)
    return routed(*args)


def solution(mesh):
    placed = (
        P(("groups", "blk"), None, None),
        P(("groups", "blk"), None, None),
        P(("groups", "blk"), None),
        P(("groups", "blk")),
        P(("groups", "blk")),
        P(("groups", "blk"), None, None),
        P(("groups", "blk")),
        P(("groups", "blk"), None),
        P(("groups", "blk")),
        P(("groups", "blk"), None, None),
        P(("groups", "blk"), None, None),
    )
    return jax.shard_map(
        on_device,
        mesh=mesh,
        in_specs=placed,
        out_specs=P(("groups", "blk"), None, None),
        check_vma=False,
    )
```

```python
import functools

import jax
import jax.numpy as jnp
from jax import lax
from jax.experimental import pallas as pl
from jax.experimental.pallas import tpu as pltpu
from jax.sharding import PartitionSpec as P

BATCH = 16, 16, 8
CHUNKS = 4
LATE = 2
UNITS = 1
PROLOGUE_VMEM = 58 << 20
NEAR_VMEM = 20 << 20
FAR_VMEM = 16 << 20


def with_halo(cells, sides, width):
    for axis, dim in sides:
        count = lax.axis_size(axis)
        head = lax.slice_in_dim(cells, 0, width, axis=dim)
        tail = lax.slice_in_dim(cells, cells.shape[dim] - width, cells.shape[dim], axis=dim)
        cells = jnp.concatenate(
            [
                lax.ppermute(tail, axis, [(i, (i + 1) % count) for i in range(count)]),
                cells,
                lax.ppermute(head, axis, [((i + 1) % count, i) for i in range(count)]),
            ],
            axis=dim,
        )
    return cells


def place_ranks(targets, count):
    onehot = (targets[:, None] == jnp.arange(count, dtype=jnp.int32)[None, :]).astype(jnp.int32)
    before = jnp.cumsum(onehot, axis=0) - onehot
    return jnp.sum(before * onehot, axis=1)


def routed(
    rhs,
    near_blocks,
    near_owner,
    near_slot,
    near_offset,
    far_coupling,
    far_slot,
    far_dev,
    far_cslot,
    basis_out,
    basis_in,
):
    clusters = rhs.shape[0]
    directions = rhs.shape[1]
    unknowns = rhs.shape[2]
    cycle_size = lax.axis_size("blk")
    stored = near_blocks.shape[0]
    capacity = max(2, 2 * stored // cycle_size)
    owners = near_owner[:, 0]
    target = owners * capacity + place_ranks(owners, cycle_size)
    outbox = (
        jnp.zeros((cycle_size * capacity, unknowns, unknowns), near_blocks.dtype)
        .at[target]
        .set(near_blocks)
    )
    labels = (
        jnp.zeros((cycle_size * capacity, 2), jnp.int32)
        .at[target]
        .set(jnp.stack([near_slot, near_offset], axis=1))
    )
    window = with_halo(rhs, (("blk", 0),), clusters)
    inbox, in_labels = (
        lax.all_to_all(outbox, "blk", split_axis=0, concat_axis=0, tiled=True),
        lax.all_to_all(labels, "blk", split_axis=0, concat_axis=0, tiled=True),
    )
    position = clusters + in_labels[:, 0] + in_labels[:, 1]
    columns = jnp.take(window, position, axis=0)
    products = jnp.einsum("srj,sij->sri", columns, inbox, preferred_element_type=jnp.float32)
    selector = (in_labels[:, 0][None, :] == jnp.arange(clusters, dtype=jnp.int32)[:, None]).astype(
        jnp.float32
    )
    near_sum = jnp.dot(
        selector,
        products.reshape(products.shape[0], -1),
        precision=lax.Precision.HIGHEST,
        preferred_element_type=jnp.float32,
    ).reshape(clusters, directions, unknowns)
    coef_local = jnp.einsum(
        "ckj,crj->crk", basis_in, rhs, preferred_element_type=jnp.float32
    ).astype(jnp.bfloat16)
    rank_k = basis_in.shape[1]
    coef_local = coef_local.reshape(clusters, directions * rank_k)
    pairs = far_slot.shape[0]
    wanted = far_dev[:, 0] * clusters + far_cslot
    piece = lax.all_gather(coef_local, "blk", axis=0, tiled=True)
    chosen = jnp.take(piece, wanted, axis=0)
    coupled = jnp.einsum(
        "pkq,prq->prk",
        far_coupling,
        chosen.reshape(pairs, directions, rank_k),
        preferred_element_type=jnp.float32,
    )
    row_pick = (far_slot[None, :] == jnp.arange(clusters, dtype=jnp.int32)[:, None]).astype(
        jnp.float32
    )
    gathered = jnp.dot(
        row_pick,
        coupled.reshape(pairs, -1),
        precision=lax.Precision.HIGHEST,
        preferred_element_type=jnp.float32,
    )
    gathered = gathered.astype(jnp.bfloat16).reshape(clusters, directions, rank_k)
    far_sum = jnp.einsum("crk,ckb->crb", gathered, basis_out, preferred_element_type=jnp.float32)
    return (near_sum + far_sum).astype(jnp.bfloat16)


def whole(space=pltpu.VMEM):
    return pl.BlockSpec(memory_space=space)


def prologue_kernel(
    count, me_ref, owner_ref, slot_ref, offset_ref, rhs_ref, basis_ref, payload_ref, list_ref
):
    clusters, directions, unknowns = rhs_ref.shape
    base = clusters * directions
    payload_ref[0:base, :] = rhs_ref[...].reshape(base, unknowns)
    rank_k = basis_ref.shape[1]
    half = clusters // 2
    rows = []
    for c in range(half):
        parts = [
            lax.dot_general(
                basis_ref[e],
                rhs_ref[e],
                (((1,), (1,)), ((), ())),
                preferred_element_type=jnp.float32,
            )
            for e in (c, c + half)
        ]
        rows.append(jnp.concatenate(parts, axis=1))
    rows = jnp.concatenate(rows, axis=0).astype(payload_ref.dtype)
    square = (rows.shape[0], rows.shape[0])
    row = lax.broadcasted_iota(jnp.int32, square, 0)
    source = (row & (half - 1)) * rank_k + row // half
    order = jnp.where(lax.broadcasted_iota(jnp.int32, square, 1) == source, 1.0, 0.0)
    payload_ref[base:, :] = jnp.dot(
        order.astype(rows.dtype), rows, preferred_element_type=jnp.float32
    ).astype(payload_ref.dtype)

    me, owner, slot = me_ref[0], owner_ref[...], slot_ref[...]
    stored = owner.shape[1]
    place = scatter_place(owner, me, count) * clusters + slot
    column = (owner * clusters + slot + offset_ref[...]) & (count * clusters - 1)
    shard = gather_place(column // clusters, me, count)
    theirs = (shard == count // 2).astype(jnp.int32)
    shard = jnp.where(theirs == 1, gather_place(column // clusters, me ^ 1, count), shard)
    column_place = shard * clusters + (column & (clusters - 1))
    late = (shard >= count // 2 - LATE + 1 - theirs).astype(jnp.int32)
    square = (stored, stored)
    group = jnp.broadcast_to((2 * theirs + late).astype(jnp.float32), square)
    group_of_row = jnp.transpose(group)
    row_at = lax.broadcasted_iota(jnp.int32, square, 0)
    lane_at = lax.broadcasted_iota(jnp.int32, square, 1)
    lane = lane_at.astype(jnp.float32)
    before = (group_of_row < group) | ((group_of_row == group) & (row_at < lane_at))
    rank = jnp.sum(jnp.where(before, 1.0, 0.0), axis=0, keepdims=True)
    rank = jnp.transpose(jnp.broadcast_to(rank, square))
    here = jnp.where(rank == lane, 1.0, 0.0).astype(jnp.bfloat16)
    starts = jnp.sum(jnp.where(group_of_row < lane, 1.0, 0.0), axis=0, keepdims=True)
    values = jnp.concatenate(
        [lane[0:1], place.astype(jnp.float32), column_place.astype(jnp.float32)]
        + [jnp.zeros((5, stored), jnp.float32)],
        axis=0,
    )
    values = jnp.dot(values.astype(jnp.bfloat16), here, preferred_element_type=jnp.float32)
    values = jnp.concatenate([values[0:3], starts, values[4:8]], axis=0)
    list_ref[...] = values.astype(jnp.int32)


def clear_kernel(token_ref, sums):
    def clear(i, carry):
        sums[i] = jnp.zeros(sums.shape[1:], sums.dtype)
        return carry

    lax.fori_loop(0, sums.shape[0] - 1, clear, 0, unroll=8)
    clear(sums.shape[0] - 1, 0)


def near_kernel(part, batch, shards, sends, list_ref, *refs):
    late = int(part == 2)
    used = LATE if late else shards
    shard_refs, refs = refs[:shards], refs[shards:]
    if part > 0:
        own_ref, refs = refs[0], refs[1:]
    if part != 1:
        mate_hbm, refs = refs[0], refs[1:]
    sums, refs = refs[1], refs[2:]
    if late:
        coef_ref, send_refs, refs = refs[0], refs[1 : 1 + sends], refs[1 + sends :]
    columns, blocks, block_sem = refs
    stored = blocks.shape[0]
    directions = sums.shape[1]
    span = columns.shape[0] // used
    dummy = sums.shape[0] - 1
    chunk = stored // CHUNKS

    begin, end = list_ref[3, late], list_ref[3, late + 1]
    begin_there, end_there = list_ref[11, 2 + late], list_ref[11, 3 + late]
    steps_there = (end_there - begin_there + batch - 1) // batch

    def fetch(j, carry):
        at = jnp.minimum(begin_there + j, end_there - 1)
        pltpu.make_async_copy(
            mate_hbm.at[list_ref[8, at]], blocks.at[j], block_sem.at[j // batch]
        ).start()
        return carry

    if late:
        lax.fori_loop(0, steps_there * batch, fetch, 0)
    elif part == 0:
        for c in range(CHUNKS):
            at = pl.ds(c * chunk, chunk)
            pltpu.make_async_copy(mate_hbm.at[at], blocks.at[at], block_sem.at[c]).start()

    for k, ref in enumerate(shard_refs[shards - used :]):

        def gather(i, carry, k=k, ref=ref):
            at = pl.multiple_of(i * directions, directions)
            columns[pl.ds(pl.multiple_of(k * span + at, directions), directions)] = ref[
                pl.ds(at, directions)
            ]
            return carry

        lax.fori_loop(0, span // directions, gather, 0, unroll=8)
    if late:
        tail = coef_ref.shape[0] // shards
        for k, ref in enumerate(shard_refs):
            coef_ref[k * tail : (k + 1) * tail] = ref[span : span + tail]

    def run(begin, end, row, swap, block_of):
        def entry(j):
            return jnp.minimum(begin + j, end - 1)

        def body(step, carry):
            first = step * batch
            products = []

            def add(i):
                place = list_ref[row + 1, entry(first + i)] ^ swap
                place = jnp.where(begin + first + i < end, place, dummy)
                sums[place] = sums[place] + products[i]

            take, carry = block_of(first, entry, carry)
            for i in range(batch):
                start = list_ref[row + 2, entry(first + i)] * directions - (shards - used) * span
                products.append(
                    lax.dot_general(
                        columns[pl.ds(pl.multiple_of(start, directions), directions)],
                        take(i),
                        (((1,), (1,)), ((), ())),
                        preferred_element_type=jnp.float32,
                    )
                )
            for i in range(batch):
                add(i)
            return carry

        return lax.fori_loop(0, (end - begin + batch - 1) // batch, body, 0)

    def own_blocks(first, entry, carry):
        return lambda i: own_ref[list_ref[0, entry(first + i)]], carry

    def wait(c, carry):
        at = pl.ds(0, chunk)
        pltpu.make_async_copy(mate_hbm.at[at], blocks.at[at], block_sem.at[c]).wait()
        return carry

    def mate_blocks(first, entry, ready):
        if late:
            pltpu.make_async_copy(
                mate_hbm.at[pl.ds(0, batch)],
                blocks.at[pl.ds(first, batch)],
                block_sem.at[first // batch],
            ).wait()
            return lambda i: blocks[first + i], ready
        needed = list_ref[8, entry(first + batch - 1)] // chunk + 1
        lax.fori_loop(ready, needed, wait, 0)
        return lambda i: blocks[list_ref[8, entry(first + i)]], jnp.maximum(ready, needed)

    if part > 0:
        run(begin, end, 0, 0, own_blocks)
    if part != 1:
        ready = run(begin_there, end_there, 8, dummy // 2, mate_blocks)
    if part == 0:
        lax.fori_loop(ready, CHUNKS, wait, 0)
    if not late:
        return
    at = dummy // 2
    for send_ref in send_refs:

        def pack(i, carry, at=at, send_ref=send_ref):
            send_ref[i] = sums[at + i].astype(send_ref.dtype)
            return carry

        lax.fori_loop(0, send_ref.shape[0], pack, 0, unroll=8)
        at += send_ref.shape[0]


def far_kernel(*refs):
    coef_refs = refs[:2]
    me_ref, couple_ref, slot_ref, dev_ref, cslot_ref, basis_ref, out_ref = refs[2:]
    clusters, rank_k, unknowns = basis_ref.shape
    pairs = couple_ref.shape[2]
    directions = out_ref.shape[1]
    half = clusters // 2
    coef = jnp.concatenate([ref[...].astype(jnp.float32) for ref in coef_refs], axis=0)
    coef = coef.reshape(-1, rank_k, half, unknowns)
    count = coef.shape[0]
    hot = (
        lax.broadcasted_iota(jnp.int32, (clusters, pairs), 0)
        == jnp.broadcast_to(slot_ref[...], (clusters, pairs))
    ).astype(jnp.float32).astype(jnp.bfloat16)
    away = gather_place(dev_ref[...], me_ref[0], count)
    theirs = count // 2 + gather_place(dev_ref[...], me_ref[0] ^ 1, count)
    away = jnp.where(away == count // 2, theirs, away)
    cslot = cslot_ref[...]
    high = (cslot >= half).astype(jnp.int32)
    at = away * half + cslot - high * half
    table_rows = (count * half, pairs)
    pick = jnp.where(
        lax.broadcasted_iota(jnp.int32, table_rows, 0) == jnp.broadcast_to(at, table_rows), 1.0, 0.0
    )
    pick = jnp.transpose(pick).astype(jnp.bfloat16)
    lanes = (unknowns, pairs)
    keep = jnp.where(
        lax.broadcasted_iota(jnp.int32, lanes, 0) // directions == jnp.broadcast_to(high, lanes),
        1.0,
        0.0,
    )
    keep = jnp.transpose(keep).astype(jnp.bfloat16)
    total = jnp.zeros((clusters * rank_k, unknowns), jnp.float32)
    for q in range(rank_k):
        table = coef[:, q].reshape(count * half, unknowns).astype(jnp.bfloat16)
        chosen = jnp.dot(pick, table, preferred_element_type=jnp.float32).astype(jnp.bfloat16)
        chosen = chosen * keep
        couple = couple_ref[q]
        weight = jnp.concatenate([couple * hot[s : s + 1] for s in range(clusters)], axis=0)
        total = total + jnp.dot(weight, chosen, preferred_element_type=jnp.float32)
    total = total + pltpu.roll(total, unknowns // 2, axis=1)
    gathered = jnp.transpose(total)[0:directions, :].astype(jnp.bfloat16).astype(jnp.float32)
    lane = lax.broadcasted_iota(jnp.int32, gathered.shape, 1) // rank_k
    basis = basis_ref[...].reshape(clusters * rank_k, unknowns)
    for s in range(clusters):
        own = jnp.where(lane == s, gathered, 0.0).astype(jnp.bfloat16)
        out_ref[s] = jnp.dot(own, basis, preferred_element_type=jnp.float32)


def ring_device(place, core, chips):
    depth = chips // 2
    place = place % chips
    z, y = (place, 0) if place < depth else (chips - 1 - place, 1)
    return (z * 2 + y) * 2 + core


def ring_pairs(count):
    chips = count // 2
    cores = [(p, c) for p in range(chips) for c in range(2)]
    ahead = [(ring_device(p, c, chips), ring_device(p + 1 - 2 * c, c, chips)) for p, c in cores]
    cross = [
        (ring_device(p, c, chips), ring_device(p - 1 + 2 * c, 1 - c, chips)) for p, c in cores
    ]
    return ahead, cross


def ring_place(device, chips):
    z, y = device >> 2, (device >> 1) & 1
    return jnp.where(y == 0, z, chips - 1 - z)


def gather_place(device, me, count):
    chips = count // 2
    depth = chips // 2
    back = (1 - 2 * (me & 1)) * (ring_place(me, chips) - ring_place(device, chips))
    back = (back + chips) & (chips - 1)
    other = (device ^ me) & 1
    here = (back < depth) & (back > 0) | (back == 0) & (other == 1) | (back == depth) & (other == 0)
    return jnp.where(here, jnp.where(back == 0, 0, 2 * back - 1 + other), chips)


def scatter_place(device, me, count):
    chips = count // 2
    depth = chips // 2
    ahead = (ring_place(device, chips) - ring_place(me, chips) + chips) & (chips - 1)
    core = device & 1
    handler = jnp.where((ahead & (depth - 1)) == 0, core, (ahead > depth).astype(jnp.int32))
    steps = jnp.where(handler == 0, ahead, (chips - ahead) & (chips - 1))
    place = jnp.where(
        steps == depth,
        0,
        jnp.where(steps == 0, chips - 1, 2 * (depth - steps) - (core ^ handler)),
    )
    return place + jnp.where(handler == (me & 1), 0, chips)


def stationary(
    rhs,
    near_blocks,
    near_owner,
    near_slot,
    near_offset,
    far_coupling,
    far_slot,
    far_dev,
    far_cslot,
    basis_out,
    basis_in,
):
    clusters, directions, unknowns = rhs.shape
    rank_k = basis_in.shape[1]
    count = lax.axis_size("blk")
    chips = count // 2
    depth = chips // 2
    me = lax.axis_index("blk")
    stored = near_blocks.shape[0]
    pairs = far_slot.shape[0]
    half = clusters // 2
    ahead, cross = ring_pairs(count)
    mate = [(i, i ^ 1) for i in range(count)]
    side = [(i, i ^ 2) for i in range(count)]

    def move(values, where):
        return lax.ppermute(values, "blk", where)

    def after(values, *others):
        return lax.optimization_barrier((values, *others))[0]

    here = me.astype(jnp.int32).reshape(1)
    base = clusters * directions
    payload, lists = pl.pallas_call(
        functools.partial(prologue_kernel, count),
        out_shape=[
            jax.ShapeDtypeStruct((base + half * rank_k, unknowns), jnp.bfloat16),
            jax.ShapeDtypeStruct((8, stored), jnp.int32),
        ],
        in_specs=[whole(pltpu.SMEM)] + [whole()] * 5,
        out_specs=[whole()] * 2,
        compiler_params=pltpu.CompilerParams(vmem_limit_bytes=PROLOGUE_VMEM),
        name="prologue",
    )(
        here,
        near_owner.reshape(1, stored),
        near_slot.reshape(1, stored),
        near_offset.reshape(1, stored),
        rhs,
        basis_in,
    )
    flow = [move(payload, ahead)]
    mate_lists = move(lists, mate)
    couple = jnp.transpose(after(far_coupling, payload), (2, 1, 0))
    mate_blocks = move(near_blocks, mate)
    flow.append(move(after(payload, couple), cross))
    shards = [move(payload, mate)]
    sums_shape = jax.ShapeDtypeStruct((count * clusters + 1, directions, unknowns), jnp.float32)
    sums = pl.pallas_call(
        clear_kernel,
        out_shape=sums_shape,
        in_specs=[whole(pltpu.SMEM)],
        out_specs=whole(),
        name="clear",
    )(after(here, couple))
    flow[0], sums = lax.optimization_barrier((flow[0], sums))
    for k in range(1, chips):
        x = 1 - k % 2
        if k == 3:
            flow[x], mate_blocks, shards[0], mate_lists = lax.optimization_barrier(
                (flow[x], mate_blocks, shards[0], mate_lists)
            )
        if k == 4:
            lists = jnp.concatenate([after(lists, flow[x]), mate_lists], axis=0)
        if k == 5:
            flow[x], lists = lax.optimization_barrier((flow[x], lists))
        shards.append(flow[x])
        if k < chips - 2:
            flow[x] = move(flow[x], ahead)

    pieces = [2, chips - 2]

    def near(part, shards, sources, sums):
        late = int(part == 2)
        sends = pieces if late else []
        return pl.pallas_call(
            functools.partial(near_kernel, part, BATCH[part], len(shards), len(sends)),
            out_shape=[sums_shape]
            + [jax.ShapeDtypeStruct((chips * half * rank_k, unknowns), jnp.bfloat16)] * late
            + [
                jax.ShapeDtypeStruct((size * clusters, directions, unknowns), jnp.bfloat16)
                for size in sends
            ],
            in_specs=[whole(pltpu.SMEM)]
            + [whole()] * len(shards)
            + [[whole(pl.ANY)], [whole()], [whole(), whole(pl.ANY)]][part]
            + [whole()],
            out_specs=[whole()] * (1 + late + len(sends)),
            input_output_aliases={1 + len(shards) + len(sources): 0},
            scratch_shapes=[
                pltpu.VMEM(((LATE if late else len(shards)) * base, unknowns), jnp.bfloat16),
                pltpu.VMEM(near_blocks.shape, jnp.bfloat16),
                pltpu.SemaphoreType.DMA((max(CHUNKS, stored // BATCH[part]),)),
            ],
            compiler_params=pltpu.CompilerParams(vmem_limit_bytes=NEAR_VMEM),
            cost_estimate=pl.CostEstimate(
                flops=16 * stored * directions * unknowns * unknowns,
                bytes_accessed=16 << 20,
                transcendentals=0,
            ),
            name="near",
        )(lists, *shards, *sources, sums)

    def far_field(couple):
        return pl.pallas_call(
            far_kernel,
            out_shape=jax.ShapeDtypeStruct((clusters, directions, unknowns), jnp.float32),
            in_specs=[whole()] * 2 + [whole(pltpu.SMEM)] + [whole()] * 5,
            out_specs=whole(),
            compiler_params=pltpu.CompilerParams(vmem_limit_bytes=FAR_VMEM),
            cost_estimate=pl.CostEstimate(
                flops=4 * clusters * rank_k * pairs * rank_k * unknowns,
                bytes_accessed=8 << 20,
                transcendentals=0,
            ),
            name="far",
        )(
            *coefs,
            here,
            couple,
            far_slot.reshape(1, pairs),
            far_dev.reshape(1, pairs),
            far_cslot.reshape(1, pairs),
            basis_out,
        )

    (sums,) = near(0, shards[: chips - LATE], [mate_blocks], sums)
    (sums,) = near(1, shards[: chips - LATE + 1], [near_blocks], sums)
    sums, coef, *sends = near(2, shards, [near_blocks, mate_blocks], sums)
    mates = [move(sends[0], mate)]
    coefs = [coef, move(coef, mate)]

    piece = clusters // UNITS

    def term(k, h):
        part, at = (0, k) if k < 2 else (1, k - 2)
        got = mates[part][at * clusters + h * piece : at * clusters + (h + 1) * piece]
        at = k * clusters + h * piece
        return sums[at : at + piece] + got.astype(jnp.float32)

    flow = lax.optimization_barrier(
        [[term(k, h).astype(jnp.bfloat16) for h in range(UNITS)] for k in range(2)]
    )
    mates.append(move(after(sends[1], *flow[0], *flow[1]), mate))
    flow = [[move(unit, ahead) for unit in units] for units in flow]
    for k in range(2, chips - 1):
        for h in range(UNITS):
            unit = (flow[k % 2][h].astype(jnp.float32) + term(k, h)).astype(jnp.bfloat16)
            unit, mates[1] = lax.optimization_barrier((unit, mates[1]))
            if (k, h) == (chips - 2, UNITS - 1):
                couple = after(couple, unit)
            flow[k % 2][h] = move(unit, ahead)
    last = [move(unit, mate) for unit in flow[1]]
    own = sums[(chips - 1) * clusters : chips * clusters]
    total = far_field(couple) + own + mates[1][(chips - 3) * clusters :].astype(jnp.float32)
    total = total + jnp.concatenate(flow[0], axis=0).astype(jnp.float32)
    total = lax.optimization_barrier(total)
    return (total + jnp.concatenate(last, axis=0).astype(jnp.float32)).astype(jnp.bfloat16)


def on_device(*args):
    rhs, near_blocks = args[0], args[1]
    clusters, directions, unknowns = rhs.shape
    small = lax.axis_size("blk") == 16 and clusters == 16
    if small and near_blocks.shape[0] == unknowns and 2 * directions == unknowns:
        return stationary(*args)
    return routed(*args)


def solution(mesh):
    placed = (
        P(("groups", "blk"), None, None),
        P(("groups", "blk"), None, None),
        P(("groups", "blk"), None),
        P(("groups", "blk")),
        P(("groups", "blk")),
        P(("groups", "blk"), None, None),
        P(("groups", "blk")),
        P(("groups", "blk"), None),
        P(("groups", "blk")),
        P(("groups", "blk"), None, None),
        P(("groups", "blk"), None, None),
    )
    return jax.shard_map(
        on_device,
        mesh=mesh,
        in_specs=placed,
        out_specs=P(("groups", "blk"), None, None),
        check_vma=False,
    )
```

```python
import functools

import jax
import jax.numpy as jnp
from jax import lax
from jax.experimental import pallas as pl
from jax.experimental.pallas import tpu as pltpu
from jax.sharding import PartitionSpec as P

BATCH = 16, 8
CHUNKS = 4
LATE = 2
UNITS = 1
PROLOGUE_VMEM = 58 << 20
NEAR_VMEM = 20 << 20
FAR_VMEM = 16 << 20


def with_halo(cells, sides, width):
    for axis, dim in sides:
        count = lax.axis_size(axis)
        head = lax.slice_in_dim(cells, 0, width, axis=dim)
        tail = lax.slice_in_dim(cells, cells.shape[dim] - width, cells.shape[dim], axis=dim)
        cells = jnp.concatenate(
            [
                lax.ppermute(tail, axis, [(i, (i + 1) % count) for i in range(count)]),
                cells,
                lax.ppermute(head, axis, [((i + 1) % count, i) for i in range(count)]),
            ],
            axis=dim,
        )
    return cells


def place_ranks(targets, count):
    onehot = (targets[:, None] == jnp.arange(count, dtype=jnp.int32)[None, :]).astype(jnp.int32)
    before = jnp.cumsum(onehot, axis=0) - onehot
    return jnp.sum(before * onehot, axis=1)


def routed(
    rhs,
    near_blocks,
    near_owner,
    near_slot,
    near_offset,
    far_coupling,
    far_slot,
    far_dev,
    far_cslot,
    basis_out,
    basis_in,
):
    clusters = rhs.shape[0]
    directions = rhs.shape[1]
    unknowns = rhs.shape[2]
    cycle_size = lax.axis_size("blk")
    stored = near_blocks.shape[0]
    capacity = max(2, 2 * stored // cycle_size)
    owners = near_owner[:, 0]
    target = owners * capacity + place_ranks(owners, cycle_size)
    outbox = (
        jnp.zeros((cycle_size * capacity, unknowns, unknowns), near_blocks.dtype)
        .at[target]
        .set(near_blocks)
    )
    labels = (
        jnp.zeros((cycle_size * capacity, 2), jnp.int32)
        .at[target]
        .set(jnp.stack([near_slot, near_offset], axis=1))
    )
    window = with_halo(rhs, (("blk", 0),), clusters)
    inbox, in_labels = (
        lax.all_to_all(outbox, "blk", split_axis=0, concat_axis=0, tiled=True),
        lax.all_to_all(labels, "blk", split_axis=0, concat_axis=0, tiled=True),
    )
    position = clusters + in_labels[:, 0] + in_labels[:, 1]
    columns = jnp.take(window, position, axis=0)
    products = jnp.einsum("srj,sij->sri", columns, inbox, preferred_element_type=jnp.float32)
    selector = (in_labels[:, 0][None, :] == jnp.arange(clusters, dtype=jnp.int32)[:, None]).astype(
        jnp.float32
    )
    near_sum = jnp.dot(
        selector,
        products.reshape(products.shape[0], -1),
        precision=lax.Precision.HIGHEST,
        preferred_element_type=jnp.float32,
    ).reshape(clusters, directions, unknowns)
    coef_local = jnp.einsum(
        "ckj,crj->crk", basis_in, rhs, preferred_element_type=jnp.float32
    ).astype(jnp.bfloat16)
    rank_k = basis_in.shape[1]
    coef_local = coef_local.reshape(clusters, directions * rank_k)
    pairs = far_slot.shape[0]
    wanted = far_dev[:, 0] * clusters + far_cslot
    piece = lax.all_gather(coef_local, "blk", axis=0, tiled=True)
    chosen = jnp.take(piece, wanted, axis=0)
    coupled = jnp.einsum(
        "pkq,prq->prk",
        far_coupling,
        chosen.reshape(pairs, directions, rank_k),
        preferred_element_type=jnp.float32,
    )
    row_pick = (far_slot[None, :] == jnp.arange(clusters, dtype=jnp.int32)[:, None]).astype(
        jnp.float32
    )
    gathered = jnp.dot(
        row_pick,
        coupled.reshape(pairs, -1),
        precision=lax.Precision.HIGHEST,
        preferred_element_type=jnp.float32,
    )
    gathered = gathered.astype(jnp.bfloat16).reshape(clusters, directions, rank_k)
    far_sum = jnp.einsum("crk,ckb->crb", gathered, basis_out, preferred_element_type=jnp.float32)
    return (near_sum + far_sum).astype(jnp.bfloat16)


def whole(space=pltpu.VMEM):
    return pl.BlockSpec(memory_space=space)


def prologue_kernel(
    count, me_ref, owner_ref, slot_ref, offset_ref, rhs_ref, basis_ref, payload_ref, list_ref
):
    clusters, directions, unknowns = rhs_ref.shape
    base = clusters * directions
    payload_ref[0:base, :] = rhs_ref[...].reshape(base, unknowns)
    rank_k = basis_ref.shape[1]
    half = clusters // 2
    rows = []
    for c in range(half):
        parts = [
            lax.dot_general(
                basis_ref[e],
                rhs_ref[e],
                (((1,), (1,)), ((), ())),
                preferred_element_type=jnp.float32,
            )
            for e in (c, c + half)
        ]
        rows.append(jnp.concatenate(parts, axis=1))
    rows = jnp.concatenate(rows, axis=0).astype(payload_ref.dtype)
    square = (rows.shape[0], rows.shape[0])
    row = lax.broadcasted_iota(jnp.int32, square, 0)
    source = (row & (half - 1)) * rank_k + row // half
    order = jnp.where(lax.broadcasted_iota(jnp.int32, square, 1) == source, 1.0, 0.0)
    payload_ref[base:, :] = jnp.dot(
        order.astype(rows.dtype), rows, preferred_element_type=jnp.float32
    ).astype(payload_ref.dtype)

    me, owner, slot = me_ref[0], owner_ref[...], slot_ref[...]
    stored = owner.shape[1]
    place = scatter_place(owner, me, count) * clusters + slot
    column = (owner * clusters + slot + offset_ref[...]) & (count * clusters - 1)
    shard = gather_place(column // clusters, me, count)
    theirs = (shard == count // 2).astype(jnp.int32)
    shard = jnp.where(theirs == 1, gather_place(column // clusters, me ^ 1, count), shard)
    column_place = shard * clusters + (column & (clusters - 1))
    late = (shard >= count // 2 - LATE).astype(jnp.int32)
    square = (stored, stored)
    group = jnp.broadcast_to((2 * theirs + late).astype(jnp.float32), square)
    group_of_row = jnp.transpose(group)
    row_at = lax.broadcasted_iota(jnp.int32, square, 0)
    lane_at = lax.broadcasted_iota(jnp.int32, square, 1)
    lane = lane_at.astype(jnp.float32)
    before = (group_of_row < group) | ((group_of_row == group) & (row_at < lane_at))
    rank = jnp.sum(jnp.where(before, 1.0, 0.0), axis=0, keepdims=True)
    rank = jnp.transpose(jnp.broadcast_to(rank, square))
    here = jnp.where(rank == lane, 1.0, 0.0).astype(jnp.bfloat16)
    starts = jnp.sum(jnp.where(group_of_row < lane, 1.0, 0.0), axis=0, keepdims=True)
    values = jnp.concatenate(
        [lane[0:1], place.astype(jnp.float32), column_place.astype(jnp.float32)]
        + [jnp.zeros((5, stored), jnp.float32)],
        axis=0,
    )
    values = jnp.dot(values.astype(jnp.bfloat16), here, preferred_element_type=jnp.float32)
    values = jnp.concatenate([values[0:3], starts, values[4:8]], axis=0)
    list_ref[...] = values.astype(jnp.int32)


def join_kernel(first_ref, second_ref, out_ref):
    rows = first_ref.shape[0]
    out_ref[0:rows] = first_ref[...]
    out_ref[rows:] = second_ref[...]


def near_kernel(late, batch, shards, sends, list_ref, *refs):
    used = LATE if late else shards
    shard_refs, refs = refs[:shards], refs[shards:]
    (own_ref, mate_hbm), refs = refs[:2], refs[2 + late :]
    sums, refs = refs[0], refs[1:]
    if late:
        coef_ref, send_refs, refs = refs[0], refs[1 : 1 + sends], refs[1 + sends :]
    columns, blocks, block_sem = refs
    stored = blocks.shape[0]
    directions = sums.shape[1]
    span = columns.shape[0] // used
    dummy = sums.shape[0] - 1
    chunk = stored // CHUNKS

    begin, end = list_ref[3, late], list_ref[3, late + 1]
    begin_there, end_there = list_ref[11, 2 + late], list_ref[11, 3 + late]
    steps_there = (end_there - begin_there + batch - 1) // batch

    def fetch(j, carry):
        at = jnp.minimum(begin_there + j, end_there - 1)
        pltpu.make_async_copy(
            mate_hbm.at[list_ref[8, at]], blocks.at[j], block_sem.at[j // batch]
        ).start()
        return carry

    if late:
        lax.fori_loop(0, steps_there * batch, fetch, 0)
    else:
        for c in range(CHUNKS):
            at = pl.ds(c * chunk, chunk)
            pltpu.make_async_copy(mate_hbm.at[at], blocks.at[at], block_sem.at[c]).start()

    for k, ref in enumerate(shard_refs[shards - used :]):

        def gather(i, carry, k=k, ref=ref):
            at = pl.multiple_of(i * directions, directions)
            columns[pl.ds(pl.multiple_of(k * span + at, directions), directions)] = ref[
                pl.ds(at, directions)
            ]
            return carry

        lax.fori_loop(0, span // directions, gather, 0, unroll=8)
    if late:
        tail = coef_ref.shape[0] // shards
        for k, ref in enumerate(shard_refs):
            coef_ref[k * tail : (k + 1) * tail] = ref[span : span + tail]
    else:

        def clear(i, carry):
            sums[i] = jnp.zeros(sums.shape[1:], sums.dtype)
            return carry

        lax.fori_loop(0, dummy, clear, 0, unroll=8)
        clear(dummy, 0)

    def run(begin, end, row, swap, block_of):
        def entry(j):
            return jnp.minimum(begin + j, end - 1)

        def body(step, carry):
            first = step * batch
            products = []

            def add(i):
                place = list_ref[row + 1, entry(first + i)] ^ swap
                place = jnp.where(begin + first + i < end, place, dummy)
                sums[place] = sums[place] + products[i]

            take, carry = block_of(first, entry, carry)
            for i in range(batch):
                start = list_ref[row + 2, entry(first + i)] * directions - (shards - used) * span
                products.append(
                    lax.dot_general(
                        columns[pl.ds(pl.multiple_of(start, directions), directions)],
                        take(i),
                        (((1,), (1,)), ((), ())),
                        preferred_element_type=jnp.float32,
                    )
                )
            for i in range(batch):
                add(i)
            return carry

        return lax.fori_loop(0, (end - begin + batch - 1) // batch, body, 0)

    def own_blocks(first, entry, carry):
        return lambda i: own_ref[list_ref[0, entry(first + i)]], carry

    def wait(c, carry):
        at = pl.ds(0, chunk)
        pltpu.make_async_copy(mate_hbm.at[at], blocks.at[at], block_sem.at[c]).wait()
        return carry

    def mate_blocks(first, entry, ready):
        if late:
            pltpu.make_async_copy(
                mate_hbm.at[pl.ds(0, batch)],
                blocks.at[pl.ds(first, batch)],
                block_sem.at[first // batch],
            ).wait()
            return lambda i: blocks[first + i], ready
        needed = list_ref[8, entry(first + batch - 1)] // chunk + 1
        lax.fori_loop(ready, needed, wait, 0)
        return lambda i: blocks[list_ref[8, entry(first + i)]], jnp.maximum(ready, needed)

    run(begin, end, 0, 0, own_blocks)
    ready = run(begin_there, end_there, 8, dummy // 2, mate_blocks)
    if not late:
        lax.fori_loop(ready, CHUNKS, wait, 0)
        return
    at = dummy // 2
    for send_ref in send_refs:

        def pack(i, carry, at=at, send_ref=send_ref):
            send_ref[i] = sums[at + i].astype(send_ref.dtype)
            return carry

        lax.fori_loop(0, send_ref.shape[0], pack, 0, unroll=8)
        at += send_ref.shape[0]


def far_kernel(*refs):
    coef_refs = refs[:2]
    me_ref, couple_ref, slot_ref, dev_ref, cslot_ref, basis_ref, out_ref = refs[2:]
    clusters, rank_k, unknowns = basis_ref.shape
    pairs = couple_ref.shape[2]
    directions = out_ref.shape[1]
    half = clusters // 2
    coef = jnp.concatenate([ref[...].astype(jnp.float32) for ref in coef_refs], axis=0)
    coef = coef.reshape(-1, rank_k, half, unknowns)
    count = coef.shape[0]
    hot = (
        lax.broadcasted_iota(jnp.int32, (clusters, pairs), 0)
        == jnp.broadcast_to(slot_ref[...], (clusters, pairs))
    ).astype(jnp.float32).astype(jnp.bfloat16)
    away = gather_place(dev_ref[...], me_ref[0], count)
    theirs = count // 2 + gather_place(dev_ref[...], me_ref[0] ^ 1, count)
    away = jnp.where(away == count // 2, theirs, away)
    cslot = cslot_ref[...]
    high = (cslot >= half).astype(jnp.int32)
    at = away * half + cslot - high * half
    table_rows = (count * half, pairs)
    pick = jnp.where(
        lax.broadcasted_iota(jnp.int32, table_rows, 0) == jnp.broadcast_to(at, table_rows), 1.0, 0.0
    )
    pick = jnp.transpose(pick).astype(jnp.bfloat16)
    lanes = (unknowns, pairs)
    keep = jnp.where(
        lax.broadcasted_iota(jnp.int32, lanes, 0) // directions == jnp.broadcast_to(high, lanes),
        1.0,
        0.0,
    )
    keep = jnp.transpose(keep).astype(jnp.bfloat16)
    total = jnp.zeros((clusters * rank_k, unknowns), jnp.float32)
    for q in range(rank_k):
        table = coef[:, q].reshape(count * half, unknowns).astype(jnp.bfloat16)
        chosen = jnp.dot(pick, table, preferred_element_type=jnp.float32).astype(jnp.bfloat16)
        chosen = chosen * keep
        couple = couple_ref[q]
        weight = jnp.concatenate([couple * hot[s : s + 1] for s in range(clusters)], axis=0)
        total = total + jnp.dot(weight, chosen, preferred_element_type=jnp.float32)
    total = total + pltpu.roll(total, unknowns // 2, axis=1)
    gathered = jnp.transpose(total)[0:directions, :].astype(jnp.bfloat16).astype(jnp.float32)
    lane = lax.broadcasted_iota(jnp.int32, gathered.shape, 1) // rank_k
    basis = basis_ref[...].reshape(clusters * rank_k, unknowns)
    for s in range(clusters):
        own = jnp.where(lane == s, gathered, 0.0).astype(jnp.bfloat16)
        out_ref[s] = jnp.dot(own, basis, preferred_element_type=jnp.float32)


def ring_device(place, core, chips):
    depth = chips // 2
    place = place % chips
    z, y = (place, 0) if place < depth else (chips - 1 - place, 1)
    return (z * 2 + y) * 2 + core


def ring_pairs(count):
    chips = count // 2
    cores = [(p, c) for p in range(chips) for c in range(2)]
    ahead = [(ring_device(p, c, chips), ring_device(p + 1 - 2 * c, c, chips)) for p, c in cores]
    cross = [
        (ring_device(p, c, chips), ring_device(p - 1 + 2 * c, 1 - c, chips)) for p, c in cores
    ]
    return ahead, cross


def ring_place(device, chips):
    z, y = device >> 2, (device >> 1) & 1
    return jnp.where(y == 0, z, chips - 1 - z)


def gather_place(device, me, count):
    chips = count // 2
    depth = chips // 2
    back = (1 - 2 * (me & 1)) * (ring_place(me, chips) - ring_place(device, chips))
    back = (back + chips) & (chips - 1)
    other = (device ^ me) & 1
    here = (back < depth) & (back > 0) | (back == 0) & (other == 1) | (back == depth) & (other == 0)
    return jnp.where(here, jnp.where(back == 0, 0, 2 * back - 1 + other), chips)


def scatter_place(device, me, count):
    chips = count // 2
    depth = chips // 2
    ahead = (ring_place(device, chips) - ring_place(me, chips) + chips) & (chips - 1)
    core = device & 1
    handler = jnp.where((ahead & (depth - 1)) == 0, core, (ahead > depth).astype(jnp.int32))
    steps = jnp.where(handler == 0, ahead, (chips - ahead) & (chips - 1))
    place = jnp.where(
        steps == depth,
        0,
        jnp.where(steps == 0, chips - 1, 2 * (depth - steps) - (core ^ handler)),
    )
    return place + jnp.where(handler == (me & 1), 0, chips)


def stationary(
    rhs,
    near_blocks,
    near_owner,
    near_slot,
    near_offset,
    far_coupling,
    far_slot,
    far_dev,
    far_cslot,
    basis_out,
    basis_in,
):
    clusters, directions, unknowns = rhs.shape
    rank_k = basis_in.shape[1]
    count = lax.axis_size("blk")
    chips = count // 2
    depth = chips // 2
    me = lax.axis_index("blk")
    stored = near_blocks.shape[0]
    pairs = far_slot.shape[0]
    half = clusters // 2
    ahead, cross = ring_pairs(count)
    mate = [(i, i ^ 1) for i in range(count)]
    side = [(i, i ^ 2) for i in range(count)]

    def move(values, where):
        return lax.ppermute(values, "blk", where)

    def after(values, *others):
        return lax.optimization_barrier((values, *others))[0]

    here = me.astype(jnp.int32).reshape(1)
    base = clusters * directions
    payload, lists = pl.pallas_call(
        functools.partial(prologue_kernel, count),
        out_shape=[
            jax.ShapeDtypeStruct((base + half * rank_k, unknowns), jnp.bfloat16),
            jax.ShapeDtypeStruct((8, stored), jnp.int32),
        ],
        in_specs=[whole(pltpu.SMEM)] + [whole()] * 5,
        out_specs=[whole()] * 2,
        compiler_params=pltpu.CompilerParams(vmem_limit_bytes=PROLOGUE_VMEM),
        name="prologue",
    )(
        here,
        near_owner.reshape(1, stored),
        near_slot.reshape(1, stored),
        near_offset.reshape(1, stored),
        rhs,
        basis_in,
    )
    flow = [move(payload, ahead)]
    mate_blocks = move(near_blocks, mate)
    mate_lists = move(lists, mate)
    couple = jnp.transpose(far_coupling, (2, 1, 0))
    flow.append(move(after(payload, couple), cross))
    shards = [move(payload, mate)]
    cost = pl.CostEstimate(
        flops=16 * stored * directions * unknowns * unknowns,
        bytes_accessed=16 << 20,
        transcendentals=0,
    )
    for k in range(1, chips):
        x = 1 - k % 2
        if k == 3:
            flow[x], mate_blocks, shards[0], mate_lists = lax.optimization_barrier(
                (flow[x], mate_blocks, shards[0], mate_lists)
            )
        if k == 4:
            lists = pl.pallas_call(
                join_kernel,
                out_shape=jax.ShapeDtypeStruct((16, stored), jnp.int32),
                in_specs=[whole()] * 2,
                out_specs=whole(),
                cost_estimate=cost,
                name="join",
            )(after(lists, flow[x]), mate_lists)
        if k == 5:
            flow[x], lists = lax.optimization_barrier((flow[x], lists))
        shards.append(flow[x])
        if k < chips - 2:
            flow[x] = move(flow[x], ahead)

    pieces = [2, chips - 2]
    sums_shape = jax.ShapeDtypeStruct((count * clusters + 1, directions, unknowns), jnp.float32)

    def near(late, shards, *sums):
        sends = pieces if late else []
        return pl.pallas_call(
            functools.partial(near_kernel, late, BATCH[late], len(shards), len(sends)),
            out_shape=[sums_shape]
            + [jax.ShapeDtypeStruct((chips * half * rank_k, unknowns), jnp.bfloat16)] * late
            + [
                jax.ShapeDtypeStruct((size * clusters, directions, unknowns), jnp.bfloat16)
                for size in sends
            ],
            in_specs=[whole(pltpu.SMEM)]
            + [whole()] * len(shards)
            + [whole(), whole(pl.ANY)]
            + [whole()] * len(sums),
            out_specs=[whole()] * (1 + late + len(sends)),
            input_output_aliases={3 + len(shards): 0} if sums else {},
            scratch_shapes=[
                pltpu.VMEM(((LATE if late else len(shards)) * base, unknowns), jnp.bfloat16),
                pltpu.VMEM(near_blocks.shape, jnp.bfloat16),
                pltpu.SemaphoreType.DMA((max(CHUNKS, stored // BATCH[late]),)),
            ],
            compiler_params=pltpu.CompilerParams(vmem_limit_bytes=NEAR_VMEM),
            cost_estimate=cost,
            name="near",
        )(lists, *shards, near_blocks, mate_blocks, *sums)

    def far_field(couple):
        return pl.pallas_call(
            far_kernel,
            out_shape=jax.ShapeDtypeStruct((clusters, directions, unknowns), jnp.float32),
            in_specs=[whole()] * 2 + [whole(pltpu.SMEM)] + [whole()] * 5,
            out_specs=whole(),
            compiler_params=pltpu.CompilerParams(vmem_limit_bytes=FAR_VMEM),
            cost_estimate=pl.CostEstimate(
                flops=4 * clusters * rank_k * pairs * rank_k * unknowns,
                bytes_accessed=8 << 20,
                transcendentals=0,
            ),
            name="far",
        )(
            *coefs,
            here,
            couple,
            far_slot.reshape(1, pairs),
            far_dev.reshape(1, pairs),
            far_cslot.reshape(1, pairs),
            basis_out,
        )

    (sums,) = near(0, shards[: chips - LATE])
    sums, coef, *sends = near(1, shards, sums)
    mates = [move(sends[0], mate)]
    coefs = [coef, move(coef, mate)]

    piece = clusters // UNITS

    def term(k, h):
        part, at = (0, k) if k < 2 else (1, k - 2)
        got = mates[part][at * clusters + h * piece : at * clusters + (h + 1) * piece]
        at = k * clusters + h * piece
        return sums[at : at + piece] + got.astype(jnp.float32)

    flow = lax.optimization_barrier(
        [[term(k, h).astype(jnp.bfloat16) for h in range(UNITS)] for k in range(2)]
    )
    mates.append(move(after(sends[1], *flow[0], *flow[1]), mate))
    flow = [[move(unit, ahead) for unit in units] for units in flow]
    for k in range(2, chips - 1):
        for h in range(UNITS):
            unit = (flow[k % 2][h].astype(jnp.float32) + term(k, h)).astype(jnp.bfloat16)
            unit, mates[1] = lax.optimization_barrier((unit, mates[1]))
            if (k, h) == (chips - 2, UNITS - 1):
                couple = after(couple, unit)
            flow[k % 2][h] = move(unit, ahead)
    last = [move(unit, mate) for unit in flow[1]]
    own = sums[(chips - 1) * clusters : chips * clusters]
    total = far_field(couple) + own + mates[1][(chips - 3) * clusters :].astype(jnp.float32)
    total = total + jnp.concatenate(flow[0], axis=0).astype(jnp.float32)
    total = lax.optimization_barrier(total)
    return (total + jnp.concatenate(last, axis=0).astype(jnp.float32)).astype(jnp.bfloat16)


def on_device(*args):
    rhs, near_blocks = args[0], args[1]
    clusters, directions, unknowns = rhs.shape
    small = lax.axis_size("blk") == 16 and clusters == 16
    if small and near_blocks.shape[0] == unknowns and 2 * directions == unknowns:
        return stationary(*args)
    return routed(*args)


def solution(mesh):
    placed = (
        P(("groups", "blk"), None, None),
        P(("groups", "blk"), None, None),
        P(("groups", "blk"), None),
        P(("groups", "blk")),
        P(("groups", "blk")),
        P(("groups", "blk"), None, None),
        P(("groups", "blk")),
        P(("groups", "blk"), None),
        P(("groups", "blk")),
        P(("groups", "blk"), None, None),
        P(("groups", "blk"), None, None),
    )
    return jax.shard_map(
        on_device,
        mesh=mesh,
        in_specs=placed,
        out_specs=P(("groups", "blk"), None, None),
        check_vma=False,
    )
```

```python
import functools

import jax
import jax.numpy as jnp
from jax import lax
from jax.experimental import pallas as pl
from jax.experimental.pallas import tpu as pltpu
from jax.sharding import PartitionSpec as P

BATCH = 16, 8
CHUNKS = 4
LATE = 2
UNITS = 1
PROLOGUE_VMEM = 58 << 20
NEAR_VMEM = 20 << 20
FAR_VMEM = 16 << 20


def with_halo(cells, sides, width):
    for axis, dim in sides:
        count = lax.axis_size(axis)
        head = lax.slice_in_dim(cells, 0, width, axis=dim)
        tail = lax.slice_in_dim(cells, cells.shape[dim] - width, cells.shape[dim], axis=dim)
        cells = jnp.concatenate(
            [
                lax.ppermute(tail, axis, [(i, (i + 1) % count) for i in range(count)]),
                cells,
                lax.ppermute(head, axis, [((i + 1) % count, i) for i in range(count)]),
            ],
            axis=dim,
        )
    return cells


def place_ranks(targets, count):
    onehot = (targets[:, None] == jnp.arange(count, dtype=jnp.int32)[None, :]).astype(jnp.int32)
    before = jnp.cumsum(onehot, axis=0) - onehot
    return jnp.sum(before * onehot, axis=1)


def routed(
    rhs,
    near_blocks,
    near_owner,
    near_slot,
    near_offset,
    far_coupling,
    far_slot,
    far_dev,
    far_cslot,
    basis_out,
    basis_in,
):
    clusters = rhs.shape[0]
    directions = rhs.shape[1]
    unknowns = rhs.shape[2]
    cycle_size = lax.axis_size("blk")
    stored = near_blocks.shape[0]
    capacity = max(2, 2 * stored // cycle_size)
    owners = near_owner[:, 0]
    target = owners * capacity + place_ranks(owners, cycle_size)
    outbox = (
        jnp.zeros((cycle_size * capacity, unknowns, unknowns), near_blocks.dtype)
        .at[target]
        .set(near_blocks)
    )
    labels = (
        jnp.zeros((cycle_size * capacity, 2), jnp.int32)
        .at[target]
        .set(jnp.stack([near_slot, near_offset], axis=1))
    )
    window = with_halo(rhs, (("blk", 0),), clusters)
    inbox, in_labels = (
        lax.all_to_all(outbox, "blk", split_axis=0, concat_axis=0, tiled=True),
        lax.all_to_all(labels, "blk", split_axis=0, concat_axis=0, tiled=True),
    )
    position = clusters + in_labels[:, 0] + in_labels[:, 1]
    columns = jnp.take(window, position, axis=0)
    products = jnp.einsum("srj,sij->sri", columns, inbox, preferred_element_type=jnp.float32)
    selector = (in_labels[:, 0][None, :] == jnp.arange(clusters, dtype=jnp.int32)[:, None]).astype(
        jnp.float32
    )
    near_sum = jnp.dot(
        selector,
        products.reshape(products.shape[0], -1),
        precision=lax.Precision.HIGHEST,
        preferred_element_type=jnp.float32,
    ).reshape(clusters, directions, unknowns)
    coef_local = jnp.einsum(
        "ckj,crj->crk", basis_in, rhs, preferred_element_type=jnp.float32
    ).astype(jnp.bfloat16)
    rank_k = basis_in.shape[1]
    coef_local = coef_local.reshape(clusters, directions * rank_k)
    pairs = far_slot.shape[0]
    wanted = far_dev[:, 0] * clusters + far_cslot
    piece = lax.all_gather(coef_local, "blk", axis=0, tiled=True)
    chosen = jnp.take(piece, wanted, axis=0)
    coupled = jnp.einsum(
        "pkq,prq->prk",
        far_coupling,
        chosen.reshape(pairs, directions, rank_k),
        preferred_element_type=jnp.float32,
    )
    row_pick = (far_slot[None, :] == jnp.arange(clusters, dtype=jnp.int32)[:, None]).astype(
        jnp.float32
    )
    gathered = jnp.dot(
        row_pick,
        coupled.reshape(pairs, -1),
        precision=lax.Precision.HIGHEST,
        preferred_element_type=jnp.float32,
    )
    gathered = gathered.astype(jnp.bfloat16).reshape(clusters, directions, rank_k)
    far_sum = jnp.einsum("crk,ckb->crb", gathered, basis_out, preferred_element_type=jnp.float32)
    return (near_sum + far_sum).astype(jnp.bfloat16)


def whole(space=pltpu.VMEM):
    return pl.BlockSpec(memory_space=space)


def prologue_kernel(
    count, me_ref, owner_ref, slot_ref, offset_ref, rhs_ref, basis_ref, payload_ref, list_ref
):
    clusters, directions, unknowns = rhs_ref.shape
    base = clusters * directions
    payload_ref[0:base, :] = rhs_ref[...].reshape(base, unknowns)
    rank_k = basis_ref.shape[1]
    half = clusters // 2
    rows = []
    for c in range(half):
        parts = [
            lax.dot_general(
                basis_ref[e],
                rhs_ref[e],
                (((1,), (1,)), ((), ())),
                preferred_element_type=jnp.float32,
            )
            for e in (c, c + half)
        ]
        rows.append(jnp.concatenate(parts, axis=1))
    rows = jnp.concatenate(rows, axis=0).astype(payload_ref.dtype)
    square = (rows.shape[0], rows.shape[0])
    row = lax.broadcasted_iota(jnp.int32, square, 0)
    source = (row & (half - 1)) * rank_k + row // half
    order = jnp.where(lax.broadcasted_iota(jnp.int32, square, 1) == source, 1.0, 0.0)
    payload_ref[base:, :] = jnp.dot(
        order.astype(rows.dtype), rows, preferred_element_type=jnp.float32
    ).astype(payload_ref.dtype)

    me, owner, slot = me_ref[0], owner_ref[...], slot_ref[...]
    stored = owner.shape[1]
    place = scatter_place(owner, me, count) * clusters + slot
    column = (owner * clusters + slot + offset_ref[...]) & (count * clusters - 1)
    shard = gather_place(column // clusters, me, count)
    theirs = (shard == count // 2).astype(jnp.int32)
    shard = jnp.where(theirs == 1, gather_place(column // clusters, me ^ 1, count), shard)
    column_place = shard * clusters + (column & (clusters - 1))
    late = (shard >= count // 2 - LATE).astype(jnp.int32)
    square = (stored, stored)
    group = jnp.broadcast_to((2 * theirs + late).astype(jnp.float32), square)
    group_of_row = jnp.transpose(group)
    row_at = lax.broadcasted_iota(jnp.int32, square, 0)
    lane_at = lax.broadcasted_iota(jnp.int32, square, 1)
    lane = lane_at.astype(jnp.float32)
    before = (group_of_row < group) | ((group_of_row == group) & (row_at < lane_at))
    rank = jnp.sum(jnp.where(before, 1.0, 0.0), axis=0, keepdims=True)
    rank = jnp.transpose(jnp.broadcast_to(rank, square))
    here = jnp.where(rank == lane, 1.0, 0.0).astype(jnp.bfloat16)
    starts = jnp.sum(jnp.where(group_of_row < lane, 1.0, 0.0), axis=0, keepdims=True)
    values = jnp.concatenate(
        [lane[0:1], place.astype(jnp.float32), column_place.astype(jnp.float32)]
        + [jnp.zeros((5, stored), jnp.float32)],
        axis=0,
    )
    values = jnp.dot(values.astype(jnp.bfloat16), here, preferred_element_type=jnp.float32)
    values = jnp.concatenate([values[0:3], starts, values[4:8]], axis=0)
    list_ref[...] = values.astype(jnp.int32)


def open_kernel(token_ref, sums):
    def clear(i, carry):
        sums[i] = jnp.zeros(sums.shape[1:], sums.dtype)
        return carry

    lax.fori_loop(0, sums.shape[0] - 1, clear, 0, unroll=8)
    clear(sums.shape[0] - 1, 0)


def near_kernel(late, batch, shards, sends, list_ref, *refs):
    used = LATE if late else shards
    shard_refs, refs = refs[:shards], refs[shards:]
    (own_ref, mate_hbm), refs = refs[:2], refs[3:]
    sums, refs = refs[0], refs[1:]
    if late:
        coef_ref, send_refs, refs = refs[0], refs[1 : 1 + sends], refs[1 + sends :]
    columns, blocks, block_sem = refs
    stored = blocks.shape[0]
    directions = sums.shape[1]
    span = columns.shape[0] // used
    dummy = sums.shape[0] - 1
    chunk = stored // CHUNKS

    begin, end = list_ref[3, late], list_ref[3, late + 1]
    begin_there, end_there = list_ref[11, 2 + late], list_ref[11, 3 + late]
    steps_there = (end_there - begin_there + batch - 1) // batch

    def fetch(j, carry):
        at = jnp.minimum(begin_there + j, end_there - 1)
        pltpu.make_async_copy(
            mate_hbm.at[list_ref[8, at]], blocks.at[j], block_sem.at[j // batch]
        ).start()
        return carry

    if late:
        lax.fori_loop(0, steps_there * batch, fetch, 0)
    else:
        for c in range(CHUNKS):
            at = pl.ds(c * chunk, chunk)
            pltpu.make_async_copy(mate_hbm.at[at], blocks.at[at], block_sem.at[c]).start()

    for k, ref in enumerate(shard_refs[shards - used :]):

        def gather(i, carry, k=k, ref=ref):
            at = pl.multiple_of(i * directions, directions)
            columns[pl.ds(pl.multiple_of(k * span + at, directions), directions)] = ref[
                pl.ds(at, directions)
            ]
            return carry

        lax.fori_loop(0, span // directions, gather, 0, unroll=8)
    if late:
        tail = coef_ref.shape[0] // shards
        for k, ref in enumerate(shard_refs):
            coef_ref[k * tail : (k + 1) * tail] = ref[span : span + tail]
    def run(begin, end, row, swap, block_of):
        def entry(j):
            return jnp.minimum(begin + j, end - 1)

        def body(step, carry):
            first = step * batch
            products = []

            def add(i):
                place = list_ref[row + 1, entry(first + i)] ^ swap
                place = jnp.where(begin + first + i < end, place, dummy)
                sums[place] = sums[place] + products[i]

            take, carry = block_of(first, entry, carry)
            for i in range(batch):
                start = list_ref[row + 2, entry(first + i)] * directions - (shards - used) * span
                products.append(
                    lax.dot_general(
                        columns[pl.ds(pl.multiple_of(start, directions), directions)],
                        take(i),
                        (((1,), (1,)), ((), ())),
                        preferred_element_type=jnp.float32,
                    )
                )
            for i in range(batch):
                add(i)
            return carry

        return lax.fori_loop(0, (end - begin + batch - 1) // batch, body, 0)

    def own_blocks(first, entry, carry):
        return lambda i: own_ref[list_ref[0, entry(first + i)]], carry

    def wait(c, carry):
        at = pl.ds(0, chunk)
        pltpu.make_async_copy(mate_hbm.at[at], blocks.at[at], block_sem.at[c]).wait()
        return carry

    def mate_blocks(first, entry, ready):
        if late:
            pltpu.make_async_copy(
                mate_hbm.at[pl.ds(0, batch)],
                blocks.at[pl.ds(first, batch)],
                block_sem.at[first // batch],
            ).wait()
            return lambda i: blocks[first + i], ready
        needed = list_ref[8, entry(first + batch - 1)] // chunk + 1
        lax.fori_loop(ready, needed, wait, 0)
        return lambda i: blocks[list_ref[8, entry(first + i)]], jnp.maximum(ready, needed)

    run(begin, end, 0, 0, own_blocks)
    ready = run(begin_there, end_there, 8, dummy // 2, mate_blocks)
    if not late:
        lax.fori_loop(ready, CHUNKS, wait, 0)
        return
    at = dummy // 2
    for send_ref in send_refs:

        def pack(i, carry, at=at, send_ref=send_ref):
            send_ref[i] = sums[at + i].astype(send_ref.dtype)
            return carry

        lax.fori_loop(0, send_ref.shape[0], pack, 0, unroll=8)
        at += send_ref.shape[0]


def far_kernel(*refs):
    coef_refs = refs[:2]
    me_ref, couple_ref, slot_ref, dev_ref, cslot_ref, basis_ref, out_ref = refs[2:]
    clusters, rank_k, unknowns = basis_ref.shape
    pairs = couple_ref.shape[2]
    directions = out_ref.shape[1]
    half = clusters // 2
    coef = jnp.concatenate([ref[...].astype(jnp.float32) for ref in coef_refs], axis=0)
    coef = coef.reshape(-1, rank_k, half, unknowns)
    count = coef.shape[0]
    hot = (
        lax.broadcasted_iota(jnp.int32, (clusters, pairs), 0)
        == jnp.broadcast_to(slot_ref[...], (clusters, pairs))
    ).astype(jnp.float32).astype(jnp.bfloat16)
    away = gather_place(dev_ref[...], me_ref[0], count)
    theirs = count // 2 + gather_place(dev_ref[...], me_ref[0] ^ 1, count)
    away = jnp.where(away == count // 2, theirs, away)
    cslot = cslot_ref[...]
    high = (cslot >= half).astype(jnp.int32)
    at = away * half + cslot - high * half
    table_rows = (count * half, pairs)
    pick = jnp.where(
        lax.broadcasted_iota(jnp.int32, table_rows, 0) == jnp.broadcast_to(at, table_rows), 1.0, 0.0
    )
    pick = jnp.transpose(pick).astype(jnp.bfloat16)
    lanes = (unknowns, pairs)
    keep = jnp.where(
        lax.broadcasted_iota(jnp.int32, lanes, 0) // directions == jnp.broadcast_to(high, lanes),
        1.0,
        0.0,
    )
    keep = jnp.transpose(keep).astype(jnp.bfloat16)
    total = jnp.zeros((clusters * rank_k, unknowns), jnp.float32)
    for q in range(rank_k):
        table = coef[:, q].reshape(count * half, unknowns).astype(jnp.bfloat16)
        chosen = jnp.dot(pick, table, preferred_element_type=jnp.float32).astype(jnp.bfloat16)
        chosen = chosen * keep
        couple = couple_ref[q]
        weight = jnp.concatenate([couple * hot[s : s + 1] for s in range(clusters)], axis=0)
        total = total + jnp.dot(weight, chosen, preferred_element_type=jnp.float32)
    total = total + pltpu.roll(total, unknowns // 2, axis=1)
    gathered = jnp.transpose(total)[0:directions, :].astype(jnp.bfloat16).astype(jnp.float32)
    lane = lax.broadcasted_iota(jnp.int32, gathered.shape, 1) // rank_k
    basis = basis_ref[...].reshape(clusters * rank_k, unknowns)
    for s in range(clusters):
        own = jnp.where(lane == s, gathered, 0.0).astype(jnp.bfloat16)
        out_ref[s] = jnp.dot(own, basis, preferred_element_type=jnp.float32)


def ring_device(place, core, chips):
    depth = chips // 2
    place = place % chips
    z, y = (place, 0) if place < depth else (chips - 1 - place, 1)
    return (z * 2 + y) * 2 + core


def ring_pairs(count):
    chips = count // 2
    cores = [(p, c) for p in range(chips) for c in range(2)]
    ahead = [(ring_device(p, c, chips), ring_device(p + 1 - 2 * c, c, chips)) for p, c in cores]
    cross = [
        (ring_device(p, c, chips), ring_device(p - 1 + 2 * c, 1 - c, chips)) for p, c in cores
    ]
    return ahead, cross


def ring_place(device, chips):
    z, y = device >> 2, (device >> 1) & 1
    return jnp.where(y == 0, z, chips - 1 - z)


def gather_place(device, me, count):
    chips = count // 2
    depth = chips // 2
    back = (1 - 2 * (me & 1)) * (ring_place(me, chips) - ring_place(device, chips))
    back = (back + chips) & (chips - 1)
    other = (device ^ me) & 1
    here = (back < depth) & (back > 0) | (back == 0) & (other == 1) | (back == depth) & (other == 0)
    return jnp.where(here, jnp.where(back == 0, 0, 2 * back - 1 + other), chips)


def scatter_place(device, me, count):
    chips = count // 2
    depth = chips // 2
    ahead = (ring_place(device, chips) - ring_place(me, chips) + chips) & (chips - 1)
    core = device & 1
    handler = jnp.where((ahead & (depth - 1)) == 0, core, (ahead > depth).astype(jnp.int32))
    steps = jnp.where(handler == 0, ahead, (chips - ahead) & (chips - 1))
    place = jnp.where(
        steps == depth,
        0,
        jnp.where(steps == 0, chips - 1, 2 * (depth - steps) - (core ^ handler)),
    )
    return place + jnp.where(handler == (me & 1), 0, chips)


def stationary(
    rhs,
    near_blocks,
    near_owner,
    near_slot,
    near_offset,
    far_coupling,
    far_slot,
    far_dev,
    far_cslot,
    basis_out,
    basis_in,
):
    clusters, directions, unknowns = rhs.shape
    rank_k = basis_in.shape[1]
    count = lax.axis_size("blk")
    chips = count // 2
    depth = chips // 2
    me = lax.axis_index("blk")
    stored = near_blocks.shape[0]
    pairs = far_slot.shape[0]
    half = clusters // 2
    ahead, cross = ring_pairs(count)
    mate = [(i, i ^ 1) for i in range(count)]
    side = [(i, i ^ 2) for i in range(count)]

    def move(values, where):
        return lax.ppermute(values, "blk", where)

    def after(values, *others):
        return lax.optimization_barrier((values, *others))[0]

    here = me.astype(jnp.int32).reshape(1)
    base = clusters * directions
    payload, lists = pl.pallas_call(
        functools.partial(prologue_kernel, count),
        out_shape=[
            jax.ShapeDtypeStruct((base + half * rank_k, unknowns), jnp.bfloat16),
            jax.ShapeDtypeStruct((8, stored), jnp.int32),
        ],
        in_specs=[whole(pltpu.SMEM)] + [whole()] * 5,
        out_specs=[whole()] * 2,
        compiler_params=pltpu.CompilerParams(vmem_limit_bytes=PROLOGUE_VMEM),
        name="prologue",
    )(
        here,
        near_owner.reshape(1, stored),
        near_slot.reshape(1, stored),
        near_offset.reshape(1, stored),
        rhs,
        basis_in,
    )
    flow = [move(payload, ahead)]
    mate_blocks = move(near_blocks, mate)
    mate_lists = move(lists, mate)
    couple = jnp.transpose(far_coupling, (2, 1, 0))
    flow.append(move(after(payload, couple), cross))
    shards = [move(payload, mate)]
    cost = pl.CostEstimate(
        flops=16 * stored * directions * unknowns * unknowns,
        bytes_accessed=16 << 20,
        transcendentals=0,
    )
    for k in range(1, chips):
        x = 1 - k % 2
        if k == 3:
            flow[x], mate_blocks, shards[0], mate_lists = lax.optimization_barrier(
                (flow[x], mate_blocks, shards[0], mate_lists)
            )
        if k == 4:
            lists = jnp.concatenate([after(lists, flow[x]), mate_lists], axis=0)
        if k == 5:
            flow[x], lists = lax.optimization_barrier((flow[x], lists))
        shards.append(flow[x])
        if k < chips - 2:
            flow[x] = move(flow[x], ahead)

    pieces = [2, chips - 2]
    sums_shape = jax.ShapeDtypeStruct((count * clusters + 1, directions, unknowns), jnp.float32)

    def near(late, shards, sums):
        sends = pieces if late else []
        return pl.pallas_call(
            functools.partial(near_kernel, late, BATCH[late], len(shards), len(sends)),
            out_shape=[sums_shape]
            + [jax.ShapeDtypeStruct((chips * half * rank_k, unknowns), jnp.bfloat16)] * late
            + [
                jax.ShapeDtypeStruct((size * clusters, directions, unknowns), jnp.bfloat16)
                for size in sends
            ],
            in_specs=[whole(pltpu.SMEM)]
            + [whole()] * len(shards)
            + [whole(), whole(pl.ANY), whole()],
            out_specs=[whole()] * (1 + late + len(sends)),
            input_output_aliases={3 + len(shards): 0},
            scratch_shapes=[
                pltpu.VMEM(((LATE if late else len(shards)) * base, unknowns), jnp.bfloat16),
                pltpu.VMEM(near_blocks.shape, jnp.bfloat16),
                pltpu.SemaphoreType.DMA((max(CHUNKS, stored // BATCH[late]),)),
            ],
            compiler_params=pltpu.CompilerParams(vmem_limit_bytes=NEAR_VMEM),
            cost_estimate=cost,
            name="near",
        )(lists, *shards, near_blocks, mate_blocks, sums)

    def far_field(couple):
        return pl.pallas_call(
            far_kernel,
            out_shape=jax.ShapeDtypeStruct((clusters, directions, unknowns), jnp.float32),
            in_specs=[whole()] * 2 + [whole(pltpu.SMEM)] + [whole()] * 5,
            out_specs=whole(),
            compiler_params=pltpu.CompilerParams(vmem_limit_bytes=FAR_VMEM),
            cost_estimate=pl.CostEstimate(
                flops=4 * clusters * rank_k * pairs * rank_k * unknowns,
                bytes_accessed=8 << 20,
                transcendentals=0,
            ),
            name="far",
        )(
            *coefs,
            here,
            couple,
            far_slot.reshape(1, pairs),
            far_dev.reshape(1, pairs),
            far_cslot.reshape(1, pairs),
            basis_out,
        )

    sums = pl.pallas_call(
        open_kernel,
        out_shape=sums_shape,
        in_specs=[whole()],
        out_specs=whole(),
        cost_estimate=cost,
        name="open",
    )(lists)
    (sums,) = near(0, shards[: chips - LATE], sums)
    sums, coef, *sends = near(1, shards, sums)
    mates = [move(sends[0], mate)]
    coefs = [coef, move(coef, mate)]

    piece = clusters // UNITS

    def term(k, h):
        part, at = (0, k) if k < 2 else (1, k - 2)
        got = mates[part][at * clusters + h * piece : at * clusters + (h + 1) * piece]
        at = k * clusters + h * piece
        return sums[at : at + piece] + got.astype(jnp.float32)

    flow = lax.optimization_barrier(
        [[term(k, h).astype(jnp.bfloat16) for h in range(UNITS)] for k in range(2)]
    )
    mates.append(move(after(sends[1], *flow[0], *flow[1]), mate))
    flow = [[move(unit, ahead) for unit in units] for units in flow]
    for k in range(2, chips - 1):
        for h in range(UNITS):
            unit = (flow[k % 2][h].astype(jnp.float32) + term(k, h)).astype(jnp.bfloat16)
            unit, mates[1] = lax.optimization_barrier((unit, mates[1]))
            if (k, h) == (chips - 2, UNITS - 1):
                couple = after(couple, unit)
            flow[k % 2][h] = move(unit, ahead)
    last = [move(unit, mate) for unit in flow[1]]
    own = sums[(chips - 1) * clusters : chips * clusters]
    total = far_field(couple) + own + mates[1][(chips - 3) * clusters :].astype(jnp.float32)
    total = total + jnp.concatenate(flow[0], axis=0).astype(jnp.float32)
    total = lax.optimization_barrier(total)
    return (total + jnp.concatenate(last, axis=0).astype(jnp.float32)).astype(jnp.bfloat16)


def on_device(*args):
    rhs, near_blocks = args[0], args[1]
    clusters, directions, unknowns = rhs.shape
    small = lax.axis_size("blk") == 16 and clusters == 16
    if small and near_blocks.shape[0] == unknowns and 2 * directions == unknowns:
        return stationary(*args)
    return routed(*args)


def solution(mesh):
    placed = (
        P(("groups", "blk"), None, None),
        P(("groups", "blk"), None, None),
        P(("groups", "blk"), None),
        P(("groups", "blk")),
        P(("groups", "blk")),
        P(("groups", "blk"), None, None),
        P(("groups", "blk")),
        P(("groups", "blk"), None),
        P(("groups", "blk")),
        P(("groups", "blk"), None, None),
        P(("groups", "blk"), None, None),
    )
    return jax.shard_map(
        on_device,
        mesh=mesh,
        in_specs=placed,
        out_specs=P(("groups", "blk"), None, None),
        check_vma=False,
    )
```

```python
import functools

import jax
import jax.numpy as jnp
from jax import lax
from jax.experimental import pallas as pl
from jax.experimental.pallas import tpu as pltpu
from jax.sharding import PartitionSpec as P

BATCH = 16, 8
CHUNKS = 4
LATE = 2
UNITS = 1
PROLOGUE_VMEM = 58 << 20
NEAR_VMEM = 20 << 20
FAR_VMEM = 16 << 20


def with_halo(cells, sides, width):
    for axis, dim in sides:
        count = lax.axis_size(axis)
        head = lax.slice_in_dim(cells, 0, width, axis=dim)
        tail = lax.slice_in_dim(cells, cells.shape[dim] - width, cells.shape[dim], axis=dim)
        cells = jnp.concatenate(
            [
                lax.ppermute(tail, axis, [(i, (i + 1) % count) for i in range(count)]),
                cells,
                lax.ppermute(head, axis, [((i + 1) % count, i) for i in range(count)]),
            ],
            axis=dim,
        )
    return cells


def place_ranks(targets, count):
    onehot = (targets[:, None] == jnp.arange(count, dtype=jnp.int32)[None, :]).astype(jnp.int32)
    before = jnp.cumsum(onehot, axis=0) - onehot
    return jnp.sum(before * onehot, axis=1)


def routed(
    rhs,
    near_blocks,
    near_owner,
    near_slot,
    near_offset,
    far_coupling,
    far_slot,
    far_dev,
    far_cslot,
    basis_out,
    basis_in,
):
    clusters = rhs.shape[0]
    directions = rhs.shape[1]
    unknowns = rhs.shape[2]
    cycle_size = lax.axis_size("blk")
    stored = near_blocks.shape[0]
    capacity = max(2, 2 * stored // cycle_size)
    owners = near_owner[:, 0]
    target = owners * capacity + place_ranks(owners, cycle_size)
    outbox = (
        jnp.zeros((cycle_size * capacity, unknowns, unknowns), near_blocks.dtype)
        .at[target]
        .set(near_blocks)
    )
    labels = (
        jnp.zeros((cycle_size * capacity, 2), jnp.int32)
        .at[target]
        .set(jnp.stack([near_slot, near_offset], axis=1))
    )
    window = with_halo(rhs, (("blk", 0),), clusters)
    inbox, in_labels = (
        lax.all_to_all(outbox, "blk", split_axis=0, concat_axis=0, tiled=True),
        lax.all_to_all(labels, "blk", split_axis=0, concat_axis=0, tiled=True),
    )
    position = clusters + in_labels[:, 0] + in_labels[:, 1]
    columns = jnp.take(window, position, axis=0)
    products = jnp.einsum("srj,sij->sri", columns, inbox, preferred_element_type=jnp.float32)
    selector = (in_labels[:, 0][None, :] == jnp.arange(clusters, dtype=jnp.int32)[:, None]).astype(
        jnp.float32
    )
    near_sum = jnp.dot(
        selector,
        products.reshape(products.shape[0], -1),
        precision=lax.Precision.HIGHEST,
        preferred_element_type=jnp.float32,
    ).reshape(clusters, directions, unknowns)
    coef_local = jnp.einsum(
        "ckj,crj->crk", basis_in, rhs, preferred_element_type=jnp.float32
    ).astype(jnp.bfloat16)
    rank_k = basis_in.shape[1]
    coef_local = coef_local.reshape(clusters, directions * rank_k)
    pairs = far_slot.shape[0]
    wanted = far_dev[:, 0] * clusters + far_cslot
    piece = lax.all_gather(coef_local, "blk", axis=0, tiled=True)
    chosen = jnp.take(piece, wanted, axis=0)
    coupled = jnp.einsum(
        "pkq,prq->prk",
        far_coupling,
        chosen.reshape(pairs, directions, rank_k),
        preferred_element_type=jnp.float32,
    )
    row_pick = (far_slot[None, :] == jnp.arange(clusters, dtype=jnp.int32)[:, None]).astype(
        jnp.float32
    )
    gathered = jnp.dot(
        row_pick,
        coupled.reshape(pairs, -1),
        precision=lax.Precision.HIGHEST,
        preferred_element_type=jnp.float32,
    )
    gathered = gathered.astype(jnp.bfloat16).reshape(clusters, directions, rank_k)
    far_sum = jnp.einsum("crk,ckb->crb", gathered, basis_out, preferred_element_type=jnp.float32)
    return (near_sum + far_sum).astype(jnp.bfloat16)


def whole(space=pltpu.VMEM):
    return pl.BlockSpec(memory_space=space)


def prologue_kernel(
    count, me_ref, owner_ref, slot_ref, offset_ref, rhs_ref, basis_ref, payload_ref, list_ref
):
    clusters, directions, unknowns = rhs_ref.shape
    base = clusters * directions
    payload_ref[0:base, :] = rhs_ref[...].reshape(base, unknowns)
    rank_k = basis_ref.shape[1]
    half = clusters // 2
    rows = []
    for c in range(half):
        parts = [
            lax.dot_general(
                basis_ref[e],
                rhs_ref[e],
                (((1,), (1,)), ((), ())),
                preferred_element_type=jnp.float32,
            )
            for e in (c, c + half)
        ]
        rows.append(jnp.concatenate(parts, axis=1))
    rows = jnp.concatenate(rows, axis=0).astype(payload_ref.dtype)
    square = (rows.shape[0], rows.shape[0])
    row = lax.broadcasted_iota(jnp.int32, square, 0)
    source = (row & (half - 1)) * rank_k + row // half
    order = jnp.where(lax.broadcasted_iota(jnp.int32, square, 1) == source, 1.0, 0.0)
    payload_ref[base:, :] = jnp.dot(
        order.astype(rows.dtype), rows, preferred_element_type=jnp.float32
    ).astype(payload_ref.dtype)

    me, owner, slot = me_ref[0], owner_ref[...], slot_ref[...]
    stored = owner.shape[1]
    place = scatter_place(owner, me, count) * clusters + slot
    column = (owner * clusters + slot + offset_ref[...]) & (count * clusters - 1)
    shard = gather_place(column // clusters, me, count)
    theirs = (shard == count // 2).astype(jnp.int32)
    shard = jnp.where(theirs == 1, gather_place(column // clusters, me ^ 1, count), shard)
    column_place = shard * clusters + (column & (clusters - 1))
    late = (shard >= count // 2 - LATE).astype(jnp.int32)
    square = (stored, stored)
    group = jnp.broadcast_to((2 * theirs + late).astype(jnp.float32), square)
    group_of_row = jnp.transpose(group)
    row_at = lax.broadcasted_iota(jnp.int32, square, 0)
    lane_at = lax.broadcasted_iota(jnp.int32, square, 1)
    lane = lane_at.astype(jnp.float32)
    before = (group_of_row < group) | ((group_of_row == group) & (row_at < lane_at))
    rank = jnp.sum(jnp.where(before, 1.0, 0.0), axis=0, keepdims=True)
    rank = jnp.transpose(jnp.broadcast_to(rank, square))
    here = jnp.where(rank == lane, 1.0, 0.0).astype(jnp.bfloat16)
    starts = jnp.sum(jnp.where(group_of_row < lane, 1.0, 0.0), axis=0, keepdims=True)
    values = jnp.concatenate(
        [lane[0:1], place.astype(jnp.float32), column_place.astype(jnp.float32)]
        + [jnp.zeros((5, stored), jnp.float32)],
        axis=0,
    )
    values = jnp.dot(values.astype(jnp.bfloat16), here, preferred_element_type=jnp.float32)
    values = jnp.concatenate([values[0:3], starts, values[4:8]], axis=0)
    list_ref[...] = values.astype(jnp.int32)


def open_kernel(token_ref, sums):
    def clear(i, carry):
        sums[i] = jnp.zeros(sums.shape[1:], sums.dtype)
        return carry

    lax.fori_loop(0, sums.shape[0] - 1, clear, 0, unroll=8)
    clear(sums.shape[0] - 1, 0)


def near_kernel(late, batch, shards, sends, list_ref, *refs):
    used = LATE if late else shards
    shard_refs, refs = refs[:shards], refs[shards:]
    (own_ref, mate_hbm), refs = refs[:2], refs[3:]
    sums, refs = refs[0], refs[1:]
    if late:
        coef_ref, send_refs, refs = refs[0], refs[1 : 1 + sends], refs[1 + sends :]
    columns, blocks, block_sem = refs
    stored = blocks.shape[0]
    directions = sums.shape[1]
    span = columns.shape[0] // used
    dummy = sums.shape[0] - 1
    chunk = stored // CHUNKS

    begin, end = list_ref[3, late], list_ref[3, late + 1]
    begin_there, end_there = list_ref[11, 2 + late], list_ref[11, 3 + late]
    steps_there = (end_there - begin_there + batch - 1) // batch

    def fetch(j, carry):
        at = jnp.minimum(begin_there + j, end_there - 1)
        pltpu.make_async_copy(
            mate_hbm.at[list_ref[8, at]], blocks.at[j], block_sem.at[j // batch]
        ).start()
        return carry

    if late:
        lax.fori_loop(0, steps_there * batch, fetch, 0)
    else:
        for c in range(CHUNKS):
            at = pl.ds(c * chunk, chunk)
            pltpu.make_async_copy(mate_hbm.at[at], blocks.at[at], block_sem.at[c]).start()

    for k, ref in enumerate(shard_refs[shards - used :]):

        def gather(i, carry, k=k, ref=ref):
            at = pl.multiple_of(i * directions, directions)
            columns[pl.ds(pl.multiple_of(k * span + at, directions), directions)] = ref[
                pl.ds(at, directions)
            ]
            return carry

        lax.fori_loop(0, span // directions, gather, 0, unroll=8)
    if late:
        tail = coef_ref.shape[0] // shards
        for k, ref in enumerate(shard_refs):
            coef_ref[k * tail : (k + 1) * tail] = ref[span : span + tail]
    def run(begin, end, row, swap, block_of):
        def entry(j):
            return jnp.minimum(begin + j, end - 1)

        def body(step, carry):
            first = step * batch
            products = []

            def add(i):
                place = list_ref[row + 1, entry(first + i)] ^ swap
                place = jnp.where(begin + first + i < end, place, dummy)
                sums[place] = sums[place] + products[i]

            take, carry = block_of(first, entry, carry)
            for i in range(batch):
                start = list_ref[row + 2, entry(first + i)] * directions - (shards - used) * span
                products.append(
                    lax.dot_general(
                        columns[pl.ds(pl.multiple_of(start, directions), directions)],
                        take(i),
                        (((1,), (1,)), ((), ())),
                        preferred_element_type=jnp.float32,
                    )
                )
            for i in range(batch):
                add(i)
            return carry

        return lax.fori_loop(0, (end - begin + batch - 1) // batch, body, 0)

    def own_blocks(first, entry, carry):
        return lambda i: own_ref[list_ref[0, entry(first + i)]], carry

    def wait(c, carry):
        at = pl.ds(0, chunk)
        pltpu.make_async_copy(mate_hbm.at[at], blocks.at[at], block_sem.at[c]).wait()
        return carry

    def mate_blocks(first, entry, ready):
        if late:
            pltpu.make_async_copy(
                mate_hbm.at[pl.ds(0, batch)],
                blocks.at[pl.ds(first, batch)],
                block_sem.at[first // batch],
            ).wait()
            return lambda i: blocks[first + i], ready
        needed = list_ref[8, entry(first + batch - 1)] // chunk + 1
        lax.fori_loop(ready, needed, wait, 0)
        return lambda i: blocks[list_ref[8, entry(first + i)]], jnp.maximum(ready, needed)

    run(begin, end, 0, 0, own_blocks)
    ready = run(begin_there, end_there, 8, dummy // 2, mate_blocks)
    if not late:
        lax.fori_loop(ready, CHUNKS, wait, 0)
        return
    at = dummy // 2
    for send_ref in send_refs:

        def pack(i, carry, at=at, send_ref=send_ref):
            send_ref[i] = sums[at + i].astype(send_ref.dtype)
            return carry

        lax.fori_loop(0, send_ref.shape[0], pack, 0, unroll=8)
        at += send_ref.shape[0]


def far_kernel(*refs):
    coef_refs = refs[:2]
    me_ref, couple_ref, slot_ref, dev_ref, cslot_ref, basis_ref, out_ref = refs[2:]
    clusters, rank_k, unknowns = basis_ref.shape
    pairs = couple_ref.shape[2]
    directions = out_ref.shape[1]
    half = clusters // 2
    coef = jnp.concatenate([ref[...].astype(jnp.float32) for ref in coef_refs], axis=0)
    coef = coef.reshape(-1, rank_k, half, unknowns)
    count = coef.shape[0]
    hot = (
        lax.broadcasted_iota(jnp.int32, (clusters, pairs), 0)
        == jnp.broadcast_to(slot_ref[...], (clusters, pairs))
    ).astype(jnp.float32).astype(jnp.bfloat16)
    away = gather_place(dev_ref[...], me_ref[0], count)
    theirs = count // 2 + gather_place(dev_ref[...], me_ref[0] ^ 1, count)
    away = jnp.where(away == count // 2, theirs, away)
    cslot = cslot_ref[...]
    high = (cslot >= half).astype(jnp.int32)
    at = away * half + cslot - high * half
    table_rows = (count * half, pairs)
    pick = jnp.where(
        lax.broadcasted_iota(jnp.int32, table_rows, 0) == jnp.broadcast_to(at, table_rows), 1.0, 0.0
    )
    pick = jnp.transpose(pick).astype(jnp.bfloat16)
    lanes = (unknowns, pairs)
    keep = jnp.where(
        lax.broadcasted_iota(jnp.int32, lanes, 0) // directions == jnp.broadcast_to(high, lanes),
        1.0,
        0.0,
    )
    keep = jnp.transpose(keep).astype(jnp.bfloat16)
    total = jnp.zeros((clusters * rank_k, unknowns), jnp.float32)
    for q in range(rank_k):
        table = coef[:, q].reshape(count * half, unknowns).astype(jnp.bfloat16)
        chosen = jnp.dot(pick, table, preferred_element_type=jnp.float32).astype(jnp.bfloat16)
        chosen = chosen * keep
        couple = couple_ref[q]
        weight = jnp.concatenate([couple * hot[s : s + 1] for s in range(clusters)], axis=0)
        total = total + jnp.dot(weight, chosen, preferred_element_type=jnp.float32)
    total = total + pltpu.roll(total, unknowns // 2, axis=1)
    gathered = jnp.transpose(total)[0:directions, :].astype(jnp.bfloat16).astype(jnp.float32)
    lane = lax.broadcasted_iota(jnp.int32, gathered.shape, 1) // rank_k
    basis = basis_ref[...].reshape(clusters * rank_k, unknowns)
    for s in range(clusters):
        own = jnp.where(lane == s, gathered, 0.0).astype(jnp.bfloat16)
        out_ref[s] = jnp.dot(own, basis, preferred_element_type=jnp.float32)


def ring_device(place, core, chips):
    depth = chips // 2
    place = place % chips
    z, y = (place, 0) if place < depth else (chips - 1 - place, 1)
    return (z * 2 + y) * 2 + core


def ring_pairs(count):
    chips = count // 2
    cores = [(p, c) for p in range(chips) for c in range(2)]
    ahead = [(ring_device(p, c, chips), ring_device(p + 1 - 2 * c, c, chips)) for p, c in cores]
    cross = [
        (ring_device(p, c, chips), ring_device(p - 1 + 2 * c, 1 - c, chips)) for p, c in cores
    ]
    return ahead, cross


def ring_place(device, chips):
    z, y = device >> 2, (device >> 1) & 1
    return jnp.where(y == 0, z, chips - 1 - z)


def gather_place(device, me, count):
    chips = count // 2
    depth = chips // 2
    back = (1 - 2 * (me & 1)) * (ring_place(me, chips) - ring_place(device, chips))
    back = (back + chips) & (chips - 1)
    other = (device ^ me) & 1
    here = (back < depth) & (back > 0) | (back == 0) & (other == 1) | (back == depth) & (other == 0)
    return jnp.where(here, jnp.where(back == 0, 0, 2 * back - 1 + other), chips)


def scatter_place(device, me, count):
    chips = count // 2
    depth = chips // 2
    ahead = (ring_place(device, chips) - ring_place(me, chips) + chips) & (chips - 1)
    core = device & 1
    handler = jnp.where((ahead & (depth - 1)) == 0, core, (ahead > depth).astype(jnp.int32))
    steps = jnp.where(handler == 0, ahead, (chips - ahead) & (chips - 1))
    place = jnp.where(
        steps == depth,
        0,
        jnp.where(steps == 0, chips - 1, 2 * (depth - steps) - (core ^ handler)),
    )
    return place + jnp.where(handler == (me & 1), 0, chips)


def stationary(
    rhs,
    near_blocks,
    near_owner,
    near_slot,
    near_offset,
    far_coupling,
    far_slot,
    far_dev,
    far_cslot,
    basis_out,
    basis_in,
):
    clusters, directions, unknowns = rhs.shape
    rank_k = basis_in.shape[1]
    count = lax.axis_size("blk")
    chips = count // 2
    depth = chips // 2
    me = lax.axis_index("blk")
    stored = near_blocks.shape[0]
    pairs = far_slot.shape[0]
    half = clusters // 2
    ahead, cross = ring_pairs(count)
    mate = [(i, i ^ 1) for i in range(count)]
    side = [(i, i ^ 2) for i in range(count)]

    def move(values, where):
        return lax.ppermute(values, "blk", where)

    def after(values, *others):
        return lax.optimization_barrier((values, *others))[0]

    here = me.astype(jnp.int32).reshape(1)
    base = clusters * directions
    payload, lists = pl.pallas_call(
        functools.partial(prologue_kernel, count),
        out_shape=[
            jax.ShapeDtypeStruct((base + half * rank_k, unknowns), jnp.bfloat16),
            jax.ShapeDtypeStruct((8, stored), jnp.int32),
        ],
        in_specs=[whole(pltpu.SMEM)] + [whole()] * 5,
        out_specs=[whole()] * 2,
        compiler_params=pltpu.CompilerParams(vmem_limit_bytes=PROLOGUE_VMEM),
        name="prologue",
    )(
        here,
        near_owner.reshape(1, stored),
        near_slot.reshape(1, stored),
        near_offset.reshape(1, stored),
        rhs,
        basis_in,
    )
    flow = [move(payload, ahead)]
    mate_blocks = move(near_blocks, mate)
    mate_lists = move(lists, mate)
    couple = jnp.transpose(far_coupling, (2, 1, 0))
    flow.append(move(after(payload, couple), cross))
    shards = [move(payload, mate)]
    cost = pl.CostEstimate(
        flops=16 * stored * directions * unknowns * unknowns,
        bytes_accessed=16 << 20,
        transcendentals=0,
    )
    sums_shape = jax.ShapeDtypeStruct((count * clusters + 1, directions, unknowns), jnp.float32)
    sums = pl.pallas_call(
        open_kernel,
        out_shape=sums_shape,
        in_specs=[whole(pltpu.SMEM)],
        out_specs=whole(),
        compiler_params=pltpu.CompilerParams(vmem_limit_bytes=NEAR_VMEM),
        cost_estimate=cost,
        name="open",
    )(after(here, couple))
    flow[0], sums = lax.optimization_barrier((flow[0], sums))
    for k in range(1, chips):
        x = 1 - k % 2
        if k == 3:
            flow[x], mate_blocks, shards[0], mate_lists = lax.optimization_barrier(
                (flow[x], mate_blocks, shards[0], mate_lists)
            )
        if k == 4:
            lists = jnp.concatenate([after(lists, flow[x]), mate_lists], axis=0)
        if k == 5:
            flow[x], lists = lax.optimization_barrier((flow[x], lists))
        shards.append(flow[x])
        if k < chips - 2:
            flow[x] = move(flow[x], ahead)

    pieces = [2, chips - 2]

    def near(late, shards, sums):
        sends = pieces if late else []
        return pl.pallas_call(
            functools.partial(near_kernel, late, BATCH[late], len(shards), len(sends)),
            out_shape=[sums_shape]
            + [jax.ShapeDtypeStruct((chips * half * rank_k, unknowns), jnp.bfloat16)] * late
            + [
                jax.ShapeDtypeStruct((size * clusters, directions, unknowns), jnp.bfloat16)
                for size in sends
            ],
            in_specs=[whole(pltpu.SMEM)]
            + [whole()] * len(shards)
            + [whole(), whole(pl.ANY), whole()],
            out_specs=[whole()] * (1 + late + len(sends)),
            input_output_aliases={3 + len(shards): 0},
            scratch_shapes=[
                pltpu.VMEM(((LATE if late else len(shards)) * base, unknowns), jnp.bfloat16),
                pltpu.VMEM(near_blocks.shape, jnp.bfloat16),
                pltpu.SemaphoreType.DMA((max(CHUNKS, stored // BATCH[late]),)),
            ],
            compiler_params=pltpu.CompilerParams(vmem_limit_bytes=NEAR_VMEM),
            cost_estimate=cost,
            name="near",
        )(lists, *shards, near_blocks, mate_blocks, sums)

    def far_field(couple):
        return pl.pallas_call(
            far_kernel,
            out_shape=jax.ShapeDtypeStruct((clusters, directions, unknowns), jnp.float32),
            in_specs=[whole()] * 2 + [whole(pltpu.SMEM)] + [whole()] * 5,
            out_specs=whole(),
            compiler_params=pltpu.CompilerParams(vmem_limit_bytes=FAR_VMEM),
            cost_estimate=pl.CostEstimate(
                flops=4 * clusters * rank_k * pairs * rank_k * unknowns,
                bytes_accessed=8 << 20,
                transcendentals=0,
            ),
            name="far",
        )(
            *coefs,
            here,
            couple,
            far_slot.reshape(1, pairs),
            far_dev.reshape(1, pairs),
            far_cslot.reshape(1, pairs),
            basis_out,
        )

    (sums,) = near(0, shards[: chips - LATE], sums)
    sums, coef, *sends = near(1, shards, sums)
    mates = [move(sends[0], mate)]
    coefs = [coef, move(coef, mate)]

    piece = clusters // UNITS

    def term(k, h):
        part, at = (0, k) if k < 2 else (1, k - 2)
        got = mates[part][at * clusters + h * piece : at * clusters + (h + 1) * piece]
        at = k * clusters + h * piece
        return sums[at : at + piece] + got.astype(jnp.float32)

    flow = lax.optimization_barrier(
        [[term(k, h).astype(jnp.bfloat16) for h in range(UNITS)] for k in range(2)]
    )
    mates.append(move(after(sends[1], *flow[0], *flow[1]), mate))
    flow = [[move(unit, ahead) for unit in units] for units in flow]
    for k in range(2, chips - 1):
        for h in range(UNITS):
            unit = (flow[k % 2][h].astype(jnp.float32) + term(k, h)).astype(jnp.bfloat16)
            unit, mates[1] = lax.optimization_barrier((unit, mates[1]))
            if (k, h) == (chips - 2, UNITS - 1):
                couple = after(couple, unit)
            flow[k % 2][h] = move(unit, ahead)
    last = [move(unit, mate) for unit in flow[1]]
    own = sums[(chips - 1) * clusters : chips * clusters]
    total = far_field(couple) + own + mates[1][(chips - 3) * clusters :].astype(jnp.float32)
    total = total + jnp.concatenate(flow[0], axis=0).astype(jnp.float32)
    total = lax.optimization_barrier(total)
    return (total + jnp.concatenate(last, axis=0).astype(jnp.float32)).astype(jnp.bfloat16)


def on_device(*args):
    rhs, near_blocks = args[0], args[1]
    clusters, directions, unknowns = rhs.shape
    small = lax.axis_size("blk") == 16 and clusters == 16
    if small and near_blocks.shape[0] == unknowns and 2 * directions == unknowns:
        return stationary(*args)
    return routed(*args)


def solution(mesh):
    placed = (
        P(("groups", "blk"), None, None),
        P(("groups", "blk"), None, None),
        P(("groups", "blk"), None),
        P(("groups", "blk")),
        P(("groups", "blk")),
        P(("groups", "blk"), None, None),
        P(("groups", "blk")),
        P(("groups", "blk"), None),
        P(("groups", "blk")),
        P(("groups", "blk"), None, None),
        P(("groups", "blk"), None, None),
    )
    return jax.shard_map(
        on_device,
        mesh=mesh,
        in_specs=placed,
        out_specs=P(("groups", "blk"), None, None),
        check_vma=False,
    )
```

```python
import functools

import jax
import jax.numpy as jnp
from jax import lax
from jax.experimental import pallas as pl
from jax.experimental.pallas import tpu as pltpu
from jax.sharding import PartitionSpec as P

BATCH = 16, 8
CHUNKS = 4
LATE = 2
UNITS = 1
PROLOGUE_VMEM = 58 << 20
NEAR_VMEM = 20 << 20
FAR_VMEM = 16 << 20


def with_halo(cells, sides, width):
    for axis, dim in sides:
        count = lax.axis_size(axis)
        head = lax.slice_in_dim(cells, 0, width, axis=dim)
        tail = lax.slice_in_dim(cells, cells.shape[dim] - width, cells.shape[dim], axis=dim)
        cells = jnp.concatenate(
            [
                lax.ppermute(tail, axis, [(i, (i + 1) % count) for i in range(count)]),
                cells,
                lax.ppermute(head, axis, [((i + 1) % count, i) for i in range(count)]),
            ],
            axis=dim,
        )
    return cells


def place_ranks(targets, count):
    onehot = (targets[:, None] == jnp.arange(count, dtype=jnp.int32)[None, :]).astype(jnp.int32)
    before = jnp.cumsum(onehot, axis=0) - onehot
    return jnp.sum(before * onehot, axis=1)


def routed(
    rhs,
    near_blocks,
    near_owner,
    near_slot,
    near_offset,
    far_coupling,
    far_slot,
    far_dev,
    far_cslot,
    basis_out,
    basis_in,
):
    clusters = rhs.shape[0]
    directions = rhs.shape[1]
    unknowns = rhs.shape[2]
    cycle_size = lax.axis_size("blk")
    stored = near_blocks.shape[0]
    capacity = max(2, 2 * stored // cycle_size)
    owners = near_owner[:, 0]
    target = owners * capacity + place_ranks(owners, cycle_size)
    outbox = (
        jnp.zeros((cycle_size * capacity, unknowns, unknowns), near_blocks.dtype)
        .at[target]
        .set(near_blocks)
    )
    labels = (
        jnp.zeros((cycle_size * capacity, 2), jnp.int32)
        .at[target]
        .set(jnp.stack([near_slot, near_offset], axis=1))
    )
    window = with_halo(rhs, (("blk", 0),), clusters)
    inbox, in_labels = (
        lax.all_to_all(outbox, "blk", split_axis=0, concat_axis=0, tiled=True),
        lax.all_to_all(labels, "blk", split_axis=0, concat_axis=0, tiled=True),
    )
    position = clusters + in_labels[:, 0] + in_labels[:, 1]
    columns = jnp.take(window, position, axis=0)
    products = jnp.einsum("srj,sij->sri", columns, inbox, preferred_element_type=jnp.float32)
    selector = (in_labels[:, 0][None, :] == jnp.arange(clusters, dtype=jnp.int32)[:, None]).astype(
        jnp.float32
    )
    near_sum = jnp.dot(
        selector,
        products.reshape(products.shape[0], -1),
        precision=lax.Precision.HIGHEST,
        preferred_element_type=jnp.float32,
    ).reshape(clusters, directions, unknowns)
    coef_local = jnp.einsum(
        "ckj,crj->crk", basis_in, rhs, preferred_element_type=jnp.float32
    ).astype(jnp.bfloat16)
    rank_k = basis_in.shape[1]
    coef_local = coef_local.reshape(clusters, directions * rank_k)
    pairs = far_slot.shape[0]
    wanted = far_dev[:, 0] * clusters + far_cslot
    piece = lax.all_gather(coef_local, "blk", axis=0, tiled=True)
    chosen = jnp.take(piece, wanted, axis=0)
    coupled = jnp.einsum(
        "pkq,prq->prk",
        far_coupling,
        chosen.reshape(pairs, directions, rank_k),
        preferred_element_type=jnp.float32,
    )
    row_pick = (far_slot[None, :] == jnp.arange(clusters, dtype=jnp.int32)[:, None]).astype(
        jnp.float32
    )
    gathered = jnp.dot(
        row_pick,
        coupled.reshape(pairs, -1),
        precision=lax.Precision.HIGHEST,
        preferred_element_type=jnp.float32,
    )
    gathered = gathered.astype(jnp.bfloat16).reshape(clusters, directions, rank_k)
    far_sum = jnp.einsum("crk,ckb->crb", gathered, basis_out, preferred_element_type=jnp.float32)
    return (near_sum + far_sum).astype(jnp.bfloat16)


def whole(space=pltpu.VMEM):
    return pl.BlockSpec(memory_space=space)


def prologue_kernel(
    count, me_ref, owner_ref, slot_ref, offset_ref, rhs_ref, basis_ref, payload_ref, list_ref
):
    clusters, directions, unknowns = rhs_ref.shape
    base = clusters * directions
    payload_ref[0:base, :] = rhs_ref[...].reshape(base, unknowns)
    rank_k = basis_ref.shape[1]
    half = clusters // 2
    rows = []
    for c in range(half):
        parts = [
            lax.dot_general(
                basis_ref[e],
                rhs_ref[e],
                (((1,), (1,)), ((), ())),
                preferred_element_type=jnp.float32,
            )
            for e in (c, c + half)
        ]
        rows.append(jnp.concatenate(parts, axis=1))
    rows = jnp.concatenate(rows, axis=0).astype(payload_ref.dtype)
    square = (rows.shape[0], rows.shape[0])
    row = lax.broadcasted_iota(jnp.int32, square, 0)
    source = (row & (half - 1)) * rank_k + row // half
    order = jnp.where(lax.broadcasted_iota(jnp.int32, square, 1) == source, 1.0, 0.0)
    payload_ref[base:, :] = jnp.dot(
        order.astype(rows.dtype), rows, preferred_element_type=jnp.float32
    ).astype(payload_ref.dtype)

    me, owner, slot = me_ref[0], owner_ref[...], slot_ref[...]
    stored = owner.shape[1]
    place = scatter_place(owner, me, count) * clusters + slot
    column = (owner * clusters + slot + offset_ref[...]) & (count * clusters - 1)
    shard = gather_place(column // clusters, me, count)
    theirs = (shard == count // 2).astype(jnp.int32)
    shard = jnp.where(theirs == 1, gather_place(column // clusters, me ^ 1, count), shard)
    column_place = shard * clusters + (column & (clusters - 1))
    late = (shard >= count // 2 - LATE).astype(jnp.int32)
    square = (stored, stored)
    group = jnp.broadcast_to((2 * theirs + late).astype(jnp.float32), square)
    group_of_row = jnp.transpose(group)
    row_at = lax.broadcasted_iota(jnp.int32, square, 0)
    lane_at = lax.broadcasted_iota(jnp.int32, square, 1)
    lane = lane_at.astype(jnp.float32)
    before = (group_of_row < group) | ((group_of_row == group) & (row_at < lane_at))
    rank = jnp.sum(jnp.where(before, 1.0, 0.0), axis=0, keepdims=True)
    rank = jnp.transpose(jnp.broadcast_to(rank, square))
    here = jnp.where(rank == lane, 1.0, 0.0).astype(jnp.bfloat16)
    starts = jnp.sum(jnp.where(group_of_row < lane, 1.0, 0.0), axis=0, keepdims=True)
    values = jnp.concatenate(
        [lane[0:1], place.astype(jnp.float32), column_place.astype(jnp.float32)]
        + [jnp.zeros((5, stored), jnp.float32)],
        axis=0,
    )
    values = jnp.dot(values.astype(jnp.bfloat16), here, preferred_element_type=jnp.float32)
    values = jnp.concatenate([values[0:3], starts, values[4:8]], axis=0)
    list_ref[...] = values.astype(jnp.int32)


def open_kernel(token_ref, sums):
    def clear(i, carry):
        sums[i] = jnp.zeros(sums.shape[1:], sums.dtype)
        return carry

    lax.fori_loop(0, sums.shape[0] - 1, clear, 0, unroll=8)
    clear(sums.shape[0] - 1, 0)


def near_kernel(late, batch, shards, sends, list_ref, *refs):
    used = LATE if late else shards
    shard_refs, refs = refs[:shards], refs[shards:]
    (own_ref, mate_hbm), refs = refs[:2], refs[3:]
    sums, refs = refs[0], refs[1:]
    if late:
        coef_ref, send_refs, refs = refs[0], refs[1 : 1 + sends], refs[1 + sends :]
    columns, blocks, block_sem = refs
    stored = blocks.shape[0]
    directions = sums.shape[1]
    span = columns.shape[0] // used
    dummy = sums.shape[0] - 1
    chunk = stored // CHUNKS

    begin, end = list_ref[3, late], list_ref[3, late + 1]
    begin_there, end_there = list_ref[11, 2 + late], list_ref[11, 3 + late]
    steps_there = (end_there - begin_there + batch - 1) // batch

    def fetch(j, carry):
        at = jnp.minimum(begin_there + j, end_there - 1)
        pltpu.make_async_copy(
            mate_hbm.at[list_ref[8, at]], blocks.at[j], block_sem.at[j // batch]
        ).start()
        return carry

    if late:
        lax.fori_loop(0, steps_there * batch, fetch, 0)
    else:
        for c in range(CHUNKS):
            at = pl.ds(c * chunk, chunk)
            pltpu.make_async_copy(mate_hbm.at[at], blocks.at[at], block_sem.at[c]).start()

    for k, ref in enumerate(shard_refs[shards - used :]):

        def gather(i, carry, k=k, ref=ref):
            at = pl.multiple_of(i * directions, directions)
            columns[pl.ds(pl.multiple_of(k * span + at, directions), directions)] = ref[
                pl.ds(at, directions)
            ]
            return carry

        lax.fori_loop(0, span // directions, gather, 0, unroll=8)
    if late:
        tail = coef_ref.shape[0] // shards
        for k, ref in enumerate(shard_refs):
            coef_ref[k * tail : (k + 1) * tail] = ref[span : span + tail]
    def run(begin, end, row, swap, block_of):
        def entry(j):
            return jnp.minimum(begin + j, end - 1)

        def body(step, carry):
            first = step * batch
            products = []

            def add(i):
                place = list_ref[row + 1, entry(first + i)] ^ swap
                place = jnp.where(begin + first + i < end, place, dummy)
                sums[place] = sums[place] + products[i]

            take, carry = block_of(first, entry, carry)
            for i in range(batch):
                start = list_ref[row + 2, entry(first + i)] * directions - (shards - used) * span
                products.append(
                    lax.dot_general(
                        columns[pl.ds(pl.multiple_of(start, directions), directions)],
                        take(i),
                        (((1,), (1,)), ((), ())),
                        preferred_element_type=jnp.float32,
                    )
                )
            for i in range(batch):
                add(i)
            return carry

        return lax.fori_loop(0, (end - begin + batch - 1) // batch, body, 0)

    def own_blocks(first, entry, carry):
        return lambda i: own_ref[list_ref[0, entry(first + i)]], carry

    def wait(c, carry):
        at = pl.ds(0, chunk)
        pltpu.make_async_copy(mate_hbm.at[at], blocks.at[at], block_sem.at[c]).wait()
        return carry

    def mate_blocks(first, entry, ready):
        if late:
            pltpu.make_async_copy(
                mate_hbm.at[pl.ds(0, batch)],
                blocks.at[pl.ds(first, batch)],
                block_sem.at[first // batch],
            ).wait()
            return lambda i: blocks[first + i], ready
        needed = list_ref[8, entry(first + batch - 1)] // chunk + 1
        lax.fori_loop(ready, needed, wait, 0)
        return lambda i: blocks[list_ref[8, entry(first + i)]], jnp.maximum(ready, needed)

    run(begin, end, 0, 0, own_blocks)
    ready = run(begin_there, end_there, 8, dummy // 2, mate_blocks)
    if not late:
        lax.fori_loop(ready, CHUNKS, wait, 0)
        return
    at = dummy // 2
    for send_ref in send_refs:

        def pack(i, carry, at=at, send_ref=send_ref):
            send_ref[i] = sums[at + i].astype(send_ref.dtype)
            return carry

        lax.fori_loop(0, send_ref.shape[0], pack, 0, unroll=8)
        at += send_ref.shape[0]


def far_kernel(*refs):
    coef_refs = refs[:2]
    me_ref, couple_ref, slot_ref, dev_ref, cslot_ref, basis_ref, out_ref = refs[2:]
    clusters, rank_k, unknowns = basis_ref.shape
    pairs = couple_ref.shape[2]
    directions = out_ref.shape[1]
    half = clusters // 2
    coef = jnp.concatenate([ref[...].astype(jnp.float32) for ref in coef_refs], axis=0)
    coef = coef.reshape(-1, rank_k, half, unknowns)
    count = coef.shape[0]
    hot = (
        lax.broadcasted_iota(jnp.int32, (clusters, pairs), 0)
        == jnp.broadcast_to(slot_ref[...], (clusters, pairs))
    ).astype(jnp.float32).astype(jnp.bfloat16)
    away = gather_place(dev_ref[...], me_ref[0], count)
    theirs = count // 2 + gather_place(dev_ref[...], me_ref[0] ^ 1, count)
    away = jnp.where(away == count // 2, theirs, away)
    cslot = cslot_ref[...]
    high = (cslot >= half).astype(jnp.int32)
    at = away * half + cslot - high * half
    table_rows = (count * half, pairs)
    pick = jnp.where(
        lax.broadcasted_iota(jnp.int32, table_rows, 0) == jnp.broadcast_to(at, table_rows), 1.0, 0.0
    )
    pick = jnp.transpose(pick).astype(jnp.bfloat16)
    lanes = (unknowns, pairs)
    keep = jnp.where(
        lax.broadcasted_iota(jnp.int32, lanes, 0) // directions == jnp.broadcast_to(high, lanes),
        1.0,
        0.0,
    )
    keep = jnp.transpose(keep).astype(jnp.bfloat16)
    total = jnp.zeros((clusters * rank_k, unknowns), jnp.float32)
    for q in range(rank_k):
        table = coef[:, q].reshape(count * half, unknowns).astype(jnp.bfloat16)
        chosen = jnp.dot(pick, table, preferred_element_type=jnp.float32).astype(jnp.bfloat16)
        chosen = chosen * keep
        couple = couple_ref[q]
        weight = jnp.concatenate([couple * hot[s : s + 1] for s in range(clusters)], axis=0)
        total = total + jnp.dot(weight, chosen, preferred_element_type=jnp.float32)
    total = total + pltpu.roll(total, unknowns // 2, axis=1)
    gathered = jnp.transpose(total)[0:directions, :].astype(jnp.bfloat16).astype(jnp.float32)
    lane = lax.broadcasted_iota(jnp.int32, gathered.shape, 1) // rank_k
    basis = basis_ref[...].reshape(clusters * rank_k, unknowns)
    for s in range(clusters):
        own = jnp.where(lane == s, gathered, 0.0).astype(jnp.bfloat16)
        out_ref[s] = jnp.dot(own, basis, preferred_element_type=jnp.float32)


def ring_device(place, core, chips):
    depth = chips // 2
    place = place % chips
    z, y = (place, 0) if place < depth else (chips - 1 - place, 1)
    return (z * 2 + y) * 2 + core


def ring_pairs(count):
    chips = count // 2
    cores = [(p, c) for p in range(chips) for c in range(2)]
    ahead = [(ring_device(p, c, chips), ring_device(p + 1 - 2 * c, c, chips)) for p, c in cores]
    cross = [
        (ring_device(p, c, chips), ring_device(p - 1 + 2 * c, 1 - c, chips)) for p, c in cores
    ]
    return ahead, cross


def ring_place(device, chips):
    z, y = device >> 2, (device >> 1) & 1
    return jnp.where(y == 0, z, chips - 1 - z)


def gather_place(device, me, count):
    chips = count // 2
    depth = chips // 2
    back = (1 - 2 * (me & 1)) * (ring_place(me, chips) - ring_place(device, chips))
    back = (back + chips) & (chips - 1)
    other = (device ^ me) & 1
    here = (back < depth) & (back > 0) | (back == 0) & (other == 1) | (back == depth) & (other == 0)
    return jnp.where(here, jnp.where(back == 0, 0, 2 * back - 1 + other), chips)


def scatter_place(device, me, count):
    chips = count // 2
    depth = chips // 2
    ahead = (ring_place(device, chips) - ring_place(me, chips) + chips) & (chips - 1)
    core = device & 1
    handler = jnp.where((ahead & (depth - 1)) == 0, core, (ahead > depth).astype(jnp.int32))
    steps = jnp.where(handler == 0, ahead, (chips - ahead) & (chips - 1))
    place = jnp.where(
        steps == depth,
        0,
        jnp.where(steps == 0, chips - 1, 2 * (depth - steps) - (core ^ handler)),
    )
    return place + jnp.where(handler == (me & 1), 0, chips)


def stationary(
    rhs,
    near_blocks,
    near_owner,
    near_slot,
    near_offset,
    far_coupling,
    far_slot,
    far_dev,
    far_cslot,
    basis_out,
    basis_in,
):
    clusters, directions, unknowns = rhs.shape
    rank_k = basis_in.shape[1]
    count = lax.axis_size("blk")
    chips = count // 2
    depth = chips // 2
    me = lax.axis_index("blk")
    stored = near_blocks.shape[0]
    pairs = far_slot.shape[0]
    half = clusters // 2
    ahead, cross = ring_pairs(count)
    mate = [(i, i ^ 1) for i in range(count)]
    side = [(i, i ^ 2) for i in range(count)]

    def move(values, where):
        return lax.ppermute(values, "blk", where)

    def after(values, *others):
        return lax.optimization_barrier((values, *others))[0]

    here = me.astype(jnp.int32).reshape(1)
    base = clusters * directions
    payload, lists = pl.pallas_call(
        functools.partial(prologue_kernel, count),
        out_shape=[
            jax.ShapeDtypeStruct((base + half * rank_k, unknowns), jnp.bfloat16),
            jax.ShapeDtypeStruct((8, stored), jnp.int32),
        ],
        in_specs=[whole(pltpu.SMEM)] + [whole()] * 5,
        out_specs=[whole()] * 2,
        compiler_params=pltpu.CompilerParams(vmem_limit_bytes=PROLOGUE_VMEM),
        name="prologue",
    )(
        here,
        near_owner.reshape(1, stored),
        near_slot.reshape(1, stored),
        near_offset.reshape(1, stored),
        rhs,
        basis_in,
    )
    cost = pl.CostEstimate(
        flops=16 * stored * directions * unknowns * unknowns,
        bytes_accessed=16 << 20,
        transcendentals=0,
    )
    flow = [move(payload, ahead)]
    mate_blocks = move(near_blocks, mate)
    mate_lists = move(lists, mate)
    couple = jnp.transpose(far_coupling, (2, 1, 0))
    sums_shape = jax.ShapeDtypeStruct((count * clusters + 1, directions, unknowns), jnp.float32)
    sums = pl.pallas_call(
        open_kernel,
        out_shape=sums_shape,
        in_specs=[whole(pltpu.SMEM)],
        out_specs=whole(),
        compiler_params=pltpu.CompilerParams(vmem_limit_bytes=NEAR_VMEM),
        cost_estimate=cost,
        name="open",
    )(after(here, couple))
    flow.append(move(after(payload, couple, sums), cross))
    shards = [move(payload, mate)]
    flow[0], sums = lax.optimization_barrier((flow[0], sums))
    for k in range(1, chips):
        x = 1 - k % 2
        if k == 3:
            flow[x], mate_blocks, shards[0], mate_lists = lax.optimization_barrier(
                (flow[x], mate_blocks, shards[0], mate_lists)
            )
        if k == 4:
            lists = jnp.concatenate([after(lists, flow[x]), mate_lists], axis=0)
        if k == 5:
            flow[x], lists = lax.optimization_barrier((flow[x], lists))
        shards.append(flow[x])
        if k < chips - 2:
            flow[x] = move(flow[x], ahead)

    pieces = [2, chips - 2]

    def near(late, shards, sums):
        sends = pieces if late else []
        return pl.pallas_call(
            functools.partial(near_kernel, late, BATCH[late], len(shards), len(sends)),
            out_shape=[sums_shape]
            + [jax.ShapeDtypeStruct((chips * half * rank_k, unknowns), jnp.bfloat16)] * late
            + [
                jax.ShapeDtypeStruct((size * clusters, directions, unknowns), jnp.bfloat16)
                for size in sends
            ],
            in_specs=[whole(pltpu.SMEM)]
            + [whole()] * len(shards)
            + [whole(), whole(pl.ANY), whole()],
            out_specs=[whole()] * (1 + late + len(sends)),
            input_output_aliases={3 + len(shards): 0},
            scratch_shapes=[
                pltpu.VMEM(((LATE if late else len(shards)) * base, unknowns), jnp.bfloat16),
                pltpu.VMEM(near_blocks.shape, jnp.bfloat16),
                pltpu.SemaphoreType.DMA((max(CHUNKS, stored // BATCH[late]),)),
            ],
            compiler_params=pltpu.CompilerParams(vmem_limit_bytes=NEAR_VMEM),
            cost_estimate=cost,
            name="near",
        )(lists, *shards, near_blocks, mate_blocks, sums)

    def far_field(couple):
        return pl.pallas_call(
            far_kernel,
            out_shape=jax.ShapeDtypeStruct((clusters, directions, unknowns), jnp.float32),
            in_specs=[whole()] * 2 + [whole(pltpu.SMEM)] + [whole()] * 5,
            out_specs=whole(),
            compiler_params=pltpu.CompilerParams(vmem_limit_bytes=FAR_VMEM),
            cost_estimate=pl.CostEstimate(
                flops=4 * clusters * rank_k * pairs * rank_k * unknowns,
                bytes_accessed=8 << 20,
                transcendentals=0,
            ),
            name="far",
        )(
            *coefs,
            here,
            couple,
            far_slot.reshape(1, pairs),
            far_dev.reshape(1, pairs),
            far_cslot.reshape(1, pairs),
            basis_out,
        )

    (sums,) = near(0, shards[: chips - LATE], sums)
    sums, coef, *sends = near(1, shards, sums)
    mates = [move(sends[0], mate)]
    coefs = [coef, move(coef, mate)]

    piece = clusters // UNITS

    def term(k, h):
        part, at = (0, k) if k < 2 else (1, k - 2)
        got = mates[part][at * clusters + h * piece : at * clusters + (h + 1) * piece]
        at = k * clusters + h * piece
        return sums[at : at + piece] + got.astype(jnp.float32)

    flow = lax.optimization_barrier(
        [[term(k, h).astype(jnp.bfloat16) for h in range(UNITS)] for k in range(2)]
    )
    mates.append(move(after(sends[1], *flow[0], *flow[1]), mate))
    flow = [[move(unit, ahead) for unit in units] for units in flow]
    for k in range(2, chips - 1):
        for h in range(UNITS):
            unit = (flow[k % 2][h].astype(jnp.float32) + term(k, h)).astype(jnp.bfloat16)
            unit, mates[1] = lax.optimization_barrier((unit, mates[1]))
            if (k, h) == (chips - 2, UNITS - 1):
                couple = after(couple, unit)
            flow[k % 2][h] = move(unit, ahead)
    last = [move(unit, mate) for unit in flow[1]]
    own = sums[(chips - 1) * clusters : chips * clusters]
    total = far_field(couple) + own + mates[1][(chips - 3) * clusters :].astype(jnp.float32)
    total = total + jnp.concatenate(flow[0], axis=0).astype(jnp.float32)
    total = lax.optimization_barrier(total)
    return (total + jnp.concatenate(last, axis=0).astype(jnp.float32)).astype(jnp.bfloat16)


def on_device(*args):
    rhs, near_blocks = args[0], args[1]
    clusters, directions, unknowns = rhs.shape
    small = lax.axis_size("blk") == 16 and clusters == 16
    if small and near_blocks.shape[0] == unknowns and 2 * directions == unknowns:
        return stationary(*args)
    return routed(*args)


def solution(mesh):
    placed = (
        P(("groups", "blk"), None, None),
        P(("groups", "blk"), None, None),
        P(("groups", "blk"), None),
        P(("groups", "blk")),
        P(("groups", "blk")),
        P(("groups", "blk"), None, None),
        P(("groups", "blk")),
        P(("groups", "blk"), None),
        P(("groups", "blk")),
        P(("groups", "blk"), None, None),
        P(("groups", "blk"), None, None),
    )
    return jax.shard_map(
        on_device,
        mesh=mesh,
        in_specs=placed,
        out_specs=P(("groups", "blk"), None, None),
        check_vma=False,
    )
```

```python
import functools

import jax
import jax.numpy as jnp
from jax import lax
from jax.experimental import pallas as pl
from jax.experimental.pallas import tpu as pltpu
from jax.sharding import PartitionSpec as P

BATCH = 16, 8
CHUNKS = 4
LATE = 2
UNITS = 1
PROLOGUE_VMEM = 58 << 20
NEAR_VMEM = 20 << 20
FAR_VMEM = 16 << 20


def with_halo(cells, sides, width):
    for axis, dim in sides:
        count = lax.axis_size(axis)
        head = lax.slice_in_dim(cells, 0, width, axis=dim)
        tail = lax.slice_in_dim(cells, cells.shape[dim] - width, cells.shape[dim], axis=dim)
        cells = jnp.concatenate(
            [
                lax.ppermute(tail, axis, [(i, (i + 1) % count) for i in range(count)]),
                cells,
                lax.ppermute(head, axis, [((i + 1) % count, i) for i in range(count)]),
            ],
            axis=dim,
        )
    return cells


def place_ranks(targets, count):
    onehot = (targets[:, None] == jnp.arange(count, dtype=jnp.int32)[None, :]).astype(jnp.int32)
    before = jnp.cumsum(onehot, axis=0) - onehot
    return jnp.sum(before * onehot, axis=1)


def routed(
    rhs,
    near_blocks,
    near_owner,
    near_slot,
    near_offset,
    far_coupling,
    far_slot,
    far_dev,
    far_cslot,
    basis_out,
    basis_in,
):
    clusters = rhs.shape[0]
    directions = rhs.shape[1]
    unknowns = rhs.shape[2]
    cycle_size = lax.axis_size("blk")
    stored = near_blocks.shape[0]
    capacity = max(2, 2 * stored // cycle_size)
    owners = near_owner[:, 0]
    target = owners * capacity + place_ranks(owners, cycle_size)
    outbox = (
        jnp.zeros((cycle_size * capacity, unknowns, unknowns), near_blocks.dtype)
        .at[target]
        .set(near_blocks)
    )
    labels = (
        jnp.zeros((cycle_size * capacity, 2), jnp.int32)
        .at[target]
        .set(jnp.stack([near_slot, near_offset], axis=1))
    )
    window = with_halo(rhs, (("blk", 0),), clusters)
    inbox, in_labels = (
        lax.all_to_all(outbox, "blk", split_axis=0, concat_axis=0, tiled=True),
        lax.all_to_all(labels, "blk", split_axis=0, concat_axis=0, tiled=True),
    )
    position = clusters + in_labels[:, 0] + in_labels[:, 1]
    columns = jnp.take(window, position, axis=0)
    products = jnp.einsum("srj,sij->sri", columns, inbox, preferred_element_type=jnp.float32)
    selector = (in_labels[:, 0][None, :] == jnp.arange(clusters, dtype=jnp.int32)[:, None]).astype(
        jnp.float32
    )
    near_sum = jnp.dot(
        selector,
        products.reshape(products.shape[0], -1),
        precision=lax.Precision.HIGHEST,
        preferred_element_type=jnp.float32,
    ).reshape(clusters, directions, unknowns)
    coef_local = jnp.einsum(
        "ckj,crj->crk", basis_in, rhs, preferred_element_type=jnp.float32
    ).astype(jnp.bfloat16)
    rank_k = basis_in.shape[1]
    coef_local = coef_local.reshape(clusters, directions * rank_k)
    pairs = far_slot.shape[0]
    wanted = far_dev[:, 0] * clusters + far_cslot
    piece = lax.all_gather(coef_local, "blk", axis=0, tiled=True)
    chosen = jnp.take(piece, wanted, axis=0)
    coupled = jnp.einsum(
        "pkq,prq->prk",
        far_coupling,
        chosen.reshape(pairs, directions, rank_k),
        preferred_element_type=jnp.float32,
    )
    row_pick = (far_slot[None, :] == jnp.arange(clusters, dtype=jnp.int32)[:, None]).astype(
        jnp.float32
    )
    gathered = jnp.dot(
        row_pick,
        coupled.reshape(pairs, -1),
        precision=lax.Precision.HIGHEST,
        preferred_element_type=jnp.float32,
    )
    gathered = gathered.astype(jnp.bfloat16).reshape(clusters, directions, rank_k)
    far_sum = jnp.einsum("crk,ckb->crb", gathered, basis_out, preferred_element_type=jnp.float32)
    return (near_sum + far_sum).astype(jnp.bfloat16)


def whole(space=pltpu.VMEM):
    return pl.BlockSpec(memory_space=space)


def prologue_kernel(
    count, me_ref, owner_ref, slot_ref, offset_ref, rhs_ref, basis_ref, payload_ref, list_ref
):
    clusters, directions, unknowns = rhs_ref.shape
    base = clusters * directions
    payload_ref[0:base, :] = rhs_ref[...].reshape(base, unknowns)
    rank_k = basis_ref.shape[1]
    half = clusters // 2
    rows = []
    for c in range(half):
        parts = [
            lax.dot_general(
                basis_ref[e],
                rhs_ref[e],
                (((1,), (1,)), ((), ())),
                preferred_element_type=jnp.float32,
            )
            for e in (c, c + half)
        ]
        rows.append(jnp.concatenate(parts, axis=1))
    rows = jnp.concatenate(rows, axis=0).astype(payload_ref.dtype)
    square = (rows.shape[0], rows.shape[0])
    row = lax.broadcasted_iota(jnp.int32, square, 0)
    source = (row & (half - 1)) * rank_k + row // half
    order = jnp.where(lax.broadcasted_iota(jnp.int32, square, 1) == source, 1.0, 0.0)
    payload_ref[base:, :] = jnp.dot(
        order.astype(rows.dtype), rows, preferred_element_type=jnp.float32
    ).astype(payload_ref.dtype)

    me, owner, slot = me_ref[0], owner_ref[...], slot_ref[...]
    stored = owner.shape[1]
    place = scatter_place(owner, me, count) * clusters + slot
    column = (owner * clusters + slot + offset_ref[...]) & (count * clusters - 1)
    shard = gather_place(column // clusters, me, count)
    theirs = (shard == count // 2).astype(jnp.int32)
    shard = jnp.where(theirs == 1, gather_place(column // clusters, me ^ 1, count), shard)
    column_place = shard * clusters + (column & (clusters - 1))
    late = (shard >= count // 2 - LATE).astype(jnp.int32)
    square = (stored, stored)
    group = jnp.broadcast_to((2 * theirs + late).astype(jnp.float32), square)
    group_of_row = jnp.transpose(group)
    row_at = lax.broadcasted_iota(jnp.int32, square, 0)
    lane_at = lax.broadcasted_iota(jnp.int32, square, 1)
    lane = lane_at.astype(jnp.float32)
    before = (group_of_row < group) | ((group_of_row == group) & (row_at < lane_at))
    rank = jnp.sum(jnp.where(before, 1.0, 0.0), axis=0, keepdims=True)
    rank = jnp.transpose(jnp.broadcast_to(rank, square))
    here = jnp.where(rank == lane, 1.0, 0.0).astype(jnp.bfloat16)
    starts = jnp.sum(jnp.where(group_of_row < lane, 1.0, 0.0), axis=0, keepdims=True)
    values = jnp.concatenate(
        [lane[0:1], place.astype(jnp.float32), column_place.astype(jnp.float32)]
        + [jnp.zeros((5, stored), jnp.float32)],
        axis=0,
    )
    values = jnp.dot(values.astype(jnp.bfloat16), here, preferred_element_type=jnp.float32)
    values = jnp.concatenate([values[0:3], starts, values[4:8]], axis=0)
    list_ref[...] = values.astype(jnp.int32)


def open_kernel(token_ref, sums):
    def clear(i, carry):
        sums[i] = jnp.zeros(sums.shape[1:], sums.dtype)
        return carry

    lax.fori_loop(0, sums.shape[0] - 1, clear, 0, unroll=8)
    clear(sums.shape[0] - 1, 0)


def near_kernel(late, batch, shards, sends, list_ref, *refs):
    used = LATE if late else shards
    shard_refs, refs = refs[:shards], refs[shards:]
    (own_ref, mate_hbm), refs = refs[:2], refs[3:]
    sums, refs = refs[0], refs[1:]
    if late:
        coef_ref, send_refs, (columns,) = refs[0], refs[1 : 1 + sends], refs[1 + sends :]
        blocks = mate_hbm
    else:
        blocks, columns, block_sem = refs
    stored = blocks.shape[0]
    directions = sums.shape[1]
    span = columns.shape[0] // used
    dummy = sums.shape[0] - 1
    chunk = stored // CHUNKS

    begin, end = list_ref[3, late], list_ref[3, late + 1]
    begin_there, end_there = list_ref[11, 2 + late], list_ref[11, 3 + late]
    if not late:
        for c in range(CHUNKS):
            at = pl.ds(c * chunk, chunk)
            pltpu.make_async_copy(mate_hbm.at[at], blocks.at[at], block_sem.at[c]).start()

    for k, ref in enumerate(shard_refs[shards - used :]):

        def gather(i, carry, k=k, ref=ref):
            at = pl.multiple_of(i * directions, directions)
            columns[pl.ds(pl.multiple_of(k * span + at, directions), directions)] = ref[
                pl.ds(at, directions)
            ]
            return carry

        lax.fori_loop(0, span // directions, gather, 0, unroll=8)
    if late:
        tail = coef_ref.shape[0] // shards
        for k, ref in enumerate(shard_refs):
            coef_ref[k * tail : (k + 1) * tail] = ref[span : span + tail]
    def run(begin, end, row, swap, block_of):
        def entry(j):
            return jnp.minimum(begin + j, end - 1)

        def body(step, carry):
            first = step * batch
            products = []

            def add(i):
                place = list_ref[row + 1, entry(first + i)] ^ swap
                place = jnp.where(begin + first + i < end, place, dummy)
                sums[place] = sums[place] + products[i]

            take, carry = block_of(first, entry, carry)
            for i in range(batch):
                start = list_ref[row + 2, entry(first + i)] * directions - (shards - used) * span
                products.append(
                    lax.dot_general(
                        columns[pl.ds(pl.multiple_of(start, directions), directions)],
                        take(i),
                        (((1,), (1,)), ((), ())),
                        preferred_element_type=jnp.float32,
                    )
                )
            for i in range(batch):
                add(i)
            return carry

        return lax.fori_loop(0, (end - begin + batch - 1) // batch, body, 0)

    def own_blocks(first, entry, carry):
        return lambda i: own_ref[list_ref[0, entry(first + i)]], carry

    def wait(c, carry):
        at = pl.ds(0, chunk)
        pltpu.make_async_copy(mate_hbm.at[at], blocks.at[at], block_sem.at[c]).wait()
        return carry

    def mate_blocks(first, entry, ready):
        take = lambda i: blocks[list_ref[8, entry(first + i)]]
        if late:
            return take, ready
        needed = list_ref[8, entry(first + batch - 1)] // chunk + 1
        lax.fori_loop(ready, needed, wait, 0)
        return take, jnp.maximum(ready, needed)

    run(begin, end, 0, 0, own_blocks)
    ready = run(begin_there, end_there, 8, dummy // 2, mate_blocks)
    if not late:
        lax.fori_loop(ready, CHUNKS, wait, 0)
        return
    at = dummy // 2
    for send_ref in send_refs:

        def pack(i, carry, at=at, send_ref=send_ref):
            send_ref[i] = sums[at + i].astype(send_ref.dtype)
            return carry

        lax.fori_loop(0, send_ref.shape[0], pack, 0, unroll=8)
        at += send_ref.shape[0]


def far_kernel(*refs):
    coef_refs = refs[:2]
    me_ref, couple_ref, slot_ref, dev_ref, cslot_ref, basis_ref, out_ref = refs[2:]
    clusters, rank_k, unknowns = basis_ref.shape
    pairs = couple_ref.shape[2]
    directions = out_ref.shape[1]
    half = clusters // 2
    coef = jnp.concatenate([ref[...].astype(jnp.float32) for ref in coef_refs], axis=0)
    coef = coef.reshape(-1, rank_k, half, unknowns)
    count = coef.shape[0]
    hot = (
        lax.broadcasted_iota(jnp.int32, (clusters, pairs), 0)
        == jnp.broadcast_to(slot_ref[...], (clusters, pairs))
    ).astype(jnp.float32).astype(jnp.bfloat16)
    away = gather_place(dev_ref[...], me_ref[0], count)
    theirs = count // 2 + gather_place(dev_ref[...], me_ref[0] ^ 1, count)
    away = jnp.where(away == count // 2, theirs, away)
    cslot = cslot_ref[...]
    high = (cslot >= half).astype(jnp.int32)
    at = away * half + cslot - high * half
    table_rows = (count * half, pairs)
    pick = jnp.where(
        lax.broadcasted_iota(jnp.int32, table_rows, 0) == jnp.broadcast_to(at, table_rows), 1.0, 0.0
    )
    pick = jnp.transpose(pick).astype(jnp.bfloat16)
    lanes = (unknowns, pairs)
    keep = jnp.where(
        lax.broadcasted_iota(jnp.int32, lanes, 0) // directions == jnp.broadcast_to(high, lanes),
        1.0,
        0.0,
    )
    keep = jnp.transpose(keep).astype(jnp.bfloat16)
    total = jnp.zeros((clusters * rank_k, unknowns), jnp.float32)
    for q in range(rank_k):
        table = coef[:, q].reshape(count * half, unknowns).astype(jnp.bfloat16)
        chosen = jnp.dot(pick, table, preferred_element_type=jnp.float32).astype(jnp.bfloat16)
        chosen = chosen * keep
        couple = couple_ref[q]
        weight = jnp.concatenate([couple * hot[s : s + 1] for s in range(clusters)], axis=0)
        total = total + jnp.dot(weight, chosen, preferred_element_type=jnp.float32)
    total = total + pltpu.roll(total, unknowns // 2, axis=1)
    gathered = jnp.transpose(total)[0:directions, :].astype(jnp.bfloat16).astype(jnp.float32)
    lane = lax.broadcasted_iota(jnp.int32, gathered.shape, 1) // rank_k
    basis = basis_ref[...].reshape(clusters * rank_k, unknowns)
    for s in range(clusters):
        own = jnp.where(lane == s, gathered, 0.0).astype(jnp.bfloat16)
        out_ref[s] = jnp.dot(own, basis, preferred_element_type=jnp.float32)


def ring_device(place, core, chips):
    depth = chips // 2
    place = place % chips
    z, y = (place, 0) if place < depth else (chips - 1 - place, 1)
    return (z * 2 + y) * 2 + core


def ring_pairs(count):
    chips = count // 2
    cores = [(p, c) for p in range(chips) for c in range(2)]
    ahead = [(ring_device(p, c, chips), ring_device(p + 1 - 2 * c, c, chips)) for p, c in cores]
    cross = [
        (ring_device(p, c, chips), ring_device(p - 1 + 2 * c, 1 - c, chips)) for p, c in cores
    ]
    return ahead, cross


def ring_place(device, chips):
    z, y = device >> 2, (device >> 1) & 1
    return jnp.where(y == 0, z, chips - 1 - z)


def gather_place(device, me, count):
    chips = count // 2
    depth = chips // 2
    back = (1 - 2 * (me & 1)) * (ring_place(me, chips) - ring_place(device, chips))
    back = (back + chips) & (chips - 1)
    other = (device ^ me) & 1
    here = (back < depth) & (back > 0) | (back == 0) & (other == 1) | (back == depth) & (other == 0)
    return jnp.where(here, jnp.where(back == 0, 0, 2 * back - 1 + other), chips)


def scatter_place(device, me, count):
    chips = count // 2
    depth = chips // 2
    ahead = (ring_place(device, chips) - ring_place(me, chips) + chips) & (chips - 1)
    core = device & 1
    handler = jnp.where((ahead & (depth - 1)) == 0, core, (ahead > depth).astype(jnp.int32))
    steps = jnp.where(handler == 0, ahead, (chips - ahead) & (chips - 1))
    place = jnp.where(
        steps == depth,
        0,
        jnp.where(steps == 0, chips - 1, 2 * (depth - steps) - (core ^ handler)),
    )
    return place + jnp.where(handler == (me & 1), 0, chips)


def stationary(
    rhs,
    near_blocks,
    near_owner,
    near_slot,
    near_offset,
    far_coupling,
    far_slot,
    far_dev,
    far_cslot,
    basis_out,
    basis_in,
):
    clusters, directions, unknowns = rhs.shape
    rank_k = basis_in.shape[1]
    count = lax.axis_size("blk")
    chips = count // 2
    depth = chips // 2
    me = lax.axis_index("blk")
    stored = near_blocks.shape[0]
    pairs = far_slot.shape[0]
    half = clusters // 2
    ahead, cross = ring_pairs(count)
    mate = [(i, i ^ 1) for i in range(count)]
    side = [(i, i ^ 2) for i in range(count)]

    def move(values, where):
        return lax.ppermute(values, "blk", where)

    def after(values, *others):
        return lax.optimization_barrier((values, *others))[0]

    here = me.astype(jnp.int32).reshape(1)
    base = clusters * directions
    payload, lists = pl.pallas_call(
        functools.partial(prologue_kernel, count),
        out_shape=[
            jax.ShapeDtypeStruct((base + half * rank_k, unknowns), jnp.bfloat16),
            jax.ShapeDtypeStruct((8, stored), jnp.int32),
        ],
        in_specs=[whole(pltpu.SMEM)] + [whole()] * 5,
        out_specs=[whole()] * 2,
        compiler_params=pltpu.CompilerParams(vmem_limit_bytes=PROLOGUE_VMEM),
        name="prologue",
    )(
        here,
        near_owner.reshape(1, stored),
        near_slot.reshape(1, stored),
        near_offset.reshape(1, stored),
        rhs,
        basis_in,
    )
    cost = pl.CostEstimate(
        flops=16 * stored * directions * unknowns * unknowns,
        bytes_accessed=16 << 20,
        transcendentals=0,
    )
    flow = [move(payload, ahead)]
    mate_blocks = move(near_blocks, mate)
    mate_lists = move(lists, mate)
    couple = jnp.transpose(far_coupling, (2, 1, 0))
    sums_shape = jax.ShapeDtypeStruct((count * clusters + 1, directions, unknowns), jnp.float32)
    sums = pl.pallas_call(
        open_kernel,
        out_shape=sums_shape,
        in_specs=[whole(pltpu.SMEM)],
        out_specs=whole(),
        compiler_params=pltpu.CompilerParams(vmem_limit_bytes=NEAR_VMEM),
        cost_estimate=cost,
        name="open",
    )(after(here, couple))
    flow.append(move(after(payload, couple, sums), cross))
    shards = [move(payload, mate)]
    flow[0], sums = lax.optimization_barrier((flow[0], sums))
    for k in range(1, chips):
        x = 1 - k % 2
        if k == 3:
            flow[x], mate_blocks, shards[0], mate_lists = lax.optimization_barrier(
                (flow[x], mate_blocks, shards[0], mate_lists)
            )
        if k == 4:
            lists = jnp.concatenate([after(lists, flow[x]), mate_lists], axis=0)
        if k == 5:
            flow[x], lists = lax.optimization_barrier((flow[x], lists))
        shards.append(flow[x])
        if k < chips - 2:
            flow[x] = move(flow[x], ahead)

    pieces = [2, chips - 2]

    def near(late, shards, theirs, sums):
        sends = pieces if late else []
        return pl.pallas_call(
            functools.partial(near_kernel, late, BATCH[late], len(shards), len(sends)),
            out_shape=[sums_shape]
            + [jax.ShapeDtypeStruct(near_blocks.shape, near_blocks.dtype)] * (1 - late)
            + [jax.ShapeDtypeStruct((chips * half * rank_k, unknowns), jnp.bfloat16)] * late
            + [
                jax.ShapeDtypeStruct((size * clusters, directions, unknowns), jnp.bfloat16)
                for size in sends
            ],
            in_specs=[whole(pltpu.SMEM)]
            + [whole()] * len(shards)
            + [whole(), whole() if late else whole(pl.ANY), whole()],
            out_specs=[whole()] * (2 + len(sends)),
            input_output_aliases={3 + len(shards): 0},
            scratch_shapes=[
                pltpu.VMEM(((LATE if late else len(shards)) * base, unknowns), jnp.bfloat16),
            ]
            + [pltpu.SemaphoreType.DMA((CHUNKS,))] * (1 - late),
            compiler_params=pltpu.CompilerParams(vmem_limit_bytes=NEAR_VMEM),
            cost_estimate=cost,
            name="near",
        )(lists, *shards, near_blocks, theirs, sums)

    def far_field(couple):
        return pl.pallas_call(
            far_kernel,
            out_shape=jax.ShapeDtypeStruct((clusters, directions, unknowns), jnp.float32),
            in_specs=[whole()] * 2 + [whole(pltpu.SMEM)] + [whole()] * 5,
            out_specs=whole(),
            compiler_params=pltpu.CompilerParams(vmem_limit_bytes=FAR_VMEM),
            cost_estimate=pl.CostEstimate(
                flops=4 * clusters * rank_k * pairs * rank_k * unknowns,
                bytes_accessed=8 << 20,
                transcendentals=0,
            ),
            name="far",
        )(
            *coefs,
            here,
            couple,
            far_slot.reshape(1, pairs),
            far_dev.reshape(1, pairs),
            far_cslot.reshape(1, pairs),
            basis_out,
        )

    sums, mate_blocks = near(0, shards[: chips - LATE], mate_blocks, sums)
    sums, coef, *sends = near(1, shards, mate_blocks, sums)
    mates = [move(sends[0], mate)]
    coefs = [coef, move(coef, mate)]

    piece = clusters // UNITS

    def term(k, h):
        part, at = (0, k) if k < 2 else (1, k - 2)
        got = mates[part][at * clusters + h * piece : at * clusters + (h + 1) * piece]
        at = k * clusters + h * piece
        return sums[at : at + piece] + got.astype(jnp.float32)

    flow = lax.optimization_barrier(
        [[term(k, h).astype(jnp.bfloat16) for h in range(UNITS)] for k in range(2)]
    )
    mates.append(move(after(sends[1], *flow[0], *flow[1]), mate))
    flow = [[move(unit, ahead) for unit in units] for units in flow]
    for k in range(2, chips - 1):
        for h in range(UNITS):
            unit = (flow[k % 2][h].astype(jnp.float32) + term(k, h)).astype(jnp.bfloat16)
            unit, mates[1] = lax.optimization_barrier((unit, mates[1]))
            if (k, h) == (chips - 2, UNITS - 1):
                couple = after(couple, unit)
            flow[k % 2][h] = move(unit, ahead)
    last = [move(unit, mate) for unit in flow[1]]
    own = sums[(chips - 1) * clusters : chips * clusters]
    total = far_field(couple) + own + mates[1][(chips - 3) * clusters :].astype(jnp.float32)
    total = total + jnp.concatenate(flow[0], axis=0).astype(jnp.float32)
    total = lax.optimization_barrier(total)
    return (total + jnp.concatenate(last, axis=0).astype(jnp.float32)).astype(jnp.bfloat16)


def on_device(*args):
    rhs, near_blocks = args[0], args[1]
    clusters, directions, unknowns = rhs.shape
    small = lax.axis_size("blk") == 16 and clusters == 16
    if small and near_blocks.shape[0] == unknowns and 2 * directions == unknowns:
        return stationary(*args)
    return routed(*args)


def solution(mesh):
    placed = (
        P(("groups", "blk"), None, None),
        P(("groups", "blk"), None, None),
        P(("groups", "blk"), None),
        P(("groups", "blk")),
        P(("groups", "blk")),
        P(("groups", "blk"), None, None),
        P(("groups", "blk")),
        P(("groups", "blk"), None),
        P(("groups", "blk")),
        P(("groups", "blk"), None, None),
        P(("groups", "blk"), None, None),
    )
    return jax.shard_map(
        on_device,
        mesh=mesh,
        in_specs=placed,
        out_specs=P(("groups", "blk"), None, None),
        check_vma=False,
    )
```

```python
import functools

import jax
import jax.numpy as jnp
from jax import lax
from jax.experimental import pallas as pl
from jax.experimental.pallas import tpu as pltpu
from jax.sharding import PartitionSpec as P

BATCH = 16, 16
CHUNKS = 4
LATE = 2
UNITS = 1
PROLOGUE_VMEM = 58 << 20
NEAR_VMEM = 20 << 20
FAR_VMEM = 16 << 20


def with_halo(cells, sides, width):
    for axis, dim in sides:
        count = lax.axis_size(axis)
        head = lax.slice_in_dim(cells, 0, width, axis=dim)
        tail = lax.slice_in_dim(cells, cells.shape[dim] - width, cells.shape[dim], axis=dim)
        cells = jnp.concatenate(
            [
                lax.ppermute(tail, axis, [(i, (i + 1) % count) for i in range(count)]),
                cells,
                lax.ppermute(head, axis, [((i + 1) % count, i) for i in range(count)]),
            ],
            axis=dim,
        )
    return cells


def place_ranks(targets, count):
    onehot = (targets[:, None] == jnp.arange(count, dtype=jnp.int32)[None, :]).astype(jnp.int32)
    before = jnp.cumsum(onehot, axis=0) - onehot
    return jnp.sum(before * onehot, axis=1)


def routed(
    rhs,
    near_blocks,
    near_owner,
    near_slot,
    near_offset,
    far_coupling,
    far_slot,
    far_dev,
    far_cslot,
    basis_out,
    basis_in,
):
    clusters = rhs.shape[0]
    directions = rhs.shape[1]
    unknowns = rhs.shape[2]
    cycle_size = lax.axis_size("blk")
    stored = near_blocks.shape[0]
    capacity = max(2, 2 * stored // cycle_size)
    owners = near_owner[:, 0]
    target = owners * capacity + place_ranks(owners, cycle_size)
    outbox = (
        jnp.zeros((cycle_size * capacity, unknowns, unknowns), near_blocks.dtype)
        .at[target]
        .set(near_blocks)
    )
    labels = (
        jnp.zeros((cycle_size * capacity, 2), jnp.int32)
        .at[target]
        .set(jnp.stack([near_slot, near_offset], axis=1))
    )
    window = with_halo(rhs, (("blk", 0),), clusters)
    inbox, in_labels = (
        lax.all_to_all(outbox, "blk", split_axis=0, concat_axis=0, tiled=True),
        lax.all_to_all(labels, "blk", split_axis=0, concat_axis=0, tiled=True),
    )
    position = clusters + in_labels[:, 0] + in_labels[:, 1]
    columns = jnp.take(window, position, axis=0)
    products = jnp.einsum("srj,sij->sri", columns, inbox, preferred_element_type=jnp.float32)
    selector = (in_labels[:, 0][None, :] == jnp.arange(clusters, dtype=jnp.int32)[:, None]).astype(
        jnp.float32
    )
    near_sum = jnp.dot(
        selector,
        products.reshape(products.shape[0], -1),
        precision=lax.Precision.HIGHEST,
        preferred_element_type=jnp.float32,
    ).reshape(clusters, directions, unknowns)
    coef_local = jnp.einsum(
        "ckj,crj->crk", basis_in, rhs, preferred_element_type=jnp.float32
    ).astype(jnp.bfloat16)
    rank_k = basis_in.shape[1]
    coef_local = coef_local.reshape(clusters, directions * rank_k)
    pairs = far_slot.shape[0]
    wanted = far_dev[:, 0] * clusters + far_cslot
    piece = lax.all_gather(coef_local, "blk", axis=0, tiled=True)
    chosen = jnp.take(piece, wanted, axis=0)
    coupled = jnp.einsum(
        "pkq,prq->prk",
        far_coupling,
        chosen.reshape(pairs, directions, rank_k),
        preferred_element_type=jnp.float32,
    )
    row_pick = (far_slot[None, :] == jnp.arange(clusters, dtype=jnp.int32)[:, None]).astype(
        jnp.float32
    )
    gathered = jnp.dot(
        row_pick,
        coupled.reshape(pairs, -1),
        precision=lax.Precision.HIGHEST,
        preferred_element_type=jnp.float32,
    )
    gathered = gathered.astype(jnp.bfloat16).reshape(clusters, directions, rank_k)
    far_sum = jnp.einsum("crk,ckb->crb", gathered, basis_out, preferred_element_type=jnp.float32)
    return (near_sum + far_sum).astype(jnp.bfloat16)


def whole(space=pltpu.VMEM):
    return pl.BlockSpec(memory_space=space)


def prologue_kernel(
    count, me_ref, owner_ref, slot_ref, offset_ref, rhs_ref, basis_ref, payload_ref, list_ref
):
    clusters, directions, unknowns = rhs_ref.shape
    base = clusters * directions
    payload_ref[0:base, :] = rhs_ref[...].reshape(base, unknowns)
    rank_k = basis_ref.shape[1]
    half = clusters // 2
    rows = []
    for c in range(half):
        parts = [
            lax.dot_general(
                basis_ref[e],
                rhs_ref[e],
                (((1,), (1,)), ((), ())),
                preferred_element_type=jnp.float32,
            )
            for e in (c, c + half)
        ]
        rows.append(jnp.concatenate(parts, axis=1))
    rows = jnp.concatenate(rows, axis=0).astype(payload_ref.dtype)
    square = (rows.shape[0], rows.shape[0])
    row = lax.broadcasted_iota(jnp.int32, square, 0)
    source = (row & (half - 1)) * rank_k + row // half
    order = jnp.where(lax.broadcasted_iota(jnp.int32, square, 1) == source, 1.0, 0.0)
    payload_ref[base:, :] = jnp.dot(
        order.astype(rows.dtype), rows, preferred_element_type=jnp.float32
    ).astype(payload_ref.dtype)

    me, owner, slot = me_ref[0], owner_ref[...], slot_ref[...]
    stored = owner.shape[1]
    place = scatter_place(owner, me, count) * clusters + slot
    column = (owner * clusters + slot + offset_ref[...]) & (count * clusters - 1)
    shard = gather_place(column // clusters, me, count)
    theirs = (shard == count // 2).astype(jnp.int32)
    shard = jnp.where(theirs == 1, gather_place(column // clusters, me ^ 1, count), shard)
    column_place = shard * clusters + (column & (clusters - 1))
    late = (shard >= count // 2 - LATE).astype(jnp.int32)
    square = (stored, stored)
    group = jnp.broadcast_to((2 * theirs + late).astype(jnp.float32), square)
    group_of_row = jnp.transpose(group)
    row_at = lax.broadcasted_iota(jnp.int32, square, 0)
    lane_at = lax.broadcasted_iota(jnp.int32, square, 1)
    lane = lane_at.astype(jnp.float32)
    before = (group_of_row < group) | ((group_of_row == group) & (row_at < lane_at))
    rank = jnp.sum(jnp.where(before, 1.0, 0.0), axis=0, keepdims=True)
    rank = jnp.transpose(jnp.broadcast_to(rank, square))
    here = jnp.where(rank == lane, 1.0, 0.0).astype(jnp.bfloat16)
    starts = jnp.sum(jnp.where(group_of_row < lane, 1.0, 0.0), axis=0, keepdims=True)
    values = jnp.concatenate(
        [lane[0:1], place.astype(jnp.float32), column_place.astype(jnp.float32)]
        + [jnp.zeros((5, stored), jnp.float32)],
        axis=0,
    )
    values = jnp.dot(values.astype(jnp.bfloat16), here, preferred_element_type=jnp.float32)
    values = jnp.concatenate([values[0:3], starts, values[4:8]], axis=0)
    list_ref[...] = values.astype(jnp.int32)


def open_kernel(token_ref, sums):
    def clear(i, carry):
        sums[i] = jnp.zeros(sums.shape[1:], sums.dtype)
        return carry

    lax.fori_loop(0, sums.shape[0] - 1, clear, 0, unroll=8)
    clear(sums.shape[0] - 1, 0)


def near_kernel(late, batch, shards, sends, list_ref, *refs):
    used = LATE if late else shards
    shard_refs, refs = refs[:shards], refs[shards:]
    (own_ref, mate_hbm), refs = refs[:2], refs[3:]
    sums, refs = refs[0], refs[1:]
    if late:
        coef_ref, send_refs, (columns,) = refs[0], refs[1 : 1 + sends], refs[1 + sends :]
        blocks = mate_hbm
    else:
        blocks, columns, block_sem = refs
    stored = blocks.shape[0]
    directions = sums.shape[1]
    span = columns.shape[0] // used
    dummy = sums.shape[0] - 1
    chunk = stored // CHUNKS

    begin, end = list_ref[3, late], list_ref[3, late + 1]
    begin_there, end_there = list_ref[11, 2 + late], list_ref[11, 3 + late]
    if not late:
        for c in range(CHUNKS):
            at = pl.ds(c * chunk, chunk)
            pltpu.make_async_copy(mate_hbm.at[at], blocks.at[at], block_sem.at[c]).start()

    for k, ref in enumerate(shard_refs[shards - used :]):

        def gather(i, carry, k=k, ref=ref):
            at = pl.multiple_of(i * directions, directions)
            columns[pl.ds(pl.multiple_of(k * span + at, directions), directions)] = ref[
                pl.ds(at, directions)
            ]
            return carry

        lax.fori_loop(0, span // directions, gather, 0, unroll=8)
    if late:
        tail = coef_ref.shape[0] // shards
        for k, ref in enumerate(shard_refs):
            coef_ref[k * tail : (k + 1) * tail] = ref[span : span + tail]
    def run(begin, end, row, swap, block_of):
        def entry(j):
            return jnp.minimum(begin + j, end - 1)

        def body(step, carry):
            first = step * batch
            products = []

            def add(i):
                place = list_ref[row + 1, entry(first + i)] ^ swap
                place = jnp.where(begin + first + i < end, place, dummy)
                sums[place] = sums[place] + products[i]

            take, carry = block_of(first, entry, carry)
            for i in range(batch):
                start = list_ref[row + 2, entry(first + i)] * directions - (shards - used) * span
                products.append(
                    lax.dot_general(
                        columns[pl.ds(pl.multiple_of(start, directions), directions)],
                        take(i),
                        (((1,), (1,)), ((), ())),
                        preferred_element_type=jnp.float32,
                    )
                )
            for i in range(batch):
                add(i)
            return carry

        return lax.fori_loop(0, (end - begin + batch - 1) // batch, body, 0)

    def own_blocks(first, entry, carry):
        return lambda i: own_ref[list_ref[0, entry(first + i)]], carry

    def wait(c, carry):
        at = pl.ds(0, chunk)
        pltpu.make_async_copy(mate_hbm.at[at], blocks.at[at], block_sem.at[c]).wait()
        return carry

    def mate_blocks(first, entry, ready):
        take = lambda i: blocks[list_ref[8, entry(first + i)]]
        if late:
            return take, ready
        needed = list_ref[8, entry(first + batch - 1)] // chunk + 1
        lax.fori_loop(ready, needed, wait, 0)
        return take, jnp.maximum(ready, needed)

    run(begin, end, 0, 0, own_blocks)
    ready = run(begin_there, end_there, 8, dummy // 2, mate_blocks)
    if not late:
        lax.fori_loop(ready, CHUNKS, wait, 0)
        return
    at = dummy // 2
    for send_ref in send_refs:

        def pack(i, carry, at=at, send_ref=send_ref):
            send_ref[i] = sums[at + i].astype(send_ref.dtype)
            return carry

        lax.fori_loop(0, send_ref.shape[0], pack, 0, unroll=8)
        at += send_ref.shape[0]


def far_kernel(*refs):
    coef_refs = refs[:2]
    me_ref, couple_ref, slot_ref, dev_ref, cslot_ref, basis_ref, out_ref = refs[2:]
    clusters, rank_k, unknowns = basis_ref.shape
    pairs = couple_ref.shape[2]
    directions = out_ref.shape[1]
    half = clusters // 2
    coef = jnp.concatenate([ref[...].astype(jnp.float32) for ref in coef_refs], axis=0)
    coef = coef.reshape(-1, rank_k, half, unknowns)
    count = coef.shape[0]
    hot = (
        lax.broadcasted_iota(jnp.int32, (clusters, pairs), 0)
        == jnp.broadcast_to(slot_ref[...], (clusters, pairs))
    ).astype(jnp.float32).astype(jnp.bfloat16)
    away = gather_place(dev_ref[...], me_ref[0], count)
    theirs = count // 2 + gather_place(dev_ref[...], me_ref[0] ^ 1, count)
    away = jnp.where(away == count // 2, theirs, away)
    cslot = cslot_ref[...]
    high = (cslot >= half).astype(jnp.int32)
    at = away * half + cslot - high * half
    table_rows = (count * half, pairs)
    pick = jnp.where(
        lax.broadcasted_iota(jnp.int32, table_rows, 0) == jnp.broadcast_to(at, table_rows), 1.0, 0.0
    )
    pick = jnp.transpose(pick).astype(jnp.bfloat16)
    lanes = (unknowns, pairs)
    keep = jnp.where(
        lax.broadcasted_iota(jnp.int32, lanes, 0) // directions == jnp.broadcast_to(high, lanes),
        1.0,
        0.0,
    )
    keep = jnp.transpose(keep).astype(jnp.bfloat16)
    total = jnp.zeros((clusters * rank_k, unknowns), jnp.float32)
    for q in range(rank_k):
        table = coef[:, q].reshape(count * half, unknowns).astype(jnp.bfloat16)
        chosen = jnp.dot(pick, table, preferred_element_type=jnp.float32).astype(jnp.bfloat16)
        chosen = chosen * keep
        couple = couple_ref[q]
        weight = jnp.concatenate([couple * hot[s : s + 1] for s in range(clusters)], axis=0)
        total = total + jnp.dot(weight, chosen, preferred_element_type=jnp.float32)
    total = total + pltpu.roll(total, unknowns // 2, axis=1)
    gathered = jnp.transpose(total)[0:directions, :].astype(jnp.bfloat16).astype(jnp.float32)
    lane = lax.broadcasted_iota(jnp.int32, gathered.shape, 1) // rank_k
    basis = basis_ref[...].reshape(clusters * rank_k, unknowns)
    for s in range(clusters):
        own = jnp.where(lane == s, gathered, 0.0).astype(jnp.bfloat16)
        out_ref[s] = jnp.dot(own, basis, preferred_element_type=jnp.float32)


def ring_device(place, core, chips):
    depth = chips // 2
    place = place % chips
    z, y = (place, 0) if place < depth else (chips - 1 - place, 1)
    return (z * 2 + y) * 2 + core


def ring_pairs(count):
    chips = count // 2
    cores = [(p, c) for p in range(chips) for c in range(2)]
    ahead = [(ring_device(p, c, chips), ring_device(p + 1 - 2 * c, c, chips)) for p, c in cores]
    cross = [
        (ring_device(p, c, chips), ring_device(p - 1 + 2 * c, 1 - c, chips)) for p, c in cores
    ]
    return ahead, cross


def ring_place(device, chips):
    z, y = device >> 2, (device >> 1) & 1
    return jnp.where(y == 0, z, chips - 1 - z)


def gather_place(device, me, count):
    chips = count // 2
    depth = chips // 2
    back = (1 - 2 * (me & 1)) * (ring_place(me, chips) - ring_place(device, chips))
    back = (back + chips) & (chips - 1)
    other = (device ^ me) & 1
    here = (back < depth) & (back > 0) | (back == 0) & (other == 1) | (back == depth) & (other == 0)
    return jnp.where(here, jnp.where(back == 0, 0, 2 * back - 1 + other), chips)


def scatter_place(device, me, count):
    chips = count // 2
    depth = chips // 2
    ahead = (ring_place(device, chips) - ring_place(me, chips) + chips) & (chips - 1)
    core = device & 1
    handler = jnp.where((ahead & (depth - 1)) == 0, core, (ahead > depth).astype(jnp.int32))
    steps = jnp.where(handler == 0, ahead, (chips - ahead) & (chips - 1))
    place = jnp.where(
        steps == depth,
        0,
        jnp.where(steps == 0, chips - 1, 2 * (depth - steps) - (core ^ handler)),
    )
    return place + jnp.where(handler == (me & 1), 0, chips)


def stationary(
    rhs,
    near_blocks,
    near_owner,
    near_slot,
    near_offset,
    far_coupling,
    far_slot,
    far_dev,
    far_cslot,
    basis_out,
    basis_in,
):
    clusters, directions, unknowns = rhs.shape
    rank_k = basis_in.shape[1]
    count = lax.axis_size("blk")
    chips = count // 2
    depth = chips // 2
    me = lax.axis_index("blk")
    stored = near_blocks.shape[0]
    pairs = far_slot.shape[0]
    half = clusters // 2
    ahead, cross = ring_pairs(count)
    mate = [(i, i ^ 1) for i in range(count)]
    side = [(i, i ^ 2) for i in range(count)]

    def move(values, where):
        return lax.ppermute(values, "blk", where)

    def after(values, *others):
        return lax.optimization_barrier((values, *others))[0]

    here = me.astype(jnp.int32).reshape(1)
    base = clusters * directions
    payload, lists = pl.pallas_call(
        functools.partial(prologue_kernel, count),
        out_shape=[
            jax.ShapeDtypeStruct((base + half * rank_k, unknowns), jnp.bfloat16),
            jax.ShapeDtypeStruct((8, stored), jnp.int32),
        ],
        in_specs=[whole(pltpu.SMEM)] + [whole()] * 5,
        out_specs=[whole()] * 2,
        compiler_params=pltpu.CompilerParams(vmem_limit_bytes=PROLOGUE_VMEM),
        name="prologue",
    )(
        here,
        near_owner.reshape(1, stored),
        near_slot.reshape(1, stored),
        near_offset.reshape(1, stored),
        rhs,
        basis_in,
    )
    cost = pl.CostEstimate(
        flops=16 * stored * directions * unknowns * unknowns,
        bytes_accessed=16 << 20,
        transcendentals=0,
    )
    flow = [move(payload, ahead)]
    mate_blocks = move(near_blocks, mate)
    mate_lists = move(lists, mate)
    couple = jnp.transpose(far_coupling, (2, 1, 0))
    sums_shape = jax.ShapeDtypeStruct((count * clusters + 1, directions, unknowns), jnp.float32)
    sums = pl.pallas_call(
        open_kernel,
        out_shape=sums_shape,
        in_specs=[whole(pltpu.SMEM)],
        out_specs=whole(),
        compiler_params=pltpu.CompilerParams(vmem_limit_bytes=NEAR_VMEM),
        cost_estimate=cost,
        name="open",
    )(after(here, couple))
    flow.append(move(after(payload, couple, sums), cross))
    shards = [move(payload, mate)]
    flow[0], sums = lax.optimization_barrier((flow[0], sums))
    for k in range(1, chips):
        x = 1 - k % 2
        if k == 3:
            flow[x], mate_blocks, shards[0], mate_lists = lax.optimization_barrier(
                (flow[x], mate_blocks, shards[0], mate_lists)
            )
        if k == 4:
            lists = jnp.concatenate([after(lists, flow[x]), mate_lists], axis=0)
        if k == 5:
            flow[x], lists = lax.optimization_barrier((flow[x], lists))
        shards.append(flow[x])
        if k < chips - 2:
            flow[x] = move(flow[x], ahead)

    pieces = [2, chips - 2]

    def near(late, shards, theirs, sums):
        sends = pieces if late else []
        return pl.pallas_call(
            functools.partial(near_kernel, late, BATCH[late], len(shards), len(sends)),
            out_shape=[sums_shape]
            + [jax.ShapeDtypeStruct(near_blocks.shape, near_blocks.dtype)] * (1 - late)
            + [jax.ShapeDtypeStruct((chips * half * rank_k, unknowns), jnp.bfloat16)] * late
            + [
                jax.ShapeDtypeStruct((size * clusters, directions, unknowns), jnp.bfloat16)
                for size in sends
            ],
            in_specs=[whole(pltpu.SMEM)]
            + [whole()] * len(shards)
            + [whole(), whole() if late else whole(pl.ANY), whole()],
            out_specs=[whole()] * (2 + len(sends)),
            input_output_aliases={3 + len(shards): 0},
            scratch_shapes=[
                pltpu.VMEM(((LATE if late else len(shards)) * base, unknowns), jnp.bfloat16),
            ]
            + [pltpu.SemaphoreType.DMA((CHUNKS,))] * (1 - late),
            compiler_params=pltpu.CompilerParams(vmem_limit_bytes=NEAR_VMEM),
            cost_estimate=cost,
            name="near",
        )(lists, *shards, near_blocks, theirs, sums)

    def far_field(couple):
        return pl.pallas_call(
            far_kernel,
            out_shape=jax.ShapeDtypeStruct((clusters, directions, unknowns), jnp.float32),
            in_specs=[whole()] * 2 + [whole(pltpu.SMEM)] + [whole()] * 5,
            out_specs=whole(),
            compiler_params=pltpu.CompilerParams(vmem_limit_bytes=FAR_VMEM),
            cost_estimate=pl.CostEstimate(
                flops=4 * clusters * rank_k * pairs * rank_k * unknowns,
                bytes_accessed=8 << 20,
                transcendentals=0,
            ),
            name="far",
        )(
            *coefs,
            here,
            couple,
            far_slot.reshape(1, pairs),
            far_dev.reshape(1, pairs),
            far_cslot.reshape(1, pairs),
            basis_out,
        )

    sums, mate_blocks = near(0, shards[: chips - LATE], mate_blocks, sums)
    sums, coef, *sends = near(1, shards, mate_blocks, sums)
    mates = [move(sends[0], mate)]
    coefs = [coef, move(coef, mate)]

    piece = clusters // UNITS

    def term(k, h):
        part, at = (0, k) if k < 2 else (1, k - 2)
        got = mates[part][at * clusters + h * piece : at * clusters + (h + 1) * piece]
        at = k * clusters + h * piece
        return sums[at : at + piece] + got.astype(jnp.float32)

    flow = lax.optimization_barrier(
        [[term(k, h).astype(jnp.bfloat16) for h in range(UNITS)] for k in range(2)]
    )
    mates.append(move(after(sends[1], *flow[0], *flow[1]), mate))
    flow = [[move(unit, ahead) for unit in units] for units in flow]
    for k in range(2, chips - 1):
        for h in range(UNITS):
            unit = (flow[k % 2][h].astype(jnp.float32) + term(k, h)).astype(jnp.bfloat16)
            unit, mates[1] = lax.optimization_barrier((unit, mates[1]))
            if (k, h) == (chips - 2, UNITS - 1):
                couple = after(couple, unit)
            flow[k % 2][h] = move(unit, ahead)
    last = [move(unit, mate) for unit in flow[1]]
    own = sums[(chips - 1) * clusters : chips * clusters]
    total = far_field(couple) + own + mates[1][(chips - 3) * clusters :].astype(jnp.float32)
    total = total + jnp.concatenate(flow[0], axis=0).astype(jnp.float32)
    total = lax.optimization_barrier(total)
    return (total + jnp.concatenate(last, axis=0).astype(jnp.float32)).astype(jnp.bfloat16)


def on_device(*args):
    rhs, near_blocks = args[0], args[1]
    clusters, directions, unknowns = rhs.shape
    small = lax.axis_size("blk") == 16 and clusters == 16
    if small and near_blocks.shape[0] == unknowns and 2 * directions == unknowns:
        return stationary(*args)
    return routed(*args)


def solution(mesh):
    placed = (
        P(("groups", "blk"), None, None),
        P(("groups", "blk"), None, None),
        P(("groups", "blk"), None),
        P(("groups", "blk")),
        P(("groups", "blk")),
        P(("groups", "blk"), None, None),
        P(("groups", "blk")),
        P(("groups", "blk"), None),
        P(("groups", "blk")),
        P(("groups", "blk"), None, None),
        P(("groups", "blk"), None, None),
    )
    return jax.shard_map(
        on_device,
        mesh=mesh,
        in_specs=placed,
        out_specs=P(("groups", "blk"), None, None),
        check_vma=False,
    )
```

```python
import functools

import jax
import jax.numpy as jnp
from jax import lax
from jax.experimental import pallas as pl
from jax.experimental.pallas import tpu as pltpu
from jax.sharding import PartitionSpec as P

BATCH = 16, 8
CHUNKS = 4
LATE = 2
UNITS = 1
PROLOGUE_VMEM = 58 << 20
NEAR_VMEM = 20 << 20
FAR_VMEM = 16 << 20


def with_halo(cells, sides, width):
    for axis, dim in sides:
        count = lax.axis_size(axis)
        head = lax.slice_in_dim(cells, 0, width, axis=dim)
        tail = lax.slice_in_dim(cells, cells.shape[dim] - width, cells.shape[dim], axis=dim)
        cells = jnp.concatenate(
            [
                lax.ppermute(tail, axis, [(i, (i + 1) % count) for i in range(count)]),
                cells,
                lax.ppermute(head, axis, [((i + 1) % count, i) for i in range(count)]),
            ],
            axis=dim,
        )
    return cells


def place_ranks(targets, count):
    onehot = (targets[:, None] == jnp.arange(count, dtype=jnp.int32)[None, :]).astype(jnp.int32)
    before = jnp.cumsum(onehot, axis=0) - onehot
    return jnp.sum(before * onehot, axis=1)


def routed(
    rhs,
    near_blocks,
    near_owner,
    near_slot,
    near_offset,
    far_coupling,
    far_slot,
    far_dev,
    far_cslot,
    basis_out,
    basis_in,
):
    clusters = rhs.shape[0]
    directions = rhs.shape[1]
    unknowns = rhs.shape[2]
    cycle_size = lax.axis_size("blk")
    stored = near_blocks.shape[0]
    capacity = max(2, 2 * stored // cycle_size)
    owners = near_owner[:, 0]
    target = owners * capacity + place_ranks(owners, cycle_size)
    outbox = (
        jnp.zeros((cycle_size * capacity, unknowns, unknowns), near_blocks.dtype)
        .at[target]
        .set(near_blocks)
    )
    labels = (
        jnp.zeros((cycle_size * capacity, 2), jnp.int32)
        .at[target]
        .set(jnp.stack([near_slot, near_offset], axis=1))
    )
    window = with_halo(rhs, (("blk", 0),), clusters)
    inbox, in_labels = (
        lax.all_to_all(outbox, "blk", split_axis=0, concat_axis=0, tiled=True),
        lax.all_to_all(labels, "blk", split_axis=0, concat_axis=0, tiled=True),
    )
    position = clusters + in_labels[:, 0] + in_labels[:, 1]
    columns = jnp.take(window, position, axis=0)
    products = jnp.einsum("srj,sij->sri", columns, inbox, preferred_element_type=jnp.float32)
    selector = (in_labels[:, 0][None, :] == jnp.arange(clusters, dtype=jnp.int32)[:, None]).astype(
        jnp.float32
    )
    near_sum = jnp.dot(
        selector,
        products.reshape(products.shape[0], -1),
        precision=lax.Precision.HIGHEST,
        preferred_element_type=jnp.float32,
    ).reshape(clusters, directions, unknowns)
    coef_local = jnp.einsum(
        "ckj,crj->crk", basis_in, rhs, preferred_element_type=jnp.float32
    ).astype(jnp.bfloat16)
    rank_k = basis_in.shape[1]
    coef_local = coef_local.reshape(clusters, directions * rank_k)
    pairs = far_slot.shape[0]
    wanted = far_dev[:, 0] * clusters + far_cslot
    piece = lax.all_gather(coef_local, "blk", axis=0, tiled=True)
    chosen = jnp.take(piece, wanted, axis=0)
    coupled = jnp.einsum(
        "pkq,prq->prk",
        far_coupling,
        chosen.reshape(pairs, directions, rank_k),
        preferred_element_type=jnp.float32,
    )
    row_pick = (far_slot[None, :] == jnp.arange(clusters, dtype=jnp.int32)[:, None]).astype(
        jnp.float32
    )
    gathered = jnp.dot(
        row_pick,
        coupled.reshape(pairs, -1),
        precision=lax.Precision.HIGHEST,
        preferred_element_type=jnp.float32,
    )
    gathered = gathered.astype(jnp.bfloat16).reshape(clusters, directions, rank_k)
    far_sum = jnp.einsum("crk,ckb->crb", gathered, basis_out, preferred_element_type=jnp.float32)
    return (near_sum + far_sum).astype(jnp.bfloat16)


def whole(space=pltpu.VMEM):
    return pl.BlockSpec(memory_space=space)


def prologue_kernel(
    count, me_ref, owner_ref, slot_ref, offset_ref, rhs_ref, basis_ref, payload_ref, list_ref
):
    clusters, directions, unknowns = rhs_ref.shape
    base = clusters * directions
    payload_ref[0:base, :] = rhs_ref[...].reshape(base, unknowns)
    rank_k = basis_ref.shape[1]
    half = clusters // 2
    rows = []
    for c in range(half):
        parts = [
            lax.dot_general(
                basis_ref[e],
                rhs_ref[e],
                (((1,), (1,)), ((), ())),
                preferred_element_type=jnp.float32,
            )
            for e in (c, c + half)
        ]
        rows.append(jnp.concatenate(parts, axis=1))
    rows = jnp.concatenate(rows, axis=0).astype(payload_ref.dtype)
    square = (rows.shape[0], rows.shape[0])
    row = lax.broadcasted_iota(jnp.int32, square, 0)
    source = (row & (half - 1)) * rank_k + row // half
    order = jnp.where(lax.broadcasted_iota(jnp.int32, square, 1) == source, 1.0, 0.0)
    payload_ref[base:, :] = jnp.dot(
        order.astype(rows.dtype), rows, preferred_element_type=jnp.float32
    ).astype(payload_ref.dtype)

    me, owner, slot = me_ref[0], owner_ref[...], slot_ref[...]
    stored = owner.shape[1]
    place = scatter_place(owner, me, count) * clusters + slot
    column = (owner * clusters + slot + offset_ref[...]) & (count * clusters - 1)
    shard = gather_place(column // clusters, me, count)
    theirs = (shard == count // 2).astype(jnp.int32)
    shard = jnp.where(theirs == 1, gather_place(column // clusters, me ^ 1, count), shard)
    column_place = shard * clusters + (column & (clusters - 1))
    late = (shard >= count // 2 - LATE).astype(jnp.int32)
    square = (stored, stored)
    group = jnp.broadcast_to((2 * theirs + late).astype(jnp.float32), square)
    group_of_row = jnp.transpose(group)
    row_at = lax.broadcasted_iota(jnp.int32, square, 0)
    lane_at = lax.broadcasted_iota(jnp.int32, square, 1)
    lane = lane_at.astype(jnp.float32)
    before = (group_of_row < group) | ((group_of_row == group) & (row_at < lane_at))
    rank = jnp.sum(jnp.where(before, 1.0, 0.0), axis=0, keepdims=True)
    rank = jnp.transpose(jnp.broadcast_to(rank, square))
    here = jnp.where(rank == lane, 1.0, 0.0).astype(jnp.bfloat16)
    starts = jnp.sum(jnp.where(group_of_row < lane, 1.0, 0.0), axis=0, keepdims=True)
    values = jnp.concatenate(
        [lane[0:1], place.astype(jnp.float32), column_place.astype(jnp.float32)]
        + [jnp.zeros((5, stored), jnp.float32)],
        axis=0,
    )
    values = jnp.dot(values.astype(jnp.bfloat16), here, preferred_element_type=jnp.float32)
    values = jnp.concatenate([values[0:3], starts, values[4:8]], axis=0)
    list_ref[...] = values.astype(jnp.int32)


def open_kernel(token_ref, sums):
    def clear(i, carry):
        sums[i] = jnp.zeros(sums.shape[1:], sums.dtype)
        return carry

    lax.fori_loop(0, sums.shape[0] - 1, clear, 0, unroll=8)
    clear(sums.shape[0] - 1, 0)


def near_kernel(late, batch, shards, sends, list_ref, *refs):
    used = LATE if late else shards
    shard_refs, refs = refs[:shards], refs[shards:]
    (own_ref, mate_hbm), refs = refs[:2], refs[3:]
    sums, refs = refs[0], refs[1:]
    if late:
        coef_ref, send_refs, (columns,) = refs[0], refs[1 : 1 + sends], refs[1 + sends :]
        blocks = mate_hbm
    else:
        blocks, columns, block_sem = refs
    stored = blocks.shape[0]
    directions = sums.shape[1]
    span = columns.shape[0] // used
    dummy = sums.shape[0] - 1
    chunk = stored // CHUNKS

    begin, end = list_ref[3, late], list_ref[3, late + 1]
    begin_there, end_there = list_ref[11, 2 + late], list_ref[11, 3 + late]
    if not late:
        for c in range(CHUNKS):
            at = pl.ds(c * chunk, chunk)
            pltpu.make_async_copy(mate_hbm.at[at], blocks.at[at], block_sem.at[c]).start()

    for k, ref in enumerate(shard_refs[shards - used :]):

        def gather(i, carry, k=k, ref=ref):
            at = pl.multiple_of(i * directions, directions)
            columns[pl.ds(pl.multiple_of(k * span + at, directions), directions)] = ref[
                pl.ds(at, directions)
            ]
            return carry

        lax.fori_loop(0, span // directions, gather, 0, unroll=8)
    if late:
        tail = coef_ref.shape[0] // shards
        for k, ref in enumerate(shard_refs):
            coef_ref[k * tail : (k + 1) * tail] = ref[span : span + tail]
    def run(begin, end, row, swap, block_of):
        def entry(j):
            return jnp.minimum(begin + j, end - 1)

        def body(step, carry):
            first = step * batch
            products = []

            def add(i):
                place = list_ref[row + 1, entry(first + i)] ^ swap
                place = jnp.where(begin + first + i < end, place, dummy)
                sums[place] = sums[place] + products[i]

            take, carry = block_of(first, entry, carry)
            for i in range(batch):
                start = list_ref[row + 2, entry(first + i)] * directions - (shards - used) * span
                products.append(
                    lax.dot_general(
                        columns[pl.ds(pl.multiple_of(start, directions), directions)],
                        take(i),
                        (((1,), (1,)), ((), ())),
                        preferred_element_type=jnp.float32,
                    )
                )
            for i in range(batch):
                add(i)
            return carry

        return lax.fori_loop(0, (end - begin + batch - 1) // batch, body, 0)

    def own_blocks(first, entry, carry):
        return lambda i: own_ref[list_ref[0, entry(first + i)]], carry

    def wait(c, carry):
        at = pl.ds(0, chunk)
        pltpu.make_async_copy(mate_hbm.at[at], blocks.at[at], block_sem.at[c]).wait()
        return carry

    def mate_blocks(first, entry, ready):
        take = lambda i: blocks[list_ref[8, entry(first + i)]]
        if late:
            return take, ready
        needed = list_ref[8, entry(first + batch - 1)] // chunk + 1
        lax.fori_loop(ready, needed, wait, 0)
        return take, jnp.maximum(ready, needed)

    run(begin, end, 0, 0, own_blocks)
    ready = run(begin_there, end_there, 8, dummy // 2, mate_blocks)
    if not late:
        lax.fori_loop(ready, CHUNKS, wait, 0)
        return
    at = dummy // 2
    for send_ref in send_refs:

        def pack(i, carry, at=at, send_ref=send_ref):
            send_ref[i] = sums[at + i].astype(send_ref.dtype)
            return carry

        lax.fori_loop(0, send_ref.shape[0], pack, 0, unroll=16)
        at += send_ref.shape[0]


def far_kernel(*refs):
    coef_refs = refs[:2]
    me_ref, couple_ref, slot_ref, dev_ref, cslot_ref, basis_ref, out_ref = refs[2:]
    clusters, rank_k, unknowns = basis_ref.shape
    pairs = couple_ref.shape[2]
    directions = out_ref.shape[1]
    half = clusters // 2
    coef = jnp.concatenate([ref[...].astype(jnp.float32) for ref in coef_refs], axis=0)
    coef = coef.reshape(-1, rank_k, half, unknowns)
    count = coef.shape[0]
    hot = (
        lax.broadcasted_iota(jnp.int32, (clusters, pairs), 0)
        == jnp.broadcast_to(slot_ref[...], (clusters, pairs))
    ).astype(jnp.float32).astype(jnp.bfloat16)
    away = gather_place(dev_ref[...], me_ref[0], count)
    theirs = count // 2 + gather_place(dev_ref[...], me_ref[0] ^ 1, count)
    away = jnp.where(away == count // 2, theirs, away)
    cslot = cslot_ref[...]
    high = (cslot >= half).astype(jnp.int32)
    at = away * half + cslot - high * half
    table_rows = (count * half, pairs)
    pick = jnp.where(
        lax.broadcasted_iota(jnp.int32, table_rows, 0) == jnp.broadcast_to(at, table_rows), 1.0, 0.0
    )
    pick = jnp.transpose(pick).astype(jnp.bfloat16)
    lanes = (unknowns, pairs)
    keep = jnp.where(
        lax.broadcasted_iota(jnp.int32, lanes, 0) // directions == jnp.broadcast_to(high, lanes),
        1.0,
        0.0,
    )
    keep = jnp.transpose(keep).astype(jnp.bfloat16)
    total = jnp.zeros((clusters * rank_k, unknowns), jnp.float32)
    for q in range(rank_k):
        table = coef[:, q].reshape(count * half, unknowns).astype(jnp.bfloat16)
        chosen = jnp.dot(pick, table, preferred_element_type=jnp.float32).astype(jnp.bfloat16)
        chosen = chosen * keep
        couple = couple_ref[q]
        weight = jnp.concatenate([couple * hot[s : s + 1] for s in range(clusters)], axis=0)
        total = total + jnp.dot(weight, chosen, preferred_element_type=jnp.float32)
    total = total + pltpu.roll(total, unknowns // 2, axis=1)
    gathered = jnp.transpose(total)[0:directions, :].astype(jnp.bfloat16).astype(jnp.float32)
    lane = lax.broadcasted_iota(jnp.int32, gathered.shape, 1) // rank_k
    basis = basis_ref[...].reshape(clusters * rank_k, unknowns)
    for s in range(clusters):
        own = jnp.where(lane == s, gathered, 0.0).astype(jnp.bfloat16)
        out_ref[s] = jnp.dot(own, basis, preferred_element_type=jnp.float32)


def ring_device(place, core, chips):
    depth = chips // 2
    place = place % chips
    z, y = (place, 0) if place < depth else (chips - 1 - place, 1)
    return (z * 2 + y) * 2 + core


def ring_pairs(count):
    chips = count // 2
    cores = [(p, c) for p in range(chips) for c in range(2)]
    ahead = [(ring_device(p, c, chips), ring_device(p + 1 - 2 * c, c, chips)) for p, c in cores]
    cross = [
        (ring_device(p, c, chips), ring_device(p - 1 + 2 * c, 1 - c, chips)) for p, c in cores
    ]
    return ahead, cross


def ring_place(device, chips):
    z, y = device >> 2, (device >> 1) & 1
    return jnp.where(y == 0, z, chips - 1 - z)


def gather_place(device, me, count):
    chips = count // 2
    depth = chips // 2
    back = (1 - 2 * (me & 1)) * (ring_place(me, chips) - ring_place(device, chips))
    back = (back + chips) & (chips - 1)
    other = (device ^ me) & 1
    here = (back < depth) & (back > 0) | (back == 0) & (other == 1) | (back == depth) & (other == 0)
    return jnp.where(here, jnp.where(back == 0, 0, 2 * back - 1 + other), chips)


def scatter_place(device, me, count):
    chips = count // 2
    depth = chips // 2
    ahead = (ring_place(device, chips) - ring_place(me, chips) + chips) & (chips - 1)
    core = device & 1
    handler = jnp.where((ahead & (depth - 1)) == 0, core, (ahead > depth).astype(jnp.int32))
    steps = jnp.where(handler == 0, ahead, (chips - ahead) & (chips - 1))
    place = jnp.where(
        steps == depth,
        0,
        jnp.where(steps == 0, chips - 1, 2 * (depth - steps) - (core ^ handler)),
    )
    return place + jnp.where(handler == (me & 1), 0, chips)


def stationary(
    rhs,
    near_blocks,
    near_owner,
    near_slot,
    near_offset,
    far_coupling,
    far_slot,
    far_dev,
    far_cslot,
    basis_out,
    basis_in,
):
    clusters, directions, unknowns = rhs.shape
    rank_k = basis_in.shape[1]
    count = lax.axis_size("blk")
    chips = count // 2
    depth = chips // 2
    me = lax.axis_index("blk")
    stored = near_blocks.shape[0]
    pairs = far_slot.shape[0]
    half = clusters // 2
    ahead, cross = ring_pairs(count)
    mate = [(i, i ^ 1) for i in range(count)]
    side = [(i, i ^ 2) for i in range(count)]

    def move(values, where):
        return lax.ppermute(values, "blk", where)

    def after(values, *others):
        return lax.optimization_barrier((values, *others))[0]

    here = me.astype(jnp.int32).reshape(1)
    base = clusters * directions
    payload, lists = pl.pallas_call(
        functools.partial(prologue_kernel, count),
        out_shape=[
            jax.ShapeDtypeStruct((base + half * rank_k, unknowns), jnp.bfloat16),
            jax.ShapeDtypeStruct((8, stored), jnp.int32),
        ],
        in_specs=[whole(pltpu.SMEM)] + [whole()] * 5,
        out_specs=[whole()] * 2,
        compiler_params=pltpu.CompilerParams(vmem_limit_bytes=PROLOGUE_VMEM),
        name="prologue",
    )(
        here,
        near_owner.reshape(1, stored),
        near_slot.reshape(1, stored),
        near_offset.reshape(1, stored),
        rhs,
        basis_in,
    )
    cost = pl.CostEstimate(
        flops=16 * stored * directions * unknowns * unknowns,
        bytes_accessed=16 << 20,
        transcendentals=0,
    )
    flow = [move(payload, ahead)]
    mate_blocks = move(near_blocks, mate)
    mate_lists = move(lists, mate)
    couple = jnp.transpose(far_coupling, (2, 1, 0))
    sums_shape = jax.ShapeDtypeStruct((count * clusters + 1, directions, unknowns), jnp.float32)
    sums = pl.pallas_call(
        open_kernel,
        out_shape=sums_shape,
        in_specs=[whole(pltpu.SMEM)],
        out_specs=whole(),
        compiler_params=pltpu.CompilerParams(vmem_limit_bytes=NEAR_VMEM),
        cost_estimate=cost,
        name="open",
    )(after(here, couple))
    flow.append(move(after(payload, couple, sums), cross))
    shards = [move(payload, mate)]
    flow[0], sums = lax.optimization_barrier((flow[0], sums))
    for k in range(1, chips):
        x = 1 - k % 2
        if k == 3:
            flow[x], mate_blocks, shards[0], mate_lists = lax.optimization_barrier(
                (flow[x], mate_blocks, shards[0], mate_lists)
            )
        if k == 4:
            lists = jnp.concatenate([after(lists, flow[x]), mate_lists], axis=0)
        if k == 5:
            flow[x], lists = lax.optimization_barrier((flow[x], lists))
        shards.append(flow[x])
        if k < chips - 2:
            flow[x] = move(flow[x], ahead)

    pieces = [2, chips - 2]

    def near(late, shards, theirs, sums):
        sends = pieces if late else []
        return pl.pallas_call(
            functools.partial(near_kernel, late, BATCH[late], len(shards), len(sends)),
            out_shape=[sums_shape]
            + [jax.ShapeDtypeStruct(near_blocks.shape, near_blocks.dtype)] * (1 - late)
            + [jax.ShapeDtypeStruct((chips * half * rank_k, unknowns), jnp.bfloat16)] * late
            + [
                jax.ShapeDtypeStruct((size * clusters, directions, unknowns), jnp.bfloat16)
                for size in sends
            ],
            in_specs=[whole(pltpu.SMEM)]
            + [whole()] * len(shards)
            + [whole(), whole() if late else whole(pl.ANY), whole()],
            out_specs=[whole()] * (2 + len(sends)),
            input_output_aliases={3 + len(shards): 0},
            scratch_shapes=[
                pltpu.VMEM(((LATE if late else len(shards)) * base, unknowns), jnp.bfloat16),
            ]
            + [pltpu.SemaphoreType.DMA((CHUNKS,))] * (1 - late),
            compiler_params=pltpu.CompilerParams(vmem_limit_bytes=NEAR_VMEM),
            cost_estimate=cost,
            name="near",
        )(lists, *shards, near_blocks, theirs, sums)

    def far_field(couple):
        return pl.pallas_call(
            far_kernel,
            out_shape=jax.ShapeDtypeStruct((clusters, directions, unknowns), jnp.float32),
            in_specs=[whole()] * 2 + [whole(pltpu.SMEM)] + [whole()] * 5,
            out_specs=whole(),
            compiler_params=pltpu.CompilerParams(vmem_limit_bytes=FAR_VMEM),
            cost_estimate=pl.CostEstimate(
                flops=4 * clusters * rank_k * pairs * rank_k * unknowns,
                bytes_accessed=8 << 20,
                transcendentals=0,
            ),
            name="far",
        )(
            *coefs,
            here,
            couple,
            far_slot.reshape(1, pairs),
            far_dev.reshape(1, pairs),
            far_cslot.reshape(1, pairs),
            basis_out,
        )

    sums, mate_blocks = near(0, shards[: chips - LATE], mate_blocks, sums)
    sums, coef, *sends = near(1, shards, mate_blocks, sums)
    mates = [move(sends[0], mate)]
    coefs = [coef, move(coef, mate)]

    piece = clusters // UNITS

    def term(k, h):
        part, at = (0, k) if k < 2 else (1, k - 2)
        got = mates[part][at * clusters + h * piece : at * clusters + (h + 1) * piece]
        at = k * clusters + h * piece
        return sums[at : at + piece] + got.astype(jnp.float32)

    flow = lax.optimization_barrier(
        [[term(k, h).astype(jnp.bfloat16) for h in range(UNITS)] for k in range(2)]
    )
    mates.append(move(after(sends[1], *flow[0], *flow[1]), mate))
    flow = [[move(unit, ahead) for unit in units] for units in flow]
    for k in range(2, chips - 1):
        for h in range(UNITS):
            unit = (flow[k % 2][h].astype(jnp.float32) + term(k, h)).astype(jnp.bfloat16)
            unit, mates[1] = lax.optimization_barrier((unit, mates[1]))
            if (k, h) == (chips - 2, UNITS - 1):
                couple = after(couple, unit)
            flow[k % 2][h] = move(unit, ahead)
    last = [move(unit, mate) for unit in flow[1]]
    own = sums[(chips - 1) * clusters : chips * clusters]
    total = far_field(couple) + own + mates[1][(chips - 3) * clusters :].astype(jnp.float32)
    total = total + jnp.concatenate(flow[0], axis=0).astype(jnp.float32)
    total = lax.optimization_barrier(total)
    return (total + jnp.concatenate(last, axis=0).astype(jnp.float32)).astype(jnp.bfloat16)


def on_device(*args):
    rhs, near_blocks = args[0], args[1]
    clusters, directions, unknowns = rhs.shape
    small = lax.axis_size("blk") == 16 and clusters == 16
    if small and near_blocks.shape[0] == unknowns and 2 * directions == unknowns:
        return stationary(*args)
    return routed(*args)


def solution(mesh):
    placed = (
        P(("groups", "blk"), None, None),
        P(("groups", "blk"), None, None),
        P(("groups", "blk"), None),
        P(("groups", "blk")),
        P(("groups", "blk")),
        P(("groups", "blk"), None, None),
        P(("groups", "blk")),
        P(("groups", "blk"), None),
        P(("groups", "blk")),
        P(("groups", "blk"), None, None),
        P(("groups", "blk"), None, None),
    )
    return jax.shard_map(
        on_device,
        mesh=mesh,
        in_specs=placed,
        out_specs=P(("groups", "blk"), None, None),
        check_vma=False,
    )
```
